32 devices in a mesh: row: 4 (over y, x), col: 8 (over z, core).
Axes of the slice: x: 2, y: 2, z: 4, core: 2. Of those that a mesh axis runs over, the one named last changes fastest.
Arguments:
- patches: bfloat16 [192, 196, 768], P(('row', 'col')), may hold values from -6 to 6
- shuffle: int32 [192, 196], P(('row', 'col')), may hold values from 0 to 195, each once within a row
- enc_w: float32 [768, 3840], P('row', 'col'), may hold values from -0.21875 to 0.21875
- enc_ffn: float32 [2, 768, 3072], P(None, 'row', 'col'), may hold values from -0.21875 to 0.21875
- dec_proj: float32 [768, 512], P('row', 'col'), may hold values from -0.21875 to 0.21875
- dec_w: float32 [512, 2048], P('row', 'col'), may hold values from -0.25 to 0.25
- dec_ffn: float32 [2, 512, 2048], P(None, 'row', 'col'), may hold values from -0.25 to 0.25
- head_w: float32 [512, 768], replicated, may hold values from -0.25 to 0.25
- smalls: float32 [21248], replicated, may hold values from 0.5 to 1.5
- first_enc_w: float32 [768, 3840], P('row', 'col'), may hold values from -0.00012207031 to 0.00012207031
- first_enc_ffn: float32 [2, 768, 3072], P(None, 'row', 'col'), may hold values from -0.00012207031 to 0.00012207031
- first_dec_proj: float32 [768, 512], P('row', 'col'), may hold values from -0.00012207031 to 0.00012207031
- first_dec_w: float32 [512, 2048], P('row', 'col'), may hold values from -0.00012207031 to 0.00012207031
- first_dec_ffn: float32 [2, 512, 2048], P(None, 'row', 'col'), may hold values from -0.00012207031 to 0.00012207031
- first_head_w: float32 [512, 768], replicated, may hold values from -0.00012207031 to 0.00012207031
- first_smalls: float32 [21248], replicated, may hold values from -0.0014648438 to 0.0014648438
- second_enc_w: float32 [768, 3840], P('row', 'col'), may hold values from 5.406317e-10 to 2.1625268e-09
- second_enc_ffn: float32 [2, 768, 3072], P(None, 'row', 'col'), may hold values from 5.406317e-10 to 2.1625268e-09
- second_dec_proj: float32 [768, 512], P('row', 'col'), may hold values from 5.406317e-10 to 2.1625268e-09
- second_dec_w: float32 [512, 2048], P('row', 'col'), may hold values from 5.406317e-10 to 2.1625268e-09
- second_dec_ffn: float32 [2, 512, 2048], P(None, 'row', 'col'), may hold values from 5.406317e-10 to 2.1625268e-09
- second_head_w: float32 [512, 768], replicated, may hold values from 5.406317e-10 to 2.1625268e-09
- second_smalls: float32 [21248], replicated, may hold values from 5.4063168e-08 to 2.1625267e-07
Outputs:
- new_enc_w: float32 [768, 3840], P('row', 'col')
- new_enc_ffn: float32 [2, 768, 3072], P(None, 'row', 'col')
- new_dec_proj: float32 [768, 512], P('row', 'col')
- new_dec_w: float32 [512, 2048], P('row', 'col')
- new_dec_ffn: float32 [2, 512, 2048], P(None, 'row', 'col')
- new_head_w: float32 [512, 768], replicated
- new_smalls: float32 [21248], replicated
- moment_enc_w: float32 [768, 3840], P('row', 'col')
- moment_enc_ffn: float32 [2, 768, 3072], P(None, 'row', 'col')
- moment_dec_proj: float32 [768, 512], P('row', 'col')
- moment_dec_w: float32 [512, 2048], P('row', 'col')
- moment_dec_ffn: float32 [2, 512, 2048], P(None, 'row', 'col')
- moment_head_w: float32 [512, 768], replicated
- moment_smalls: float32 [21248], replicated
- square_enc_w: float32 [768, 3840], P('row', 'col')
- square_enc_ffn: float32 [2, 768, 3072], P(None, 'row', 'col')
- square_dec_proj: float32 [768, 512], P('row', 'col')
- square_dec_w: float32 [512, 2048], P('row', 'col')
- square_dec_ffn: float32 [2, 512, 2048], P(None, 'row', 'col')
- square_head_w: float32 [512, 768], replicated
- square_smalls: float32 [21248], replicated
- loss: float32 [], replicated
The draws below stay inside these ranges and needn't reach their ends.
Inputs may be any that keep to these rules, and one draw needn't show every extreme that they name: `shuffle`: each image's row names every patch index once.
All inputs are finite; a program needn't handle non-finite values.
Results may differ from the reference program's by a relative error of at most 0.00095.
The reference program's roundings to bfloat16 on the way count: a program that leaves them out, or rounds other values in their place, can miss the bound.
Values may be sent and summed in bfloat16 or wider, within the bound.
A program may use at most 256 MiB of HBM per device.

```python
import math
import jax
import jax.numpy as jnp
from jax import lax

D = 768
HE = 12
F = 3072
E = 512
HD = 16
H = 2048
P_SIZE = 768
SIDE = 14
KEEP = 49
STEP = 5
PATCHES = 196
MASKED = 147
IMAGES = 192
NS = 21248


def shard_levels(rng, shape, cuts, low, high):
    def one(position, parts):
        draws = jax.random.uniform(jax.random.fold_in(jax.random.fold_in(rng, 6), position), (parts,), jnp.float32, low / len(cuts), high / len(cuts))
        return jnp.repeat(jnp.exp(draws), shape[position] // parts).reshape((-1,) + (1,) * (len(shape) - position - 1))

    level = one(*cuts[0])
    for cut in cuts[1:]:
        level = level * one(*cut)
    return level


def scatter_about(rng, shape, scale, limit, cuts=(), kind=jnp.bfloat16):
    level = shard_levels(rng, shape, cuts, -0.22, 0.18) if cuts else 1.0
    result = jax.random.normal(rng, shape, jnp.float32) * scale * level
    return jnp.minimum(jnp.maximum(result, -limit), limit).astype(kind)


def setup_inputs(seed: int = 0) -> dict:
    key_list = jax.random.split(jax.random.key(seed), 24)
    return {
        "patches": scatter_about(key_list[0], (IMAGES, PATCHES, P_SIZE), 1.0, 6.0, ((0, 32),)),
        "shuffle": jax.vmap(lambda own: jax.random.permutation(own, PATCHES))(jax.random.split(key_list[1], IMAGES)).reshape((IMAGES, PATCHES)).astype(jnp.int32),
        "enc_w": scatter_about(key_list[2], (D, 5 * D), D ** -0.5, 0.21875, ((0, 4), (1, 8)), jnp.float32),
        "enc_ffn": scatter_about(key_list[3], (2, D, F), D ** -0.5, 0.21875, ((1, 4), (2, 8)), jnp.float32),
        "dec_proj": scatter_about(key_list[4], (D, E), D ** -0.5, 0.21875, ((0, 4), (1, 8)), jnp.float32),
        "dec_w": scatter_about(key_list[5], (E, 4 * E), E ** -0.5, 0.25, ((0, 4), (1, 8)), jnp.float32),
        "dec_ffn": scatter_about(key_list[6], (2, E, H), E ** -0.5, 0.25, ((1, 4), (2, 8)), jnp.float32),
        "head_w": scatter_about(key_list[7], (E, P_SIZE), E ** -0.5, 0.25, (), jnp.float32),
        "smalls": jnp.clip(jax.random.uniform(key_list[8], (NS,), jnp.float32, 0.5, 1.5), 0.5, 1.5),
        "first_enc_w": scatter_about(key_list[9], (D, 5 * D), (3.0 / (P_SIZE * (IMAGES * MASKED) ** 0.5)), 0.00012207031, ((0, 4), (1, 8)), jnp.float32),
        "first_enc_ffn": scatter_about(key_list[10], (2, D, F), (3.0 / (P_SIZE * (IMAGES * MASKED) ** 0.5)), 0.00012207031, ((1, 4), (2, 8)), jnp.float32),
        "first_dec_proj": scatter_about(key_list[11], (D, E), (3.0 / (P_SIZE * (IMAGES * MASKED) ** 0.5)), 0.00012207031, ((0, 4), (1, 8)), jnp.float32),
        "first_dec_w": scatter_about(key_list[12], (E, 4 * E), (3.0 / (P_SIZE * (IMAGES * MASKED) ** 0.5)), 0.00012207031, ((0, 4), (1, 8)), jnp.float32),
        "first_dec_ffn": scatter_about(key_list[13], (2, E, H), (3.0 / (P_SIZE * (IMAGES * MASKED) ** 0.5)), 0.00012207031, ((1, 4), (2, 8)), jnp.float32),
        "first_head_w": scatter_about(key_list[14], (E, P_SIZE), (3.0 / (P_SIZE * (IMAGES * MASKED) ** 0.5)), 0.00012207031, (), jnp.float32),
        "first_smalls": scatter_about(key_list[15], (NS,), (30.0 / (P_SIZE * (IMAGES * MASKED) ** 0.5)), 0.0014648438, (), jnp.float32),
        "second_enc_w": jnp.clip(jnp.exp(math.log(2.1625268242786433e-09) - 1.3862944 * jax.random.uniform(key_list[16], (D, 5 * D), jnp.float32) ** shard_levels(key_list[16], (D, 5 * D), ((0, 4), (1, 8)), -0.2, 0.2)), 5.406317060696608e-10, 2.1625268242786433e-09),
        "second_enc_ffn": jnp.clip(jnp.exp(math.log(2.1625268242786433e-09) - 1.3862944 * jax.random.uniform(key_list[17], (2, D, F), jnp.float32) ** shard_levels(key_list[17], (2, D, F), ((1, 4), (2, 8)), -0.2, 0.2)), 5.406317060696608e-10, 2.1625268242786433e-09),
        "second_dec_proj": jnp.clip(jnp.exp(math.log(2.1625268242786433e-09) - 1.3862944 * jax.random.uniform(key_list[18], (D, E), jnp.float32) ** shard_levels(key_list[18], (D, E), ((0, 4), (1, 8)), -0.2, 0.2)), 5.406317060696608e-10, 2.1625268242786433e-09),
        "second_dec_w": jnp.clip(jnp.exp(math.log(2.1625268242786433e-09) - 1.3862944 * jax.random.uniform(key_list[19], (E, 4 * E), jnp.float32) ** shard_levels(key_list[19], (E, 4 * E), ((0, 4), (1, 8)), -0.2, 0.2)), 5.406317060696608e-10, 2.1625268242786433e-09),
        "second_dec_ffn": jnp.clip(jnp.exp(math.log(2.1625268242786433e-09) - 1.3862944 * jax.random.uniform(key_list[20], (2, E, H), jnp.float32) ** shard_levels(key_list[20], (2, E, H), ((1, 4), (2, 8)), -0.2, 0.2)), 5.406317060696608e-10, 2.1625268242786433e-09),
        "second_head_w": jnp.clip(jnp.exp(jax.random.uniform(key_list[21], (E, P_SIZE), jnp.float32, math.log(5.406317060696608e-10), math.log(2.1625268242786433e-09))), 5.406317060696608e-10, 2.1625268242786433e-09),
        "second_smalls": jnp.clip(jnp.exp(jax.random.uniform(key_list[22], (NS,), jnp.float32, math.log(5.406316816447543e-08), math.log(2.162526726579017e-07))), 5.406316816447543e-08, 2.162526726579017e-07),
    }


@jax.custom_vjp
def low(v):
    return lax.optimization_barrier(v.astype(jnp.bfloat16)).astype(jnp.float32)

@jax.custom_vjp
def low_back(v):
    return v

def low_keep(v):
    return (low(v), None)

def low_pass(kept, grad):
    return (grad,)

def back_keep(v):
    return (v, None)

def back_low(kept, grad):
    return (low(grad),)
low.defvjp(low_keep, low_pass)
low_back.defvjp(back_keep, back_low)

def mat(left, right):
    return jnp.matmul(left, right, precision=lax.Precision.HIGHEST)

def mixing(form, left, right):
    return jnp.einsum(form, left, right, precision=lax.Precision.HIGHEST)

def layer_norm(rows, gain, shift):
    mean = lax.optimization_barrier(jnp.mean(rows, -1, keepdims=True))
    centred = rows - mean
    spread = lax.optimization_barrier(jnp.mean(centred * centred, -1, keepdims=True))
    return centred * lax.rsqrt(spread + 1e-06) * gain + shift

def sincos_table(width):
    quarter = width // 4
    omega = 1.0 / 10000.0 ** (jnp.arange(quarter).astype(jnp.float32) / quarter)
    coord = jnp.arange(SIDE * SIDE)

    def half(place):
        angle = place.astype(jnp.float32)[:, None] * omega[None, :]
        return jnp.concatenate([jnp.sin(angle), jnp.cos(angle)], 1)
    return jnp.concatenate([half(coord // SIDE), half(coord % SIDE)], 1)

def unpack(smalls):
    first = 12 * D
    second = first + F
    third = second + 12 * E
    fourth = third + H
    return (smalls[:first].reshape(12, D), smalls[first:second], smalls[second:third].reshape(12, E), smalls[third:fourth], smalls[fourth:])

def layer(hidden, wide, ffn, vectors, bias_up, heads):
    batch, length, width = hidden.shape
    head_dim = width // heads
    scale = 1.0 / math.sqrt(head_dim)
    normed = low(layer_norm(hidden, vectors[2], vectors[3]))
    pre_query = low_back(mat(normed, wide[:, :width]) + vectors[4])
    query_rows = low(pre_query * scale).reshape(batch, length, heads, head_dim)
    key_rows = low(low_back(mat(normed, wide[:, width:2 * width]))).reshape(batch, length, heads, head_dim)
    value_rows = low(low_back(mat(normed, wide[:, 2 * width:3 * width]) + vectors[5])).reshape(batch, length, heads, head_dim)
    scores = low_back(mixing('bqhd,bkhd->bhqk', query_rows, key_rows))
    attention = low(jax.nn.softmax(scores, axis=-1))
    mixed = low(low_back(mixing('bhqk,bkhd->bqhd', attention, value_rows).reshape(batch, length, width)))
    middle = hidden + low_back(mat(mixed, wide[:, 3 * width:]) + vectors[6])
    normed_two = low(layer_norm(middle, vectors[7], vectors[8]))
    active = low(jax.nn.gelu(low_back(mat(normed_two, ffn[0]) + bias_up), approximate=False))
    return middle + low_back(mat(active, ffn[1].T) + vectors[9])

def image_block(weights, vectors, pixels, shuffle):
    enc_w, enc_ffn, dec_proj, dec_w, dec_ffn, head_w = weights
    enc_vec, enc_up, dec_vec, dec_up, head_bias = vectors
    batch = pixels.shape[0]
    picks = (shuffle[:, :KEEP, None] == jnp.arange(PATCHES)[None, None, :]).astype(jnp.float32)
    kept_mask = lax.optimization_barrier(jnp.sum(picks, 1))
    masked = 1.0 - kept_mask
    kept = mixing('bjp,bpc->bjc', picks, pixels)
    embed = low_back(mat(kept, enc_w[:, :D]) + enc_vec[0]) + mixing('bjp,pc->bjc', picks, sincos_table(D))
    hidden = jnp.concatenate([jnp.broadcast_to(enc_vec[1], (batch, 1, D)), embed], 1)
    hidden = layer(hidden, enc_w[:, D:], enc_ffn, enc_vec, enc_up, HE)
    latent = low(layer_norm(hidden, enc_vec[10], enc_vec[11]))
    entry = low_back(mat(latent, dec_proj) + dec_vec[0])
    placed = mixing('bjp,bjc->bpc', picks, entry[:, 1:]) + masked[:, :, None] * dec_vec[1] + sincos_table(E)
    hidden = layer(jnp.concatenate([entry[:, :1], placed], 1), dec_w, dec_ffn, dec_vec, dec_up, HD)
    final = low(layer_norm(hidden[:, 1:], dec_vec[10], dec_vec[11]))
    predict = low_back(mat(final, head_w) + head_bias)
    centred = pixels - lax.optimization_barrier(jnp.mean(pixels, -1, keepdims=True))
    target = centred * lax.rsqrt(lax.optimization_barrier(jnp.mean(centred * centred, -1, keepdims=True)) + 1e-06)
    error = predict - target
    return jnp.sum(masked[:, :, None] * error * error)

def adam_update(weight, grad, first, second, bias_one, bias_two, decay):
    first_new = 0.5 * first + 0.5 * grad
    second_new = 0.5 * second + 0.5 * grad * grad
    direction = first_new / bias_one / (jnp.sqrt(second_new / bias_two) + 1e-08)
    return (weight - 0.02 * (direction + decay * weight), first_new, second_new)

def reference(patches, shuffle, enc_w, enc_ffn, dec_proj, dec_w, dec_ffn, head_w, smalls, first_enc_w, first_enc_ffn, first_dec_proj, first_dec_w, first_dec_ffn, first_head_w, first_smalls, second_enc_w, second_enc_ffn, second_dec_proj, second_dec_w, second_dec_ffn, second_head_w, second_smalls):
    params = (enc_w, enc_ffn, dec_proj, dec_w, dec_ffn, head_w, smalls)
    block = min(IMAGES, 16)
    pixel_blocks = patches.astype(jnp.float32).reshape(IMAGES // block, block, PATCHES, P_SIZE)
    shuffle_blocks = shuffle.reshape(IMAGES // block, block, PATCHES)

    def total_loss(params):
        weights = tuple((low(item) for item in params[:6]))
        vectors = unpack(params[6])

        def one_block(pair):
            return jax.checkpoint(image_block)(weights, vectors, pair[0], pair[1])
        return jnp.sum(lax.map(one_block, (pixel_blocks, shuffle_blocks))) / (IMAGES * MASKED * P_SIZE)
    loss, pullback = jax.vjp(total_loss, params)
    grads = pullback(jnp.ones((), loss.dtype))[0]
    bias_one = 1.0 - 0.5 ** STEP
    bias_two = 1.0 - 0.5 ** STEP
    firsts = (first_enc_w, first_enc_ffn, first_dec_proj, first_dec_w, first_dec_ffn, first_head_w, first_smalls)
    seconds = (second_enc_w, second_enc_ffn, second_dec_proj, second_dec_w, second_dec_ffn, second_head_w, second_smalls)
    decays = (0.05, 0.05, 0.05, 0.05, 0.05, 0.05, 0.0)
    results = [adam_update(params[index], grads[index], firsts[index], seconds[index], bias_one, bias_two, decays[index]) for index in range(7)]
    news = [item[0] for item in results]
    moments = [item[1] for item in results]
    squares = [item[2] for item in results]
    return (news[0], news[1], news[2], news[3], news[4], news[5], news[6], moments[0], moments[1], moments[2], moments[3], moments[4], moments[5], moments[6], squares[0], squares[1], squares[2], squares[3], squares[4], squares[5], squares[6], loss)
```

```python
import functools
import math

import jax
import jax.numpy as jnp
from jax import lax
from jax.experimental import pallas as pl
from jax.experimental.pallas import tpu as pltpu
from jax.sharding import PartitionSpec as P

D = 768
HE = 12
F = 3072
E = 512
HD = 16
H = 2048
P_SIZE = 768
SIDE = 14
KEEP = 49
STEP = 5
PATCHES = 196


norm_eps = 1e-06
low_type = jnp.bfloat16
high_type = jnp.float32


MESH = pl.DeviceIdType.MESH


def gather_kernel(depth, rows, half, own, out, zs, zr, xs, xr, ys, yr, dxs, dxr, dys, dyr, cs, cr, local):
    row = lax.axis_index("row")
    col = lax.axis_index("col")
    y, x, z, k = row // 2, row % 2, col // 2, col % 2
    row_x = y * 2 + (1 - x)
    row_y = (1 - y) * 2 + x
    row_d = (1 - y) * 2 + (1 - x)
    near_x, near_y = (row_x, col), (row_y, col)
    twin = (row, z * 2 + (1 - k))
    lower, upper = (row, col - 2), (row, col + 2)
    has_lower, has_upper = z > 0, z < depth - 1

    barrier = pltpu.get_barrier_semaphore()
    for other in (near_x, near_y, twin):
        pl.semaphore_signal(barrier, inc=1, device_id=other, device_id_type=MESH)

    @pl.when(has_lower)
    def _():
        pl.semaphore_signal(barrier, inc=1, device_id=lower, device_id_type=MESH)

    @pl.when(has_upper)
    def _():
        pl.semaphore_signal(barrier, inc=1, device_id=upper, device_id_type=MESH)

    pl.semaphore_wait(barrier, 3 + jnp.where(has_lower, 1, 0) + jnp.where(has_upper, 1, 0))

    levels = [(0, 0)] + [(d, way) for d in range(1, depth) for way in (0, 1)]
    level_of = {item: number for number, item in enumerate(levels)}
    first, second = pl.ds(0, half), pl.ds(half, rows - half)

    def place(level):
        d, way = level
        return z - d if way == 0 else z + d

    def valid(level):
        d, way = level
        return z - d >= 0 if way == 0 else z + d < depth

    def slot(level, row_now):
        return out.at[place(level) * 2 + k, row_now]

    def source(level):
        return own if level == (0, 0) else slot(level, row)

    def copy(src, dst, send, recv, target):
        return pltpu.make_async_remote_copy(
            src_ref=src, dst_ref=dst, send_sem=send, recv_sem=recv, device_id=target, device_id_type=MESH
        )

    def z_copy(level, way):
        d = level[0]
        src = source(level)
        dst = out.at[place(level) * 2 + k, row]
        n = level_of[level]
        return copy(src, dst, zs.at[n, way], zr.at[d, way], upper if way == 0 else lower)

    def x_copy(level):
        n = level_of[level]
        return copy(source(level), slot(level, row), xs.at[n], xr.at[n], near_x)

    def y_copy(level):
        n = level_of[level]
        return copy(source(level), slot(level, row), ys.at[n], yr.at[n], near_y)

    def dx_copy(level):
        n = level_of[level]
        ref = slot(level, row_y).at[second]
        return copy(ref, ref, dxs.at[n], dxr.at[n], near_x)

    def dy_copy(level):
        n = level_of[level]
        ref = slot(level, row_x).at[first]
        return copy(ref, ref, dys.at[n], dyr.at[n], near_y)

    def twin_copy(level, kind):
        n = level_of[level]
        src = (source(level), slot(level, row_x), slot(level, row_y), slot(level, row_d))[kind]
        dst = slot(level, (row, row_x, row_y, row_d)[kind])
        return copy(src, dst, cs.at[n, kind], cr.at[n, kind], twin)

    def guarded(level, action):
        if level == (0, 0):
            action()
        else:
            pl.when(valid(level))(action)

    def spread(level):
        d, way = level

        def action():
            if level != (0, 0):
                z_copy((d - 1, way if d > 1 else 0), way).wait_recv()
            for direction in (0, 1):
                if level == (0, 0) or direction == way:
                    @pl.when(has_upper if direction == 0 else has_lower)
                    def _():
                        z_copy(level, direction).start()
            x_copy(level).start()
            y_copy(level).start()
            twin_copy(level, 0).start()

        guarded(level, action)

    def turn(level):
        def action():
            x_copy(level).wait_recv()
            dy_copy(level).start()
            twin_copy(level, 1).start()
            y_copy(level).wait_recv()
            dx_copy(level).start()
            twin_copy(level, 2).start()

        guarded(level, action)

    def close(level):
        def action():
            dx_copy(level).wait_recv()
            dy_copy(level).wait_recv()
            twin_copy(level, 3).start()

        guarded(level, action)

    def drain(level):
        d, way = level

        def action():
            for direction in (0, 1):
                if level == (0, 0) or direction == way:
                    @pl.when(has_upper if direction == 0 else has_lower)
                    def _():
                        z_copy(level, direction).wait_send()
            x_copy(level).wait_send()
            y_copy(level).wait_send()
            dx_copy(level).wait_send()
            dy_copy(level).wait_send()
            for kind in range(4):
                twin_copy(level, kind).wait()

        guarded(level, action)

    keep = pltpu.make_async_copy(own, out.at[col, row], local)
    keep.start()
    for step in range(depth + 2):
        for level in levels:
            if level[0] == step:
                spread(level)
        for level in levels:
            if level[0] == step - 1:
                turn(level)
        for level in levels:
            if level[0] == step - 2:
                close(level)
    keep.wait()
    for level in levels:
        drain(level)


def gather_blocks(own, depth):
    rows, lanes = own.shape
    half = (rows // 32) * 16
    count = 2 * depth - 1
    dma = pltpu.SemaphoreType.DMA
    anywhere = pl.BlockSpec(memory_space=pltpu.HBM)
    return pl.pallas_call(
        functools.partial(gather_kernel, depth, rows, half),
        out_shape=jax.ShapeDtypeStruct((2 * depth, 4, rows, lanes), own.dtype),
        in_specs=[anywhere],
        out_specs=anywhere,
        scratch_shapes=[dma((count, 2)), dma((depth, 2))]
        + [dma((count,)) for _ in range(8)]
        + [dma((count, 4)), dma((count, 4)), dma],
        compiler_params=pltpu.CompilerParams(collective_id=0, has_side_effects=True),
        name="gather_blocks",
    )(own)


def far_first(depth):
    orders = []
    for z in range(depth):
        orders.append(sorted(range(depth), key=lambda t: (-abs(t - z), -abs(2 * t - depth + 1))))
    return orders


code_type = jnp.int16
code_top = 32767.0


def encode(values):
    peak = jnp.max(jnp.abs(values), axis=0, keepdims=True)
    unit = jnp.maximum(peak, 1e-30) * (1.0 / code_top)
    codes = jnp.round(values * (1.0 / unit))
    codes = jnp.clip(codes, -code_top, code_top)
    return codes.astype(jnp.int32).astype(code_type), unit


def decode(codes, unit):
    return codes.astype(jnp.int32).astype(high_type) * unit


def reduce_kernel(depth, devices, cols, parts, chunk, half, blob, small, out, small_out,
                  arrived, mine, stage_x, stage_y, recv_x, recv_y, turn_x, turn_y, back_x, back_y, line_out, line,
                  units_out, units_in, line_units, box,
                  s_load, s_cs, s_cr, s_xs, s_xr, s_ys, s_yr, s_txs, s_txr, s_tys, s_tyr, s_zs, s_zr,
                  u_xs, u_xr, u_ys, u_yr, u_txs, u_txr, u_tys, u_tyr, u_zs, u_zr,
                  s_ps, s_pr, s_qs, s_qr):
    row = lax.axis_index("row")
    col = lax.axis_index("col")
    y, x, z, k = row // 2, row % 2, col // 2, col % 2
    me = row * cols + col
    near_x, near_y = (y * 2 + (1 - x), col), ((1 - y) * 2 + x, col)
    twin = (row, z * 2 + (1 - k))
    lower, upper = (row, col - 2), (row, col + 2)
    has_lower, has_upper = z > 0, z < depth - 1
    steps = depth * parts
    slots = mine.shape[0]
    ahead = slots - 1
    a_rows, b_rows = pl.ds(0, half), pl.ds(half, chunk - half)

    def device(offset):
        index = (me + offset) % devices
        return (index // cols, index % cols)

    barrier = pltpu.get_barrier_semaphore()
    for offset in range(1, devices):
        pl.semaphore_signal(barrier, inc=1, device_id=device(offset), device_id_type=MESH)
    pl.semaphore_wait(barrier, devices - 1)

    def copy(src, dst, send, recv, target):
        return pltpu.make_async_remote_copy(
            src_ref=src, dst_ref=dst, send_sem=send, recv_sem=recv, device_id=target, device_id_type=MESH
        )

    class Pair:
        def __init__(self, *copies):
            self.copies = copies

        def start(self):
            for item in self.copies:
                item.start()

        def wait_recv(self):
            for item in self.copies:
                item.wait_recv()

        def wait_send(self):
            for item in self.copies:
                item.wait_send()

    orders = far_first(depth)

    def goal(t):
        turn = t // parts
        value = 0
        for a in range(depth):
            for b in range(depth):
                value = jnp.where((z == a) & (turn == b), orders[a][b], value)
        return value

    def span(t):
        return pl.ds(pl.multiple_of((t % parts) * chunk, 16), chunk)

    def load(t):
        return pltpu.make_async_copy(
            blob.at[goal(t) * 2 + k, :, span(t)], mine.at[t % slots], s_load.at[t % slots]
        )

    def core(t):
        return copy(blob.at[goal(t) * 2 + (1 - k), :, span(t)], arrived.at[t], s_cs.at[t], s_cr.at[t], twin)

    def paired(kind, src, dst, send, recv, unit_send, unit_recv, target):
        def make(t):
            return Pair(
                copy(src.at[t], dst.at[t], send.at[t], recv.at[t], target),
                copy(units_out.at[t, kind], units_in.at[t, kind], unit_send.at[t], unit_recv.at[t], target),
            )

        return make

    first_x = paired(0, stage_x, recv_x, s_xs, s_xr, u_xs, u_xr, near_x)
    first_y = paired(1, stage_y, recv_y, s_ys, s_yr, u_ys, u_yr, near_y)
    second_x = paired(2, turn_x, back_x, s_txs, s_txr, u_txs, u_txr, near_x)
    second_y = paired(3, turn_y, back_y, s_tys, s_tyr, u_tys, u_tyr, near_y)

    def along(t, index, target):
        return Pair(
            copy(line_out.at[t], line.at[index], s_zs.at[t], s_zr.at[index], target),
            copy(units_out.at[t, 4], line_units.at[index], u_zs.at[t], u_zr.at[index], target),
        )

    def upper_index(t):
        return (goal(t) + 1) * parts + t % parts

    def lower_index(t):
        return goal(t) * parts + t % parts

    def to_upper(t):
        return along(t, upper_index(t), upper)

    def to_lower(t):
        return along(t, lower_index(t), lower)

    def small_send(offset):
        target = device(offset)
        return copy(small.at[target[0] * cols + target[1]], box.at[offset], s_ps.at[offset], s_pr.at[offset], target)

    def small_back(offset):
        return copy(small_out.at[me], small_out.at[me], s_qs.at[offset], s_qr.at[offset], device(offset))

    def small_back_recv(offset):
        origin = (me + devices - offset) % devices
        return copy(small_out.at[origin], small_out.at[origin], s_qs.at[offset], s_qr.at[offset], device(offset))

    for t in range(ahead):
        load(t).start()
        core(t).start()
    for offset in range(1, devices):
        small_send(offset).start()

    def stage_one(t):
        load(t).wait()
        core(t).wait_recv()
        slot = t % slots
        for other in (0, 1):
            away = other * 2 + (1 - x)
            stay = other * 2 + x
            codes, unit = encode(mine[slot, away, a_rows] + arrived[t, away, a_rows])
            stage_x[t, other] = codes
            units_out[t, 0, pl.ds(other, 1)] = unit
            arrived[t, stay, a_rows] += mine[slot, stay, a_rows]
        first_x(t).start()
        for other in (0, 1):
            away = (1 - y) * 2 + other
            stay = y * 2 + other
            codes, unit = encode(mine[slot, away, b_rows] + arrived[t, away, b_rows])
            stage_y[t, other] = codes
            units_out[t, 1, pl.ds(other, 1)] = unit
            arrived[t, stay, b_rows] += mine[slot, stay, b_rows]
        first_y(t).start()

    def stage_two(t):
        first_x(t).wait_recv()
        away = (1 - y) * 2 + x
        codes, unit = encode(arrived[t, away, a_rows] + decode(recv_x[t, 1 - y], units_in[t, 0, pl.ds(1 - y, 1)]))
        turn_y[t] = codes
        units_out[t, 3, pl.ds(0, 1)] = unit
        second_y(t).start()
        arrived[t, row, a_rows] += decode(recv_x[t, y], units_in[t, 0, pl.ds(y, 1)])
        first_y(t).wait_recv()
        away = y * 2 + (1 - x)
        codes, unit = encode(arrived[t, away, b_rows] + decode(recv_y[t, 1 - x], units_in[t, 1, pl.ds(1 - x, 1)]))
        turn_x[t] = codes
        units_out[t, 2, pl.ds(0, 1)] = unit
        second_x(t).start()
        arrived[t, row, b_rows] += decode(recv_y[t, x], units_in[t, 1, pl.ds(x, 1)])

    def stage_three(t):
        second_y(t).wait_recv()
        arrived[t, row, a_rows] += decode(back_y[t], units_in[t, 3, pl.ds(0, 1)])
        second_x(t).wait_recv()
        arrived[t, row, b_rows] += decode(back_x[t], units_in[t, 2, pl.ds(0, 1)])

    def take(index):
        return decode(line[index], line_units[index, pl.ds(0, 1)])

    def pack(t):
        codes, unit = encode(arrived[t, row])
        line_out[t] = codes
        units_out[t, 4, pl.ds(0, 1)] = unit

    def stage_four(t):
        target = goal(t)

        @pl.when((target >= z) & has_lower)
        def _():
            to_upper(t).wait_recv()
            arrived[t, row] += take(upper_index(t))

        @pl.when((target <= z) & has_upper)
        def _():
            to_lower(t).wait_recv()
            arrived[t, row] += take(lower_index(t))

        @pl.when(target != z)
        def _():
            pack(t)

        @pl.when(target > z)
        def _():
            to_upper(t).start()

        @pl.when(target < z)
        def _():
            to_lower(t).start()

        @pl.when(target == z)
        def _():
            out[span(t)] = arrived[t, row]

    lags = (2, 4, 6)

    def body(i, carry):
        @pl.when(i + ahead < steps)
        def _():
            load(i + ahead).start()
            core(i + ahead).start()

        @pl.when(i < steps)
        def _():
            stage_one(i)

        for lag, stage in zip(lags, (stage_two, stage_three, stage_four)):
            @pl.when((i >= lag) & (i - lag < steps))
            def _():
                stage(i - lag)

        @pl.when(i == steps // 2)
        def _():
            total = small[me]
            for offset in range(1, devices):
                small_send(offset).wait_recv()
                total = total + box[offset]
            small_out[me] = total
            for offset in range(1, devices):
                small_back(offset).start()

        return carry

    lax.fori_loop(0, steps + lags[-1], body, 0)

    def finish(t, carry):
        core(t).wait_send()
        first_x(t).wait_send()
        first_y(t).wait_send()
        second_x(t).wait_send()
        second_y(t).wait_send()

        @pl.when(goal(t) > z)
        def _():
            to_upper(t).wait_send()

        @pl.when(goal(t) < z)
        def _():
            to_lower(t).wait_send()

        return carry

    lax.fori_loop(0, steps, finish, 0)
    for offset in range(1, devices):
        small_send(offset).wait_send()
        small_back(offset).wait_send()
        small_back_recv(offset).wait_recv()


def reduce_blocks(blob, small, depth, parts):
    cols, _, rows, lanes = blob.shape
    devices = 4 * cols
    chunk = rows // parts
    half = -(-chunk // 32) * 16
    rest = chunk - half
    steps = depth * parts
    lines = (depth + 1) * parts
    dma = pltpu.SemaphoreType.DMA
    vm = pltpu.VMEM
    return pl.pallas_call(
        functools.partial(reduce_kernel, depth, devices, cols, parts, chunk, half),
        out_shape=(
            jax.ShapeDtypeStruct((rows, lanes), high_type),
            jax.ShapeDtypeStruct(small.shape, high_type),
        ),
        in_specs=[pl.BlockSpec(memory_space=pltpu.HBM), pl.BlockSpec(memory_space=pltpu.VMEM)],
        out_specs=[pl.BlockSpec(memory_space=pltpu.VMEM)] * 2,
        scratch_shapes=[
            vm((steps, 4, chunk, lanes), high_type),
            vm((4, 4, chunk, lanes), high_type),
            vm((steps, 2, half, lanes), code_type),
            vm((steps, 2, rest, lanes), code_type),
            vm((steps, 2, half, lanes), code_type),
            vm((steps, 2, rest, lanes), code_type),
            vm((steps, rest, lanes), code_type),
            vm((steps, half, lanes), code_type),
            vm((steps, rest, lanes), code_type),
            vm((steps, half, lanes), code_type),
            vm((steps, chunk, lanes), code_type),
            vm((lines, chunk, lanes), code_type),
            vm((steps, 5, 8, lanes), high_type),
            vm((steps, 4, 8, lanes), high_type),
            vm((lines, 8, lanes), high_type),
            vm((devices,) + small.shape[1:], high_type),
            dma((4,)),
        ]
        + ([dma((steps,)) for _ in range(11)] + [dma((lines,))])
        + ([dma((steps,)) for _ in range(9)] + [dma((lines,))])
        + [dma((devices,)) for _ in range(4)],
        compiler_params=pltpu.CompilerParams(
            collective_id=1, has_side_effects=True, vmem_limit_bytes=62 << 20
        ),
        name="reduce_blocks",
    )(blob, small)


LANES = 128


def tiles_of(block):
    rows, width = block.shape
    tiles = -(-width // LANES)
    block = jnp.pad(block, ((0, 0), (0, tiles * LANES - width)))
    return block.reshape(rows, tiles, LANES).transpose(1, 0, 2).reshape(tiles * rows, LANES)


def untile(block, rows, width):
    tiles = -(-width // LANES)
    return block.reshape(tiles, rows, LANES).transpose(1, 0, 2).reshape(rows, tiles * LANES)[:, :width]


def fold_proj(block):
    half = block.shape[0] // 2
    return jnp.concatenate([block[:half], block[half:]], 1)


def unfold_proj(block):
    width = block.shape[1] // 2
    return jnp.concatenate([block[:, :width], block[:, width:]], 0)


def pack_shards(enc_w, enc_ffn, dec_proj, dec_w, dec_ffn):
    return jnp.concatenate(
        [
            tiles_of(enc_w),
            tiles_of(enc_ffn[0]),
            tiles_of(enc_ffn[1]),
            tiles_of(dec_w),
            tiles_of(dec_ffn[0]),
            tiles_of(dec_ffn[1]),
            fold_proj(dec_proj),
        ],
        0,
    )


def unpack_shards(blob):
    cuts = [0, 768, 576, 576, 256, 256, 256, 96]
    places = [sum(cuts[: index + 1]) for index in range(len(cuts))]
    piece = [blob[places[index] : places[index + 1]] for index in range(7)]
    return (
        untile(piece[0], 192, 480),
        jnp.stack([untile(piece[1], 192, 384), untile(piece[2], 192, 384)]),
        unfold_proj(piece[6]),
        untile(piece[3], 128, 256),
        jnp.stack([untile(piece[4], 128, 256), untile(piece[5], 128, 256)]),
    )


def whole_blob(enc, enc_ffn, proj, dec, dec_ffn, row_size, col_size):
    def blocks(array):
        rows, width = array.shape[0] // row_size, array.shape[1] // col_size
        return array.reshape(row_size, rows, col_size, width).transpose(2, 0, 1, 3)

    def tiled(array):
        cut = blocks(array)
        return jax.vmap(jax.vmap(tiles_of))(cut)

    return jnp.concatenate(
        [
            tiled(enc),
            tiled(enc_ffn[0]),
            tiled(enc_ffn[1]),
            tiled(dec),
            tiled(dec_ffn[0]),
            tiled(dec_ffn[1]),
            jax.vmap(jax.vmap(fold_proj))(blocks(proj)),
        ],
        2,
    )


def whole_arrays(blob):
    col_size, row_size = blob.shape[:2]
    parts = jax.vmap(jax.vmap(unpack_shards))(blob)

    def joined(array):
        if array.ndim == 4:
            return array.transpose(1, 2, 0, 3).reshape(row_size * array.shape[2], col_size * array.shape[3])
        return array.transpose(2, 1, 3, 0, 4).reshape(2, row_size * array.shape[3], col_size * array.shape[4])

    return tuple(joined(item) for item in parts)


def gather_weights(enc_w, enc_ffn, dec_proj, dec_w, dec_ffn):
    shards = (enc_w, enc_ffn, dec_proj, dec_w, dec_ffn)
    if lax.axis_size("row") == 4 and lax.axis_size("col") == 8:
        own = pack_shards(*[item.astype(low_type) for item in shards])
        return whole_arrays(gather_blocks(own, lax.axis_size("col") // 2))
    full = []
    for item in shards:
        rowed = lax.all_gather(item.astype(low_type), "row", axis=item.ndim - 2, tiled=True)
        full.append(lax.all_gather(rowed, "col", axis=item.ndim - 1, tiled=True))
    return tuple(full)


def reduce_grads(grads, smalls, loss):
    count = smalls.shape[0]
    if lax.axis_size("row") == 4 and lax.axis_size("col") == 8:
        blob = whole_blob(*grads, 4, 8)
        small = jnp.concatenate([smalls, loss[None], jnp.zeros((32 * 8 * LANES - count - 1,), high_type)])
        summed, small = reduce_blocks(blob, small.reshape(32, 8, LANES), 4, 6)
        small = small.reshape(-1)
        return unpack_shards(summed), small[:count], small[count]
    shards = []
    for item in grads:
        done = lax.psum_scatter(item, "col", scatter_dimension=item.ndim - 1, tiled=True)
        shards.append(lax.psum_scatter(done, "row", scatter_dimension=item.ndim - 2, tiled=True))
    smalls, loss = lax.psum((smalls, loss), ("row", "col"))
    return tuple(shards), smalls, loss


def product_of(left, right):
    return jnp.dot(left, right, preferred_element_type=high_type)


def against_rows(left, right):
    return lax.dot_general(left, right, (((1,), (1,)), ((), ())), preferred_element_type=high_type)


def weight_grad(left, right):
    return lax.dot_general(left, right, (((0,), (0,)), ((), ())), preferred_element_type=high_type)


def layer_norm(rows, gain, shift):
    mean = jnp.mean(rows, -1, keepdims=True)
    centred = rows - mean
    spread = jnp.mean(centred * centred, -1, keepdims=True)
    return centred * lax.rsqrt(spread + norm_eps) * gain + shift


def norm_back(rows, gain, shift, grad):
    return jax.vjp(layer_norm, rows, gain, shift)[1](grad)


def gelu_exact(inputs):
    return jax.nn.gelu(inputs, approximate=False)


def sincos_table(width):
    quarter = width // 4
    omega = 1.0 / 10000.0 ** (jnp.arange(quarter).astype(high_type) / quarter)
    coord = jnp.arange(SIDE * SIDE)

    def half(place):
        angle = place.astype(high_type)[:, None] * omega[None, :]
        return jnp.concatenate([jnp.sin(angle), jnp.cos(angle)], 1)

    return jnp.concatenate([half(coord // SIDE), half(coord % SIDE)], 1)


def unpack(smalls):
    first = 12 * D
    second = first + F
    third = second + 12 * E
    fourth = third + H
    return (
        smalls[:first].reshape(12, D),
        smalls[first:second],
        smalls[second:third].reshape(12, E),
        smalls[third:fourth],
        smalls[fourth:],
    )


def split_heads(tensor, batch, heads):
    return tensor.reshape(batch, tensor.shape[0] // batch, heads, tensor.shape[1] // heads)


def column_sums(tensor):
    return jnp.sum(tensor.astype(high_type), 0)


def layer_forward(hidden, wide, ffn_w, vectors, bias_up, heads, batch):
    width = hidden.shape[1]
    scale = 1.0 / math.sqrt(width // heads)
    normed = layer_norm(hidden, vectors[2], vectors[3]).astype(low_type)
    projected = product_of(normed, wide[:, : 3 * width])
    query_rows = ((projected[:, :width] + vectors[4]) * scale).astype(low_type)
    key_rows = projected[:, width : 2 * width].astype(low_type)
    value_rows = (projected[:, 2 * width :] + vectors[5]).astype(low_type)
    scores = jnp.einsum(
        "bqhd,bkhd->bhqk",
        split_heads(query_rows, batch, heads),
        split_heads(key_rows, batch, heads),
        preferred_element_type=high_type,
    )
    row_max = jnp.max(scores, -1, keepdims=True)
    raised = jnp.exp(scores - row_max)
    total = jnp.sum(raised, -1, keepdims=True)
    log_total = row_max + jnp.log(total)
    attention = (raised / total).astype(low_type)
    mixed = (
        jnp.einsum(
            "bhqk,bkhd->bqhd",
            attention,
            split_heads(value_rows, batch, heads),
            preferred_element_type=high_type,
        )
        .reshape(hidden.shape)
        .astype(low_type)
    )
    middle = hidden + (product_of(mixed, wide[:, 3 * width :]) + vectors[6])
    normed_two = layer_norm(middle, vectors[7], vectors[8]).astype(low_type)
    up_out = product_of(normed_two, ffn_w[0]) + bias_up
    active = gelu_exact(up_out).astype(low_type)
    down = against_rows(active, ffn_w[1])
    output = middle + (down + vectors[9])
    saved = (
        hidden,
        normed,
        query_rows,
        key_rows,
        value_rows,
        log_total,
        mixed,
        middle,
        normed_two,
        up_out,
        active,
    )
    return (output, saved)


def layer_backward(grad_out, saved, wide, ffn_w, vectors, heads, batch):
    (
        hidden,
        normed,
        query_rows,
        key_rows,
        value_rows,
        log_total,
        mixed,
        middle,
        source,
        up_out,
        active,
    ) = saved
    width = hidden.shape[1]
    scale = 1.0 / math.sqrt(width // heads)
    grad_down = grad_out.astype(low_type)
    grad_active = product_of(grad_down, ffn_w[1])
    grad_w_down = weight_grad(grad_down, active)
    grad_up = jax.vjp(gelu_exact, up_out)[1](grad_active)[0].astype(low_type)
    grad_w_up = weight_grad(source, grad_up)
    grad_normed_two = against_rows(grad_up, ffn_w[0])
    grad_middle, gain_two, shift_two = norm_back(middle, vectors[7], vectors[8], grad_normed_two)
    grad_middle = grad_middle + grad_out
    grad_branch = grad_middle.astype(low_type)
    grad_w_out = weight_grad(mixed, grad_branch)
    grad_mixed = split_heads(
        against_rows(grad_branch, wide[:, 3 * width :]).astype(low_type), batch, heads
    )
    query_heads = split_heads(query_rows, batch, heads)
    key_heads = split_heads(key_rows, batch, heads)
    value_heads = split_heads(value_rows, batch, heads)
    scores = jnp.einsum("bqhd,bkhd->bhqk", query_heads, key_heads, preferred_element_type=high_type)
    attention = jnp.exp(scores - log_total)
    grad_values = jnp.einsum(
        "bhqk,bqhd->bkhd", attention.astype(low_type), grad_mixed, preferred_element_type=high_type
    )
    grad_attention = jnp.einsum(
        "bqhd,bkhd->bhqk", grad_mixed, value_heads, preferred_element_type=high_type
    )
    grad_scores = (
        attention * (grad_attention - jnp.sum(grad_attention * attention, -1, keepdims=True))
    ).astype(low_type)
    grad_query = (
        jnp.einsum("bhqk,bkhd->bqhd", grad_scores, key_heads, preferred_element_type=high_type)
        * scale
    )
    grad_keys = jnp.einsum(
        "bhqk,bqhd->bkhd", grad_scores, query_heads, preferred_element_type=high_type
    )
    grad_projected = jnp.concatenate(
        [
            grad_query.reshape(hidden.shape),
            grad_keys.reshape(hidden.shape),
            grad_values.reshape(hidden.shape),
        ],
        1,
    ).astype(low_type)
    grad_w_in = weight_grad(normed, grad_projected)
    grad_normed = against_rows(grad_projected, wide[:, : 3 * width])
    grad_hidden, gain_one, shift_one = norm_back(hidden, vectors[2], vectors[3], grad_normed)
    sums = column_sums(grad_projected)
    zero_row = jnp.zeros((width,), high_type)
    grad_vectors = jnp.stack(
        [
            zero_row,
            zero_row,
            gain_one,
            shift_one,
            sums[:width],
            sums[2 * width :],
            column_sums(grad_branch),
            gain_two,
            shift_two,
            column_sums(grad_down),
            zero_row,
            zero_row,
        ]
    )
    grad_wide = jnp.concatenate([grad_w_in, grad_w_out], 1)
    return (
        grad_hidden + grad_middle,
        grad_wide,
        jnp.stack([grad_w_up, grad_w_down]),
        grad_vectors,
        column_sums(grad_up),
    )


def adam_update(weight, grad, first, second, bias_one, bias_two, decay):
    first_new = 0.5 * first + 0.5 * grad
    second_new = 0.5 * second + 0.5 * grad * grad
    direction = first_new / bias_one / (jnp.sqrt(second_new / bias_two) + 1e-08)
    return (weight - 0.02 * (direction + decay * weight), first_new, second_new)


def body(
    patches,
    shuffle,
    enc_w,
    enc_ffn,
    dec_proj,
    dec_w,
    dec_ffn,
    head_w,
    smalls,
    first_enc_w,
    first_enc_ffn,
    first_dec_proj,
    first_dec_w,
    first_dec_ffn,
    first_head_w,
    first_smalls,
    second_enc_w,
    second_enc_ffn,
    second_dec_proj,
    second_dec_w,
    second_dec_ffn,
    second_head_w,
    second_smalls,
):
    enc_full, enc_ffn_w, proj_full, dec_full, dec_ffn_w = gather_weights(
        enc_w, enc_ffn, dec_proj, dec_w, dec_ffn
    )
    head_low = head_w.astype(low_type)
    enc_vec, enc_up, dec_vec, dec_up, head_bias = unpack(smalls)
    batch = patches.shape[0]
    picks = shuffle[:, :KEEP, None] == jnp.arange(PATCHES)[None, None, :]
    pick_float = picks.astype(high_type)
    masked = 1.0 - jnp.sum(pick_float, 1)
    kept = (
        jnp.einsum(
            "bjp,bpc->bjc", picks.astype(low_type), patches, preferred_element_type=high_type
        )
        .astype(low_type)
        .reshape(batch * KEEP, P_SIZE)
    )
    embed = (product_of(kept, enc_full[:, :D]) + enc_vec[0]).reshape(batch, KEEP, D)
    embed = embed + jnp.einsum(
        "bjp,pc->bjc", pick_float, sincos_table(D), precision=lax.Precision.HIGHEST
    )
    start_rows = jnp.concatenate([jnp.broadcast_to(enc_vec[1], (batch, 1, D)), embed], 1).reshape(
        batch * (KEEP + 1), D
    )
    enc_out, enc_saved = layer_forward(
        start_rows, enc_full[:, D:], enc_ffn_w, enc_vec, enc_up, HE, batch
    )
    latent = layer_norm(enc_out, enc_vec[10], enc_vec[11]).astype(low_type)
    entry = (product_of(latent, proj_full) + dec_vec[0]).reshape(batch, KEEP + 1, E)
    placed = (
        jnp.einsum("bjp,bjc->bpc", pick_float, entry[:, 1:], precision=lax.Precision.HIGHEST)
        + masked[:, :, None] * dec_vec[1]
        + sincos_table(E)
    )
    dec_rows = jnp.concatenate([entry[:, :1], placed], 1).reshape(batch * (PATCHES + 1), E)
    dec_out, dec_saved = layer_forward(dec_rows, dec_full, dec_ffn_w, dec_vec, dec_up, HD, batch)
    patch_rows = dec_out.reshape(batch, PATCHES + 1, E)[:, 1:].reshape(batch * PATCHES, E)
    final = layer_norm(patch_rows, dec_vec[10], dec_vec[11]).astype(low_type)
    predict = product_of(final, head_low) + head_bias
    pixels = patches.astype(high_type).reshape(batch * PATCHES, P_SIZE)
    centred = pixels - jnp.mean(pixels, -1, keepdims=True)
    target = centred * lax.rsqrt(jnp.mean(centred * centred, -1, keepdims=True) + norm_eps)
    weight_mask = masked.reshape(batch * PATCHES, 1)
    error = predict - target
    loss_local = jnp.sum(weight_mask * error * error)
    count = batch * lax.axis_size("row") * lax.axis_size("col") * (PATCHES - KEEP) * P_SIZE
    grad_predict = (2.0 * weight_mask * error / count).astype(low_type)
    summed_head = lax.psum(weight_grad(final, grad_predict), ("row", "col"))
    grad_final = against_rows(grad_predict, head_low)
    grad_patch_rows, dec_gain, dec_shift = norm_back(
        patch_rows, dec_vec[10], dec_vec[11], grad_final
    )
    grad_dec_out = jnp.concatenate(
        [jnp.zeros((batch, 1, E), high_type), grad_patch_rows.reshape(batch, PATCHES, E)], 1
    ).reshape(batch * (PATCHES + 1), E)
    grad_dec_rows, grad_dec_wide, grad_dec_ffn, grad_dec_vec, grad_dec_up = layer_backward(
        grad_dec_out, dec_saved, dec_full, dec_ffn_w, dec_vec, HD, batch
    )
    grad_placed = grad_dec_rows.reshape(batch, PATCHES + 1, E)
    grad_mask_token = jnp.sum(masked[:, :, None] * grad_placed[:, 1:], (0, 1))
    grad_entry = jnp.concatenate(
        [
            grad_placed[:, :1],
            jnp.einsum(
                "bjp,bpc->bjc", pick_float, grad_placed[:, 1:], precision=lax.Precision.HIGHEST
            ),
        ],
        1,
    )
    grad_entry = grad_entry.reshape(batch * (KEEP + 1), E).astype(low_type)
    grad_proj = weight_grad(latent, grad_entry)
    grad_latent = against_rows(grad_entry, proj_full)
    grad_enc_out, enc_gain, enc_shift = norm_back(enc_out, enc_vec[10], enc_vec[11], grad_latent)
    grad_start, grad_enc_wide, grad_enc_ffn, grad_enc_vec, grad_enc_up = layer_backward(
        grad_enc_out, enc_saved, enc_full[:, D:], enc_ffn_w, enc_vec, HE, batch
    )
    grad_start = grad_start.reshape(batch, KEEP + 1, D)
    grad_embed = grad_start[:, 1:].reshape(batch * KEEP, D).astype(low_type)
    grad_patch = weight_grad(kept, grad_embed)
    enc_extra = (
        jnp.zeros((12, D), high_type)
        .at[0]
        .set(column_sums(grad_embed))
        .at[1]
        .set(jnp.sum(grad_start[:, 0], 0))
        .at[10]
        .set(enc_gain)
        .at[11]
        .set(enc_shift)
    )
    dec_extra = (
        jnp.zeros((12, E), high_type)
        .at[0]
        .set(column_sums(grad_entry))
        .at[1]
        .set(grad_mask_token)
        .at[10]
        .set(dec_gain)
        .at[11]
        .set(dec_shift)
    )
    grad_smalls = jnp.concatenate(
        [
            (grad_enc_vec + enc_extra).reshape(-1),
            grad_enc_up,
            (grad_dec_vec + dec_extra).reshape(-1),
            grad_dec_up,
            column_sums(grad_predict),
        ]
    )
    grad_enc_full = jnp.concatenate([grad_patch, grad_enc_wide], 1)
    sharded, summed_smalls, loss_sum = reduce_grads(
        (grad_enc_full, grad_enc_ffn, grad_proj, grad_dec_wide, grad_dec_ffn), grad_smalls, loss_local
    )
    grads = (sharded[0], sharded[1], sharded[2], sharded[3], sharded[4], summed_head, summed_smalls)
    params = (enc_w, enc_ffn, dec_proj, dec_w, dec_ffn, head_w, smalls)
    firsts = (
        first_enc_w,
        first_enc_ffn,
        first_dec_proj,
        first_dec_w,
        first_dec_ffn,
        first_head_w,
        first_smalls,
    )
    seconds = (
        second_enc_w,
        second_enc_ffn,
        second_dec_proj,
        second_dec_w,
        second_dec_ffn,
        second_head_w,
        second_smalls,
    )
    decays = (0.05, 0.05, 0.05, 0.05, 0.05, 0.05, 0.0)
    bias_one = 1.0 - 0.5**STEP
    bias_two = 1.0 - 0.5**STEP
    results = [
        adam_update(
            params[index],
            grads[index],
            firsts[index],
            seconds[index],
            bias_one,
            bias_two,
            decays[index],
        )
        for index in range(7)
    ]
    news = [item[0] for item in results]
    moments = [item[1] for item in results]
    squares = [item[2] for item in results]
    return (
        news[0],
        news[1],
        news[2],
        news[3],
        news[4],
        news[5],
        news[6],
        moments[0],
        moments[1],
        moments[2],
        moments[3],
        moments[4],
        moments[5],
        moments[6],
        squares[0],
        squares[1],
        squares[2],
        squares[3],
        squares[4],
        squares[5],
        squares[6],
        loss_sum / count,
    )


def solution(mesh):
    in_specs = (
        P(("row", "col"), None, None),
        P(("row", "col"), None),
        P("row", "col"),
        P(None, "row", "col"),
        P("row", "col"),
        P("row", "col"),
        P(None, "row", "col"),
        P(),
        P(),
        P("row", "col"),
        P(None, "row", "col"),
        P("row", "col"),
        P("row", "col"),
        P(None, "row", "col"),
        P(),
        P(),
        P("row", "col"),
        P(None, "row", "col"),
        P("row", "col"),
        P("row", "col"),
        P(None, "row", "col"),
        P(),
        P(),
    )
    out_specs = (
        P("row", "col"),
        P(None, "row", "col"),
        P("row", "col"),
        P("row", "col"),
        P(None, "row", "col"),
        P(),
        P(),
        P("row", "col"),
        P(None, "row", "col"),
        P("row", "col"),
        P("row", "col"),
        P(None, "row", "col"),
        P(),
        P(),
        P("row", "col"),
        P(None, "row", "col"),
        P("row", "col"),
        P("row", "col"),
        P(None, "row", "col"),
        P(),
        P(),
        P(),
    )
    return jax.shard_map(body, mesh=mesh, in_specs=in_specs, out_specs=out_specs, check_vma=False)
```

```python
import functools
import math

import jax
import jax.numpy as jnp
import numpy as np
from jax import lax
from jax.experimental import pallas as pl
from jax.experimental.pallas import tpu as pltpu
from jax.sharding import PartitionSpec as P

D = 768
HE = 12
F = 3072
E = 512
HD = 16
H = 2048
P_SIZE = 768
SIDE = 14
KEEP = 49
STEP = 5
PATCHES = 196
LANES = 128

norm_eps = 1e-06
low_type = jnp.bfloat16
high_type = jnp.float32


def unpack(smalls):
    first = 12 * D
    second = first + F
    third = second + 12 * E
    fourth = third + H
    return (
        smalls[:first].reshape(12, D),
        smalls[first:second],
        smalls[second:third].reshape(12, E),
        smalls[third:fourth],
        smalls[fourth:],
    )


MESH = pl.DeviceIdType.MESH


class Group:
    def __init__(self, copies):
        self.copies = copies

    def start(self):
        for item in self.copies:
            item.start()

    def wait_recv(self):
        for item in self.copies:
            item.wait_recv()

    def wait_send(self):
        for item in self.copies:
            item.wait_send()

    def wait(self):
        for item in self.copies:
            item.wait()


def gather_kernel(depth, own_enc, own_ffn, own_proj, own_dec, enc, ffn, proj, dec,
                  zs, zr, xs, xr, ys, yr, dxs, dxr, dys, dyr, cs, cr, local):
    row = lax.axis_index("row")
    col = lax.axis_index("col")
    y, x, z, k = row // 2, row % 2, col // 2, col % 2
    row_x = y * 2 + (1 - x)
    row_y = (1 - y) * 2 + x
    row_d = (1 - y) * 2 + (1 - x)
    near_x, near_y = (row_x, col), (row_y, col)
    twin = (row, z * 2 + (1 - k))
    lower, upper = (row, col - 2), (row, col + 2)
    has_lower, has_upper = z > 0, z < depth - 1
    own = (own_enc, own_ffn, own_proj, own_dec)

    barrier = pltpu.get_barrier_semaphore()
    for other in (near_x, near_y, twin):
        pl.semaphore_signal(barrier, inc=1, device_id=other, device_id_type=MESH)

    @pl.when(has_lower)
    def _():
        pl.semaphore_signal(barrier, inc=1, device_id=lower, device_id_type=MESH)

    @pl.when(has_upper)
    def _():
        pl.semaphore_signal(barrier, inc=1, device_id=upper, device_id_type=MESH)

    pl.semaphore_wait(barrier, 3 + jnp.where(has_lower, 1, 0) + jnp.where(has_upper, 1, 0))

    levels = [(0, 0)] + [(d, way) for d in range(1, depth) for way in (0, 1)]
    level_of = {item: number for number, item in enumerate(levels)}

    def place(level):
        d, way = level
        return z - d if way == 0 else z + d

    def valid(level):
        d, way = level
        return z - d >= 0 if way == 0 else z + d < depth

    def cut(index, row_now, half=None):
        def rows(size, unit):
            part = size if half is None else size // 2
            first = 0 if half is None else half * part
            return pl.ds(pl.multiple_of(row_now * size + first, 16), part)

        tall, short = own_enc.shape[0], own_dec.shape[1]
        wide, thin = own_ffn.shape[2], own_dec.shape[2]
        return (
            enc.at[index, rows(tall, 16)],
            ffn.at[:, rows(tall, 16), pl.ds(pl.multiple_of(index * wide, LANES), wide)],
            proj.at[index, rows(tall, 16)],
            dec.at[:, rows(short, 16), pl.ds(pl.multiple_of(index * thin, LANES), thin)],
        )

    def slot(level, row_now, half=None):
        return cut(place(level) * 2 + k, row_now, half)

    def source(level):
        return own if level == (0, 0) else slot(level, row)

    def copy(src, dst, send, recv, target):
        return Group(
            [
                pltpu.make_async_remote_copy(
                    src_ref=src[item],
                    dst_ref=dst[item],
                    send_sem=send.at[item],
                    recv_sem=recv.at[item],
                    device_id=target,
                    device_id_type=MESH,
                )
                for item in range(4)
            ]
        )

    def z_copy(level, way):
        d = level[0]
        n = level_of[level]
        return copy(source(level), slot(level, row), zs.at[n, way], zr.at[d, way], upper if way == 0 else lower)

    def x_copy(level):
        n = level_of[level]
        return copy(source(level), slot(level, row), xs.at[n], xr.at[n], near_x)

    def y_copy(level):
        n = level_of[level]
        return copy(source(level), slot(level, row), ys.at[n], yr.at[n], near_y)

    def dx_copy(level):
        n = level_of[level]
        refs = slot(level, row_y, 1)
        return copy(refs, refs, dxs.at[n], dxr.at[n], near_x)

    def dy_copy(level):
        n = level_of[level]
        refs = slot(level, row_x, 0)
        return copy(refs, refs, dys.at[n], dyr.at[n], near_y)

    def twin_copy(level, kind):
        n = level_of[level]
        row_now = (row, row_x, row_y, row_d)[kind]
        src = source(level) if kind == 0 else slot(level, row_now)
        return copy(src, slot(level, row_now), cs.at[n, kind], cr.at[n, kind], twin)

    def guarded(level, action):
        if level == (0, 0):
            action()
        else:
            pl.when(valid(level))(action)

    def spread(level):
        d, way = level

        def action():
            if level != (0, 0):
                z_copy((d - 1, way if d > 1 else 0), way).wait_recv()
            for direction in (0, 1):
                if level == (0, 0) or direction == way:
                    @pl.when(has_upper if direction == 0 else has_lower)
                    def _():
                        z_copy(level, direction).start()
            x_copy(level).start()
            y_copy(level).start()
            twin_copy(level, 0).start()

        guarded(level, action)

    def turn(level):
        def action():
            x_copy(level).wait_recv()
            dy_copy(level).start()
            twin_copy(level, 1).start()
            y_copy(level).wait_recv()
            dx_copy(level).start()
            twin_copy(level, 2).start()

        guarded(level, action)

    def close(level):
        def action():
            dx_copy(level).wait_recv()
            dy_copy(level).wait_recv()
            twin_copy(level, 3).start()

        guarded(level, action)

    def drain(level):
        d, way = level

        def action():
            for direction in (0, 1):
                if level == (0, 0) or direction == way:
                    @pl.when(has_upper if direction == 0 else has_lower)
                    def _():
                        z_copy(level, direction).wait_send()
            x_copy(level).wait_send()
            y_copy(level).wait_send()
            dx_copy(level).wait_send()
            dy_copy(level).wait_send()
            for kind in range(4):
                twin_copy(level, kind).wait()

        guarded(level, action)

    keep = Group(
        [pltpu.make_async_copy(src, dst, local.at[item]) for item, (src, dst) in enumerate(zip(own, cut(col, row)))]
    )
    keep.start()
    for step in range(depth + 2):
        for level in levels:
            if level[0] == step:
                spread(level)
        for level in levels:
            if level[0] == step - 1:
                turn(level)
        for level in levels:
            if level[0] == step - 2:
                close(level)
    keep.wait()
    for level in levels:
        drain(level)


def gather_blocks(own_enc, own_ffn, own_proj, own_dec, depth):
    count = 2 * depth - 1
    cols = 2 * depth
    dma = pltpu.SemaphoreType.DMA
    anywhere = pl.BlockSpec(memory_space=pltpu.HBM)
    tall, width = own_enc.shape
    shape = jax.ShapeDtypeStruct
    kind = own_enc.dtype
    return pl.pallas_call(
        functools.partial(gather_kernel, depth),
        out_shape=(
            shape((cols, 4 * tall, width), kind),
            shape((2, 4 * tall, cols * own_ffn.shape[2]), kind),
            shape((cols, 4 * tall, own_proj.shape[1]), kind),
            shape((3, 4 * own_dec.shape[1], cols * own_dec.shape[2]), kind),
        ),
        in_specs=[anywhere] * 4,
        out_specs=[anywhere] * 4,
        scratch_shapes=[dma((count, 2, 4)), dma((depth, 2, 4))]
        + [dma((count, 4)) for _ in range(8)]
        + [dma((count, 4, 4)), dma((count, 4, 4)), dma((4,))],
        compiler_params=pltpu.CompilerParams(collective_id=0, has_side_effects=True),
        name="gather_blocks",
    )(own_enc, own_ffn, own_proj, own_dec)


def far_first(depth):
    orders = []
    for z in range(depth):
        orders.append(sorted(range(depth), key=lambda t: (-abs(t - z), -abs(2 * t - depth + 1))))
    return orders


code_type = jnp.int16
code_top = 32767.0


def encode(values):
    peak = jnp.max(jnp.abs(values), axis=0, keepdims=True)
    unit = jnp.maximum(peak, 1e-30) * (1.0 / code_top)
    codes = jnp.round(values * (1.0 / unit))
    codes = jnp.clip(codes, -code_top, code_top)
    return codes.astype(jnp.int32).astype(code_type), unit


def decode(codes, unit):
    return codes.astype(jnp.int32).astype(high_type) * unit


def reduce_kernel(depth, devices, cols, parts, chunk, half, blob, small, out, small_out,
                  arrived, mine, stage_x, stage_y, recv_x, recv_y, turn_x, turn_y, back_x, back_y, line_out, line,
                  units_out, units_in, line_units, box,
                  s_load, s_cs, s_cr, s_xs, s_xr, s_ys, s_yr, s_txs, s_txr, s_tys, s_tyr, s_zs, s_zr,
                  u_xs, u_xr, u_ys, u_yr, u_txs, u_txr, u_tys, u_tyr, u_zs, u_zr,
                  s_ps, s_pr, s_qs, s_qr):
    row = lax.axis_index("row")
    col = lax.axis_index("col")
    y, x, z, k = row // 2, row % 2, col // 2, col % 2
    me = row * cols + col
    near_x, near_y = (y * 2 + (1 - x), col), ((1 - y) * 2 + x, col)
    twin = (row, z * 2 + (1 - k))
    lower, upper = (row, col - 2), (row, col + 2)
    has_lower, has_upper = z > 0, z < depth - 1
    steps = depth * parts
    slots = mine.shape[0]
    ahead = slots - 1
    a_rows, b_rows = pl.ds(0, half), pl.ds(half, chunk - half)

    def device(offset):
        index = (me + offset) % devices
        return (index // cols, index % cols)

    barrier = pltpu.get_barrier_semaphore()
    for offset in range(1, devices):
        pl.semaphore_signal(barrier, inc=1, device_id=device(offset), device_id_type=MESH)
    pl.semaphore_wait(barrier, devices - 1)

    def copy(src, dst, send, recv, target):
        return pltpu.make_async_remote_copy(
            src_ref=src, dst_ref=dst, send_sem=send, recv_sem=recv, device_id=target, device_id_type=MESH
        )

    orders = far_first(depth)

    def goal(t):
        turn = t // parts
        value = 0
        for a in range(depth):
            for b in range(depth):
                value = jnp.where((z == a) & (turn == b), orders[a][b], value)
        return value

    def span(t):
        return pl.ds(pl.multiple_of((t % parts) * chunk, 16), chunk)

    def load(t):
        return pltpu.make_async_copy(
            blob.at[goal(t) * 2 + k, :, span(t)], mine.at[t % slots], s_load.at[t % slots]
        )

    def core(t):
        return copy(blob.at[goal(t) * 2 + (1 - k), :, span(t)], arrived.at[t], s_cs.at[t], s_cr.at[t], twin)

    def paired(kind, src, dst, send, recv, unit_send, unit_recv, target):
        def make(t):
            return Group([
                copy(src.at[t], dst.at[t], send.at[t], recv.at[t], target),
                copy(units_out.at[t, kind], units_in.at[t, kind], unit_send.at[t], unit_recv.at[t], target),
            ])

        return make

    first_x = paired(0, stage_x, recv_x, s_xs, s_xr, u_xs, u_xr, near_x)
    first_y = paired(1, stage_y, recv_y, s_ys, s_yr, u_ys, u_yr, near_y)
    second_x = paired(2, turn_x, back_x, s_txs, s_txr, u_txs, u_txr, near_x)
    second_y = paired(3, turn_y, back_y, s_tys, s_tyr, u_tys, u_tyr, near_y)

    def along(t, index, target):
        return Group([
            copy(line_out.at[t], line.at[index], s_zs.at[t], s_zr.at[index], target),
            copy(units_out.at[t, 4], line_units.at[index], u_zs.at[t], u_zr.at[index], target),
        ])

    def upper_index(t):
        return (goal(t) + 1) * parts + t % parts

    def lower_index(t):
        return goal(t) * parts + t % parts

    def to_upper(t):
        return along(t, upper_index(t), upper)

    def to_lower(t):
        return along(t, lower_index(t), lower)

    def small_send(offset):
        target = device(offset)
        return copy(small.at[target[0] * cols + target[1]], box.at[offset], s_ps.at[offset], s_pr.at[offset], target)

    def small_back(offset):
        return copy(small_out.at[me], small_out.at[me], s_qs.at[offset], s_qr.at[offset], device(offset))

    def small_back_recv(offset):
        origin = (me + devices - offset) % devices
        return copy(small_out.at[origin], small_out.at[origin], s_qs.at[offset], s_qr.at[offset], device(offset))

    for t in range(ahead):
        load(t).start()
        core(t).start()
    for offset in range(1, devices):
        small_send(offset).start()

    def stage_one(t):
        load(t).wait()
        core(t).wait_recv()
        slot = t % slots
        for other in (0, 1):
            away = other * 2 + (1 - x)
            stay = other * 2 + x
            codes, unit = encode(mine[slot, away, a_rows] + arrived[t, away, a_rows])
            stage_x[t, other] = codes
            units_out[t, 0, pl.ds(other, 1)] = unit
            arrived[t, stay, a_rows] += mine[slot, stay, a_rows]
        first_x(t).start()
        for other in (0, 1):
            away = (1 - y) * 2 + other
            stay = y * 2 + other
            codes, unit = encode(mine[slot, away, b_rows] + arrived[t, away, b_rows])
            stage_y[t, other] = codes
            units_out[t, 1, pl.ds(other, 1)] = unit
            arrived[t, stay, b_rows] += mine[slot, stay, b_rows]
        first_y(t).start()

    def stage_two(t):
        first_x(t).wait_recv()
        away = (1 - y) * 2 + x
        codes, unit = encode(arrived[t, away, a_rows] + decode(recv_x[t, 1 - y], units_in[t, 0, pl.ds(1 - y, 1)]))
        turn_y[t] = codes
        units_out[t, 3, pl.ds(0, 1)] = unit
        second_y(t).start()
        arrived[t, row, a_rows] += decode(recv_x[t, y], units_in[t, 0, pl.ds(y, 1)])
        first_y(t).wait_recv()
        away = y * 2 + (1 - x)
        codes, unit = encode(arrived[t, away, b_rows] + decode(recv_y[t, 1 - x], units_in[t, 1, pl.ds(1 - x, 1)]))
        turn_x[t] = codes
        units_out[t, 2, pl.ds(0, 1)] = unit
        second_x(t).start()
        arrived[t, row, b_rows] += decode(recv_y[t, x], units_in[t, 1, pl.ds(x, 1)])

    def stage_three(t):
        second_y(t).wait_recv()
        arrived[t, row, a_rows] += decode(back_y[t], units_in[t, 3, pl.ds(0, 1)])
        second_x(t).wait_recv()
        arrived[t, row, b_rows] += decode(back_x[t], units_in[t, 2, pl.ds(0, 1)])

    def take(index):
        return decode(line[index], line_units[index, pl.ds(0, 1)])

    def pack(t):
        codes, unit = encode(arrived[t, row])
        line_out[t] = codes
        units_out[t, 4, pl.ds(0, 1)] = unit

    def stage_four(t):
        target = goal(t)

        @pl.when((target >= z) & has_lower)
        def _():
            to_upper(t).wait_recv()
            arrived[t, row] += take(upper_index(t))

        @pl.when((target <= z) & has_upper)
        def _():
            to_lower(t).wait_recv()
            arrived[t, row] += take(lower_index(t))

        @pl.when(target != z)
        def _():
            pack(t)

        @pl.when(target > z)
        def _():
            to_upper(t).start()

        @pl.when(target < z)
        def _():
            to_lower(t).start()

        @pl.when(target == z)
        def _():
            out[span(t)] = arrived[t, row]

    lags = (2, 4, 6)

    def body(i, carry):
        @pl.when(i + ahead < steps)
        def _():
            load(i + ahead).start()
            core(i + ahead).start()

        @pl.when(i < steps)
        def _():
            stage_one(i)

        for lag, stage in zip(lags, (stage_two, stage_three, stage_four)):
            @pl.when((i >= lag) & (i - lag < steps))
            def _():
                stage(i - lag)

        @pl.when(i == steps // 2)
        def _():
            total = small[me]
            for offset in range(1, devices):
                small_send(offset).wait_recv()
                total = total + box[offset]
            small_out[me] = total
            for offset in range(1, devices):
                small_back(offset).start()

        return carry

    lax.fori_loop(0, steps + lags[-1], body, 0)

    def finish(t, carry):
        core(t).wait_send()
        first_x(t).wait_send()
        first_y(t).wait_send()
        second_x(t).wait_send()
        second_y(t).wait_send()

        @pl.when(goal(t) > z)
        def _():
            to_upper(t).wait_send()

        @pl.when(goal(t) < z)
        def _():
            to_lower(t).wait_send()

        return carry

    lax.fori_loop(0, steps, finish, 0)
    for offset in range(1, devices):
        small_send(offset).wait_send()
        small_back(offset).wait_send()
        small_back_recv(offset).wait_recv()


def reduce_blocks(blob, small, depth, parts):
    cols, _, rows, lanes = blob.shape
    devices = 4 * cols
    chunk = rows // parts
    half = -(-chunk // 32) * 16
    rest = chunk - half
    steps = depth * parts
    lines = (depth + 1) * parts
    dma = pltpu.SemaphoreType.DMA
    vm = pltpu.VMEM
    return pl.pallas_call(
        functools.partial(reduce_kernel, depth, devices, cols, parts, chunk, half),
        out_shape=(
            jax.ShapeDtypeStruct((rows, lanes), high_type),
            jax.ShapeDtypeStruct(small.shape, high_type),
        ),
        in_specs=[pl.BlockSpec(memory_space=pltpu.HBM), pl.BlockSpec(memory_space=pltpu.VMEM)],
        out_specs=[pl.BlockSpec(memory_space=pltpu.VMEM)] * 2,
        scratch_shapes=[
            vm((steps, 4, chunk, lanes), high_type),
            vm((4, 4, chunk, lanes), high_type),
            vm((steps, 2, half, lanes), code_type),
            vm((steps, 2, rest, lanes), code_type),
            vm((steps, 2, half, lanes), code_type),
            vm((steps, 2, rest, lanes), code_type),
            vm((steps, rest, lanes), code_type),
            vm((steps, half, lanes), code_type),
            vm((steps, rest, lanes), code_type),
            vm((steps, half, lanes), code_type),
            vm((steps, chunk, lanes), code_type),
            vm((lines, chunk, lanes), code_type),
            vm((steps, 5, 8, lanes), high_type),
            vm((steps, 4, 8, lanes), high_type),
            vm((lines, 8, lanes), high_type),
            vm((devices,) + small.shape[1:], high_type),
            dma((4,)),
        ]
        + ([dma((steps,)) for _ in range(11)] + [dma((lines,))])
        + ([dma((steps,)) for _ in range(9)] + [dma((lines,))])
        + [dma((devices,)) for _ in range(4)],
        compiler_params=pltpu.CompilerParams(
            collective_id=1, has_side_effects=True, vmem_limit_bytes=62 << 20
        ),
        name="reduce_blocks",
    )(blob, small)


ENC_ROWS = 64
DEC_ROWS = 208
CLASS_ENC = KEEP
CLASS_DEC = PATCHES
NEGATIVE = -1e30


def nn(left, right):
    return jnp.dot(left, right, preferred_element_type=high_type)


def nt(left, right):
    return lax.dot_general(left, right, (((1,), (1,)), ((), ())), preferred_element_type=high_type)


def tn(left, right):
    return lax.dot_general(left, right, (((0,), (0,)), ((), ())), preferred_element_type=high_type)


def standard(rows):
    mean = jnp.mean(rows, -1, keepdims=True)
    centred = rows - mean
    spread = jnp.mean(centred * centred, -1, keepdims=True)
    rate = lax.rsqrt(spread + norm_eps)
    return centred * rate, rate


def standard_back(unit, rate, grad):
    return rate * (grad - jnp.mean(grad, -1, keepdims=True) - unit * jnp.mean(grad * unit, -1, keepdims=True))


def col_sum(rows):
    return jnp.sum(rows.astype(high_type), 0, keepdims=True)


def erf_of(value):
    value = jnp.clip(value, -4.0, 4.0)
    square = value * value
    top = -2.72614225801306e-10
    for item in (
        2.77068142495902e-08,
        -2.10102402082508e-06,
        -5.69250639462346e-05,
        -7.34990630326855e-04,
        -2.95459980854025e-03,
        -1.60960333262415e-02,
    ):
        top = top * square + item
    low = -1.45660718464996e-05
    for item in (-2.13374055278905e-04, -1.68282697438203e-03, -7.37332916720468e-03, -1.42647390514189e-02):
        low = low * square + item
    return value * top / low


def gelu_pair(value):
    half = 0.5 + 0.5 * erf_of(value * math.sqrt(0.5))
    slope = half + value * jnp.exp(-0.5 * value * value) * (1.0 / math.sqrt(2.0 * math.pi))
    return value * half, slope


def three_way(value):
    high = value.astype(low_type)
    rest = value - high.astype(high_type)
    middle = rest.astype(low_type)
    return high, middle, (rest - middle.astype(high_type)).astype(low_type)


def place_rows(picks, value):
    parts = three_way(value)
    return nn(picks, parts[0]) + nn(picks, parts[1]) + nn(picks, parts[2])


def stack_heads(value, heads):
    width = LANES // heads
    lane = lax.broadcasted_iota(jnp.int32, value.shape, 1) // width
    return jnp.concatenate([jnp.where(lane == head, value, jnp.zeros_like(value)) for head in range(heads)], 0)


def merge_heads(stacked, heads):
    rows = stacked.shape[0] // heads
    width = LANES // heads
    lane = lax.broadcasted_iota(jnp.int32, (rows, LANES), 1) // width
    merged = stacked[:rows]
    for head in range(1, heads):
        merged = jnp.where(lane == head, stacked[head * rows : (head + 1) * rows], merged)
    return merged


def attend(query, key, value, heads, length):
    scores = nt(stack_heads(query, heads), key)
    column = lax.broadcasted_iota(jnp.int32, scores.shape, 1)
    scores = jnp.where(column < length, scores, NEGATIVE)
    raised = jnp.exp(scores - jnp.max(scores, -1, keepdims=True))
    attention = (raised / jnp.sum(raised, -1, keepdims=True)).astype(low_type)
    return merge_heads(nn(attention, value), heads)


def attend_back(query, key, value, grad, heads, length):
    queries = stack_heads(query, heads)
    grads = stack_heads(grad, heads)
    scores = nt(key, queries)
    place = lax.broadcasted_iota(jnp.int32, scores.shape, 0)
    scores = jnp.where(place < length, scores, NEGATIVE)
    raised = jnp.exp(scores - jnp.max(scores, 0, keepdims=True))
    attention = raised * (1.0 / jnp.sum(raised, 0, keepdims=True))
    inner = nt(value, grads)
    grad_scores = (attention * (inner - jnp.sum(inner * attention, 0, keepdims=True))).astype(low_type)
    grad_value = nn(attention.astype(low_type), grads)
    grad_key = nn(grad_scores, queries)
    grad_query = merge_heads(tn(grad_scores, key), heads)
    return grad_query, grad_key, grad_value


def wide_kernel(blocks, wide):
    count, _, width = blocks.shape
    for index in range(count):
        wide[:, index * width : (index + 1) * width] = blocks[index]


def enc_attend_kernel(batch, pick, patches, wide, vec, pos, kept, start, normed, qkv, mixed, middle, normed_two):
    rows = ENC_ROWS
    for image in range(batch):
        span = pl.ds(image * rows, rows)
        kept[span] = nn(pick[image], patches[image]).astype(low_type)
    start[...] = nn(kept[...], wide[:, :D]) + vec[0:1]
    parts = three_way(pos[...])
    for image in range(batch):
        span = pl.ds(image * rows, rows)
        picks = pick[image]
        placed = nn(picks, parts[0]) + nn(picks, parts[1]) + nn(picks, parts[2])
        inner = lax.broadcasted_iota(jnp.int32, placed.shape, 0)
        start[span] = jnp.where(inner == CLASS_ENC, vec[1:2], start[span] + placed)
    unit, _ = standard(start[...])
    normed[...] = (unit * vec[2:3] + vec[3:4]).astype(low_type)
    scale = 1.0 / math.sqrt(D // HE)
    rows_in = normed[...]
    qkv[:, :D] = ((nn(rows_in, wide[:, D : 2 * D]) + vec[4:5]) * scale).astype(low_type)
    qkv[:, D : 2 * D] = nn(rows_in, wide[:, 2 * D : 3 * D]).astype(low_type)
    qkv[:, 2 * D :] = (nn(rows_in, wide[:, 3 * D : 4 * D]) + vec[5:6]).astype(low_type)
    heads = LANES * HE // D
    for image in range(batch):
        span = pl.ds(image * rows, rows)
        for group in range(D // LANES):
            lane = group * LANES
            mixed[span, lane : lane + LANES] = attend(
                qkv[span, lane : lane + LANES],
                qkv[span, D + lane : D + lane + LANES],
                qkv[span, 2 * D + lane : 2 * D + lane + LANES],
                heads,
                KEEP + 1,
            ).astype(low_type)
    middle[...] = start[...] + (nn(mixed[...], wide[:, 4 * D :]) + vec[6:7])
    unit, _ = standard(middle[...])
    normed_two[...] = (unit * vec[7:8] + vec[8:9]).astype(low_type)


def enc_ffn_kernel(middle, normed_two, ffn, vec, up_bias, proj, dec_vec, slope, active, output, latent, entry):
    source = normed_two[...]
    total = middle[...] + vec[9:10]
    step = 512
    for place in range(0, F, step):
        span = slice(place, place + step)
        value, gain = gelu_pair(nn(source, ffn[0, :, span]) + up_bias[:, span])
        slope[:, span] = gain
        value = value.astype(low_type)
        active[:, span] = value
        total = total + nt(value, ffn[1, :, span])
    output[...] = total
    unit, _ = standard(total)
    rows = (unit * vec[10:11] + vec[11:12]).astype(low_type)
    latent[...] = rows
    entry[...] = nn(rows, proj[...]) + dec_vec[0:1]


def dec_attend_kernel(entry, picked, pos, wide, vec, start, normed, qkv, mixed, middle, normed_two):
    picks = picked[0]
    kept = jnp.sum(picks.astype(high_type), 1, keepdims=True)
    rows = place_rows(picks, entry[...]) + (1.0 - kept) * vec[1:2] + pos[...]
    start[...] = rows
    unit, _ = standard(rows)
    rows_in = (unit * vec[2:3] + vec[3:4]).astype(low_type)
    normed[...] = rows_in
    scale = 1.0 / math.sqrt(E // HD)
    qkv[:, :E] = ((nn(rows_in, wide[0, :, :E]) + vec[4:5]) * scale).astype(low_type)
    qkv[:, E : 2 * E] = nn(rows_in, wide[0, :, E : 2 * E]).astype(low_type)
    qkv[:, 2 * E :] = (nn(rows_in, wide[0, :, 2 * E : 3 * E]) + vec[5:6]).astype(low_type)
    heads = LANES * HD // E
    for group in range(E // LANES):
        lane = group * LANES
        mixed[:, lane : lane + LANES] = attend(
            qkv[:, lane : lane + LANES],
            qkv[:, E + lane : E + lane + LANES],
            qkv[:, 2 * E + lane : 2 * E + lane + LANES],
            heads,
            PATCHES + 1,
        ).astype(low_type)
    total = rows + (nn(mixed[...], wide[0, :, 3 * E :]) + vec[6:7])
    middle[...] = total
    unit, _ = standard(total)
    normed_two[...] = (unit * vec[7:8] + vec[8:9]).astype(low_type)


def send_tiles(acc, blob, sem, tiles, rows, per_block, base, stride):
    def go(index, carry):
        tile, part = index // 4, index % 4
        block, inner = tile // per_block, tile % per_block
        pltpu.make_async_copy(
            acc.at[tile, pl.ds(pl.multiple_of(part * rows, 16), rows)],
            blob.at[block, part, pl.ds(pl.multiple_of(base + inner * stride, 16), rows)],
            sem,
        ).start()
        return carry

    lax.fori_loop(0, tiles * 4, go, 0)


def wait_tiles(acc, sem):
    pltpu.make_async_copy(acc, acc, sem).wait()


def dec_ffn_kernel(images, last, count, middle, normed_two, mixed, pixels, picked, weights, head, vec, up_bias, head_bias,
                   grad_middle, grad_mixed, grad_head, vec_grad, up_grad, bias_grad, loss, blob,
                   active, slope, acc_up, acc_down, acc_out, sems):
    step = pl.program_id(0)
    source = normed_two[...]
    rows = source.shape[0]

    @pl.when(step == 0)
    def _():
        grad_head[...] = jnp.zeros_like(grad_head)
        vec_grad[...] = jnp.zeros_like(vec_grad)
        up_grad[...] = jnp.zeros_like(up_grad)
        bias_grad[...] = jnp.zeros_like(bias_grad)
        loss[...] = jnp.zeros_like(loss)
        acc_up[...] = jnp.zeros_like(acc_up)
        acc_down[...] = jnp.zeros_like(acc_down)
        acc_out[...] = jnp.zeros_like(acc_out)

    wide = 512
    total = middle[...] + vec[9:10]
    for place in range(0, H, wide):
        span = slice(place, place + wide)
        value, gain = gelu_pair(nn(source, weights[1, :, span]) + up_bias[:, span])
        slope[:, span] = gain
        value = value.astype(low_type)
        active[:, span] = value
        total = total + nt(value, weights[2, :, span])
    unit, rate = standard(total)
    final = (unit * vec[10:11] + vec[11:12]).astype(low_type)
    predict = nn(final, head[...]) + head_bias[...]
    target, _ = standard(pixels[...].astype(high_type))
    kept = jnp.concatenate([jnp.sum(picked[image].astype(high_type), 1, keepdims=True) for image in range(images)], 0)
    inner = lax.broadcasted_iota(jnp.int32, (rows, 1), 0) % DEC_ROWS
    masked = jnp.where(inner < PATCHES, 1.0 - kept, 0.0)
    error = predict - target
    loss[...] += jnp.sum(masked * error * error)
    grad_predict = (2.0 * masked * error / count).astype(low_type)
    grad_head[...] += tn(final, grad_predict)
    bias_grad[...] += col_sum(grad_predict)
    grad_final = nt(grad_predict, head[...])
    vec_grad[10:11] += col_sum(grad_final * unit)
    vec_grad[11:12] += col_sum(grad_final)
    grad_out = standard_back(unit, rate, grad_final * vec[10:11])
    grad_down = grad_out.astype(low_type)
    vec_grad[9:10] += col_sum(grad_down)
    grad_source = jnp.zeros_like(total)
    for place in range(0, H, wide):
        span = slice(place, place + wide)
        grad_up = (slope[:, span] * nn(grad_down, weights[2, :, span])).astype(low_type)
        up_grad[:, span] += col_sum(grad_up)
        grad_source = grad_source + nt(grad_up, weights[1, :, span])
        piece = tn(grad_down, active[:, span])
        other = tn(source, grad_up)
        for tile in range(wide // LANES):
            lane = slice(tile * LANES, (tile + 1) * LANES)
            acc_down[place // LANES + tile] += piece[:, lane]
            acc_up[place // LANES + tile] += other[:, lane]
    unit, rate = standard(middle[...])
    vec_grad[7:8] += col_sum(grad_source * unit)
    vec_grad[8:9] += col_sum(grad_source)
    grad_rows = standard_back(unit, rate, grad_source * vec[7:8]) + grad_out
    grad_middle[...] = grad_rows
    branch = grad_rows.astype(low_type)
    vec_grad[6:7] += col_sum(branch)
    piece = tn(mixed[...], branch)
    for tile in range(E // LANES):
        acc_out[tile] += piece[:, tile * LANES : (tile + 1) * LANES]
    grad_mixed[...] = nt(branch, weights[0, :, 3 * E :]).astype(low_type)

    @pl.when(step == last)
    def _():
        rows_block = E // 4
        send_tiles(acc_up, blob, sems.at[0], H // LANES, rows_block, 2, 2176, rows_block)
        send_tiles(acc_down, blob, sems.at[1], H // LANES, rows_block, 2, 2432, rows_block)
        send_tiles(acc_out, blob.at[pl.ds(6, 2)], sems.at[2], E // LANES, rows_block, 2, 1920, rows_block)
        wait_tiles(acc_up, sems.at[0])
        wait_tiles(acc_down, sems.at[1])
        wait_tiles(acc_out, sems.at[2])


def dec_back_kernel(last, blob_in, qkv, normed, start, grad_middle, grad_mixed, pick, picked, weights, vec,
                    grad_entry, vec_grad, blob, grads, acc, sem):
    step = pl.program_id(0)

    @pl.when(step == 0)
    def _():
        vec_grad[...] = jnp.zeros_like(vec_grad)
        acc[...] = jnp.zeros_like(acc)

    scale = 1.0 / math.sqrt(E // HD)
    heads = LANES * HD // E
    for group in range(E // LANES):
        lane = group * LANES
        span = slice(lane, lane + LANES)
        query, key, value = attend_back(
            qkv[:, lane : lane + LANES],
            qkv[:, E + lane : E + lane + LANES],
            qkv[:, 2 * E + lane : 2 * E + lane + LANES],
            grad_mixed[:, span],
            heads,
            PATCHES + 1,
        )
        grads[:, span] = (query * scale).astype(low_type)
        grads[:, E + lane : E + lane + LANES] = key.astype(low_type)
        grads[:, 2 * E + lane : 2 * E + lane + LANES] = value.astype(low_type)
    vec_grad[4:5] += col_sum(grads[:, :E])
    vec_grad[5:6] += col_sum(grads[:, 2 * E :])
    rows = normed[...]
    for part in range(3):
        piece = tn(rows, grads[:, part * E : (part + 1) * E])
        for tile in range(E // LANES):
            acc[part * (E // LANES) + tile] += piece[:, tile * LANES : (tile + 1) * LANES]
    grad_normed = nt(grads[...], weights[0, :, : 3 * E])
    unit, rate = standard(start[...])
    vec_grad[2:3] += col_sum(grad_normed * unit)
    vec_grad[3:4] += col_sum(grad_normed)
    grad_rows = standard_back(unit, rate, grad_normed * vec[2:3]) + grad_middle[...]
    kept = jnp.sum(picked[0].astype(high_type), 1, keepdims=True)
    vec_grad[1:2] += col_sum((1.0 - kept) * grad_rows)
    grad_entry[...] = nn(pick[0], grad_rows.astype(low_type)).astype(low_type)

    @pl.when(step == last)
    def _():
        rows_block = E // 4
        send_tiles(acc, blob, sem, 3 * E // LANES, rows_block, 2, 1920, rows_block)
        wait_tiles(acc, sem)


def enc_ffn_back_kernel(blob_in, grad_entry, latent, output, middle, normed_two, slope, active, ffn, proj, vec,
                        grad_middle, grad_proj, vec_grad, up_grad, entry_grad, blob, acc_up, acc_down, sems):
    vec_grad[...] = jnp.zeros_like(vec_grad)
    entries = grad_entry[...]
    entry_grad[...] = col_sum(entries)
    grad_proj[...] = tn(latent[...], entries)
    grad_latent = nt(entries, proj[...])
    unit, rate = standard(output[...])
    vec_grad[10:11] = col_sum(grad_latent * unit)
    vec_grad[11:12] = col_sum(grad_latent)
    grad_out = standard_back(unit, rate, grad_latent * vec[10:11])
    grad_down = grad_out.astype(low_type)
    vec_grad[9:10] = col_sum(grad_down)
    source = normed_two[...]
    grad_source = jnp.zeros_like(grad_out)
    wide = 512
    for place in range(0, F, wide):
        span = slice(place, place + wide)
        grad_up = (slope[:, span] * nn(grad_down, ffn[1, :, span])).astype(low_type)
        up_grad[:, span] = col_sum(grad_up)
        grad_source = grad_source + nt(grad_up, ffn[0, :, span])
        piece = tn(grad_down, active[:, span])
        other = tn(source, grad_up)
        for tile in range(wide // LANES):
            lane = slice(tile * LANES, (tile + 1) * LANES)
            acc_down[place // LANES + tile] = piece[:, lane]
            acc_up[place // LANES + tile] = other[:, lane]
    rows_block = D // 4
    send_tiles(acc_up, blob, sems.at[0], F // LANES, rows_block, 3, 768, rows_block)
    send_tiles(acc_down, blob, sems.at[1], F // LANES, rows_block, 3, 1344, rows_block)
    unit, rate = standard(middle[...])
    vec_grad[7:8] = col_sum(grad_source * unit)
    vec_grad[8:9] = col_sum(grad_source)
    grad_rows = standard_back(unit, rate, grad_source * vec[7:8]) + grad_out
    grad_middle[...] = grad_rows
    vec_grad[6:7] = col_sum(grad_rows.astype(low_type))
    wait_tiles(acc_up, sems.at[0])
    wait_tiles(acc_down, sems.at[1])


def enc_back_kernel(batch, blob_in, proj_fold, qkv, kept, normed, start, mixed, grad_middle, wide, vec,
                    vec_grad, blob, grads, grad_wide, tiles, sems):
    rows = ENC_ROWS
    folded = pltpu.make_async_copy(proj_fold, blob.at[:, :, pl.ds(2688, 96)], sems.at[0])
    folded.start()
    vec_grad[...] = jnp.zeros_like(vec_grad)
    branch = grad_middle[...].astype(low_type)
    grad_mixed = nt(branch, wide[:, 4 * D :]).astype(low_type)
    grad_wide[:, 4 * D :] = tn(mixed[...], branch)
    scale = 1.0 / math.sqrt(D // HE)
    heads = LANES * HE // D
    for image in range(batch):
        span = pl.ds(image * rows, rows)
        for group in range(D // LANES):
            lane = group * LANES
            query, key, value = attend_back(
                qkv[span, lane : lane + LANES],
                qkv[span, D + lane : D + lane + LANES],
                qkv[span, 2 * D + lane : 2 * D + lane + LANES],
                grad_mixed[image * rows : (image + 1) * rows, lane : lane + LANES],
                heads,
                KEEP + 1,
            )
            grads[span, lane : lane + LANES] = (query * scale).astype(low_type)
            grads[span, D + lane : D + lane + LANES] = key.astype(low_type)
            grads[span, 2 * D + lane : 2 * D + lane + LANES] = value.astype(low_type)
    vec_grad[4:5] = col_sum(grads[:, :D])
    vec_grad[5:6] = col_sum(grads[:, 2 * D :])
    rows_in = normed[...]
    for part in range(3):
        grad_wide[:, (part + 1) * D : (part + 2) * D] = tn(rows_in, grads[:, part * D : (part + 1) * D])
    grad_normed = nt(grads[...], wide[:, D : 4 * D])
    unit, rate = standard(start[...])
    vec_grad[2:3] = col_sum(grad_normed * unit)
    vec_grad[3:4] = col_sum(grad_normed)
    grad_rows = standard_back(unit, rate, grad_normed * vec[2:3]) + grad_middle[...]
    inner = lax.broadcasted_iota(jnp.int32, (grad_rows.shape[0], 1), 0) % rows
    vec_grad[1:2] = col_sum(jnp.where(inner == CLASS_ENC, grad_rows, 0.0))
    embed = jnp.where(inner < KEEP, grad_rows, 0.0).astype(low_type)
    vec_grad[0:1] = col_sum(embed)
    grad_wide[:, :D] = tn(kept[...], embed)
    width = 5 * D // 8
    for block in range(8):
        for tile in range(4):
            lane = block * width + tile * LANES
            size = min(LANES, (block + 1) * width - lane)
            piece = grad_wide[:, lane : lane + size]
            if size < LANES:
                piece = jnp.concatenate([piece, jnp.zeros((D, LANES - size), high_type)], 1)
            tiles[block * 4 + tile] = piece
    rows_block = D // 4
    send_tiles(tiles, blob, sems.at[1], 32, rows_block, 4, 0, rows_block)
    folded.wait()
    wait_tiles(tiles, sems.at[1])


def table_of(width, rows):
    quarter = width // 4
    omega = (np.float32(1.0) / np.float32(10000.0) ** (np.arange(quarter, dtype=np.float32) / np.float32(quarter))).astype(np.float32)
    coord = np.arange(SIDE * SIDE)

    def half(place):
        angle = place.astype(np.float32)[:, None] * omega[None, :]
        return np.concatenate([np.sin(angle), np.cos(angle)], 1)

    table = np.concatenate([half(coord // SIDE), half(coord % SIDE)], 1).astype(np.float32)
    return np.concatenate([table, np.zeros((rows - table.shape[0], width), np.float32)], 0)


def whole():
    return pl.BlockSpec(memory_space=pltpu.VMEM)


def hbm():
    return pl.BlockSpec(memory_space=pltpu.HBM)


def params(**more):
    return pltpu.CompilerParams(vmem_limit_bytes=60 << 20, **more)


def local_grads(enc_blocks, enc_ffn, proj, dec3, head_low, smalls_parts, patches, shuffle, count):
    enc_vec, enc_up, dec_vec, dec_up, head_bias = smalls_parts
    enc_up, dec_up, head_bias = enc_up[None], dec_up[None], head_bias[None]
    batch = patches.shape[0]
    shape = jax.ShapeDtypeStruct
    keep = jnp.concatenate(
        [
            shuffle[:, :KEEP],
            jnp.full((batch, 1), CLASS_DEC, jnp.int32),
            jnp.full((batch, ENC_ROWS - KEEP - 1), -1, jnp.int32),
        ],
        1,
    )
    places = jnp.arange(DEC_ROWS, dtype=jnp.int32)
    pick = (keep[:, :, None] == places[None, None, :]).astype(low_type)
    picked = (keep[:, None, :] == places[None, :, None]).astype(low_type)
    padded = jnp.pad(patches, ((0, 0), (0, DEC_ROWS - PATCHES), (0, 0)))
    enc_pos = jnp.asarray(table_of(D, DEC_ROWS))
    dec_pos = jnp.asarray(table_of(E, DEC_ROWS))
    rows, dec_rows = batch * ENC_ROWS, batch * DEC_ROWS

    wide = pl.pallas_call(
        wide_kernel,
        out_shape=shape((D, 5 * D), low_type),
        in_specs=[whole()],
        out_specs=whole(),
        compiler_params=params(),
        name="wide",
    )(enc_blocks)
    kept, start, normed, qkv, mixed, middle, normed_two = pl.pallas_call(
        functools.partial(enc_attend_kernel, batch),
        out_shape=(
            shape((rows, D), low_type),
            shape((rows, D), high_type),
            shape((rows, D), low_type),
            shape((rows, 3 * D), low_type),
            shape((rows, D), low_type),
            shape((rows, D), high_type),
            shape((rows, D), low_type),
        ),
        in_specs=[whole()] * 5,
        out_specs=[whole()] * 7,
        compiler_params=params(),
        name="enc_attend",
    )(pick, padded, wide, enc_vec, enc_pos)
    slope, active, enc_out, latent, entry = pl.pallas_call(
        enc_ffn_kernel,
        out_shape=(
            shape((rows, F), high_type),
            shape((rows, F), low_type),
            shape((rows, D), high_type),
            shape((rows, D), low_type),
            shape((rows, E), high_type),
        ),
        in_specs=[whole()] * 7,
        out_specs=[whole()] * 5,
        compiler_params=params(),
        name="enc_ffn",
    )(middle, normed_two, enc_ffn, enc_vec, enc_up, proj, dec_vec)

    def by_image(*block):
        return pl.BlockSpec(block, lambda i: (i,) + (0,) * (len(block) - 1))

    def fixed(*block):
        return pl.BlockSpec(block, lambda i: (0,) * len(block))

    dec_start, dec_normed, dec_qkv, dec_mixed, dec_middle, dec_normed_two = pl.pallas_call(
        dec_attend_kernel,
        grid=(batch,),
        out_shape=(
            shape((dec_rows, E), high_type),
            shape((dec_rows, E), low_type),
            shape((dec_rows, 3 * E), low_type),
            shape((dec_rows, E), low_type),
            shape((dec_rows, E), high_type),
            shape((dec_rows, E), low_type),
        ),
        in_specs=[
            by_image(ENC_ROWS, E),
            by_image(1, DEC_ROWS, ENC_ROWS),
            fixed(DEC_ROWS, E),
            fixed(1, E, 4 * E),
            fixed(12, E),
        ],
        out_specs=[
            by_image(DEC_ROWS, E),
            by_image(DEC_ROWS, E),
            by_image(DEC_ROWS, 3 * E),
            by_image(DEC_ROWS, E),
            by_image(DEC_ROWS, E),
            by_image(DEC_ROWS, E),
        ],
        compiler_params=params(),
        name="dec_attend",
    )(entry, picked, dec_pos, dec3, dec_vec)

    images = 2 if batch % 2 == 0 else 1
    block = images * DEC_ROWS
    blob_shape = shape((8, 4, 2784, LANES), high_type)
    vm = pltpu.VMEM
    dma = pltpu.SemaphoreType.DMA
    grad_middle, grad_mixed, grad_head, dec_grad_one, dec_up_grad, head_bias_grad, loss, blob = pl.pallas_call(
        functools.partial(dec_ffn_kernel, images, batch // images - 1, count),
        grid=(batch // images,),
        out_shape=(
            shape((dec_rows, E), high_type),
            shape((dec_rows, E), low_type),
            shape((E, P_SIZE), high_type),
            shape((12, E), high_type),
            shape((1, H), high_type),
            shape((1, P_SIZE), high_type),
            shape((8, LANES), high_type),
            blob_shape,
        ),
        in_specs=[
            by_image(block, E),
            by_image(block, E),
            by_image(block, E),
            by_image(block, P_SIZE),
            by_image(images, DEC_ROWS, ENC_ROWS),
            fixed(3, E, H),
            fixed(E, P_SIZE),
            fixed(12, E),
            fixed(1, H),
            fixed(1, P_SIZE),
        ],
        out_specs=[
            by_image(block, E),
            by_image(block, E),
            fixed(E, P_SIZE),
            fixed(12, E),
            fixed(1, H),
            fixed(1, P_SIZE),
            fixed(8, LANES),
            hbm(),
        ],
        scratch_shapes=[
            vm((block, H), low_type),
            vm((block, H), high_type),
            vm((H // LANES, E, LANES), high_type),
            vm((H // LANES, E, LANES), high_type),
            vm((E // LANES, E, LANES), high_type),
            dma((3,)),
        ],
        compiler_params=params(),
        name="dec_ffn",
    )(dec_middle, dec_normed_two, dec_mixed, padded.reshape(dec_rows, P_SIZE), picked, dec3, head_low, dec_vec, dec_up, head_bias)

    grad_entry, dec_grad_two, blob = pl.pallas_call(
        functools.partial(dec_back_kernel, batch - 1),
        grid=(batch,),
        out_shape=(shape((rows, E), low_type), shape((12, E), high_type), blob_shape),
        in_specs=[
            hbm(),
            by_image(DEC_ROWS, 3 * E),
            by_image(DEC_ROWS, E),
            by_image(DEC_ROWS, E),
            by_image(DEC_ROWS, E),
            by_image(DEC_ROWS, E),
            by_image(1, ENC_ROWS, DEC_ROWS),
            by_image(1, DEC_ROWS, ENC_ROWS),
            fixed(1, E, 4 * E),
            fixed(12, E),
        ],
        out_specs=[by_image(ENC_ROWS, E), fixed(12, E), hbm()],
        scratch_shapes=[vm((DEC_ROWS, 3 * E), low_type), vm((3 * E // LANES, E, LANES), high_type), dma],
        input_output_aliases={0: 2},
        compiler_params=params(),
        name="dec_back",
    )(blob, dec_qkv, dec_normed, dec_start, grad_middle, grad_mixed, pick, picked, dec3, dec_vec)

    enc_grad_middle, grad_proj, enc_grad_one, enc_up_grad, entry_grad, blob = pl.pallas_call(
        enc_ffn_back_kernel,
        out_shape=(
            shape((rows, D), high_type),
            shape((D, E), high_type),
            shape((12, D), high_type),
            shape((1, F), high_type),
            shape((1, E), high_type),
            blob_shape,
        ),
        in_specs=[hbm()] + [whole()] * 10,
        out_specs=[whole()] * 5 + [hbm()],
        scratch_shapes=[
            vm((F // LANES, D, LANES), high_type),
            vm((F // LANES, D, LANES), high_type),
            dma((2,)),
        ],
        input_output_aliases={0: 5},
        compiler_params=params(),
        name="enc_ffn_back",
    )(blob, grad_entry, latent, enc_out, middle, normed_two, slope, active, enc_ffn, proj, enc_vec)
    folded = grad_proj.reshape(4, 2, 96, 8, 64).transpose(3, 0, 2, 1, 4).reshape(8, 4, 96, LANES)
    enc_grad_two, blob = pl.pallas_call(
        functools.partial(enc_back_kernel, batch),
        out_shape=(shape((12, D), high_type), blob_shape),
        in_specs=[hbm(), hbm()] + [whole()] * 8,
        out_specs=[whole(), hbm()],
        scratch_shapes=[
            vm((rows, 3 * D), low_type),
            vm((D, 5 * D), high_type),
            vm((32, D, LANES), high_type),
            dma((2,)),
        ],
        input_output_aliases={0: 1},
        compiler_params=params(),
        name="enc_back",
    )(blob, folded, qkv, kept, normed, start, mixed, enc_grad_middle, wide, enc_vec)
    dec_grad = (dec_grad_one + dec_grad_two).at[0].set(entry_grad[0])
    smalls = jnp.concatenate(
        [
            (enc_grad_one + enc_grad_two).reshape(-1),
            enc_up_grad[0],
            dec_grad.reshape(-1),
            dec_up_grad[0],
            head_bias_grad[0],
        ]
    )
    return blob, grad_head, smalls, loss[0, 0]


def untile(block, rows, width):
    tiles = -(-width // LANES)
    return block.reshape(tiles, rows, LANES).transpose(1, 0, 2).reshape(rows, tiles * LANES)[:, :width]


def unfold_proj(block):
    width = block.shape[1] // 2
    return jnp.concatenate([block[:, :width], block[:, width:]], 0)


def unpack_shards(blob):
    cuts = [0, 768, 576, 576, 256, 256, 256, 96]
    places = [sum(cuts[: index + 1]) for index in range(len(cuts))]
    piece = [blob[places[index] : places[index + 1]] for index in range(7)]
    return (
        untile(piece[0], 192, 480),
        jnp.stack([untile(piece[1], 192, 384), untile(piece[2], 192, 384)]),
        unfold_proj(piece[6]),
        untile(piece[3], 128, 256),
        jnp.stack([untile(piece[4], 128, 256), untile(piece[5], 128, 256)]),
    )


def whole_arrays(blob):
    col_size, row_size = blob.shape[:2]
    parts = jax.vmap(jax.vmap(unpack_shards))(blob)

    def joined(array):
        if array.ndim == 4:
            return array.transpose(1, 2, 0, 3).reshape(row_size * array.shape[2], col_size * array.shape[3])
        return array.transpose(2, 1, 3, 0, 4).reshape(2, row_size * array.shape[3], col_size * array.shape[4])

    return tuple(joined(item) for item in parts)


def on_small_plane():
    return lax.axis_size("row") == 4 and lax.axis_size("col") == 8


def gather_weights(enc_w, enc_ffn, dec_proj, dec_w, dec_ffn):
    shards = [item.astype(low_type) for item in (enc_w, enc_ffn, dec_proj, jnp.concatenate([dec_w[None], dec_ffn], 0))]
    if on_small_plane():
        enc, ffn, proj, dec = gather_blocks(*shards, lax.axis_size("col") // 2)
        return enc, ffn, proj.transpose(1, 0, 2).reshape(D, E), dec
    full = []
    for item in shards:
        rowed = lax.all_gather(item, "row", axis=item.ndim - 2, tiled=True)
        full.append(lax.all_gather(rowed, "col", axis=item.ndim - 1, tiled=True))
    return full[0].reshape(D, 8, 5 * D // 8).transpose(1, 0, 2), full[1], full[2], full[3]


def reduce_grads(blob, smalls, loss):
    count = smalls.shape[0]
    if on_small_plane():
        small = jnp.concatenate([smalls, loss[None], jnp.zeros((32 * 8 * LANES - count - 1,), high_type)])
        summed, small = reduce_blocks(blob, small.reshape(32, 8, LANES), lax.axis_size("col") // 2, 6)
        small = small.reshape(-1)
        return unpack_shards(summed), small[:count], small[count]
    shards = []
    for item in whole_arrays(blob):
        done = lax.psum_scatter(item, "col", scatter_dimension=item.ndim - 1, tiled=True)
        shards.append(lax.psum_scatter(done, "row", scatter_dimension=item.ndim - 2, tiled=True))
    smalls, loss = lax.psum((smalls, loss), ("row", "col"))
    return tuple(shards), smalls, loss


def adam_update(weight, grad, first, second, bias_one, bias_two, decay):
    first_new = 0.5 * first + 0.5 * grad
    second_new = 0.5 * second + 0.5 * grad * grad
    direction = first_new / bias_one / (jnp.sqrt(second_new / bias_two) + 1e-08)
    return (weight - 0.02 * (direction + decay * weight), first_new, second_new)


def body(
    patches,
    shuffle,
    enc_w,
    enc_ffn,
    dec_proj,
    dec_w,
    dec_ffn,
    head_w,
    smalls,
    first_enc_w,
    first_enc_ffn,
    first_dec_proj,
    first_dec_w,
    first_dec_ffn,
    first_head_w,
    first_smalls,
    second_enc_w,
    second_enc_ffn,
    second_dec_proj,
    second_dec_w,
    second_dec_ffn,
    second_head_w,
    second_smalls,
):
    enc_blocks, enc_ffn_w, proj, dec3 = gather_weights(enc_w, enc_ffn, dec_proj, dec_w, dec_ffn)
    count = patches.shape[0] * lax.axis_size("row") * lax.axis_size("col") * (PATCHES - KEEP) * P_SIZE
    blob, grad_head, grad_smalls, loss_local = local_grads(
        enc_blocks, enc_ffn_w, proj, dec3, head_w.astype(low_type), unpack(smalls), patches, shuffle, count
    )
    summed_head = lax.psum(grad_head, ("row", "col"))
    sharded, summed_smalls, loss_sum = reduce_grads(blob, grad_smalls, loss_local)
    grads = (sharded[0], sharded[1], sharded[2], sharded[3], sharded[4], summed_head, summed_smalls)
    params = (enc_w, enc_ffn, dec_proj, dec_w, dec_ffn, head_w, smalls)
    firsts = (
        first_enc_w,
        first_enc_ffn,
        first_dec_proj,
        first_dec_w,
        first_dec_ffn,
        first_head_w,
        first_smalls,
    )
    seconds = (
        second_enc_w,
        second_enc_ffn,
        second_dec_proj,
        second_dec_w,
        second_dec_ffn,
        second_head_w,
        second_smalls,
    )
    decays = (0.05, 0.05, 0.05, 0.05, 0.05, 0.05, 0.0)
    bias_one = 1.0 - 0.5**STEP
    bias_two = 1.0 - 0.5**STEP
    results = [
        adam_update(
            params[index],
            grads[index],
            firsts[index],
            seconds[index],
            bias_one,
            bias_two,
            decays[index],
        )
        for index in range(7)
    ]
    news = [item[0] for item in results]
    moments = [item[1] for item in results]
    squares = [item[2] for item in results]
    return (
        news[0],
        news[1],
        news[2],
        news[3],
        news[4],
        news[5],
        news[6],
        moments[0],
        moments[1],
        moments[2],
        moments[3],
        moments[4],
        moments[5],
        moments[6],
        squares[0],
        squares[1],
        squares[2],
        squares[3],
        squares[4],
        squares[5],
        squares[6],
        loss_sum / count,
    )


def solution(mesh):
    in_specs = (
        P(("row", "col"), None, None),
        P(("row", "col"), None),
        P("row", "col"),
        P(None, "row", "col"),
        P("row", "col"),
        P("row", "col"),
        P(None, "row", "col"),
        P(),
        P(),
        P("row", "col"),
        P(None, "row", "col"),
        P("row", "col"),
        P("row", "col"),
        P(None, "row", "col"),
        P(),
        P(),
        P("row", "col"),
        P(None, "row", "col"),
        P("row", "col"),
        P("row", "col"),
        P(None, "row", "col"),
        P(),
        P(),
    )
    out_specs = (
        P("row", "col"),
        P(None, "row", "col"),
        P("row", "col"),
        P("row", "col"),
        P(None, "row", "col"),
        P(),
        P(),
        P("row", "col"),
        P(None, "row", "col"),
        P("row", "col"),
        P("row", "col"),
        P(None, "row", "col"),
        P(),
        P(),
        P("row", "col"),
        P(None, "row", "col"),
        P("row", "col"),
        P("row", "col"),
        P(None, "row", "col"),
        P(),
        P(),
        P(),
    )
    return jax.shard_map(body, mesh=mesh, in_specs=in_specs, out_specs=out_specs, check_vma=False)
```

```python
import functools
import math

import jax
import jax.numpy as jnp
import numpy as np
from jax import lax
from jax.experimental import pallas as pl
from jax.experimental.pallas import tpu as pltpu
from jax.sharding import PartitionSpec as P

D = 768
HE = 12
F = 3072
E = 512
HD = 16
H = 2048
P_SIZE = 768
SIDE = 14
KEEP = 49
STEP = 5
PATCHES = 196
LANES = 128

norm_eps = 1e-06
low_type = jnp.bfloat16
high_type = jnp.float32


def unpack(smalls):
    first = 12 * D
    second = first + F
    third = second + 12 * E
    fourth = third + H
    return (
        smalls[:first].reshape(12, D),
        smalls[first:second],
        smalls[second:third].reshape(12, E),
        smalls[third:fourth],
        smalls[fourth:],
    )


MESH = pl.DeviceIdType.MESH


class Group:
    def __init__(self, copies):
        self.copies = copies

    def start(self):
        for item in self.copies:
            item.start()

    def wait_recv(self):
        for item in self.copies:
            item.wait_recv()

    def wait_send(self):
        for item in self.copies:
            item.wait_send()

    def wait(self):
        for item in self.copies:
            item.wait()


def gather_kernel(depth, own_enc, own_ffn, own_proj, own_dec, enc, ffn, proj, dec,
                  zs, zr, xs, xr, ys, yr, dxs, dxr, dys, dyr, cs, cr, local):
    row = lax.axis_index("row")
    col = lax.axis_index("col")
    y, x, z, k = row // 2, row % 2, col // 2, col % 2
    row_x = y * 2 + (1 - x)
    row_y = (1 - y) * 2 + x
    row_d = (1 - y) * 2 + (1 - x)
    near_x, near_y = (row_x, col), (row_y, col)
    twin = (row, z * 2 + (1 - k))
    lower, upper = (row, col - 2), (row, col + 2)
    has_lower, has_upper = z > 0, z < depth - 1
    own = (own_enc, own_ffn, own_proj, own_dec)

    barrier = pltpu.get_barrier_semaphore()
    for other in (near_x, near_y, twin):
        pl.semaphore_signal(barrier, inc=1, device_id=other, device_id_type=MESH)

    @pl.when(has_lower)
    def _():
        pl.semaphore_signal(barrier, inc=1, device_id=lower, device_id_type=MESH)

    @pl.when(has_upper)
    def _():
        pl.semaphore_signal(barrier, inc=1, device_id=upper, device_id_type=MESH)

    pl.semaphore_wait(barrier, 3 + jnp.where(has_lower, 1, 0) + jnp.where(has_upper, 1, 0))

    levels = [(0, 0)] + [(d, way) for d in range(1, depth) for way in (0, 1)]
    level_of = {item: number for number, item in enumerate(levels)}

    def place(level):
        d, way = level
        return z - d if way == 0 else z + d

    def valid(level):
        d, way = level
        return z - d >= 0 if way == 0 else z + d < depth

    def cut(index, row_now, half=None):
        def rows(size, unit):
            part = size if half is None else size // 2
            first = 0 if half is None else half * part
            return pl.ds(pl.multiple_of(row_now * size + first, 16), part)

        tall, short = own_enc.shape[0], own_dec.shape[1]
        wide, thin = own_ffn.shape[2], own_dec.shape[2]
        return (
            enc.at[index, rows(tall, 16)],
            ffn.at[:, rows(tall, 16), pl.ds(pl.multiple_of(index * wide, LANES), wide)],
            proj.at[index, rows(tall, 16)],
            dec.at[:, rows(short, 16), pl.ds(pl.multiple_of(index * thin, LANES), thin)],
        )

    def slot(level, row_now, half=None):
        return cut(place(level) * 2 + k, row_now, half)

    def source(level):
        return own if level == (0, 0) else slot(level, row)

    def copy(src, dst, send, recv, target):
        return Group(
            [
                pltpu.make_async_remote_copy(
                    src_ref=src[item],
                    dst_ref=dst[item],
                    send_sem=send.at[item],
                    recv_sem=recv.at[item],
                    device_id=target,
                    device_id_type=MESH,
                )
                for item in range(4)
            ]
        )

    def z_copy(level, way):
        d = level[0]
        n = level_of[level]
        return copy(source(level), slot(level, row), zs.at[n, way], zr.at[d, way], upper if way == 0 else lower)

    def x_copy(level):
        n = level_of[level]
        return copy(source(level), slot(level, row), xs.at[n], xr.at[n], near_x)

    def y_copy(level):
        n = level_of[level]
        return copy(source(level), slot(level, row), ys.at[n], yr.at[n], near_y)

    def dx_copy(level):
        n = level_of[level]
        refs = slot(level, row_y, 1)
        return copy(refs, refs, dxs.at[n], dxr.at[n], near_x)

    def dy_copy(level):
        n = level_of[level]
        refs = slot(level, row_x, 0)
        return copy(refs, refs, dys.at[n], dyr.at[n], near_y)

    def twin_copy(level, kind):
        n = level_of[level]
        row_now = (row, row_x, row_y, row_d)[kind]
        src = source(level) if kind == 0 else slot(level, row_now)
        return copy(src, slot(level, row_now), cs.at[n, kind], cr.at[n, kind], twin)

    def guarded(level, action):
        if level == (0, 0):
            action()
        else:
            pl.when(valid(level))(action)

    def spread(level):
        d, way = level

        def action():
            if level != (0, 0):
                z_copy((d - 1, way if d > 1 else 0), way).wait_recv()
            for direction in (0, 1):
                if level == (0, 0) or direction == way:
                    @pl.when(has_upper if direction == 0 else has_lower)
                    def _():
                        z_copy(level, direction).start()
            x_copy(level).start()
            y_copy(level).start()
            twin_copy(level, 0).start()

        guarded(level, action)

    def turn(level):
        def action():
            x_copy(level).wait_recv()
            dy_copy(level).start()
            twin_copy(level, 1).start()
            y_copy(level).wait_recv()
            dx_copy(level).start()
            twin_copy(level, 2).start()

        guarded(level, action)

    def close(level):
        def action():
            dx_copy(level).wait_recv()
            dy_copy(level).wait_recv()
            twin_copy(level, 3).start()

        guarded(level, action)

    def drain(level):
        d, way = level

        def action():
            for direction in (0, 1):
                if level == (0, 0) or direction == way:
                    @pl.when(has_upper if direction == 0 else has_lower)
                    def _():
                        z_copy(level, direction).wait_send()
            x_copy(level).wait_send()
            y_copy(level).wait_send()
            dx_copy(level).wait_send()
            dy_copy(level).wait_send()
            for kind in range(4):
                twin_copy(level, kind).wait()

        guarded(level, action)

    keep = Group(
        [pltpu.make_async_copy(src, dst, local.at[item]) for item, (src, dst) in enumerate(zip(own, cut(col, row)))]
    )
    keep.start()
    for step in range(depth + 2):
        for level in levels:
            if level[0] == step:
                spread(level)
        for level in levels:
            if level[0] == step - 1:
                turn(level)
        for level in levels:
            if level[0] == step - 2:
                close(level)
    keep.wait()
    for level in levels:
        drain(level)


def gather_blocks(own_enc, own_ffn, own_proj, own_dec, depth):
    count = 2 * depth - 1
    cols = 2 * depth
    dma = pltpu.SemaphoreType.DMA
    anywhere = pl.BlockSpec(memory_space=pltpu.HBM)
    tall, width = own_enc.shape
    shape = jax.ShapeDtypeStruct
    kind = own_enc.dtype
    return pl.pallas_call(
        functools.partial(gather_kernel, depth),
        out_shape=(
            shape((cols, 4 * tall, width), kind),
            shape((2, 4 * tall, cols * own_ffn.shape[2]), kind),
            shape((cols, 4 * tall, own_proj.shape[1]), kind),
            shape((3, 4 * own_dec.shape[1], cols * own_dec.shape[2]), kind),
        ),
        in_specs=[anywhere] * 4,
        out_specs=[anywhere] * 4,
        scratch_shapes=[dma((count, 2, 4)), dma((depth, 2, 4))]
        + [dma((count, 4)) for _ in range(8)]
        + [dma((count, 4, 4)), dma((count, 4, 4)), dma((4,))],
        compiler_params=pltpu.CompilerParams(collective_id=0, has_side_effects=True),
        name="gather_blocks",
    )(own_enc, own_ffn, own_proj, own_dec)


def far_first(depth):
    orders = []
    for z in range(depth):
        orders.append(sorted(range(depth), key=lambda t: (-abs(t - z), -abs(2 * t - depth + 1))))
    return orders


code_type = jnp.int16
code_top = 32767.0


def encode(values):
    peak = jnp.max(jnp.abs(values), axis=0, keepdims=True)
    unit = jnp.maximum(peak, 1e-30) * (1.0 / code_top)
    codes = jnp.round(values * (1.0 / unit))
    codes = jnp.clip(codes, -code_top, code_top)
    return codes.astype(jnp.int32).astype(code_type), unit


def decode(codes, unit):
    return codes.astype(jnp.int32).astype(high_type) * unit


def reduce_kernel(depth, devices, cols, parts, chunk, half, blob, small, out, small_out,
                  arrived, mine, stage_x, stage_y, recv_x, recv_y, turn_x, turn_y, back_x, back_y, line_out, line,
                  units_out, units_in, line_units, box,
                  s_load, s_cs, s_cr, s_xs, s_xr, s_ys, s_yr, s_txs, s_txr, s_tys, s_tyr, s_zs, s_zr,
                  u_xs, u_xr, u_ys, u_yr, u_txs, u_txr, u_tys, u_tyr, u_zs, u_zr,
                  s_ps, s_pr, s_qs, s_qr):
    row = lax.axis_index("row")
    col = lax.axis_index("col")
    y, x, z, k = row // 2, row % 2, col // 2, col % 2
    me = row * cols + col
    near_x, near_y = (y * 2 + (1 - x), col), ((1 - y) * 2 + x, col)
    twin = (row, z * 2 + (1 - k))
    lower, upper = (row, col - 2), (row, col + 2)
    has_lower, has_upper = z > 0, z < depth - 1
    steps = depth * parts
    slots = mine.shape[0]
    ahead = slots - 1
    a_rows, b_rows = pl.ds(0, half), pl.ds(half, chunk - half)

    def device(offset):
        index = (me + offset) % devices
        return (index // cols, index % cols)

    barrier = pltpu.get_barrier_semaphore()
    for offset in range(1, devices):
        pl.semaphore_signal(barrier, inc=1, device_id=device(offset), device_id_type=MESH)
    pl.semaphore_wait(barrier, devices - 1)

    def copy(src, dst, send, recv, target):
        return pltpu.make_async_remote_copy(
            src_ref=src, dst_ref=dst, send_sem=send, recv_sem=recv, device_id=target, device_id_type=MESH
        )

    orders = far_first(depth)

    def goal(t):
        turn = t // parts
        value = 0
        for a in range(depth):
            for b in range(depth):
                value = jnp.where((z == a) & (turn == b), orders[a][b], value)
        return value

    def span(t):
        return pl.ds(pl.multiple_of((t % parts) * chunk, 16), chunk)

    def load(t):
        return pltpu.make_async_copy(
            blob.at[goal(t) * 2 + k, :, span(t)], mine.at[t % slots], s_load.at[t % slots]
        )

    def core(t):
        return copy(blob.at[goal(t) * 2 + (1 - k), :, span(t)], arrived.at[t], s_cs.at[t], s_cr.at[t], twin)

    def paired(kind, src, dst, send, recv, unit_send, unit_recv, target):
        def make(t):
            return Group([
                copy(src.at[t], dst.at[t], send.at[t], recv.at[t], target),
                copy(units_out.at[t, kind], units_in.at[t, kind], unit_send.at[t], unit_recv.at[t], target),
            ])

        return make

    first_x = paired(0, stage_x, recv_x, s_xs, s_xr, u_xs, u_xr, near_x)
    first_y = paired(1, stage_y, recv_y, s_ys, s_yr, u_ys, u_yr, near_y)
    second_x = paired(2, turn_x, back_x, s_txs, s_txr, u_txs, u_txr, near_x)
    second_y = paired(3, turn_y, back_y, s_tys, s_tyr, u_tys, u_tyr, near_y)

    def along(t, index, target):
        return Group([
            copy(line_out.at[t], line.at[index], s_zs.at[t], s_zr.at[index], target),
            copy(units_out.at[t, 4], line_units.at[index], u_zs.at[t], u_zr.at[index], target),
        ])

    def upper_index(t):
        return (goal(t) + 1) * parts + t % parts

    def lower_index(t):
        return goal(t) * parts + t % parts

    def to_upper(t):
        return along(t, upper_index(t), upper)

    def to_lower(t):
        return along(t, lower_index(t), lower)

    def small_send(offset):
        target = device(offset)
        return copy(small.at[target[0] * cols + target[1]], box.at[offset], s_ps.at[offset], s_pr.at[offset], target)

    def small_back(offset):
        return copy(small_out.at[me], small_out.at[me], s_qs.at[offset], s_qr.at[offset], device(offset))

    def small_back_recv(offset):
        origin = (me + devices - offset) % devices
        return copy(small_out.at[origin], small_out.at[origin], s_qs.at[offset], s_qr.at[offset], device(offset))

    for t in range(ahead):
        load(t).start()
        core(t).start()
    for offset in range(1, devices):
        small_send(offset).start()

    def stage_one(t):
        load(t).wait()
        core(t).wait_recv()
        slot = t % slots
        for other in (0, 1):
            away = other * 2 + (1 - x)
            stay = other * 2 + x
            codes, unit = encode(mine[slot, away, a_rows] + arrived[t, away, a_rows])
            stage_x[t, other] = codes
            units_out[t, 0, pl.ds(other, 1)] = unit
            arrived[t, stay, a_rows] += mine[slot, stay, a_rows]
        first_x(t).start()
        for other in (0, 1):
            away = (1 - y) * 2 + other
            stay = y * 2 + other
            codes, unit = encode(mine[slot, away, b_rows] + arrived[t, away, b_rows])
            stage_y[t, other] = codes
            units_out[t, 1, pl.ds(other, 1)] = unit
            arrived[t, stay, b_rows] += mine[slot, stay, b_rows]
        first_y(t).start()

    def stage_two(t):
        first_x(t).wait_recv()
        away = (1 - y) * 2 + x
        codes, unit = encode(arrived[t, away, a_rows] + decode(recv_x[t, 1 - y], units_in[t, 0, pl.ds(1 - y, 1)]))
        turn_y[t] = codes
        units_out[t, 3, pl.ds(0, 1)] = unit
        second_y(t).start()
        arrived[t, row, a_rows] += decode(recv_x[t, y], units_in[t, 0, pl.ds(y, 1)])
        first_y(t).wait_recv()
        away = y * 2 + (1 - x)
        codes, unit = encode(arrived[t, away, b_rows] + decode(recv_y[t, 1 - x], units_in[t, 1, pl.ds(1 - x, 1)]))
        turn_x[t] = codes
        units_out[t, 2, pl.ds(0, 1)] = unit
        second_x(t).start()
        arrived[t, row, b_rows] += decode(recv_y[t, x], units_in[t, 1, pl.ds(x, 1)])

    def stage_three(t):
        second_y(t).wait_recv()
        arrived[t, row, a_rows] += decode(back_y[t], units_in[t, 3, pl.ds(0, 1)])
        second_x(t).wait_recv()
        arrived[t, row, b_rows] += decode(back_x[t], units_in[t, 2, pl.ds(0, 1)])

    def take(index):
        return decode(line[index], line_units[index, pl.ds(0, 1)])

    def pack(t):
        codes, unit = encode(arrived[t, row])
        line_out[t] = codes
        units_out[t, 4, pl.ds(0, 1)] = unit

    def stage_four(t):
        target = goal(t)

        @pl.when((target >= z) & has_lower)
        def _():
            to_upper(t).wait_recv()
            arrived[t, row] += take(upper_index(t))

        @pl.when((target <= z) & has_upper)
        def _():
            to_lower(t).wait_recv()
            arrived[t, row] += take(lower_index(t))

        @pl.when(target != z)
        def _():
            pack(t)

        @pl.when(target > z)
        def _():
            to_upper(t).start()

        @pl.when(target < z)
        def _():
            to_lower(t).start()

        @pl.when(target == z)
        def _():
            out[span(t)] = arrived[t, row]

    lags = (2, 4, 6)

    def body(i, carry):
        @pl.when(i + ahead < steps)
        def _():
            load(i + ahead).start()
            core(i + ahead).start()

        @pl.when(i < steps)
        def _():
            stage_one(i)

        for lag, stage in zip(lags, (stage_two, stage_three, stage_four)):
            @pl.when((i >= lag) & (i - lag < steps))
            def _():
                stage(i - lag)

        @pl.when(i == steps // 2)
        def _():
            total = small[me]
            for offset in range(1, devices):
                small_send(offset).wait_recv()
                total = total + box[offset]
            small_out[me] = total
            for offset in range(1, devices):
                small_back(offset).start()

        return carry

    lax.fori_loop(0, steps + lags[-1], body, 0)

    def finish(t, carry):
        core(t).wait_send()
        first_x(t).wait_send()
        first_y(t).wait_send()
        second_x(t).wait_send()
        second_y(t).wait_send()

        @pl.when(goal(t) > z)
        def _():
            to_upper(t).wait_send()

        @pl.when(goal(t) < z)
        def _():
            to_lower(t).wait_send()

        return carry

    lax.fori_loop(0, steps, finish, 0)
    for offset in range(1, devices):
        small_send(offset).wait_send()
        small_back(offset).wait_send()
        small_back_recv(offset).wait_recv()


def reduce_blocks(blob, small, depth, parts):
    cols, _, rows, lanes = blob.shape
    devices = 4 * cols
    chunk = rows // parts
    half = -(-chunk // 32) * 16
    rest = chunk - half
    steps = depth * parts
    lines = (depth + 1) * parts
    dma = pltpu.SemaphoreType.DMA
    vm = pltpu.VMEM
    return pl.pallas_call(
        functools.partial(reduce_kernel, depth, devices, cols, parts, chunk, half),
        out_shape=(
            jax.ShapeDtypeStruct((rows, lanes), high_type),
            jax.ShapeDtypeStruct(small.shape, high_type),
        ),
        in_specs=[pl.BlockSpec(memory_space=pltpu.HBM), pl.BlockSpec(memory_space=pltpu.VMEM)],
        out_specs=[pl.BlockSpec(memory_space=pltpu.VMEM)] * 2,
        scratch_shapes=[
            vm((steps, 4, chunk, lanes), high_type),
            vm((4, 4, chunk, lanes), high_type),
            vm((steps, 2, half, lanes), code_type),
            vm((steps, 2, rest, lanes), code_type),
            vm((steps, 2, half, lanes), code_type),
            vm((steps, 2, rest, lanes), code_type),
            vm((steps, rest, lanes), code_type),
            vm((steps, half, lanes), code_type),
            vm((steps, rest, lanes), code_type),
            vm((steps, half, lanes), code_type),
            vm((steps, chunk, lanes), code_type),
            vm((lines, chunk, lanes), code_type),
            vm((steps, 5, 8, lanes), high_type),
            vm((steps, 4, 8, lanes), high_type),
            vm((lines, 8, lanes), high_type),
            vm((devices,) + small.shape[1:], high_type),
            dma((4,)),
        ]
        + ([dma((steps,)) for _ in range(11)] + [dma((lines,))])
        + ([dma((steps,)) for _ in range(9)] + [dma((lines,))])
        + [dma((devices,)) for _ in range(4)],
        compiler_params=pltpu.CompilerParams(
            collective_id=1, has_side_effects=True, vmem_limit_bytes=62 << 20
        ),
        name="reduce_blocks",
    )(blob, small)


ENC_ROWS = 64
DEC_ROWS = 208
CLASS_ENC = KEEP
CLASS_DEC = PATCHES
NEGATIVE = -1e30


def nn(left, right):
    return jnp.dot(left, right, preferred_element_type=high_type)


def nt(left, right):
    return lax.dot_general(left, right, (((1,), (1,)), ((), ())), preferred_element_type=high_type)


def tn(left, right):
    return lax.dot_general(left, right, (((0,), (0,)), ((), ())), preferred_element_type=high_type)


def standard(rows):
    mean = jnp.mean(rows, -1, keepdims=True)
    centred = rows - mean
    spread = jnp.mean(centred * centred, -1, keepdims=True)
    rate = lax.rsqrt(spread + norm_eps)
    return centred * rate, rate


def standard_back(unit, rate, grad):
    return rate * (grad - jnp.mean(grad, -1, keepdims=True) - unit * jnp.mean(grad * unit, -1, keepdims=True))


def col_sum(rows):
    return jnp.sum(rows.astype(high_type), 0, keepdims=True)


def gelu_pair(value):
    size = jnp.abs(value)
    below = 1.0 + (0.3275911 * math.sqrt(0.5)) * size
    t = pl.reciprocal(below, approx=True)
    t = t * (2.0 - below * t)
    t = t * (2.0 - below * t)
    fall = jnp.exp(-0.5 * value * value)
    series = 1.061405429
    for item in (-1.453152027, 1.421413741, -0.284496736, 0.254829592):
        series = series * t + item
    tail = 0.5 * series * t * fall
    part = jnp.where(value < 0.0, tail, 1.0 - tail)
    return value * part, part + value * fall * (1.0 / math.sqrt(2.0 * math.pi))


def three_way(value):
    high = value.astype(low_type)
    rest = value - high.astype(high_type)
    middle = rest.astype(low_type)
    return high, middle, (rest - middle.astype(high_type)).astype(low_type)


def place_rows(picks, value):
    parts = three_way(value)
    return nn(picks, parts[0]) + nn(picks, parts[1]) + nn(picks, parts[2])


def stack_heads(value, heads):
    width = LANES // heads
    lane = lax.broadcasted_iota(jnp.int32, value.shape, 1) // width
    return jnp.concatenate([jnp.where(lane == head, value, jnp.zeros_like(value)) for head in range(heads)], 0)


def merge_heads(stacked, heads):
    rows = stacked.shape[0] // heads
    width = LANES // heads
    lane = lax.broadcasted_iota(jnp.int32, (rows, LANES), 1) // width
    merged = stacked[:rows]
    for head in range(1, heads):
        merged = jnp.where(lane == head, stacked[head * rows : (head + 1) * rows], merged)
    return merged


def attend(query, key, value, heads, length):
    scores = nt(stack_heads(query, heads), key)
    column = lax.broadcasted_iota(jnp.int32, scores.shape, 1)
    scores = jnp.where(column < length, scores, NEGATIVE)
    raised = jnp.exp(scores - jnp.max(scores, -1, keepdims=True))
    attention = (raised / jnp.sum(raised, -1, keepdims=True)).astype(low_type)
    return merge_heads(nn(attention, value), heads)


def attend_back(query, key, value, grad, heads, length):
    queries = stack_heads(query, heads)
    grads = stack_heads(grad, heads)
    scores = nt(key, queries)
    place = lax.broadcasted_iota(jnp.int32, scores.shape, 0)
    scores = jnp.where(place < length, scores, NEGATIVE)
    raised = jnp.exp(scores - jnp.max(scores, 0, keepdims=True))
    attention = raised * (1.0 / jnp.sum(raised, 0, keepdims=True))
    inner = nt(value, grads)
    grad_scores = (attention * (inner - jnp.sum(inner * attention, 0, keepdims=True))).astype(low_type)
    grad_value = nn(attention.astype(low_type), grads)
    grad_key = nn(grad_scores, queries)
    grad_query = merge_heads(tn(grad_scores, key), heads)
    return grad_query, grad_key, grad_value


def attend_back_many(batch, query, key, value, grad, heads, length):
    rows = query.shape[0] // batch
    spans = [slice(image * rows, (image + 1) * rows) for image in range(batch)]
    queries = [stack_heads(query[span], heads) for span in spans]
    grads = [stack_heads(grad[span], heads) for span in spans]
    scores = jnp.concatenate([nt(key[span], item) for span, item in zip(spans, queries)], 0)
    inner = jnp.concatenate([nt(value[span], item) for span, item in zip(spans, grads)], 0)
    scores = scores.reshape(batch, rows, scores.shape[1])
    inner = inner.reshape(batch, rows, inner.shape[1])
    place = lax.broadcasted_iota(jnp.int32, scores.shape, 1)
    scores = jnp.where(place < length, scores, NEGATIVE)
    raised = jnp.exp(scores - jnp.max(scores, 1, keepdims=True))
    attention = raised * (1.0 / jnp.sum(raised, 1, keepdims=True))
    grad_scores = (attention * (inner - jnp.sum(inner * attention, 1, keepdims=True))).astype(low_type)
    attention = attention.astype(low_type)
    grad_value = [nn(attention[image], grads[image]) for image in range(batch)]
    grad_key = [nn(grad_scores[image], queries[image]) for image in range(batch)]
    grad_query = [merge_heads(tn(grad_scores[image], key[spans[image]]), heads) for image in range(batch)]
    return tuple(jnp.concatenate(item, 0) for item in (grad_query, grad_key, grad_value))


def wide_kernel(blocks, wide):
    count, _, width = blocks.shape
    for index in range(count):
        wide[:, index * width : (index + 1) * width] = blocks[index]


def enc_attend_kernel(batch, pick, patches, wide, vec, pos, kept, start, normed, qkv, mixed, middle, normed_two):
    rows = ENC_ROWS
    for image in range(batch):
        span = pl.ds(image * rows, rows)
        kept[span] = nn(pick[image], patches[image]).astype(low_type)
    start[...] = nn(kept[...], wide[:, :D]) + vec[0:1]
    parts = three_way(pos[...])
    for image in range(batch):
        span = pl.ds(image * rows, rows)
        picks = pick[image]
        placed = nn(picks, parts[0]) + nn(picks, parts[1]) + nn(picks, parts[2])
        inner = lax.broadcasted_iota(jnp.int32, placed.shape, 0)
        start[span] = jnp.where(inner == CLASS_ENC, vec[1:2], start[span] + placed)
    unit, _ = standard(start[...])
    normed[...] = (unit * vec[2:3] + vec[3:4]).astype(low_type)
    scale = 1.0 / math.sqrt(D // HE)
    rows_in = normed[...]
    qkv[:, :D] = ((nn(rows_in, wide[:, D : 2 * D]) + vec[4:5]) * scale).astype(low_type)
    qkv[:, D : 2 * D] = nn(rows_in, wide[:, 2 * D : 3 * D]).astype(low_type)
    qkv[:, 2 * D :] = (nn(rows_in, wide[:, 3 * D : 4 * D]) + vec[5:6]).astype(low_type)
    heads = LANES * HE // D
    for image in range(batch):
        span = pl.ds(image * rows, rows)
        for group in range(D // LANES):
            lane = group * LANES
            mixed[span, lane : lane + LANES] = attend(
                qkv[span, lane : lane + LANES],
                qkv[span, D + lane : D + lane + LANES],
                qkv[span, 2 * D + lane : 2 * D + lane + LANES],
                heads,
                KEEP + 1,
            ).astype(low_type)
    middle[...] = start[...] + (nn(mixed[...], wide[:, 4 * D :]) + vec[6:7])
    unit, _ = standard(middle[...])
    normed_two[...] = (unit * vec[7:8] + vec[8:9]).astype(low_type)


def enc_ffn_kernel(last, middle, normed_two, ffn, vec, up_bias, proj, dec_vec, slope, active, output, latent, entry):
    step = pl.program_id(0)

    @pl.when(step == 0)
    def _():
        output[...] = middle[...] + vec[9:10]

    value, gain = gelu_pair(nn(normed_two[...], ffn[0]) + up_bias[...])
    slope[...] = gain
    value = value.astype(low_type)
    active[...] = value
    output[...] += nt(value, ffn[1])

    @pl.when(step == last)
    def _():
        unit, _ = standard(output[...])
        rows = (unit * vec[10:11] + vec[11:12]).astype(low_type)
        latent[...] = rows
        entry[...] = nn(rows, proj[...]) + dec_vec[0:1]


def dec_attend_kernel(entry, picked, pos, wide, vec, start, normed, qkv, mixed, middle, normed_two):
    picks = picked[0]
    kept = jnp.sum(picks.astype(high_type), 1, keepdims=True)
    rows = place_rows(picks, entry[...]) + (1.0 - kept) * vec[1:2] + pos[...]
    start[...] = rows
    unit, _ = standard(rows)
    rows_in = (unit * vec[2:3] + vec[3:4]).astype(low_type)
    normed[...] = rows_in
    scale = 1.0 / math.sqrt(E // HD)
    qkv[:, :E] = ((nn(rows_in, wide[0, :, :E]) + vec[4:5]) * scale).astype(low_type)
    qkv[:, E : 2 * E] = nn(rows_in, wide[0, :, E : 2 * E]).astype(low_type)
    qkv[:, 2 * E :] = (nn(rows_in, wide[0, :, 2 * E : 3 * E]) + vec[5:6]).astype(low_type)
    heads = LANES * HD // E
    for group in range(E // LANES):
        lane = group * LANES
        mixed[:, lane : lane + LANES] = attend(
            qkv[:, lane : lane + LANES],
            qkv[:, E + lane : E + lane + LANES],
            qkv[:, 2 * E + lane : 2 * E + lane + LANES],
            heads,
            PATCHES + 1,
        ).astype(low_type)
    total = rows + (nn(mixed[...], wide[0, :, 3 * E :]) + vec[6:7])
    middle[...] = total
    unit, _ = standard(total)
    normed_two[...] = (unit * vec[7:8] + vec[8:9]).astype(low_type)


def send_tiles(acc, blob, sem, tiles, rows, per_block, base, stride):
    def go(index, carry):
        tile, part = index // 4, index % 4
        block, inner = tile // per_block, tile % per_block
        pltpu.make_async_copy(
            acc.at[tile, pl.ds(pl.multiple_of(part * rows, 16), rows)],
            blob.at[block, part, pl.ds(pl.multiple_of(base + inner * stride, 16), rows)],
            sem,
        ).start()
        return carry

    lax.fori_loop(0, tiles * 4, go, 0)


def wait_tiles(acc, sem):
    pltpu.make_async_copy(acc, acc, sem).wait()


def dec_ffn_kernel(images, last, count, middle, normed_two, mixed, pixels, picked, weights, head, vec, up_bias, head_bias,
                   grad_middle, grad_mixed, grad_head, vec_grad, up_grad, bias_grad, loss, blob,
                   active, slope, acc_up, acc_down, acc_out, sems):
    step = pl.program_id(0)
    source = normed_two[...]
    rows = source.shape[0]

    @pl.when(step == 0)
    def _():
        grad_head[...] = jnp.zeros_like(grad_head)
        vec_grad[...] = jnp.zeros_like(vec_grad)
        up_grad[...] = jnp.zeros_like(up_grad)
        bias_grad[...] = jnp.zeros_like(bias_grad)
        loss[...] = jnp.zeros_like(loss)
        acc_up[...] = jnp.zeros_like(acc_up)
        acc_down[...] = jnp.zeros_like(acc_down)
        acc_out[...] = jnp.zeros_like(acc_out)

    wide = 512
    total = middle[...] + vec[9:10]
    for place in range(0, H, wide):
        span = slice(place, place + wide)
        value, gain = gelu_pair(nn(source, weights[1, :, span]) + up_bias[:, span])
        slope[:, span] = gain
        value = value.astype(low_type)
        active[:, span] = value
        total = total + nt(value, weights[2, :, span])
    unit, rate = standard(total)
    final = (unit * vec[10:11] + vec[11:12]).astype(low_type)
    predict = nn(final, head[...]) + head_bias[...]
    target, _ = standard(pixels[...].astype(high_type))
    kept = jnp.concatenate([jnp.sum(picked[image].astype(high_type), 1, keepdims=True) for image in range(images)], 0)
    inner = lax.broadcasted_iota(jnp.int32, (rows, 1), 0) % DEC_ROWS
    masked = jnp.where(inner < PATCHES, 1.0 - kept, 0.0)
    error = predict - target
    loss[...] += jnp.sum(masked * error * error)
    grad_predict = (2.0 * masked * error / count).astype(low_type)
    grad_head[...] += tn(final, grad_predict)
    bias_grad[...] += col_sum(grad_predict)
    grad_final = nt(grad_predict, head[...])
    vec_grad[10:11] += col_sum(grad_final * unit)
    vec_grad[11:12] += col_sum(grad_final)
    grad_out = standard_back(unit, rate, grad_final * vec[10:11])
    grad_down = grad_out.astype(low_type)
    vec_grad[9:10] += col_sum(grad_down)
    grad_source = jnp.zeros_like(total)
    for place in range(0, H, wide):
        span = slice(place, place + wide)
        grad_up = (slope[:, span] * nn(grad_down, weights[2, :, span])).astype(low_type)
        up_grad[:, span] += col_sum(grad_up)
        grad_source = grad_source + nt(grad_up, weights[1, :, span])
        piece = tn(grad_down, active[:, span])
        other = tn(source, grad_up)
        for tile in range(wide // LANES):
            lane = slice(tile * LANES, (tile + 1) * LANES)
            acc_down[place // LANES + tile] += piece[:, lane]
            acc_up[place // LANES + tile] += other[:, lane]
    unit, rate = standard(middle[...])
    vec_grad[7:8] += col_sum(grad_source * unit)
    vec_grad[8:9] += col_sum(grad_source)
    grad_rows = standard_back(unit, rate, grad_source * vec[7:8]) + grad_out
    grad_middle[...] = grad_rows
    branch = grad_rows.astype(low_type)
    vec_grad[6:7] += col_sum(branch)
    piece = tn(mixed[...], branch)
    for tile in range(E // LANES):
        acc_out[tile] += piece[:, tile * LANES : (tile + 1) * LANES]
    grad_mixed[...] = nt(branch, weights[0, :, 3 * E :]).astype(low_type)

    @pl.when(step == last)
    def _():
        rows_block = E // 4
        send_tiles(acc_up, blob, sems.at[0], H // LANES, rows_block, 2, 2176, rows_block)
        send_tiles(acc_down, blob, sems.at[1], H // LANES, rows_block, 2, 2432, rows_block)
        send_tiles(acc_out, blob.at[pl.ds(6, 2)], sems.at[2], E // LANES, rows_block, 2, 1920, rows_block)
        wait_tiles(acc_up, sems.at[0])
        wait_tiles(acc_down, sems.at[1])
        wait_tiles(acc_out, sems.at[2])


def dec_back_kernel(last, blob_in, qkv, normed, start, grad_middle, grad_mixed, pick, picked, weights, vec,
                    grad_entry, vec_grad, blob, grads, acc, sem):
    step = pl.program_id(0)

    @pl.when(step == 0)
    def _():
        vec_grad[...] = jnp.zeros_like(vec_grad)
        acc[...] = jnp.zeros_like(acc)

    scale = 1.0 / math.sqrt(E // HD)
    heads = LANES * HD // E
    for group in range(E // LANES):
        lane = group * LANES
        span = slice(lane, lane + LANES)
        query, key, value = attend_back(
            qkv[:, lane : lane + LANES],
            qkv[:, E + lane : E + lane + LANES],
            qkv[:, 2 * E + lane : 2 * E + lane + LANES],
            grad_mixed[:, span],
            heads,
            PATCHES + 1,
        )
        grads[:, span] = (query * scale).astype(low_type)
        grads[:, E + lane : E + lane + LANES] = key.astype(low_type)
        grads[:, 2 * E + lane : 2 * E + lane + LANES] = value.astype(low_type)
    vec_grad[4:5] += col_sum(grads[:, :E])
    vec_grad[5:6] += col_sum(grads[:, 2 * E :])
    rows = normed[...]
    for part in range(3):
        piece = tn(rows, grads[:, part * E : (part + 1) * E])
        for tile in range(E // LANES):
            acc[part * (E // LANES) + tile] += piece[:, tile * LANES : (tile + 1) * LANES]
    grad_normed = nt(grads[...], weights[0, :, : 3 * E])
    unit, rate = standard(start[...])
    vec_grad[2:3] += col_sum(grad_normed * unit)
    vec_grad[3:4] += col_sum(grad_normed)
    grad_rows = standard_back(unit, rate, grad_normed * vec[2:3]) + grad_middle[...]
    kept = jnp.sum(picked[0].astype(high_type), 1, keepdims=True)
    vec_grad[1:2] += col_sum((1.0 - kept) * grad_rows)
    grad_entry[...] = nn(pick[0], grad_rows.astype(low_type)).astype(low_type)

    @pl.when(step == last)
    def _():
        rows_block = E // 4
        send_tiles(acc, blob, sem, 3 * E // LANES, rows_block, 2, 1920, rows_block)
        wait_tiles(acc, sem)


def enc_ffn_back_kernel(last, blob_in, grad_entry, latent, output, middle, normed_two, slope, active, ffn, proj, vec,
                        grad_middle, vec_grad, up_grad, entry_grad, blob,
                        grad_out, grad_down, grad_source, folded, acc_up, acc_down, fold_sem, sems):
    step = pl.program_id(0)
    fold_copy = pltpu.make_async_copy(folded, blob.at[:, :, pl.ds(2688, 96)], fold_sem)
    part_rows = D // 4

    @pl.when(step == 0)
    def _():
        vec_grad[...] = jnp.zeros_like(vec_grad)
        entries = grad_entry[...]
        entry_grad[...] = col_sum(entries)
        grad_proj = tn(latent[...], entries)
        lane = lax.broadcasted_iota(jnp.int32, (96, LANES), 1)
        for part in range(4):
            for pair in range(4):
                first = grad_proj[part * 192 : part * 192 + 96, pair * LANES : (pair + 1) * LANES]
                second = grad_proj[part * 192 + 96 : part * 192 + 192, pair * LANES : (pair + 1) * LANES]
                folded[2 * pair, part] = jnp.where(lane < 64, first, pltpu.roll(second, 64, 1))
                folded[2 * pair + 1, part] = jnp.where(lane < 64, pltpu.roll(first, 64, 1), second)
        fold_copy.start()
        grad_latent = nt(entries, proj[...])
        unit, rate = standard(output[...])
        vec_grad[10:11] = col_sum(grad_latent * unit)
        vec_grad[11:12] = col_sum(grad_latent)
        rows = standard_back(unit, rate, grad_latent * vec[10:11])
        grad_out[...] = rows
        grad_down[...] = rows.astype(low_type)
        vec_grad[9:10] = col_sum(rows.astype(low_type))
        grad_source[...] = jnp.zeros_like(grad_source)

    slot = step % 2

    @pl.when(step >= 2)
    def _():
        wait_tiles(acc_up.at[slot], sems.at[0, slot])
        wait_tiles(acc_down.at[slot], sems.at[1, slot])

    grads = grad_down[...]
    grad_up = (slope[...] * nn(grads, ffn[1])).astype(low_type)
    up_grad[...] = col_sum(grad_up)
    grad_source[...] += nt(grad_up, ffn[0])
    piece = tn(grads, active[...])
    other = tn(normed_two[...], grad_up)
    count = grad_up.shape[1] // LANES
    for tile in range(count):
        lane = slice(tile * LANES, (tile + 1) * LANES)
        acc_down[slot, tile] = piece[:, lane]
        acc_up[slot, tile] = other[:, lane]

    def go(index, carry):
        tile, part = index // 4, index % 4
        place = step * count + tile
        block, inner = place // 3, place % 3
        rows = pl.ds(pl.multiple_of(part * part_rows, 16), part_rows)
        for number, (acc, base) in enumerate(((acc_up, 768), (acc_down, 1344))):
            pltpu.make_async_copy(
                acc.at[slot, tile, rows],
                blob.at[block, part, pl.ds(pl.multiple_of(base + inner * part_rows, 16), part_rows)],
                sems.at[number, slot],
            ).start()
        return carry

    lax.fori_loop(0, count * 4, go, 0)

    @pl.when(step == last)
    def _():
        unit, rate = standard(middle[...])
        vec_grad[7:8] = col_sum(grad_source[...] * unit)
        vec_grad[8:9] = col_sum(grad_source[...])
        grad_rows = standard_back(unit, rate, grad_source[...] * vec[7:8]) + grad_out[...]
        grad_middle[...] = grad_rows
        vec_grad[6:7] = col_sum(grad_rows.astype(low_type))
        fold_copy.wait()
        for item in (0, 1):
            wait_tiles(acc_up.at[item], sems.at[0, item])
            wait_tiles(acc_down.at[item], sems.at[1, item])


def enc_back_kernel(batch, blob_in, qkv, kept, normed, start, mixed, grad_middle, wide, vec,
                    vec_grad, blob, grads, grad_wide, tiles, sem):
    rows = ENC_ROWS
    vec_grad[...] = jnp.zeros_like(vec_grad)
    branch = grad_middle[...].astype(low_type)
    grad_mixed = nt(branch, wide[:, 4 * D :]).astype(low_type)
    grad_wide[:, 4 * D :] = tn(mixed[...], branch)
    scale = 1.0 / math.sqrt(D // HE)
    heads = LANES * HE // D
    for group in range(D // LANES):
        lane = group * LANES
        query, key, value = attend_back_many(
            batch,
            qkv[:, lane : lane + LANES],
            qkv[:, D + lane : D + lane + LANES],
            qkv[:, 2 * D + lane : 2 * D + lane + LANES],
            grad_mixed[:, lane : lane + LANES],
            heads,
            KEEP + 1,
        )
        grads[:, lane : lane + LANES] = (query * scale).astype(low_type)
        grads[:, D + lane : D + lane + LANES] = key.astype(low_type)
        grads[:, 2 * D + lane : 2 * D + lane + LANES] = value.astype(low_type)
    vec_grad[4:5] = col_sum(grads[:, :D])
    vec_grad[5:6] = col_sum(grads[:, 2 * D :])
    rows_in = normed[...]
    for part in range(3):
        grad_wide[:, (part + 1) * D : (part + 2) * D] = tn(rows_in, grads[:, part * D : (part + 1) * D])
    width = 5 * D // 8
    tall = D // 4

    def assemble(block):
        for part in range(4):
            span = slice(part * tall, (part + 1) * tall)
            piece = grad_wide[span, block * width : (block + 1) * width]
            for tile in range(4):
                size = min(LANES, width - tile * LANES)
                value = piece[:, tile * LANES : tile * LANES + size]
                if size < LANES:
                    value = jnp.concatenate([value, jnp.zeros((tall, LANES - size), high_type)], 1)
                tiles[block, part, tile * tall : (tile + 1) * tall] = value
        pltpu.make_async_copy(tiles.at[block], blob.at[block, :, pl.ds(0, 4 * tall)], sem).start()

    for block in range(2, 8):
        assemble(block)
    grad_normed = nt(grads[...], wide[:, D : 4 * D])
    unit, rate = standard(start[...])
    vec_grad[2:3] = col_sum(grad_normed * unit)
    vec_grad[3:4] = col_sum(grad_normed)
    grad_rows = standard_back(unit, rate, grad_normed * vec[2:3]) + grad_middle[...]
    inner = lax.broadcasted_iota(jnp.int32, (grad_rows.shape[0], 1), 0) % rows
    vec_grad[1:2] = col_sum(jnp.where(inner == CLASS_ENC, grad_rows, 0.0))
    embed = jnp.where(inner < KEEP, grad_rows, 0.0).astype(low_type)
    vec_grad[0:1] = col_sum(embed)
    grad_wide[:, :D] = tn(kept[...], embed)
    assemble(0)
    assemble(1)
    wait_tiles(tiles, sem)


def adam_parts(weight, grad, first, second, decay):
    first_new = 0.5 * first + 0.5 * grad
    second_new = 0.5 * second + 0.5 * grad * grad
    bias = 1.0 - 0.5**STEP
    direction = first_new / bias / (jnp.sqrt(second_new / bias) + 1e-08)
    return weight - 0.02 * (direction + decay * weight), first_new, second_new


def adam_kernel(*refs):
    summed, head, small = refs[:3]
    ins, outs = refs[3:24], refs[24:]

    def update(index, place, grad, decay=0.05):
        for target, value in zip(
            range(3), adam_parts(ins[index][place], grad, ins[7 + index][place], ins[14 + index][place], decay)
        ):
            outs[7 * target + index][place] = value

    base = 0
    for index, lead, tall, width in ((0, None, 192, 480), (1, 0, 192, 384), (1, 1, 192, 384),
                                     (3, None, 128, 256), (4, 0, 128, 256), (4, 1, 128, 256)):
        for lane in range(0, width, LANES):
            size = min(LANES, width - lane)
            place = (slice(None), slice(lane, lane + size))
            update(index, place if lead is None else (lead,) + place, summed[base : base + tall, :size])
            base += tall
    folded = summed[base : base + 96]
    update(2, (slice(0, 96),), folded[:, :64])
    update(2, (slice(96, 192),), folded[:, 64:])
    update(5, (slice(None),), head[...])
    update(6, (slice(None),), small[...], 0.0)


def table_of(width, rows):
    quarter = width // 4
    omega = (np.float32(1.0) / np.float32(10000.0) ** (np.arange(quarter, dtype=np.float32) / np.float32(quarter))).astype(np.float32)
    coord = np.arange(SIDE * SIDE)

    def half(place):
        angle = place.astype(np.float32)[:, None] * omega[None, :]
        return np.concatenate([np.sin(angle), np.cos(angle)], 1)

    table = np.concatenate([half(coord // SIDE), half(coord % SIDE)], 1).astype(np.float32)
    return np.concatenate([table, np.zeros((rows - table.shape[0], width), np.float32)], 0)


def whole():
    return pl.BlockSpec(memory_space=pltpu.VMEM)


def hbm():
    return pl.BlockSpec(memory_space=pltpu.HBM)


def params(**more):
    return pltpu.CompilerParams(vmem_limit_bytes=60 << 20, **more)


def local_grads(enc_blocks, enc_ffn, proj, dec3, head_low, smalls_parts, patches, shuffle, count):
    enc_vec, enc_up, dec_vec, dec_up, head_bias = smalls_parts
    enc_up, dec_up, head_bias = enc_up[None], dec_up[None], head_bias[None]
    batch = patches.shape[0]
    shape = jax.ShapeDtypeStruct
    keep = jnp.concatenate(
        [
            shuffle[:, :KEEP],
            jnp.full((batch, 1), CLASS_DEC, jnp.int32),
            jnp.full((batch, ENC_ROWS - KEEP - 1), -1, jnp.int32),
        ],
        1,
    )
    places = jnp.arange(DEC_ROWS, dtype=jnp.int32)
    pick = (keep[:, :, None] == places[None, None, :]).astype(low_type)
    picked = (keep[:, None, :] == places[None, :, None]).astype(low_type)
    padded = jnp.pad(patches, ((0, 0), (0, DEC_ROWS - PATCHES), (0, 0)))
    enc_pos = jnp.asarray(table_of(D, DEC_ROWS))
    dec_pos = jnp.asarray(table_of(E, DEC_ROWS))
    rows, dec_rows = batch * ENC_ROWS, batch * DEC_ROWS

    wide = pl.pallas_call(
        wide_kernel,
        out_shape=shape((D, 5 * D), low_type),
        in_specs=[whole()],
        out_specs=whole(),
        compiler_params=params(),
        name="wide",
    )(enc_blocks)
    kept, start, normed, qkv, mixed, middle, normed_two = pl.pallas_call(
        functools.partial(enc_attend_kernel, batch),
        out_shape=(
            shape((rows, D), low_type),
            shape((rows, D), high_type),
            shape((rows, D), low_type),
            shape((rows, 3 * D), low_type),
            shape((rows, D), low_type),
            shape((rows, D), high_type),
            shape((rows, D), low_type),
        ),
        in_specs=[whole()] * 5,
        out_specs=[whole()] * 7,
        compiler_params=params(),
        name="enc_attend",
    )(pick, padded, wide, enc_vec, enc_pos)
    def by_image(*block):
        return pl.BlockSpec(block, lambda i: (i,) + (0,) * (len(block) - 1))

    def fixed(*block):
        return pl.BlockSpec(block, lambda i: (0,) * len(block))

    chunk = 512
    rows_whole = lambda width: fixed(rows, width)
    slope, active, enc_out, latent, entry = pl.pallas_call(
        functools.partial(enc_ffn_kernel, F // chunk - 1),
        grid=(F // chunk,),
        out_shape=(
            shape((rows, F), high_type),
            shape((rows, F), low_type),
            shape((rows, D), high_type),
            shape((rows, D), low_type),
            shape((rows, E), high_type),
        ),
        in_specs=[
            rows_whole(D),
            rows_whole(D),
            pl.BlockSpec((2, D, chunk), lambda i: (0, 0, i)),
            fixed(12, D),
            pl.BlockSpec((1, chunk), lambda i: (0, i)),
            fixed(D, E),
            fixed(12, E),
        ],
        out_specs=[
            pl.BlockSpec((rows, chunk), lambda i: (0, i)),
            pl.BlockSpec((rows, chunk), lambda i: (0, i)),
            rows_whole(D),
            rows_whole(D),
            rows_whole(E),
        ],
        compiler_params=params(),
        name="enc_ffn",
    )(middle, normed_two, enc_ffn, enc_vec, enc_up, proj, dec_vec)

    dec_start, dec_normed, dec_qkv, dec_mixed, dec_middle, dec_normed_two = pl.pallas_call(
        dec_attend_kernel,
        grid=(batch,),
        out_shape=(
            shape((dec_rows, E), high_type),
            shape((dec_rows, E), low_type),
            shape((dec_rows, 3 * E), low_type),
            shape((dec_rows, E), low_type),
            shape((dec_rows, E), high_type),
            shape((dec_rows, E), low_type),
        ),
        in_specs=[
            by_image(ENC_ROWS, E),
            by_image(1, DEC_ROWS, ENC_ROWS),
            fixed(DEC_ROWS, E),
            fixed(1, E, 4 * E),
            fixed(12, E),
        ],
        out_specs=[
            by_image(DEC_ROWS, E),
            by_image(DEC_ROWS, E),
            by_image(DEC_ROWS, 3 * E),
            by_image(DEC_ROWS, E),
            by_image(DEC_ROWS, E),
            by_image(DEC_ROWS, E),
        ],
        compiler_params=params(),
        name="dec_attend",
    )(entry, picked, dec_pos, dec3, dec_vec)

    images = 2 if batch % 2 == 0 else 1
    block = images * DEC_ROWS
    blob_shape = shape((8, 4, 2784, LANES), high_type)
    vm = pltpu.VMEM
    dma = pltpu.SemaphoreType.DMA
    grad_middle, grad_mixed, grad_head, dec_grad_one, dec_up_grad, head_bias_grad, loss, blob = pl.pallas_call(
        functools.partial(dec_ffn_kernel, images, batch // images - 1, count),
        grid=(batch // images,),
        out_shape=(
            shape((dec_rows, E), high_type),
            shape((dec_rows, E), low_type),
            shape((E, P_SIZE), high_type),
            shape((12, E), high_type),
            shape((1, H), high_type),
            shape((1, P_SIZE), high_type),
            shape((8, LANES), high_type),
            blob_shape,
        ),
        in_specs=[
            by_image(block, E),
            by_image(block, E),
            by_image(block, E),
            by_image(block, P_SIZE),
            by_image(images, DEC_ROWS, ENC_ROWS),
            fixed(3, E, H),
            fixed(E, P_SIZE),
            fixed(12, E),
            fixed(1, H),
            fixed(1, P_SIZE),
        ],
        out_specs=[
            by_image(block, E),
            by_image(block, E),
            fixed(E, P_SIZE),
            fixed(12, E),
            fixed(1, H),
            fixed(1, P_SIZE),
            fixed(8, LANES),
            hbm(),
        ],
        scratch_shapes=[
            vm((block, H), low_type),
            vm((block, H), high_type),
            vm((H // LANES, E, LANES), high_type),
            vm((H // LANES, E, LANES), high_type),
            vm((E // LANES, E, LANES), high_type),
            dma((3,)),
        ],
        compiler_params=params(),
        name="dec_ffn",
    )(dec_middle, dec_normed_two, dec_mixed, padded.reshape(dec_rows, P_SIZE), picked, dec3, head_low, dec_vec, dec_up, head_bias)

    grad_entry, dec_grad_two, blob = pl.pallas_call(
        functools.partial(dec_back_kernel, batch - 1),
        grid=(batch,),
        out_shape=(shape((rows, E), low_type), shape((12, E), high_type), blob_shape),
        in_specs=[
            hbm(),
            by_image(DEC_ROWS, 3 * E),
            by_image(DEC_ROWS, E),
            by_image(DEC_ROWS, E),
            by_image(DEC_ROWS, E),
            by_image(DEC_ROWS, E),
            by_image(1, ENC_ROWS, DEC_ROWS),
            by_image(1, DEC_ROWS, ENC_ROWS),
            fixed(1, E, 4 * E),
            fixed(12, E),
        ],
        out_specs=[by_image(ENC_ROWS, E), fixed(12, E), hbm()],
        scratch_shapes=[vm((DEC_ROWS, 3 * E), low_type), vm((3 * E // LANES, E, LANES), high_type), dma],
        input_output_aliases={0: 2},
        compiler_params=params(),
        name="dec_back",
    )(blob, dec_qkv, dec_normed, dec_start, grad_middle, grad_mixed, pick, picked, dec3, dec_vec)

    enc_grad_middle, enc_grad_one, enc_up_grad, entry_grad, blob = pl.pallas_call(
        functools.partial(enc_ffn_back_kernel, F // chunk - 1),
        grid=(F // chunk,),
        out_shape=(
            shape((rows, D), high_type),
            shape((12, D), high_type),
            shape((1, F), high_type),
            shape((1, E), high_type),
            blob_shape,
        ),
        in_specs=[
            hbm(),
            rows_whole(E),
            rows_whole(D),
            rows_whole(D),
            rows_whole(D),
            rows_whole(D),
            pl.BlockSpec((rows, chunk), lambda i: (0, i)),
            pl.BlockSpec((rows, chunk), lambda i: (0, i)),
            pl.BlockSpec((2, D, chunk), lambda i: (0, 0, i)),
            fixed(D, E),
            fixed(12, D),
        ],
        out_specs=[
            rows_whole(D),
            fixed(12, D),
            pl.BlockSpec((1, chunk), lambda i: (0, i)),
            fixed(1, E),
            hbm(),
        ],
        scratch_shapes=[
            vm((rows, D), high_type),
            vm((rows, D), low_type),
            vm((rows, D), high_type),
            vm((8, 4, 96, LANES), high_type),
            vm((2, chunk // LANES, D, LANES), high_type),
            vm((2, chunk // LANES, D, LANES), high_type),
            dma,
            dma((2, 2)),
        ],
        input_output_aliases={0: 4},
        compiler_params=params(),
        name="enc_ffn_back",
    )(blob, grad_entry, latent, enc_out, middle, normed_two, slope, active, enc_ffn, proj, enc_vec)
    enc_grad_two, blob = pl.pallas_call(
        functools.partial(enc_back_kernel, batch),
        out_shape=(shape((12, D), high_type), blob_shape),
        in_specs=[hbm()] + [whole()] * 8,
        out_specs=[whole(), hbm()],
        scratch_shapes=[
            vm((rows, 3 * D), low_type),
            vm((D, 5 * D), high_type),
            vm((8, 4, D, LANES), high_type),
            dma,
        ],
        input_output_aliases={0: 1},
        compiler_params=params(),
        name="enc_back",
    )(blob, qkv, kept, normed, start, mixed, enc_grad_middle, wide, enc_vec)
    dec_grad = (dec_grad_one + dec_grad_two).at[0].set(entry_grad[0])
    smalls = jnp.concatenate(
        [
            (enc_grad_one + enc_grad_two).reshape(-1),
            enc_up_grad[0],
            dec_grad.reshape(-1),
            dec_up_grad[0],
            head_bias_grad[0],
        ]
    )
    return blob, grad_head, smalls, loss[0, 0]


def untile(block, rows, width):
    tiles = -(-width // LANES)
    return block.reshape(tiles, rows, LANES).transpose(1, 0, 2).reshape(rows, tiles * LANES)[:, :width]


def unfold_proj(block):
    width = block.shape[1] // 2
    return jnp.concatenate([block[:, :width], block[:, width:]], 0)


def unpack_shards(blob):
    cuts = [0, 768, 576, 576, 256, 256, 256, 96]
    places = [sum(cuts[: index + 1]) for index in range(len(cuts))]
    piece = [blob[places[index] : places[index + 1]] for index in range(7)]
    return (
        untile(piece[0], 192, 480),
        jnp.stack([untile(piece[1], 192, 384), untile(piece[2], 192, 384)]),
        unfold_proj(piece[6]),
        untile(piece[3], 128, 256),
        jnp.stack([untile(piece[4], 128, 256), untile(piece[5], 128, 256)]),
    )


def whole_arrays(blob):
    col_size, row_size = blob.shape[:2]
    parts = jax.vmap(jax.vmap(unpack_shards))(blob)

    def joined(array):
        if array.ndim == 4:
            return array.transpose(1, 2, 0, 3).reshape(row_size * array.shape[2], col_size * array.shape[3])
        return array.transpose(2, 1, 3, 0, 4).reshape(2, row_size * array.shape[3], col_size * array.shape[4])

    return tuple(joined(item) for item in parts)


def on_small_plane():
    return lax.axis_size("row") == 4 and lax.axis_size("col") == 8


def gather_weights(enc_w, enc_ffn, dec_proj, dec_w, dec_ffn):
    shards = [item.astype(low_type) for item in (enc_w, enc_ffn, dec_proj, jnp.concatenate([dec_w[None], dec_ffn], 0))]
    if on_small_plane():
        enc, ffn, proj, dec = gather_blocks(*shards, lax.axis_size("col") // 2)
        return enc, ffn, proj.transpose(1, 0, 2).reshape(D, E), dec
    full = []
    for item in shards:
        rowed = lax.all_gather(item, "row", axis=item.ndim - 2, tiled=True)
        full.append(lax.all_gather(rowed, "col", axis=item.ndim - 1, tiled=True))
    return full[0].reshape(D, 8, 5 * D // 8).transpose(1, 0, 2), full[1], full[2], full[3]


def apply_updates(blob, grad_head, smalls, loss, params_now, firsts, seconds):
    count = smalls.shape[0]
    summed_head = lax.psum(grad_head, ("row", "col"))
    if on_small_plane():
        small = jnp.concatenate([smalls, loss[None], jnp.zeros((32 * 8 * LANES - count - 1,), high_type)])
        summed, small = reduce_blocks(blob, small.reshape(32, 8, LANES), lax.axis_size("col") // 2, 6)
        small = small.reshape(-1, LANES)
        flat = lambda group: group[:6] + (group[6].reshape(-1, LANES),)
        ins = flat(params_now) + flat(firsts) + flat(seconds)
        outs = pl.pallas_call(
            adam_kernel,
            out_shape=tuple(jax.ShapeDtypeStruct(item.shape, high_type) for item in ins),
            in_specs=[whole()] * 24,
            out_specs=[whole()] * 21,
            compiler_params=params(),
            name="adam",
        )(summed, summed_head, small[: count // LANES], *ins)
        outs = [item.reshape(-1) if index % 7 == 6 else item for index, item in enumerate(outs)]
        return outs, small[count // LANES, count % LANES]
    shards = []
    for item in whole_arrays(blob):
        done = lax.psum_scatter(item, "col", scatter_dimension=item.ndim - 1, tiled=True)
        shards.append(lax.psum_scatter(done, "row", scatter_dimension=item.ndim - 2, tiled=True))
    smalls, loss = lax.psum((smalls, loss), ("row", "col"))
    grads = tuple(shards) + (summed_head, smalls)
    decays = (0.05,) * 6 + (0.0,)
    results = [adam_parts(*item) for item in zip(params_now, grads, firsts, seconds, decays)]
    return [item[kind] for kind in range(3) for item in results], loss


def body(
    patches,
    shuffle,
    enc_w,
    enc_ffn,
    dec_proj,
    dec_w,
    dec_ffn,
    head_w,
    smalls,
    first_enc_w,
    first_enc_ffn,
    first_dec_proj,
    first_dec_w,
    first_dec_ffn,
    first_head_w,
    first_smalls,
    second_enc_w,
    second_enc_ffn,
    second_dec_proj,
    second_dec_w,
    second_dec_ffn,
    second_head_w,
    second_smalls,
):
    enc_blocks, enc_ffn_w, proj, dec3 = gather_weights(enc_w, enc_ffn, dec_proj, dec_w, dec_ffn)
    count = patches.shape[0] * lax.axis_size("row") * lax.axis_size("col") * (PATCHES - KEEP) * P_SIZE
    blob, grad_head, grad_smalls, loss_local = local_grads(
        enc_blocks, enc_ffn_w, proj, dec3, head_w.astype(low_type), unpack(smalls), patches, shuffle, count
    )
    params_now = (enc_w, enc_ffn, dec_proj, dec_w, dec_ffn, head_w, smalls)
    firsts = (
        first_enc_w,
        first_enc_ffn,
        first_dec_proj,
        first_dec_w,
        first_dec_ffn,
        first_head_w,
        first_smalls,
    )
    seconds = (
        second_enc_w,
        second_enc_ffn,
        second_dec_proj,
        second_dec_w,
        second_dec_ffn,
        second_head_w,
        second_smalls,
    )
    outs, loss_sum = apply_updates(blob, grad_head, grad_smalls, loss_local, params_now, firsts, seconds)
    return tuple(outs) + (loss_sum / count,)


def solution(mesh):
    in_specs = (
        P(("row", "col"), None, None),
        P(("row", "col"), None),
        P("row", "col"),
        P(None, "row", "col"),
        P("row", "col"),
        P("row", "col"),
        P(None, "row", "col"),
        P(),
        P(),
        P("row", "col"),
        P(None, "row", "col"),
        P("row", "col"),
        P("row", "col"),
        P(None, "row", "col"),
        P(),
        P(),
        P("row", "col"),
        P(None, "row", "col"),
        P("row", "col"),
        P("row", "col"),
        P(None, "row", "col"),
        P(),
        P(),
    )
    out_specs = (
        P("row", "col"),
        P(None, "row", "col"),
        P("row", "col"),
        P("row", "col"),
        P(None, "row", "col"),
        P(),
        P(),
        P("row", "col"),
        P(None, "row", "col"),
        P("row", "col"),
        P("row", "col"),
        P(None, "row", "col"),
        P(),
        P(),
        P("row", "col"),
        P(None, "row", "col"),
        P("row", "col"),
        P("row", "col"),
        P(None, "row", "col"),
        P(),
        P(),
        P(),
    )
    return jax.shard_map(body, mesh=mesh, in_specs=in_specs, out_specs=out_specs, check_vma=False)
```

```python
import functools
import math

import jax
import jax.numpy as jnp
import numpy as np
from jax import lax
from jax.experimental import pallas as pl
from jax.experimental.pallas import tpu as pltpu
from jax.sharding import PartitionSpec as P

D = 768
HE = 12
F = 3072
E = 512
HD = 16
H = 2048
P_SIZE = 768
SIDE = 14
KEEP = 49
STEP = 5
PATCHES = 196
LANES = 128

norm_eps = 1e-06
low_type = jnp.bfloat16
high_type = jnp.float32


def unpack(smalls):
    first = 12 * D
    second = first + F
    third = second + 12 * E
    fourth = third + H
    return (
        smalls[:first].reshape(12, D),
        smalls[first:second],
        smalls[second:third].reshape(12, E),
        smalls[third:fourth],
        smalls[fourth:],
    )


MESH = pl.DeviceIdType.MESH
LAGS = (2, 4, 6)


class Group:
    def __init__(self, copies):
        self.copies = copies

    def start(self):
        for item in self.copies:
            item.start()

    def wait_recv(self):
        for item in self.copies:
            item.wait_recv()

    def wait_send(self):
        for item in self.copies:
            item.wait_send()

    def wait(self):
        for item in self.copies:
            item.wait()


def gather_steps(depth, place_ids, own, cut, sems):
    row, row_x, row_y, row_d, z, k, near_x, near_y, twin, lower, upper, has_lower, has_upper = place_ids
    zs, zr, xs, xr, ys, yr, dxs, dxr, dys, dyr, cs, cr = sems
    levels = [(0, 0)] + [(d, way) for d in range(1, depth) for way in (0, 1)]
    level_of = {item: number for number, item in enumerate(levels)}

    def place(level):
        d, way = level
        return z - d if way == 0 else z + d

    def valid(level):
        d, way = level
        return z - d >= 0 if way == 0 else z + d < depth

    def slot(level, row_now, half=None):
        return cut(place(level) * 2 + k, row_now, half)

    def source(level):
        return own if level == (0, 0) else slot(level, row)

    def copy(src, dst, send, recv, target):
        return Group(
            [
                pltpu.make_async_remote_copy(
                    src_ref=src[item],
                    dst_ref=dst[item],
                    send_sem=send.at[item],
                    recv_sem=recv.at[item],
                    device_id=target,
                    device_id_type=MESH,
                )
                for item in range(len(own))
            ]
        )

    def z_copy(level, way):
        d = level[0]
        n = level_of[level]
        return copy(source(level), slot(level, row), zs.at[n, way], zr.at[d, way], upper if way == 0 else lower)

    def x_copy(level):
        n = level_of[level]
        return copy(source(level), slot(level, row), xs.at[n], xr.at[n], near_x)

    def y_copy(level):
        n = level_of[level]
        return copy(source(level), slot(level, row), ys.at[n], yr.at[n], near_y)

    def dx_copy(level):
        n = level_of[level]
        refs = slot(level, row_y, 1)
        return copy(refs, refs, dxs.at[n], dxr.at[n], near_x)

    def dy_copy(level):
        n = level_of[level]
        refs = slot(level, row_x, 0)
        return copy(refs, refs, dys.at[n], dyr.at[n], near_y)

    def twin_copy(level, kind):
        n = level_of[level]
        row_now = (row, row_x, row_y, row_d)[kind]
        src = source(level) if kind == 0 else slot(level, row_now)
        return copy(src, slot(level, row_now), cs.at[n, kind], cr.at[n, kind], twin)

    def guarded(level, action):
        if level == (0, 0):
            action()
        else:
            pl.when(valid(level))(action)

    def spread(level):
        d, way = level

        def action():
            if level != (0, 0):
                z_copy((d - 1, way if d > 1 else 0), way).wait_recv()
            for direction in (0, 1):
                if level == (0, 0) or direction == way:
                    @pl.when(has_upper if direction == 0 else has_lower)
                    def _():
                        z_copy(level, direction).start()
            x_copy(level).start()
            y_copy(level).start()
            twin_copy(level, 0).start()

        guarded(level, action)

    def turn(level):
        def action():
            x_copy(level).wait_recv()
            dy_copy(level).start()
            twin_copy(level, 1).start()
            y_copy(level).wait_recv()
            dx_copy(level).start()
            twin_copy(level, 2).start()

        guarded(level, action)

    def close(level):
        def action():
            dx_copy(level).wait_recv()
            dy_copy(level).wait_recv()
            twin_copy(level, 3).start()

        guarded(level, action)

    def drain(level):
        d, way = level

        def action():
            for direction in (0, 1):
                if level == (0, 0) or direction == way:
                    @pl.when(has_upper if direction == 0 else has_lower)
                    def _():
                        z_copy(level, direction).wait_send()
            x_copy(level).wait_send()
            y_copy(level).wait_send()
            dx_copy(level).wait_send()
            dy_copy(level).wait_send()
            for kind in range(4):
                twin_copy(level, kind).wait()

        guarded(level, action)

    def step_action(step):
        for level in levels:
            if level[0] == step:
                spread(level)
        for level in levels:
            if level[0] == step - 1:
                turn(level)
        for level in levels:
            if level[0] == step - 2:
                close(level)

    def finish():
        for level in levels:
            drain(level)

    return step_action, finish


def gather_encode_kernel(depth, batch, own_enc, own_ffn, own_proj, own_dec, pick, patches, vec, up_bias, pos,
                         ffn, proj, dec, wide_out, *rest):
    outs, rest = rest[:11], rest[11:]
    blocks, wide, ffn_here = rest[:3]
    held = rest[3:14]
    kept, start, normed, qkv, mixed, middle, normed_two, slope, active, output, latent = held
    first_sems, second_sems, local, load_sem, wide_sem, out_sems = rest[14:26], rest[26:38], *rest[38:]
    row = lax.axis_index("row")
    col = lax.axis_index("col")
    y, x, z, k = row // 2, row % 2, col // 2, col % 2
    row_x = y * 2 + (1 - x)
    row_y = (1 - y) * 2 + x
    row_d = (1 - y) * 2 + (1 - x)
    near_x, near_y = (row_x, col), (row_y, col)
    twin = (row, z * 2 + (1 - k))
    lower, upper = (row, col - 2), (row, col + 2)
    has_lower, has_upper = z > 0, z < depth - 1

    barrier = pltpu.get_barrier_semaphore()
    for other in (near_x, near_y, twin):
        pl.semaphore_signal(barrier, inc=1, device_id=other, device_id_type=MESH)

    @pl.when(has_lower)
    def _():
        pl.semaphore_signal(barrier, inc=1, device_id=lower, device_id_type=MESH)

    @pl.when(has_upper)
    def _():
        pl.semaphore_signal(barrier, inc=1, device_id=upper, device_id_type=MESH)

    pl.semaphore_wait(barrier, 3 + jnp.where(has_lower, 1, 0) + jnp.where(has_upper, 1, 0))
    ids = (row, row_x, row_y, row_d, z, k, near_x, near_y, twin, lower, upper, has_lower, has_upper)
    tall, short = own_enc.shape[0], own_dec.shape[1]
    broad, thin = own_ffn.shape[2], own_dec.shape[2]

    def rows_of(row_now, size, half):
        part = size if half is None else size // 2
        first = 0 if half is None else half * part
        return pl.ds(pl.multiple_of(row_now * size + first, 16), part)

    def cut_first(index, row_now, half=None):
        rows = rows_of(row_now, tall, half)
        return blocks.at[index, rows], ffn.at[:, rows, pl.ds(pl.multiple_of(index * broad, LANES), broad)]

    def cut_second(index, row_now, half=None):
        return (
            proj.at[index, rows_of(row_now, tall, half)],
            dec.at[:, rows_of(row_now, short, half), pl.ds(pl.multiple_of(index * thin, LANES), thin)],
        )

    own_first, own_second = (own_enc, own_ffn), (own_proj, own_dec)
    step_first, finish_first = gather_steps(depth, ids, own_first, cut_first, first_sems)
    step_second, finish_second = gather_steps(depth, ids, own_second, cut_second, second_sems)
    keep = [
        pltpu.make_async_copy(src, dst, local.at[item])
        for item, (src, dst) in enumerate(
            zip(own_first + own_second, cut_first(col, row) + cut_second(col, row))
        )
    ]
    for item in keep:
        item.start()
    for step in range(depth + 1):
        step_first(step)
    step_second(0)
    step_first(depth + 1)
    finish_first()
    for item in keep:
        item.wait()
    load = pltpu.make_async_copy(ffn, ffn_here, load_sem)
    load.start()
    count, _, width = blocks.shape

    def assemble(first, last):
        for index in range(first, last):
            wide[:, index * width : (index + 1) * width] = blocks[index]

    def flush(index):
        return pltpu.make_async_copy(held[index], outs[index], out_sems.at[index])

    assemble(0, count // 2)
    step_second(1)
    assemble(count // 2, count)
    wide_copy = pltpu.make_async_copy(wide, wide_out, wide_sem)
    wide_copy.start()
    enc_embed(batch, pick, patches, wide, vec, pos, kept, start)
    flush(0).start()
    flush(1).start()
    step_second(2)
    enc_project(wide, vec, start, normed, qkv)
    flush(2).start()
    flush(3).start()
    enc_mix(batch, qkv, mixed)
    flush(4).start()
    step_second(3)
    enc_join(wide, vec, start, mixed, middle, normed_two)
    flush(5).start()
    flush(6).start()
    load.wait()
    total = middle[...] + vec[9:10]
    source = normed_two[...]
    step = 512
    for place in range(0, F, step):
        span = slice(place, place + step)
        value, gain = gelu_pair(nn(source, ffn_here[0, :, span]) + up_bias[:, span])
        slope[:, span] = gain
        value = value.astype(low_type)
        active[:, span] = value
        total = total + nt(value, ffn_here[1, :, span])
        if place == 2 * step:
            step_second(4)
    flush(7).start()
    flush(8).start()
    step_second(5)
    output[...] = total
    unit, _ = standard(total)
    latent[...] = (unit * vec[10:11] + vec[11:12]).astype(low_type)
    flush(9).start()
    flush(10).start()
    for step in range(6, depth + 2):
        step_second(step)
    finish_second()
    wide_copy.wait()
    for index in range(11):
        flush(index).wait()


def gather_encode(own_enc, own_ffn, own_proj, own_dec, depth, pick, padded, vec, up_bias):
    count = 2 * depth - 1
    cols = 2 * depth
    dma = pltpu.SemaphoreType.DMA
    tall, width = own_enc.shape
    shape = jax.ShapeDtypeStruct
    kind = own_enc.dtype
    batch = padded.shape[0]
    first, second = encoder_shapes(batch)
    made = first + second
    sems = [dma((count, 2, 2)), dma((depth, 2, 2))] + [dma((count, 2)) for _ in range(8)]
    sems = sems + [dma((count, 4, 2)), dma((count, 4, 2))]
    outs = pl.pallas_call(
        functools.partial(gather_encode_kernel, depth, batch),
        out_shape=(
            shape((2, 4 * tall, cols * own_ffn.shape[2]), kind),
            shape((cols, 4 * tall, own_proj.shape[1]), kind),
            shape((3, 4 * own_dec.shape[1], cols * own_dec.shape[2]), kind),
            shape((D, 5 * D), kind),
        )
        + made,
        in_specs=[hbm()] * 4 + [whole()] * 5,
        out_specs=[hbm()] * 15,
        scratch_shapes=[
            pltpu.VMEM((cols, 4 * tall, width), kind),
            pltpu.VMEM((D, 5 * D), kind),
            pltpu.VMEM((2, D, F), kind),
        ]
        + [pltpu.VMEM(item.shape, item.dtype) for item in made]
        + sems
        + sems
        + [dma((4,)), dma, dma, dma((11,))],
        compiler_params=pltpu.CompilerParams(
            collective_id=0, has_side_effects=True, vmem_limit_bytes=60 << 20
        ),
        name="gather_encode",
    )(own_enc, own_ffn, own_proj, own_dec, pick, padded, vec, up_bias, jnp.asarray(table_of(D, DEC_ROWS)))
    ffn, proj, dec, wide = outs[:4]
    return ffn, proj, dec, wide, tuple(outs[4:])


def far_first(depth):
    orders = []
    for z in range(depth):
        orders.append(sorted(range(depth), key=lambda t: (-abs(t - z), -abs(2 * t - depth + 1))))
    return orders


code_type = jnp.int16
code_top = 32767.0


def encode(values):
    peak = jnp.max(jnp.abs(values), axis=0, keepdims=True)
    unit = jnp.maximum(peak, 1e-30) * (1.0 / code_top)
    codes = jnp.round(values * (1.0 / unit))
    codes = jnp.clip(codes, -code_top, code_top)
    return codes.astype(jnp.int32).astype(code_type), unit


def decode(codes, unit):
    return codes.astype(jnp.int32).astype(high_type) * unit


def reduce_kernel(depth, devices, cols, parts, chunk, half, blob, small, out, small_out,
                  arrived, mine, stage_x, stage_y, recv_x, recv_y, turn_x, turn_y, back_x, back_y, line_out, line,
                  units_out, units_in, line_units, box,
                  s_load, s_cs, s_cr, s_xs, s_xr, s_ys, s_yr, s_txs, s_txr, s_tys, s_tyr, s_zs, s_zr,
                  u_xs, u_xr, u_ys, u_yr, u_txs, u_txr, u_tys, u_tyr, u_zs, u_zr,
                  s_ps, s_pr, s_qs, s_qr):
    row = lax.axis_index("row")
    col = lax.axis_index("col")
    y, x, z, k = row // 2, row % 2, col // 2, col % 2
    me = row * cols + col
    near_x, near_y = (y * 2 + (1 - x), col), ((1 - y) * 2 + x, col)
    twin = (row, z * 2 + (1 - k))
    lower, upper = (row, col - 2), (row, col + 2)
    has_lower, has_upper = z > 0, z < depth - 1
    steps = depth * parts
    slots = mine.shape[0]
    ahead = slots - 1
    a_rows, b_rows = pl.ds(0, half), pl.ds(half, chunk - half)

    def device(offset):
        index = (me + offset) % devices
        return (index // cols, index % cols)

    barrier = pltpu.get_barrier_semaphore()
    for offset in range(1, devices):
        pl.semaphore_signal(barrier, inc=1, device_id=device(offset), device_id_type=MESH)
    pl.semaphore_wait(barrier, devices - 1)

    def copy(src, dst, send, recv, target):
        return pltpu.make_async_remote_copy(
            src_ref=src, dst_ref=dst, send_sem=send, recv_sem=recv, device_id=target, device_id_type=MESH
        )

    orders = far_first(depth)

    def goal(t):
        turn = t // parts
        value = 0
        for a in range(depth):
            for b in range(depth):
                value = jnp.where((z == a) & (turn == b), orders[a][b], value)
        return value

    def span(t):
        return pl.ds(pl.multiple_of((t % parts) * chunk, 16), chunk)

    def load(t):
        return pltpu.make_async_copy(
            blob.at[goal(t) * 2 + k, :, span(t)], mine.at[t % slots], s_load.at[t % slots]
        )

    def core(t):
        return copy(blob.at[goal(t) * 2 + (1 - k), :, span(t)], arrived.at[t], s_cs.at[t], s_cr.at[t], twin)

    def paired(kind, src, dst, send, recv, unit_send, unit_recv, target):
        def make(t):
            return Group([
                copy(src.at[t], dst.at[t], send.at[t], recv.at[t], target),
                copy(units_out.at[t, kind], units_in.at[t, kind], unit_send.at[t], unit_recv.at[t], target),
            ])

        return make

    first_x = paired(0, stage_x, recv_x, s_xs, s_xr, u_xs, u_xr, near_x)
    first_y = paired(1, stage_y, recv_y, s_ys, s_yr, u_ys, u_yr, near_y)
    second_x = paired(2, turn_x, back_x, s_txs, s_txr, u_txs, u_txr, near_x)
    second_y = paired(3, turn_y, back_y, s_tys, s_tyr, u_tys, u_tyr, near_y)

    def along(t, index, target):
        return Group([
            copy(line_out.at[t], line.at[index], s_zs.at[t], s_zr.at[index], target),
            copy(units_out.at[t, 4], line_units.at[index], u_zs.at[t], u_zr.at[index], target),
        ])

    def upper_index(t):
        return (goal(t) + 1) * parts + t % parts

    def lower_index(t):
        return goal(t) * parts + t % parts

    def to_upper(t):
        return along(t, upper_index(t), upper)

    def to_lower(t):
        return along(t, lower_index(t), lower)

    def small_send(offset):
        target = device(offset)
        return copy(small.at[target[0] * cols + target[1]], box.at[offset], s_ps.at[offset], s_pr.at[offset], target)

    def small_back(offset):
        return copy(small_out.at[me], small_out.at[me], s_qs.at[offset], s_qr.at[offset], device(offset))

    def small_back_recv(offset):
        origin = (me + devices - offset) % devices
        return copy(small_out.at[origin], small_out.at[origin], s_qs.at[offset], s_qr.at[offset], device(offset))

    for t in range(ahead):
        load(t).start()
        core(t).start()
    for offset in range(1, devices):
        small_send(offset).start()

    def stage_one(t):
        load(t).wait()
        core(t).wait_recv()
        slot = t % slots
        for other in (0, 1):
            away = other * 2 + (1 - x)
            stay = other * 2 + x
            codes, unit = encode(mine[slot, away, a_rows] + arrived[t, away, a_rows])
            stage_x[t, other] = codes
            units_out[t, 0, pl.ds(other, 1)] = unit
            arrived[t, stay, a_rows] += mine[slot, stay, a_rows]
        first_x(t).start()
        for other in (0, 1):
            away = (1 - y) * 2 + other
            stay = y * 2 + other
            codes, unit = encode(mine[slot, away, b_rows] + arrived[t, away, b_rows])
            stage_y[t, other] = codes
            units_out[t, 1, pl.ds(other, 1)] = unit
            arrived[t, stay, b_rows] += mine[slot, stay, b_rows]
        first_y(t).start()

    def stage_two(t):
        first_x(t).wait_recv()
        away = (1 - y) * 2 + x
        codes, unit = encode(arrived[t, away, a_rows] + decode(recv_x[t, 1 - y], units_in[t, 0, pl.ds(1 - y, 1)]))
        turn_y[t] = codes
        units_out[t, 3, pl.ds(0, 1)] = unit
        second_y(t).start()
        arrived[t, row, a_rows] += decode(recv_x[t, y], units_in[t, 0, pl.ds(y, 1)])
        first_y(t).wait_recv()
        away = y * 2 + (1 - x)
        codes, unit = encode(arrived[t, away, b_rows] + decode(recv_y[t, 1 - x], units_in[t, 1, pl.ds(1 - x, 1)]))
        turn_x[t] = codes
        units_out[t, 2, pl.ds(0, 1)] = unit
        second_x(t).start()
        arrived[t, row, b_rows] += decode(recv_y[t, x], units_in[t, 1, pl.ds(x, 1)])

    def stage_three(t):
        second_y(t).wait_recv()
        arrived[t, row, a_rows] += decode(back_y[t], units_in[t, 3, pl.ds(0, 1)])
        second_x(t).wait_recv()
        arrived[t, row, b_rows] += decode(back_x[t], units_in[t, 2, pl.ds(0, 1)])

    def take(index):
        return decode(line[index], line_units[index, pl.ds(0, 1)])

    def pack(t):
        codes, unit = encode(arrived[t, row])
        line_out[t] = codes
        units_out[t, 4, pl.ds(0, 1)] = unit

    def stage_four(t):
        target = goal(t)

        @pl.when((target >= z) & has_lower)
        def _():
            to_upper(t).wait_recv()
            arrived[t, row] += take(upper_index(t))

        @pl.when((target <= z) & has_upper)
        def _():
            to_lower(t).wait_recv()
            arrived[t, row] += take(lower_index(t))

        @pl.when(target != z)
        def _():
            pack(t)

        @pl.when(target > z)
        def _():
            to_upper(t).start()

        @pl.when(target < z)
        def _():
            to_lower(t).start()

        @pl.when(target == z)
        def _():
            out[span(t)] = arrived[t, row]

    lags = LAGS

    def body(i, carry):
        @pl.when(i + ahead < steps)
        def _():
            load(i + ahead).start()
            core(i + ahead).start()

        @pl.when(i < steps)
        def _():
            stage_one(i)

        for lag, stage in zip(lags, (stage_two, stage_three, stage_four)):
            @pl.when((i >= lag) & (i - lag < steps))
            def _():
                stage(i - lag)

        @pl.when(i == steps // 2)
        def _():
            total = small[me]
            for offset in range(1, devices):
                small_send(offset).wait_recv()
                total = total + box[offset]
            small_out[me] = total
            for offset in range(1, devices):
                small_back(offset).start()

        return carry

    lax.fori_loop(0, steps + lags[-1], body, 0)

    def finish(t, carry):
        core(t).wait_send()
        first_x(t).wait_send()
        first_y(t).wait_send()
        second_x(t).wait_send()
        second_y(t).wait_send()

        @pl.when(goal(t) > z)
        def _():
            to_upper(t).wait_send()

        @pl.when(goal(t) < z)
        def _():
            to_lower(t).wait_send()

        return carry

    lax.fori_loop(0, steps, finish, 0)
    for offset in range(1, devices):
        small_send(offset).wait_send()
        small_back(offset).wait_send()
        small_back_recv(offset).wait_recv()


def reduce_blocks(blob, small, depth, parts):
    cols, _, rows, lanes = blob.shape
    devices = 4 * cols
    chunk = rows // parts
    half = -(-chunk // 32) * 16
    rest = chunk - half
    steps = depth * parts
    lines = (depth + 1) * parts
    dma = pltpu.SemaphoreType.DMA
    vm = pltpu.VMEM
    return pl.pallas_call(
        functools.partial(reduce_kernel, depth, devices, cols, parts, chunk, half),
        out_shape=(
            jax.ShapeDtypeStruct((rows, lanes), high_type),
            jax.ShapeDtypeStruct(small.shape, high_type),
        ),
        in_specs=[pl.BlockSpec(memory_space=pltpu.HBM), pl.BlockSpec(memory_space=pltpu.VMEM)],
        out_specs=[pl.BlockSpec(memory_space=pltpu.VMEM)] * 2,
        scratch_shapes=[
            vm((steps, 4, chunk, lanes), high_type),
            vm((4, 4, chunk, lanes), high_type),
            vm((steps, 2, half, lanes), code_type),
            vm((steps, 2, rest, lanes), code_type),
            vm((steps, 2, half, lanes), code_type),
            vm((steps, 2, rest, lanes), code_type),
            vm((steps, rest, lanes), code_type),
            vm((steps, half, lanes), code_type),
            vm((steps, rest, lanes), code_type),
            vm((steps, half, lanes), code_type),
            vm((steps, chunk, lanes), code_type),
            vm((lines, chunk, lanes), code_type),
            vm((steps, 5, 8, lanes), high_type),
            vm((steps, 4, 8, lanes), high_type),
            vm((lines, 8, lanes), high_type),
            vm((devices,) + small.shape[1:], high_type),
            dma((4,)),
        ]
        + ([dma((steps,)) for _ in range(11)] + [dma((lines,))])
        + ([dma((steps,)) for _ in range(9)] + [dma((lines,))])
        + [dma((devices,)) for _ in range(4)],
        compiler_params=pltpu.CompilerParams(
            collective_id=1, has_side_effects=True, vmem_limit_bytes=62 << 20
        ),
        name="reduce_blocks",
    )(blob, small)


ENC_ROWS = 64
DEC_ROWS = 208
CLASS_ENC = KEEP
CLASS_DEC = PATCHES
NEGATIVE = -1e30


def nn(left, right):
    return jnp.dot(left, right, preferred_element_type=high_type)


def nt(left, right):
    return lax.dot_general(left, right, (((1,), (1,)), ((), ())), preferred_element_type=high_type)


def tn(left, right):
    return lax.dot_general(left, right, (((0,), (0,)), ((), ())), preferred_element_type=high_type)


def standard(rows):
    mean = jnp.mean(rows, -1, keepdims=True)
    centred = rows - mean
    spread = jnp.mean(centred * centred, -1, keepdims=True)
    rate = lax.rsqrt(spread + norm_eps)
    return centred * rate, rate


def standard_back(unit, rate, grad):
    return rate * (grad - jnp.mean(grad, -1, keepdims=True) - unit * jnp.mean(grad * unit, -1, keepdims=True))


def col_sum(rows):
    return jnp.sum(rows.astype(high_type), 0, keepdims=True)


def gelu_pair(value):
    size = jnp.abs(value)
    below = 1.0 + (0.3275911 * math.sqrt(0.5)) * size
    t = pl.reciprocal(below, approx=True)
    t = t * (2.0 - below * t)
    t = t * (2.0 - below * t)
    fall = jnp.exp(-0.5 * value * value)
    series = 1.061405429
    for item in (-1.453152027, 1.421413741, -0.284496736, 0.254829592):
        series = series * t + item
    tail = 0.5 * series * t * fall
    part = jnp.where(value < 0.0, tail, 1.0 - tail)
    return value * part, part + value * fall * (1.0 / math.sqrt(2.0 * math.pi))


def three_way(value):
    high = value.astype(low_type)
    rest = value - high.astype(high_type)
    middle = rest.astype(low_type)
    return high, middle, (rest - middle.astype(high_type)).astype(low_type)


def place_rows(picks, value):
    parts = three_way(value)
    return nn(picks, parts[0]) + nn(picks, parts[1]) + nn(picks, parts[2])


def stack_heads(value, heads):
    width = LANES // heads
    lane = lax.broadcasted_iota(jnp.int32, value.shape, 1) // width
    return jnp.concatenate([jnp.where(lane == head, value, jnp.zeros_like(value)) for head in range(heads)], 0)


def merge_heads(stacked, heads):
    rows = stacked.shape[0] // heads
    width = LANES // heads
    lane = lax.broadcasted_iota(jnp.int32, (rows, LANES), 1) // width
    merged = stacked[:rows]
    for head in range(1, heads):
        merged = jnp.where(lane == head, stacked[head * rows : (head + 1) * rows], merged)
    return merged


def attend(query, key, value, heads, length):
    scores = nt(stack_heads(query, heads), key)
    column = lax.broadcasted_iota(jnp.int32, scores.shape, 1)
    scores = jnp.where(column < length, scores, NEGATIVE)
    raised = jnp.exp(scores - jnp.max(scores, -1, keepdims=True))
    attention = (raised / jnp.sum(raised, -1, keepdims=True)).astype(low_type)
    return merge_heads(nn(attention, value), heads)


def attend_back(query, key, value, grad, heads, length):
    queries = stack_heads(query, heads)
    grads = stack_heads(grad, heads)
    scores = nt(key, queries)
    place = lax.broadcasted_iota(jnp.int32, scores.shape, 0)
    scores = jnp.where(place < length, scores, NEGATIVE)
    raised = jnp.exp(scores - jnp.max(scores, 0, keepdims=True))
    attention = raised * (1.0 / jnp.sum(raised, 0, keepdims=True))
    inner = nt(value, grads)
    grad_scores = (attention * (inner - jnp.sum(inner * attention, 0, keepdims=True))).astype(low_type)
    grad_value = nn(attention.astype(low_type), grads)
    grad_key = nn(grad_scores, queries)
    grad_query = merge_heads(tn(grad_scores, key), heads)
    return grad_query, grad_key, grad_value


def attend_back_many(batch, query, key, value, grad, heads, length):
    rows = query.shape[0] // batch
    spans = [slice(image * rows, (image + 1) * rows) for image in range(batch)]
    queries = [stack_heads(query[span], heads) for span in spans]
    grads = [stack_heads(grad[span], heads) for span in spans]
    scores = jnp.concatenate([nt(key[span], item) for span, item in zip(spans, queries)], 0)
    inner = jnp.concatenate([nt(value[span], item) for span, item in zip(spans, grads)], 0)
    scores = scores.reshape(batch, rows, scores.shape[1])
    inner = inner.reshape(batch, rows, inner.shape[1])
    place = lax.broadcasted_iota(jnp.int32, scores.shape, 1)
    scores = jnp.where(place < length, scores, NEGATIVE)
    raised = jnp.exp(scores - jnp.max(scores, 1, keepdims=True))
    attention = raised * (1.0 / jnp.sum(raised, 1, keepdims=True))
    grad_scores = (attention * (inner - jnp.sum(inner * attention, 1, keepdims=True))).astype(low_type)
    attention = attention.astype(low_type)
    grad_value = [nn(attention[image], grads[image]) for image in range(batch)]
    grad_key = [nn(grad_scores[image], queries[image]) for image in range(batch)]
    grad_query = [merge_heads(tn(grad_scores[image], key[spans[image]]), heads) for image in range(batch)]
    return tuple(jnp.concatenate(item, 0) for item in (grad_query, grad_key, grad_value))


def wide_kernel(blocks, wide):
    count, _, width = blocks.shape
    for index in range(count):
        wide[:, index * width : (index + 1) * width] = blocks[index]


def enc_embed(batch, pick, patches, wide, vec, pos, kept, start):
    rows = ENC_ROWS
    for image in range(batch):
        span = pl.ds(image * rows, rows)
        kept[span] = nn(pick[image], patches[image]).astype(low_type)
    start[...] = nn(kept[...], wide[:, :D]) + vec[0:1]
    parts = three_way(pos[...])
    for image in range(batch):
        span = pl.ds(image * rows, rows)
        picks = pick[image]
        placed = nn(picks, parts[0]) + nn(picks, parts[1]) + nn(picks, parts[2])
        inner = lax.broadcasted_iota(jnp.int32, placed.shape, 0)
        start[span] = jnp.where(inner == CLASS_ENC, vec[1:2], start[span] + placed)


def enc_project(wide, vec, start, normed, qkv):
    unit, _ = standard(start[...])
    normed[...] = (unit * vec[2:3] + vec[3:4]).astype(low_type)
    scale = 1.0 / math.sqrt(D // HE)
    rows_in = normed[...]
    qkv[:, :D] = ((nn(rows_in, wide[:, D : 2 * D]) + vec[4:5]) * scale).astype(low_type)
    qkv[:, D : 2 * D] = nn(rows_in, wide[:, 2 * D : 3 * D]).astype(low_type)
    qkv[:, 2 * D :] = (nn(rows_in, wide[:, 3 * D : 4 * D]) + vec[5:6]).astype(low_type)


def enc_mix(batch, qkv, mixed):
    rows = ENC_ROWS
    heads = LANES * HE // D
    for image in range(batch):
        span = pl.ds(image * rows, rows)
        for group in range(D // LANES):
            lane = group * LANES
            mixed[span, lane : lane + LANES] = attend(
                qkv[span, lane : lane + LANES],
                qkv[span, D + lane : D + lane + LANES],
                qkv[span, 2 * D + lane : 2 * D + lane + LANES],
                heads,
                KEEP + 1,
            ).astype(low_type)


def enc_join(wide, vec, start, mixed, middle, normed_two):
    middle[...] = start[...] + (nn(mixed[...], wide[:, 4 * D :]) + vec[6:7])
    unit, _ = standard(middle[...])
    normed_two[...] = (unit * vec[7:8] + vec[8:9]).astype(low_type)


def enc_attend_kernel(batch, pick, patches, wide, vec, pos, kept, start, normed, qkv, mixed, middle, normed_two):
    enc_embed(batch, pick, patches, wide, vec, pos, kept, start)
    enc_project(wide, vec, start, normed, qkv)
    enc_mix(batch, qkv, mixed)
    enc_join(wide, vec, start, mixed, middle, normed_two)


def enc_ffn_kernel(last, middle, normed_two, ffn, vec, up_bias, slope, active, output, latent):
    step = pl.program_id(0)

    @pl.when(step == 0)
    def _():
        output[...] = middle[...] + vec[9:10]

    value, gain = gelu_pair(nn(normed_two[...], ffn[0]) + up_bias[...])
    slope[...] = gain
    value = value.astype(low_type)
    active[...] = value
    output[...] += nt(value, ffn[1])

    @pl.when(step == last)
    def _():
        unit, _ = standard(output[...])
        latent[...] = (unit * vec[10:11] + vec[11:12]).astype(low_type)


def dec_attend_kernel(latent, proj, picked, pos, wide, vec, start, normed, qkv, mixed, middle, normed_two):
    picks = picked[0]
    kept = jnp.sum(picks.astype(high_type), 1, keepdims=True)
    entry = nn(latent[...], proj[...]) + vec[0:1]
    rows = place_rows(picks, entry) + (1.0 - kept) * vec[1:2] + pos[...]
    start[...] = rows
    unit, _ = standard(rows)
    rows_in = (unit * vec[2:3] + vec[3:4]).astype(low_type)
    normed[...] = rows_in
    scale = 1.0 / math.sqrt(E // HD)
    qkv[:, :E] = ((nn(rows_in, wide[0, :, :E]) + vec[4:5]) * scale).astype(low_type)
    qkv[:, E : 2 * E] = nn(rows_in, wide[0, :, E : 2 * E]).astype(low_type)
    qkv[:, 2 * E :] = (nn(rows_in, wide[0, :, 2 * E : 3 * E]) + vec[5:6]).astype(low_type)
    heads = LANES * HD // E
    for group in range(E // LANES):
        lane = group * LANES
        mixed[:, lane : lane + LANES] = attend(
            qkv[:, lane : lane + LANES],
            qkv[:, E + lane : E + lane + LANES],
            qkv[:, 2 * E + lane : 2 * E + lane + LANES],
            heads,
            PATCHES + 1,
        ).astype(low_type)
    total = rows + (nn(mixed[...], wide[0, :, 3 * E :]) + vec[6:7])
    middle[...] = total
    unit, _ = standard(total)
    normed_two[...] = (unit * vec[7:8] + vec[8:9]).astype(low_type)


def send_tiles(acc, blob, sem, tiles, rows, per_block, base, stride):
    def go(index, carry):
        tile, part = index // 4, index % 4
        block, inner = tile // per_block, tile % per_block
        pltpu.make_async_copy(
            acc.at[tile, pl.ds(pl.multiple_of(part * rows, 16), rows)],
            blob.at[block, part, pl.ds(pl.multiple_of(base + inner * stride, 16), rows)],
            sem,
        ).start()
        return carry

    lax.fori_loop(0, tiles * 4, go, 0)


def wait_tiles(acc, sem):
    pltpu.make_async_copy(acc, acc, sem).wait()


def dec_ffn_kernel(images, last, count, middle, normed_two, mixed, pixels, picked, weights, head, vec, up_bias, head_bias,
                   grad_middle, grad_mixed, grad_head, vec_grad, up_grad, bias_grad, loss, blob,
                   active, slope, acc_up, acc_down, acc_out, sems):
    step = pl.program_id(0)
    source = normed_two[...]
    rows = source.shape[0]

    @pl.when(step == 0)
    def _():
        grad_head[...] = jnp.zeros_like(grad_head)
        vec_grad[...] = jnp.zeros_like(vec_grad)
        up_grad[...] = jnp.zeros_like(up_grad)
        bias_grad[...] = jnp.zeros_like(bias_grad)
        loss[...] = jnp.zeros_like(loss)
        acc_up[...] = jnp.zeros_like(acc_up)
        acc_down[...] = jnp.zeros_like(acc_down)
        acc_out[...] = jnp.zeros_like(acc_out)

    wide = 512
    total = middle[...] + vec[9:10]
    for place in range(0, H, wide):
        span = slice(place, place + wide)
        value, gain = gelu_pair(nn(source, weights[1, :, span]) + up_bias[:, span])
        slope[:, span] = gain
        value = value.astype(low_type)
        active[:, span] = value
        total = total + nt(value, weights[2, :, span])
    unit, rate = standard(total)
    final = (unit * vec[10:11] + vec[11:12]).astype(low_type)
    predict = nn(final, head[...]) + head_bias[...]
    target, _ = standard(pixels[...].astype(high_type))
    kept = jnp.concatenate([jnp.sum(picked[image].astype(high_type), 1, keepdims=True) for image in range(images)], 0)
    inner = lax.broadcasted_iota(jnp.int32, (rows, 1), 0) % DEC_ROWS
    masked = jnp.where(inner < PATCHES, 1.0 - kept, 0.0)
    error = predict - target
    loss[...] += jnp.sum(masked * error * error)
    grad_predict = (2.0 * masked * error / count).astype(low_type)
    grad_head[...] += tn(final, grad_predict)
    bias_grad[...] += col_sum(grad_predict)
    grad_final = nt(grad_predict, head[...])
    vec_grad[10:11] += col_sum(grad_final * unit)
    vec_grad[11:12] += col_sum(grad_final)
    grad_out = standard_back(unit, rate, grad_final * vec[10:11])
    grad_down = grad_out.astype(low_type)
    vec_grad[9:10] += col_sum(grad_down)
    grad_source = jnp.zeros_like(total)
    for place in range(0, H, wide):
        span = slice(place, place + wide)
        grad_up = (slope[:, span] * nn(grad_down, weights[2, :, span])).astype(low_type)
        up_grad[:, span] += col_sum(grad_up)
        grad_source = grad_source + nt(grad_up, weights[1, :, span])
        piece = tn(grad_down, active[:, span])
        other = tn(source, grad_up)
        for tile in range(wide // LANES):
            lane = slice(tile * LANES, (tile + 1) * LANES)
            acc_down[place // LANES + tile] += piece[:, lane]
            acc_up[place // LANES + tile] += other[:, lane]
    unit, rate = standard(middle[...])
    vec_grad[7:8] += col_sum(grad_source * unit)
    vec_grad[8:9] += col_sum(grad_source)
    grad_rows = standard_back(unit, rate, grad_source * vec[7:8]) + grad_out
    grad_middle[...] = grad_rows
    branch = grad_rows.astype(low_type)
    vec_grad[6:7] += col_sum(branch)
    piece = tn(mixed[...], branch)
    for tile in range(E // LANES):
        acc_out[tile] += piece[:, tile * LANES : (tile + 1) * LANES]
    grad_mixed[...] = nt(branch, weights[0, :, 3 * E :]).astype(low_type)

    @pl.when(step == last)
    def _():
        rows_block = E // 4
        send_tiles(acc_up, blob, sems.at[0], H // LANES, rows_block, 2, 2176, rows_block)
        send_tiles(acc_down, blob, sems.at[1], H // LANES, rows_block, 2, 2432, rows_block)
        send_tiles(acc_out, blob.at[pl.ds(6, 2)], sems.at[2], E // LANES, rows_block, 2, 1920, rows_block)
        wait_tiles(acc_up, sems.at[0])
        wait_tiles(acc_down, sems.at[1])
        wait_tiles(acc_out, sems.at[2])


def dec_back_kernel(last, blob_in, qkv, normed, start, grad_middle, grad_mixed, pick, picked, weights, vec,
                    grad_entry, vec_grad, blob, grads, acc, sem):
    step = pl.program_id(0)

    @pl.when(step == 0)
    def _():
        vec_grad[...] = jnp.zeros_like(vec_grad)
        acc[...] = jnp.zeros_like(acc)

    scale = 1.0 / math.sqrt(E // HD)
    heads = LANES * HD // E
    for group in range(E // LANES):
        lane = group * LANES
        span = slice(lane, lane + LANES)
        query, key, value = attend_back(
            qkv[:, lane : lane + LANES],
            qkv[:, E + lane : E + lane + LANES],
            qkv[:, 2 * E + lane : 2 * E + lane + LANES],
            grad_mixed[:, span],
            heads,
            PATCHES + 1,
        )
        grads[:, span] = (query * scale).astype(low_type)
        grads[:, E + lane : E + lane + LANES] = key.astype(low_type)
        grads[:, 2 * E + lane : 2 * E + lane + LANES] = value.astype(low_type)
    vec_grad[4:5] += col_sum(grads[:, :E])
    vec_grad[5:6] += col_sum(grads[:, 2 * E :])
    rows = normed[...]
    for part in range(3):
        piece = tn(rows, grads[:, part * E : (part + 1) * E])
        for tile in range(E // LANES):
            acc[part * (E // LANES) + tile] += piece[:, tile * LANES : (tile + 1) * LANES]
    grad_normed = nt(grads[...], weights[0, :, : 3 * E])
    unit, rate = standard(start[...])
    vec_grad[2:3] += col_sum(grad_normed * unit)
    vec_grad[3:4] += col_sum(grad_normed)
    grad_rows = standard_back(unit, rate, grad_normed * vec[2:3]) + grad_middle[...]
    kept = jnp.sum(picked[0].astype(high_type), 1, keepdims=True)
    vec_grad[1:2] += col_sum((1.0 - kept) * grad_rows)
    grad_entry[...] = nn(pick[0], grad_rows.astype(low_type)).astype(low_type)

    @pl.when(step == last)
    def _():
        rows_block = E // 4
        send_tiles(acc, blob, sem, 3 * E // LANES, rows_block, 2, 1920, rows_block)
        wait_tiles(acc, sem)


def enc_ffn_back_kernel(last, blob_in, grad_entry, latent, output, middle, normed_two, slope, active, ffn, proj, vec,
                        grad_middle, vec_grad, up_grad, entry_grad, blob,
                        grad_out, grad_down, grad_source, folded, acc_up, acc_down, fold_sem, sems):
    step = pl.program_id(0)
    fold_copy = pltpu.make_async_copy(folded, blob.at[:, :, pl.ds(2688, 96)], fold_sem)
    part_rows = D // 4

    @pl.when(step == 0)
    def _():
        vec_grad[...] = jnp.zeros_like(vec_grad)
        entries = grad_entry[...]
        entry_grad[...] = col_sum(entries)
        grad_proj = tn(latent[...], entries)
        lane = lax.broadcasted_iota(jnp.int32, (96, LANES), 1)
        for part in range(4):
            for pair in range(4):
                first = grad_proj[part * 192 : part * 192 + 96, pair * LANES : (pair + 1) * LANES]
                second = grad_proj[part * 192 + 96 : part * 192 + 192, pair * LANES : (pair + 1) * LANES]
                folded[2 * pair, part] = jnp.where(lane < 64, first, pltpu.roll(second, 64, 1))
                folded[2 * pair + 1, part] = jnp.where(lane < 64, pltpu.roll(first, 64, 1), second)
        fold_copy.start()
        grad_latent = nt(entries, proj[...])
        unit, rate = standard(output[...])
        vec_grad[10:11] = col_sum(grad_latent * unit)
        vec_grad[11:12] = col_sum(grad_latent)
        rows = standard_back(unit, rate, grad_latent * vec[10:11])
        grad_out[...] = rows
        grad_down[...] = rows.astype(low_type)
        vec_grad[9:10] = col_sum(rows.astype(low_type))
        grad_source[...] = jnp.zeros_like(grad_source)

    slot = step % 2

    @pl.when(step >= 2)
    def _():
        wait_tiles(acc_up.at[slot], sems.at[0, slot])
        wait_tiles(acc_down.at[slot], sems.at[1, slot])

    grads = grad_down[...]
    grad_up = (slope[...] * nn(grads, ffn[1])).astype(low_type)
    up_grad[...] = col_sum(grad_up)
    grad_source[...] += nt(grad_up, ffn[0])
    piece = tn(grads, active[...])
    other = tn(normed_two[...], grad_up)
    count = grad_up.shape[1] // LANES
    for tile in range(count):
        lane = slice(tile * LANES, (tile + 1) * LANES)
        acc_down[slot, tile] = piece[:, lane]
        acc_up[slot, tile] = other[:, lane]

    def go(index, carry):
        tile, part = index // 4, index % 4
        place = step * count + tile
        block, inner = place // 3, place % 3
        rows = pl.ds(pl.multiple_of(part * part_rows, 16), part_rows)
        for number, (acc, base) in enumerate(((acc_up, 768), (acc_down, 1344))):
            pltpu.make_async_copy(
                acc.at[slot, tile, rows],
                blob.at[block, part, pl.ds(pl.multiple_of(base + inner * part_rows, 16), part_rows)],
                sems.at[number, slot],
            ).start()
        return carry

    lax.fori_loop(0, count * 4, go, 0)

    @pl.when(step == last)
    def _():
        unit, rate = standard(middle[...])
        vec_grad[7:8] = col_sum(grad_source[...] * unit)
        vec_grad[8:9] = col_sum(grad_source[...])
        grad_rows = standard_back(unit, rate, grad_source[...] * vec[7:8]) + grad_out[...]
        grad_middle[...] = grad_rows
        vec_grad[6:7] = col_sum(grad_rows.astype(low_type))
        fold_copy.wait()
        for item in (0, 1):
            wait_tiles(acc_up.at[item], sems.at[0, item])
            wait_tiles(acc_down.at[item], sems.at[1, item])


def enc_back_kernel(batch, blob_in, qkv, kept, normed, start, mixed, grad_middle, wide, vec,
                    vec_grad, blob, grads, grad_wide, tiles, sem):
    rows = ENC_ROWS
    vec_grad[...] = jnp.zeros_like(vec_grad)
    branch = grad_middle[...].astype(low_type)
    grad_mixed = nt(branch, wide[:, 4 * D :]).astype(low_type)
    grad_wide[:, 4 * D :] = tn(mixed[...], branch)
    scale = 1.0 / math.sqrt(D // HE)
    heads = LANES * HE // D
    for group in range(D // LANES):
        lane = group * LANES
        query, key, value = attend_back_many(
            batch,
            qkv[:, lane : lane + LANES],
            qkv[:, D + lane : D + lane + LANES],
            qkv[:, 2 * D + lane : 2 * D + lane + LANES],
            grad_mixed[:, lane : lane + LANES],
            heads,
            KEEP + 1,
        )
        grads[:, lane : lane + LANES] = (query * scale).astype(low_type)
        grads[:, D + lane : D + lane + LANES] = key.astype(low_type)
        grads[:, 2 * D + lane : 2 * D + lane + LANES] = value.astype(low_type)
    vec_grad[4:5] = col_sum(grads[:, :D])
    vec_grad[5:6] = col_sum(grads[:, 2 * D :])
    rows_in = normed[...]
    for part in range(3):
        grad_wide[:, (part + 1) * D : (part + 2) * D] = tn(rows_in, grads[:, part * D : (part + 1) * D])
    width = 5 * D // 8
    tall = D // 4

    def assemble(block):
        for part in range(4):
            span = slice(part * tall, (part + 1) * tall)
            piece = grad_wide[span, block * width : (block + 1) * width]
            for tile in range(4):
                size = min(LANES, width - tile * LANES)
                value = piece[:, tile * LANES : tile * LANES + size]
                if size < LANES:
                    value = jnp.concatenate([value, jnp.zeros((tall, LANES - size), high_type)], 1)
                tiles[block, part, tile * tall : (tile + 1) * tall] = value
        pltpu.make_async_copy(tiles.at[block], blob.at[block, :, pl.ds(0, 4 * tall)], sem).start()

    for block in range(2, 8):
        assemble(block)
    grad_normed = nt(grads[...], wide[:, D : 4 * D])
    unit, rate = standard(start[...])
    vec_grad[2:3] = col_sum(grad_normed * unit)
    vec_grad[3:4] = col_sum(grad_normed)
    grad_rows = standard_back(unit, rate, grad_normed * vec[2:3]) + grad_middle[...]
    inner = lax.broadcasted_iota(jnp.int32, (grad_rows.shape[0], 1), 0) % rows
    vec_grad[1:2] = col_sum(jnp.where(inner == CLASS_ENC, grad_rows, 0.0))
    embed = jnp.where(inner < KEEP, grad_rows, 0.0).astype(low_type)
    vec_grad[0:1] = col_sum(embed)
    grad_wide[:, :D] = tn(kept[...], embed)
    assemble(0)
    assemble(1)
    wait_tiles(tiles, sem)


def adam_parts(weight, grad, first, second, decay):
    first_new = 0.5 * first + 0.5 * grad
    second_new = 0.5 * second + 0.5 * grad * grad
    bias = 1.0 - 0.5**STEP
    direction = first_new / bias / (jnp.sqrt(second_new / bias) + 1e-08)
    return weight - 0.02 * (direction + decay * weight), first_new, second_new


def adam_kernel(*refs):
    summed, head, small = refs[:3]
    ins, outs = refs[3:24], refs[24:]

    def update(index, place, grad, decay=0.05):
        for target, value in zip(
            range(3), adam_parts(ins[index][place], grad, ins[7 + index][place], ins[14 + index][place], decay)
        ):
            outs[7 * target + index][place] = value

    base = 0
    for index, lead, tall, width in ((0, None, 192, 480), (1, 0, 192, 384), (1, 1, 192, 384),
                                     (3, None, 128, 256), (4, 0, 128, 256), (4, 1, 128, 256)):
        for lane in range(0, width, LANES):
            size = min(LANES, width - lane)
            place = (slice(None), slice(lane, lane + size))
            update(index, place if lead is None else (lead,) + place, summed[base : base + tall, :size])
            base += tall
    folded = summed[base : base + 96]
    update(2, (slice(0, 96),), folded[:, :64])
    update(2, (slice(96, 192),), folded[:, 64:])
    update(5, (slice(None),), head[...])
    update(6, (slice(None),), small[...], 0.0)


def table_of(width, rows):
    quarter = width // 4
    omega = (np.float32(1.0) / np.float32(10000.0) ** (np.arange(quarter, dtype=np.float32) / np.float32(quarter))).astype(np.float32)
    coord = np.arange(SIDE * SIDE)

    def half(place):
        angle = place.astype(np.float32)[:, None] * omega[None, :]
        return np.concatenate([np.sin(angle), np.cos(angle)], 1)

    table = np.concatenate([half(coord // SIDE), half(coord % SIDE)], 1).astype(np.float32)
    return np.concatenate([table, np.zeros((rows - table.shape[0], width), np.float32)], 0)


def whole():
    return pl.BlockSpec(memory_space=pltpu.VMEM)


def hbm():
    return pl.BlockSpec(memory_space=pltpu.HBM)


def params(**more):
    return pltpu.CompilerParams(vmem_limit_bytes=60 << 20, **more)


def picks_of(shuffle):
    batch = shuffle.shape[0]
    keep = jnp.concatenate(
        [
            shuffle[:, :KEEP],
            jnp.full((batch, 1), CLASS_DEC, jnp.int32),
            jnp.full((batch, ENC_ROWS - KEEP - 1), -1, jnp.int32),
        ],
        1,
    )
    places = jnp.arange(DEC_ROWS, dtype=jnp.int32)
    pick = (keep[:, :, None] == places[None, None, :]).astype(low_type)
    picked = (keep[:, None, :] == places[None, :, None]).astype(low_type)
    return pick, picked


def by_image(*block):
    return pl.BlockSpec(block, lambda i: (i,) + (0,) * (len(block) - 1))


def fixed(*block):
    return pl.BlockSpec(block, lambda i: (0,) * len(block))


def encoder_shapes(batch):
    rows = batch * ENC_ROWS
    shape = jax.ShapeDtypeStruct
    first = (
        shape((rows, D), low_type),
        shape((rows, D), high_type),
        shape((rows, D), low_type),
        shape((rows, 3 * D), low_type),
        shape((rows, D), low_type),
        shape((rows, D), high_type),
        shape((rows, D), low_type),
    )
    second = (
        shape((rows, F), high_type),
        shape((rows, F), low_type),
        shape((rows, D), high_type),
        shape((rows, D), low_type),
    )
    return first, second


def encode_images(enc_blocks, enc_ffn, enc_vec, enc_up, pick, padded):
    batch = padded.shape[0]
    rows = batch * ENC_ROWS
    first, second = encoder_shapes(batch)
    wide = pl.pallas_call(
        wide_kernel,
        out_shape=jax.ShapeDtypeStruct((D, 5 * D), low_type),
        in_specs=[whole()],
        out_specs=whole(),
        compiler_params=params(),
        name="wide",
    )(enc_blocks)
    early = pl.pallas_call(
        functools.partial(enc_attend_kernel, batch),
        out_shape=first,
        in_specs=[whole()] * 5,
        out_specs=[whole()] * 7,
        compiler_params=params(),
        name="enc_attend",
    )(pick, padded, wide, enc_vec, jnp.asarray(table_of(D, DEC_ROWS)))
    chunk = 512
    late = pl.pallas_call(
        functools.partial(enc_ffn_kernel, F // chunk - 1),
        grid=(F // chunk,),
        out_shape=second,
        in_specs=[
            fixed(rows, D),
            fixed(rows, D),
            pl.BlockSpec((2, D, chunk), lambda i: (0, 0, i)),
            fixed(12, D),
            pl.BlockSpec((1, chunk), lambda i: (0, i)),
        ],
        out_specs=[
            pl.BlockSpec((rows, chunk), lambda i: (0, i)),
            pl.BlockSpec((rows, chunk), lambda i: (0, i)),
            fixed(rows, D),
            fixed(rows, D),
        ],
        compiler_params=params(),
        name="enc_ffn",
    )(early[5], early[6], enc_ffn, enc_vec, enc_up)
    return wide, early + tuple(late)


def local_grads(wide, enc_ffn, proj, dec3, encoded, head_low, smalls_parts, pick, picked, padded, count):
    enc_vec, _, dec_vec, dec_up, head_bias = smalls_parts
    dec_up, head_bias = dec_up[None], head_bias[None]
    kept, start, normed, qkv, mixed, middle, normed_two, slope, active, enc_out, latent = encoded
    batch = padded.shape[0]
    shape = jax.ShapeDtypeStruct
    dec_pos = jnp.asarray(table_of(E, DEC_ROWS))
    rows, dec_rows = batch * ENC_ROWS, batch * DEC_ROWS
    chunk = 512

    dec_start, dec_normed, dec_qkv, dec_mixed, dec_middle, dec_normed_two = pl.pallas_call(
        dec_attend_kernel,
        grid=(batch,),
        out_shape=(
            shape((dec_rows, E), high_type),
            shape((dec_rows, E), low_type),
            shape((dec_rows, 3 * E), low_type),
            shape((dec_rows, E), low_type),
            shape((dec_rows, E), high_type),
            shape((dec_rows, E), low_type),
        ),
        in_specs=[
            by_image(ENC_ROWS, D),
            fixed(D, E),
            by_image(1, DEC_ROWS, ENC_ROWS),
            fixed(DEC_ROWS, E),
            fixed(1, E, 4 * E),
            fixed(12, E),
        ],
        out_specs=[
            by_image(DEC_ROWS, E),
            by_image(DEC_ROWS, E),
            by_image(DEC_ROWS, 3 * E),
            by_image(DEC_ROWS, E),
            by_image(DEC_ROWS, E),
            by_image(DEC_ROWS, E),
        ],
        compiler_params=params(),
        name="dec_attend",
    )(latent, proj, picked, dec_pos, dec3, dec_vec)

    images = 2 if batch % 2 == 0 else 1
    block = images * DEC_ROWS
    blob_shape = shape((8, 4, 2784, LANES), high_type)
    vm = pltpu.VMEM
    dma = pltpu.SemaphoreType.DMA
    grad_middle, grad_mixed, grad_head, dec_grad_one, dec_up_grad, head_bias_grad, loss, blob = pl.pallas_call(
        functools.partial(dec_ffn_kernel, images, batch // images - 1, count),
        grid=(batch // images,),
        out_shape=(
            shape((dec_rows, E), high_type),
            shape((dec_rows, E), low_type),
            shape((E, P_SIZE), high_type),
            shape((12, E), high_type),
            shape((1, H), high_type),
            shape((1, P_SIZE), high_type),
            shape((8, LANES), high_type),
            blob_shape,
        ),
        in_specs=[
            by_image(block, E),
            by_image(block, E),
            by_image(block, E),
            by_image(block, P_SIZE),
            by_image(images, DEC_ROWS, ENC_ROWS),
            fixed(3, E, H),
            fixed(E, P_SIZE),
            fixed(12, E),
            fixed(1, H),
            fixed(1, P_SIZE),
        ],
        out_specs=[
            by_image(block, E),
            by_image(block, E),
            fixed(E, P_SIZE),
            fixed(12, E),
            fixed(1, H),
            fixed(1, P_SIZE),
            fixed(8, LANES),
            hbm(),
        ],
        scratch_shapes=[
            vm((block, H), low_type),
            vm((block, H), high_type),
            vm((H // LANES, E, LANES), high_type),
            vm((H // LANES, E, LANES), high_type),
            vm((E // LANES, E, LANES), high_type),
            dma((3,)),
        ],
        compiler_params=params(),
        name="dec_ffn",
    )(dec_middle, dec_normed_two, dec_mixed, padded.reshape(dec_rows, P_SIZE), picked, dec3, head_low, dec_vec, dec_up, head_bias)

    grad_entry, dec_grad_two, blob = pl.pallas_call(
        functools.partial(dec_back_kernel, batch - 1),
        grid=(batch,),
        out_shape=(shape((rows, E), low_type), shape((12, E), high_type), blob_shape),
        in_specs=[
            hbm(),
            by_image(DEC_ROWS, 3 * E),
            by_image(DEC_ROWS, E),
            by_image(DEC_ROWS, E),
            by_image(DEC_ROWS, E),
            by_image(DEC_ROWS, E),
            by_image(1, ENC_ROWS, DEC_ROWS),
            by_image(1, DEC_ROWS, ENC_ROWS),
            fixed(1, E, 4 * E),
            fixed(12, E),
        ],
        out_specs=[by_image(ENC_ROWS, E), fixed(12, E), hbm()],
        scratch_shapes=[vm((DEC_ROWS, 3 * E), low_type), vm((3 * E // LANES, E, LANES), high_type), dma],
        input_output_aliases={0: 2},
        compiler_params=params(),
        name="dec_back",
    )(blob, dec_qkv, dec_normed, dec_start, grad_middle, grad_mixed, pick, picked, dec3, dec_vec)

    enc_grad_middle, enc_grad_one, enc_up_grad, entry_grad, blob = pl.pallas_call(
        functools.partial(enc_ffn_back_kernel, F // chunk - 1),
        grid=(F // chunk,),
        out_shape=(
            shape((rows, D), high_type),
            shape((12, D), high_type),
            shape((1, F), high_type),
            shape((1, E), high_type),
            blob_shape,
        ),
        in_specs=[
            hbm(),
            fixed(rows, E),
            fixed(rows, D),
            fixed(rows, D),
            fixed(rows, D),
            fixed(rows, D),
            pl.BlockSpec((rows, chunk), lambda i: (0, i)),
            pl.BlockSpec((rows, chunk), lambda i: (0, i)),
            pl.BlockSpec((2, D, chunk), lambda i: (0, 0, i)),
            fixed(D, E),
            fixed(12, D),
        ],
        out_specs=[
            fixed(rows, D),
            fixed(12, D),
            pl.BlockSpec((1, chunk), lambda i: (0, i)),
            fixed(1, E),
            hbm(),
        ],
        scratch_shapes=[
            vm((rows, D), high_type),
            vm((rows, D), low_type),
            vm((rows, D), high_type),
            vm((8, 4, 96, LANES), high_type),
            vm((2, chunk // LANES, D, LANES), high_type),
            vm((2, chunk // LANES, D, LANES), high_type),
            dma,
            dma((2, 2)),
        ],
        input_output_aliases={0: 4},
        compiler_params=params(),
        name="enc_ffn_back",
    )(blob, grad_entry, latent, enc_out, middle, normed_two, slope, active, enc_ffn, proj, enc_vec)
    enc_grad_two, blob = pl.pallas_call(
        functools.partial(enc_back_kernel, batch),
        out_shape=(shape((12, D), high_type), blob_shape),
        in_specs=[hbm()] + [whole()] * 8,
        out_specs=[whole(), hbm()],
        scratch_shapes=[
            vm((rows, 3 * D), low_type),
            vm((D, 5 * D), high_type),
            vm((8, 4, D, LANES), high_type),
            dma,
        ],
        input_output_aliases={0: 1},
        compiler_params=params(),
        name="enc_back",
    )(blob, qkv, kept, normed, start, mixed, enc_grad_middle, wide, enc_vec)
    dec_grad = (dec_grad_one + dec_grad_two).at[0].set(entry_grad[0])
    smalls = jnp.concatenate(
        [
            (enc_grad_one + enc_grad_two).reshape(-1),
            enc_up_grad[0],
            dec_grad.reshape(-1),
            dec_up_grad[0],
            head_bias_grad[0],
        ]
    )
    return blob, grad_head, smalls, loss[0, 0]


def untile(block, rows, width):
    tiles = -(-width // LANES)
    return block.reshape(tiles, rows, LANES).transpose(1, 0, 2).reshape(rows, tiles * LANES)[:, :width]


def unfold_proj(block):
    width = block.shape[1] // 2
    return jnp.concatenate([block[:, :width], block[:, width:]], 0)


def unpack_shards(blob):
    cuts = [0, 768, 576, 576, 256, 256, 256, 96]
    places = [sum(cuts[: index + 1]) for index in range(len(cuts))]
    piece = [blob[places[index] : places[index + 1]] for index in range(7)]
    return (
        untile(piece[0], 192, 480),
        jnp.stack([untile(piece[1], 192, 384), untile(piece[2], 192, 384)]),
        unfold_proj(piece[6]),
        untile(piece[3], 128, 256),
        jnp.stack([untile(piece[4], 128, 256), untile(piece[5], 128, 256)]),
    )


def whole_arrays(blob):
    col_size, row_size = blob.shape[:2]
    parts = jax.vmap(jax.vmap(unpack_shards))(blob)

    def joined(array):
        if array.ndim == 4:
            return array.transpose(1, 2, 0, 3).reshape(row_size * array.shape[2], col_size * array.shape[3])
        return array.transpose(2, 1, 3, 0, 4).reshape(2, row_size * array.shape[3], col_size * array.shape[4])

    return tuple(joined(item) for item in parts)


def on_small_plane():
    return lax.axis_size("row") == 4 and lax.axis_size("col") == 8


def gather_and_encode(enc_w, enc_ffn, dec_proj, dec_w, dec_ffn, enc_vec, enc_up, pick, padded):
    shards = [item.astype(low_type) for item in (enc_w, enc_ffn, dec_proj, jnp.concatenate([dec_w[None], dec_ffn], 0))]
    if on_small_plane():
        ffn, proj, dec, wide, encoded = gather_encode(
            *shards, lax.axis_size("col") // 2, pick, padded, enc_vec, enc_up[None]
        )
        return wide, ffn, proj.transpose(1, 0, 2).reshape(D, E), dec, encoded
    full = []
    for item in shards:
        rowed = lax.all_gather(item, "row", axis=item.ndim - 2, tiled=True)
        full.append(lax.all_gather(rowed, "col", axis=item.ndim - 1, tiled=True))
    blocks = full[0].reshape(D, 8, 5 * D // 8).transpose(1, 0, 2)
    wide, encoded = encode_images(blocks, full[1], enc_vec, enc_up[None], pick, padded)
    return wide, full[1], full[2], full[3], encoded


def apply_updates(blob, grad_head, smalls, loss, params_now, firsts, seconds):
    count = smalls.shape[0]
    summed_head = lax.psum(grad_head, ("row", "col"))
    if on_small_plane():
        small = jnp.concatenate([smalls, loss[None], jnp.zeros((32 * 8 * LANES - count - 1,), high_type)])
        summed, small = reduce_blocks(blob, small.reshape(32, 8, LANES), lax.axis_size("col") // 2, 6)
        small = small.reshape(-1, LANES)
        flat = lambda group: group[:6] + (group[6].reshape(-1, LANES),)
        ins = flat(params_now) + flat(firsts) + flat(seconds)
        outs = pl.pallas_call(
            adam_kernel,
            out_shape=tuple(jax.ShapeDtypeStruct(item.shape, high_type) for item in ins),
            in_specs=[whole()] * 24,
            out_specs=[whole()] * 21,
            compiler_params=params(),
            name="adam",
        )(summed, summed_head, small[: count // LANES], *ins)
        outs = [item.reshape(-1) if index % 7 == 6 else item for index, item in enumerate(outs)]
        return outs, small[count // LANES, count % LANES]
    shards = []
    for item in whole_arrays(blob):
        done = lax.psum_scatter(item, "col", scatter_dimension=item.ndim - 1, tiled=True)
        shards.append(lax.psum_scatter(done, "row", scatter_dimension=item.ndim - 2, tiled=True))
    smalls, loss = lax.psum((smalls, loss), ("row", "col"))
    grads = tuple(shards) + (summed_head, smalls)
    decays = (0.05,) * 6 + (0.0,)
    results = [adam_parts(*item) for item in zip(params_now, grads, firsts, seconds, decays)]
    return [item[kind] for kind in range(3) for item in results], loss


def body(
    patches,
    shuffle,
    enc_w,
    enc_ffn,
    dec_proj,
    dec_w,
    dec_ffn,
    head_w,
    smalls,
    first_enc_w,
    first_enc_ffn,
    first_dec_proj,
    first_dec_w,
    first_dec_ffn,
    first_head_w,
    first_smalls,
    second_enc_w,
    second_enc_ffn,
    second_dec_proj,
    second_dec_w,
    second_dec_ffn,
    second_head_w,
    second_smalls,
):
    pick, picked = picks_of(shuffle)
    padded = jnp.pad(patches, ((0, 0), (0, DEC_ROWS - PATCHES), (0, 0)))
    parts = unpack(smalls)
    wide, ffn, proj, dec, encoded = gather_and_encode(
        enc_w, enc_ffn, dec_proj, dec_w, dec_ffn, parts[0], parts[1], pick, padded
    )
    count = patches.shape[0] * lax.axis_size("row") * lax.axis_size("col") * (PATCHES - KEEP) * P_SIZE
    blob, grad_head, grad_smalls, loss_local = local_grads(
        wide, ffn, proj, dec, encoded, head_w.astype(low_type), parts, pick, picked, padded, count
    )
    params_now = (enc_w, enc_ffn, dec_proj, dec_w, dec_ffn, head_w, smalls)
    firsts = (
        first_enc_w,
        first_enc_ffn,
        first_dec_proj,
        first_dec_w,
        first_dec_ffn,
        first_head_w,
        first_smalls,
    )
    seconds = (
        second_enc_w,
        second_enc_ffn,
        second_dec_proj,
        second_dec_w,
        second_dec_ffn,
        second_head_w,
        second_smalls,
    )
    outs, loss_sum = apply_updates(blob, grad_head, grad_smalls, loss_local, params_now, firsts, seconds)
    return tuple(outs) + (loss_sum / count,)


def solution(mesh):
    in_specs = (
        P(("row", "col"), None, None),
        P(("row", "col"), None),
        P("row", "col"),
        P(None, "row", "col"),
        P("row", "col"),
        P("row", "col"),
        P(None, "row", "col"),
        P(),
        P(),
        P("row", "col"),
        P(None, "row", "col"),
        P("row", "col"),
        P("row", "col"),
        P(None, "row", "col"),
        P(),
        P(),
        P("row", "col"),
        P(None, "row", "col"),
        P("row", "col"),
        P("row", "col"),
        P(None, "row", "col"),
        P(),
        P(),
    )
    out_specs = (
        P("row", "col"),
        P(None, "row", "col"),
        P("row", "col"),
        P("row", "col"),
        P(None, "row", "col"),
        P(),
        P(),
        P("row", "col"),
        P(None, "row", "col"),
        P("row", "col"),
        P("row", "col"),
        P(None, "row", "col"),
        P(),
        P(),
        P("row", "col"),
        P(None, "row", "col"),
        P("row", "col"),
        P("row", "col"),
        P(None, "row", "col"),
        P(),
        P(),
        P(),
    )
    return jax.shard_map(body, mesh=mesh, in_specs=in_specs, out_specs=out_specs, check_vma=False)
```

```python
import functools
import math

import jax
import jax.numpy as jnp
import numpy as np
from jax import lax
from jax.experimental import pallas as pl
from jax.experimental.pallas import tpu as pltpu
from jax.sharding import PartitionSpec as P

D = 768
HE = 12
F = 3072
E = 512
HD = 16
H = 2048
P_SIZE = 768
SIDE = 14
KEEP = 49
STEP = 5
PATCHES = 196
LANES = 128

norm_eps = 1e-06
low_type = jnp.bfloat16
high_type = jnp.float32


MESH = pl.DeviceIdType.MESH
LAGS = (2, 4, 6)


class Group:
    def __init__(self, copies):
        self.copies = copies

    def start(self):
        for item in self.copies:
            item.start()

    def wait_recv(self):
        for item in self.copies:
            item.wait_recv()

    def wait_send(self):
        for item in self.copies:
            item.wait_send()

    def wait(self):
        for item in self.copies:
            item.wait()


def gather_steps(depth, place_ids, own, cut, sems):
    row, row_x, row_y, row_d, z, k, near_x, near_y, twin, lower, upper, has_lower, has_upper = place_ids
    zs, zr, xs, xr, ys, yr, dxs, dxr, dys, dyr, cs, cr = sems
    levels = [(0, 0)] + [(d, way) for d in range(1, depth) for way in (0, 1)]
    level_of = {item: number for number, item in enumerate(levels)}

    def place(level):
        d, way = level
        return z - d if way == 0 else z + d

    def valid(level):
        d, way = level
        return z - d >= 0 if way == 0 else z + d < depth

    def slot(level, row_now, half=None):
        return cut(place(level) * 2 + k, row_now, half)

    def source(level):
        return own if level == (0, 0) else slot(level, row)

    def copy(src, dst, send, recv, target):
        return Group(
            [
                pltpu.make_async_remote_copy(
                    src_ref=src[item],
                    dst_ref=dst[item],
                    send_sem=send.at[item],
                    recv_sem=recv.at[item],
                    device_id=target,
                    device_id_type=MESH,
                )
                for item in range(len(own))
            ]
        )

    def z_copy(level, way):
        d = level[0]
        n = level_of[level]
        return copy(source(level), slot(level, row), zs.at[n, way], zr.at[d, way], upper if way == 0 else lower)

    def x_copy(level):
        n = level_of[level]
        return copy(source(level), slot(level, row), xs.at[n], xr.at[n], near_x)

    def y_copy(level):
        n = level_of[level]
        return copy(source(level), slot(level, row), ys.at[n], yr.at[n], near_y)

    def dx_copy(level):
        n = level_of[level]
        refs = slot(level, row_y, 1)
        return copy(refs, refs, dxs.at[n], dxr.at[n], near_x)

    def dy_copy(level):
        n = level_of[level]
        refs = slot(level, row_x, 0)
        return copy(refs, refs, dys.at[n], dyr.at[n], near_y)

    def twin_copy(level, kind):
        n = level_of[level]
        row_now = (row, row_x, row_y, row_d)[kind]
        src = source(level) if kind == 0 else slot(level, row_now)
        return copy(src, slot(level, row_now), cs.at[n, kind], cr.at[n, kind], twin)

    def guarded(level, action):
        if level == (0, 0):
            action()
        else:
            pl.when(valid(level))(action)

    def spread(level):
        d, way = level

        def action():
            if level != (0, 0):
                z_copy((d - 1, way if d > 1 else 0), way).wait_recv()
            for direction in (0, 1):
                if level == (0, 0) or direction == way:
                    @pl.when(has_upper if direction == 0 else has_lower)
                    def _():
                        z_copy(level, direction).start()
            x_copy(level).start()
            y_copy(level).start()
            twin_copy(level, 0).start()

        guarded(level, action)

    def turn(level):
        def action():
            x_copy(level).wait_recv()
            dy_copy(level).start()
            twin_copy(level, 1).start()
            y_copy(level).wait_recv()
            dx_copy(level).start()
            twin_copy(level, 2).start()

        guarded(level, action)

    def close(level):
        def action():
            dx_copy(level).wait_recv()
            dy_copy(level).wait_recv()
            twin_copy(level, 3).start()

        guarded(level, action)

    def drain(level):
        d, way = level

        def action():
            for direction in (0, 1):
                if level == (0, 0) or direction == way:
                    @pl.when(has_upper if direction == 0 else has_lower)
                    def _():
                        z_copy(level, direction).wait_send()
            x_copy(level).wait_send()
            y_copy(level).wait_send()
            dx_copy(level).wait_send()
            dy_copy(level).wait_send()
            for kind in range(4):
                twin_copy(level, kind).wait()

        guarded(level, action)

    def step_action(step):
        for level in levels:
            if level[0] == step:
                spread(level)
        for level in levels:
            if level[0] == step - 1:
                turn(level)
        for level in levels:
            if level[0] == step - 2:
                close(level)

    def finish():
        for level in levels:
            drain(level)

    return step_action, finish


def gather_encode_kernel(depth, batch, own_enc, own_ffn, own_proj, own_dec, pick, patches, vec, up_bias, pos,
                         ffn, proj, dec, wide_out, *rest):
    outs, rest = rest[:11], rest[11:]
    blocks, wide, ffn_here = rest[:3]
    held = rest[3:14]
    kept, start, normed, qkv, mixed, middle, normed_two, slope, active, output, latent = held
    first_sems, second_sems, local, load_sem, wide_sem, out_sems = rest[14:26], rest[26:38], *rest[38:]
    row = lax.axis_index("row")
    col = lax.axis_index("col")
    y, x, z, k = row // 2, row % 2, col // 2, col % 2
    row_x = y * 2 + (1 - x)
    row_y = (1 - y) * 2 + x
    row_d = (1 - y) * 2 + (1 - x)
    near_x, near_y = (row_x, col), (row_y, col)
    twin = (row, z * 2 + (1 - k))
    lower, upper = (row, col - 2), (row, col + 2)
    has_lower, has_upper = z > 0, z < depth - 1

    barrier = pltpu.get_barrier_semaphore()
    for other in (near_x, near_y, twin):
        pl.semaphore_signal(barrier, inc=1, device_id=other, device_id_type=MESH)

    @pl.when(has_lower)
    def _():
        pl.semaphore_signal(barrier, inc=1, device_id=lower, device_id_type=MESH)

    @pl.when(has_upper)
    def _():
        pl.semaphore_signal(barrier, inc=1, device_id=upper, device_id_type=MESH)

    pl.semaphore_wait(barrier, 3 + jnp.where(has_lower, 1, 0) + jnp.where(has_upper, 1, 0))
    ids = (row, row_x, row_y, row_d, z, k, near_x, near_y, twin, lower, upper, has_lower, has_upper)
    tall, short = own_enc.shape[0], own_dec.shape[1]
    broad, thin = own_ffn.shape[2], own_dec.shape[2]

    def rows_of(row_now, size, half):
        part = size if half is None else size // 2
        first = 0 if half is None else half * part
        return pl.ds(pl.multiple_of(row_now * size + first, 16), part)

    def cut_first(index, row_now, half=None):
        rows = rows_of(row_now, tall, half)
        return blocks.at[index, rows], ffn.at[:, rows, pl.ds(pl.multiple_of(index * broad, LANES), broad)]

    def cut_second(index, row_now, half=None):
        return (
            proj.at[index, rows_of(row_now, tall, half)],
            dec.at[:, rows_of(row_now, short, half), pl.ds(pl.multiple_of(index * thin, LANES), thin)],
        )

    own_first, own_second = (own_enc, own_ffn), (own_proj, own_dec)
    step_first, finish_first = gather_steps(depth, ids, own_first, cut_first, first_sems)
    step_second, finish_second = gather_steps(depth, ids, own_second, cut_second, second_sems)
    keep = [
        pltpu.make_async_copy(src, dst, local.at[item])
        for item, (src, dst) in enumerate(
            zip(own_first + own_second, cut_first(col, row) + cut_second(col, row))
        )
    ]
    for item in keep:
        item.start()
    for step in range(depth + 1):
        step_first(step)
    step_second(0)
    step_first(depth + 1)
    finish_first()
    for item in keep:
        item.wait()
    load = pltpu.make_async_copy(ffn, ffn_here, load_sem)
    load.start()
    count, _, width = blocks.shape

    def assemble(first, last):
        for index in range(first, last):
            wide[:, index * width : (index + 1) * width] = blocks[index]

    def flush(index):
        return pltpu.make_async_copy(held[index], outs[index], out_sems.at[index])

    assemble(0, count // 2)
    step_second(1)
    assemble(count // 2, count)
    wide_copy = pltpu.make_async_copy(wide, wide_out, wide_sem)
    wide_copy.start()
    enc_embed(batch, pick, patches, wide, vec, pos, kept, start)
    flush(0).start()
    flush(1).start()
    step_second(2)
    enc_project(wide, vec, start, normed, qkv)
    flush(2).start()
    flush(3).start()
    enc_mix(batch, qkv, mixed)
    flush(4).start()
    step_second(3)
    enc_join(wide, vec, start, mixed, middle, normed_two)
    flush(5).start()
    flush(6).start()
    load.wait()
    total = middle[...] + vec[9:10]
    source = normed_two[...]
    step = 512
    for place in range(0, F, step):
        span = slice(place, place + step)
        value, gain = gelu_pair(nn(source, ffn_here[0, :, span]) + up_bias[:, span])
        slope[:, span] = gain
        value = value.astype(low_type)
        active[:, span] = value
        total = total + nt(value, ffn_here[1, :, span])
        if place == 2 * step:
            step_second(4)
    flush(7).start()
    flush(8).start()
    step_second(5)
    output[...] = total
    unit, _ = standard(total)
    latent[...] = (unit * vec[10:11] + vec[11:12]).astype(low_type)
    flush(9).start()
    flush(10).start()
    for step in range(6, depth + 2):
        step_second(step)
    finish_second()
    wide_copy.wait()
    for index in range(11):
        flush(index).wait()


def gather_encode(own_enc, own_ffn, own_proj, own_dec, depth, pick, padded, vec, up_bias):
    count = 2 * depth - 1
    cols = 2 * depth
    dma = pltpu.SemaphoreType.DMA
    tall, width = own_enc.shape
    shape = jax.ShapeDtypeStruct
    kind = own_enc.dtype
    batch = padded.shape[0]
    first, second = encoder_shapes(batch)
    made = first + second
    sems = [dma((count, 2, 2)), dma((depth, 2, 2))] + [dma((count, 2)) for _ in range(8)]
    sems = sems + [dma((count, 4, 2)), dma((count, 4, 2))]
    outs = pl.pallas_call(
        functools.partial(gather_encode_kernel, depth, batch),
        out_shape=(
            shape((2, 4 * tall, cols * own_ffn.shape[2]), kind),
            shape((cols, 4 * tall, own_proj.shape[1]), kind),
            shape((3, 4 * own_dec.shape[1], cols * own_dec.shape[2]), kind),
            shape((D, 5 * D), kind),
        )
        + made,
        in_specs=[hbm()] * 4 + [whole()] * 5,
        out_specs=[hbm()] * 15,
        scratch_shapes=[
            pltpu.VMEM((cols, 4 * tall, width), kind),
            pltpu.VMEM((D, 5 * D), kind),
            pltpu.VMEM((2, D, F), kind),
        ]
        + [pltpu.VMEM(item.shape, item.dtype) for item in made]
        + sems
        + sems
        + [dma((4,)), dma, dma, dma((11,))],
        compiler_params=pltpu.CompilerParams(
            collective_id=0, has_side_effects=True, vmem_limit_bytes=60 << 20
        ),
        name="gather_encode",
    )(own_enc, own_ffn, own_proj, own_dec, pick, padded, vec, up_bias, jnp.asarray(table_of(D, DEC_ROWS)))
    ffn, proj, dec, wide = outs[:4]
    return ffn, proj, dec, wide, tuple(outs[4:])


def far_first(depth):
    orders = []
    for z in range(depth):
        orders.append(sorted(range(depth), key=lambda t: (-abs(t - z), -abs(2 * t - depth + 1))))
    return orders


code_type = jnp.int16
code_top = 32767.0


def encode(values):
    peak = jnp.max(jnp.abs(values), axis=0, keepdims=True)
    unit = jnp.maximum(peak, 1e-30) * (1.0 / code_top)
    codes = jnp.round(values * (1.0 / unit))
    codes = jnp.clip(codes, -code_top, code_top)
    return codes.astype(jnp.int32).astype(code_type), unit


def decode(codes, unit):
    return codes.astype(jnp.int32).astype(high_type) * unit


def reduce_kernel(depth, devices, cols, parts, chunk, half, blob, small, out, small_out,
                  arrived, mine, stage_x, stage_y, recv_x, recv_y, turn_x, turn_y, back_x, back_y, line_out, line,
                  units_out, units_in, line_units, box,
                  s_load, s_cs, s_cr, s_xs, s_xr, s_ys, s_yr, s_txs, s_txr, s_tys, s_tyr, s_zs, s_zr,
                  u_xs, u_xr, u_ys, u_yr, u_txs, u_txr, u_tys, u_tyr, u_zs, u_zr,
                  s_ps, s_pr, s_qs, s_qr):
    row = lax.axis_index("row")
    col = lax.axis_index("col")
    y, x, z, k = row // 2, row % 2, col // 2, col % 2
    me = row * cols + col
    near_x, near_y = (y * 2 + (1 - x), col), ((1 - y) * 2 + x, col)
    twin = (row, z * 2 + (1 - k))
    lower, upper = (row, col - 2), (row, col + 2)
    has_lower, has_upper = z > 0, z < depth - 1
    steps = depth * parts
    slots = mine.shape[0]
    ahead = slots - 1
    a_rows, b_rows = pl.ds(0, half), pl.ds(half, chunk - half)

    def device(offset):
        index = (me + offset) % devices
        return (index // cols, index % cols)

    barrier = pltpu.get_barrier_semaphore()
    for offset in range(1, devices):
        pl.semaphore_signal(barrier, inc=1, device_id=device(offset), device_id_type=MESH)
    pl.semaphore_wait(barrier, devices - 1)

    def copy(src, dst, send, recv, target):
        return pltpu.make_async_remote_copy(
            src_ref=src, dst_ref=dst, send_sem=send, recv_sem=recv, device_id=target, device_id_type=MESH
        )

    orders = far_first(depth)

    def goal(t):
        turn = t // parts
        value = 0
        for a in range(depth):
            for b in range(depth):
                value = jnp.where((z == a) & (turn == b), orders[a][b], value)
        return value

    def span(t):
        return pl.ds(pl.multiple_of((t % parts) * chunk, 16), chunk)

    def load(t):
        return pltpu.make_async_copy(
            blob.at[goal(t) * 2 + k, :, span(t)], mine.at[t % slots], s_load.at[t % slots]
        )

    def core(t):
        return copy(blob.at[goal(t) * 2 + (1 - k), :, span(t)], arrived.at[t], s_cs.at[t], s_cr.at[t], twin)

    def paired(kind, src, dst, send, recv, unit_send, unit_recv, target):
        def make(t):
            return Group([
                copy(src.at[t], dst.at[t], send.at[t], recv.at[t], target),
                copy(units_out.at[t, kind], units_in.at[t, kind], unit_send.at[t], unit_recv.at[t], target),
            ])

        return make

    first_x = paired(0, stage_x, recv_x, s_xs, s_xr, u_xs, u_xr, near_x)
    first_y = paired(1, stage_y, recv_y, s_ys, s_yr, u_ys, u_yr, near_y)
    second_x = paired(2, turn_x, back_x, s_txs, s_txr, u_txs, u_txr, near_x)
    second_y = paired(3, turn_y, back_y, s_tys, s_tyr, u_tys, u_tyr, near_y)

    def along(t, index, target):
        return Group([
            copy(line_out.at[t], line.at[index], s_zs.at[t], s_zr.at[index], target),
            copy(units_out.at[t, 4], line_units.at[index], u_zs.at[t], u_zr.at[index], target),
        ])

    def upper_index(t):
        return (goal(t) + 1) * parts + t % parts

    def lower_index(t):
        return goal(t) * parts + t % parts

    def to_upper(t):
        return along(t, upper_index(t), upper)

    def to_lower(t):
        return along(t, lower_index(t), lower)

    def small_send(offset):
        target = device(offset)
        return copy(small.at[target[0] * cols + target[1]], box.at[offset], s_ps.at[offset], s_pr.at[offset], target)

    def small_back(offset):
        return copy(small_out.at[me], small_out.at[me], s_qs.at[offset], s_qr.at[offset], device(offset))

    def small_back_recv(offset):
        origin = (me + devices - offset) % devices
        return copy(small_out.at[origin], small_out.at[origin], s_qs.at[offset], s_qr.at[offset], device(offset))

    for t in range(ahead):
        load(t).start()
        core(t).start()
    for offset in range(1, devices):
        small_send(offset).start()

    def stage_one(t):
        load(t).wait()
        core(t).wait_recv()
        slot = t % slots
        for other in (0, 1):
            away = other * 2 + (1 - x)
            stay = other * 2 + x
            codes, unit = encode(mine[slot, away, a_rows] + arrived[t, away, a_rows])
            stage_x[t, other] = codes
            units_out[t, 0, pl.ds(other, 1)] = unit
            arrived[t, stay, a_rows] += mine[slot, stay, a_rows]
        first_x(t).start()
        for other in (0, 1):
            away = (1 - y) * 2 + other
            stay = y * 2 + other
            codes, unit = encode(mine[slot, away, b_rows] + arrived[t, away, b_rows])
            stage_y[t, other] = codes
            units_out[t, 1, pl.ds(other, 1)] = unit
            arrived[t, stay, b_rows] += mine[slot, stay, b_rows]
        first_y(t).start()

    def stage_two(t):
        first_x(t).wait_recv()
        away = (1 - y) * 2 + x
        codes, unit = encode(arrived[t, away, a_rows] + decode(recv_x[t, 1 - y], units_in[t, 0, pl.ds(1 - y, 1)]))
        turn_y[t] = codes
        units_out[t, 3, pl.ds(0, 1)] = unit
        second_y(t).start()
        arrived[t, row, a_rows] += decode(recv_x[t, y], units_in[t, 0, pl.ds(y, 1)])
        first_y(t).wait_recv()
        away = y * 2 + (1 - x)
        codes, unit = encode(arrived[t, away, b_rows] + decode(recv_y[t, 1 - x], units_in[t, 1, pl.ds(1 - x, 1)]))
        turn_x[t] = codes
        units_out[t, 2, pl.ds(0, 1)] = unit
        second_x(t).start()
        arrived[t, row, b_rows] += decode(recv_y[t, x], units_in[t, 1, pl.ds(x, 1)])

    def stage_three(t):
        second_y(t).wait_recv()
        arrived[t, row, a_rows] += decode(back_y[t], units_in[t, 3, pl.ds(0, 1)])
        second_x(t).wait_recv()
        arrived[t, row, b_rows] += decode(back_x[t], units_in[t, 2, pl.ds(0, 1)])

    def take(index):
        return decode(line[index], line_units[index, pl.ds(0, 1)])

    def pack(t):
        codes, unit = encode(arrived[t, row])
        line_out[t] = codes
        units_out[t, 4, pl.ds(0, 1)] = unit

    def stage_four(t):
        target = goal(t)

        @pl.when((target >= z) & has_lower)
        def _():
            to_upper(t).wait_recv()
            arrived[t, row] += take(upper_index(t))

        @pl.when((target <= z) & has_upper)
        def _():
            to_lower(t).wait_recv()
            arrived[t, row] += take(lower_index(t))

        @pl.when(target != z)
        def _():
            pack(t)

        @pl.when(target > z)
        def _():
            to_upper(t).start()

        @pl.when(target < z)
        def _():
            to_lower(t).start()

        @pl.when(target == z)
        def _():
            out[span(t)] = arrived[t, row]

    lags = LAGS

    def body(i, carry):
        @pl.when(i + ahead < steps)
        def _():
            load(i + ahead).start()
            core(i + ahead).start()

        @pl.when(i < steps)
        def _():
            stage_one(i)

        for lag, stage in zip(lags, (stage_two, stage_three, stage_four)):
            @pl.when((i >= lag) & (i - lag < steps))
            def _():
                stage(i - lag)

        @pl.when(i == steps // 2)
        def _():
            total = small[me]
            for offset in range(1, devices):
                small_send(offset).wait_recv()
                total = total + box[offset]
            small_out[me] = total
            for offset in range(1, devices):
                small_back(offset).start()

        return carry

    lax.fori_loop(0, steps + lags[-1], body, 0)

    def finish(t, carry):
        core(t).wait_send()
        first_x(t).wait_send()
        first_y(t).wait_send()
        second_x(t).wait_send()
        second_y(t).wait_send()

        @pl.when(goal(t) > z)
        def _():
            to_upper(t).wait_send()

        @pl.when(goal(t) < z)
        def _():
            to_lower(t).wait_send()

        return carry

    lax.fori_loop(0, steps, finish, 0)
    for offset in range(1, devices):
        small_send(offset).wait_send()
        small_back(offset).wait_send()
        small_back_recv(offset).wait_recv()


def reduce_blocks(blob, small, depth, parts):
    cols, _, rows, lanes = blob.shape
    devices = 4 * cols
    chunk = rows // parts
    half = -(-chunk // 32) * 16
    rest = chunk - half
    steps = depth * parts
    lines = (depth + 1) * parts
    dma = pltpu.SemaphoreType.DMA
    vm = pltpu.VMEM
    return pl.pallas_call(
        functools.partial(reduce_kernel, depth, devices, cols, parts, chunk, half),
        out_shape=(
            jax.ShapeDtypeStruct((rows, lanes), high_type),
            jax.ShapeDtypeStruct(small.shape, high_type),
        ),
        in_specs=[pl.BlockSpec(memory_space=pltpu.HBM), pl.BlockSpec(memory_space=pltpu.VMEM)],
        out_specs=[pl.BlockSpec(memory_space=pltpu.VMEM)] * 2,
        scratch_shapes=[
            vm((steps, 4, chunk, lanes), high_type),
            vm((4, 4, chunk, lanes), high_type),
            vm((steps, 2, half, lanes), code_type),
            vm((steps, 2, rest, lanes), code_type),
            vm((steps, 2, half, lanes), code_type),
            vm((steps, 2, rest, lanes), code_type),
            vm((steps, rest, lanes), code_type),
            vm((steps, half, lanes), code_type),
            vm((steps, rest, lanes), code_type),
            vm((steps, half, lanes), code_type),
            vm((steps, chunk, lanes), code_type),
            vm((lines, chunk, lanes), code_type),
            vm((steps, 5, 8, lanes), high_type),
            vm((steps, 4, 8, lanes), high_type),
            vm((lines, 8, lanes), high_type),
            vm((devices,) + small.shape[1:], high_type),
            dma((4,)),
        ]
        + ([dma((steps,)) for _ in range(11)] + [dma((lines,))])
        + ([dma((steps,)) for _ in range(9)] + [dma((lines,))])
        + [dma((devices,)) for _ in range(4)],
        compiler_params=pltpu.CompilerParams(
            collective_id=1, has_side_effects=True, vmem_limit_bytes=62 << 20
        ),
        name="reduce_blocks",
    )(blob, small)


ENC_ROWS = 64
DEC_ROWS = 208
CLASS_ENC = KEEP
CLASS_DEC = PATCHES
NEGATIVE = -1e30


def nn(left, right):
    return jnp.dot(left, right, preferred_element_type=high_type)


def nt(left, right):
    return lax.dot_general(left, right, (((1,), (1,)), ((), ())), preferred_element_type=high_type)


def tn(left, right):
    return lax.dot_general(left, right, (((0,), (0,)), ((), ())), preferred_element_type=high_type)


def standard(rows):
    mean = jnp.mean(rows, -1, keepdims=True)
    centred = rows - mean
    spread = jnp.mean(centred * centred, -1, keepdims=True)
    rate = lax.rsqrt(spread + norm_eps)
    return centred * rate, rate


def standard_back(unit, rate, grad):
    return rate * (grad - jnp.mean(grad, -1, keepdims=True) - unit * jnp.mean(grad * unit, -1, keepdims=True))


def col_sum(rows):
    return jnp.sum(rows.astype(high_type), 0, keepdims=True)


def gelu_pair(value):
    size = jnp.abs(value)
    below = 1.0 + (0.3275911 * math.sqrt(0.5)) * size
    t = pl.reciprocal(below, approx=True)
    t = t * (2.0 - below * t)
    t = t * (2.0 - below * t)
    fall = jnp.exp(-0.5 * value * value)
    series = 1.061405429
    for item in (-1.453152027, 1.421413741, -0.284496736, 0.254829592):
        series = series * t + item
    tail = 0.5 * series * t * fall
    part = jnp.where(value < 0.0, tail, 1.0 - tail)
    return value * part, part + value * fall * (1.0 / math.sqrt(2.0 * math.pi))


def three_way(value):
    high = value.astype(low_type)
    rest = value - high.astype(high_type)
    middle = rest.astype(low_type)
    return high, middle, (rest - middle.astype(high_type)).astype(low_type)


def place_rows(picks, value):
    parts = three_way(value)
    return nn(picks, parts[0]) + nn(picks, parts[1]) + nn(picks, parts[2])


def stack_heads(value, heads):
    width = LANES // heads
    lane = lax.broadcasted_iota(jnp.int32, value.shape, 1) // width
    return jnp.concatenate([jnp.where(lane == head, value, jnp.zeros_like(value)) for head in range(heads)], 0)


def merge_heads(stacked, heads):
    rows = stacked.shape[0] // heads
    width = LANES // heads
    lane = lax.broadcasted_iota(jnp.int32, (rows, LANES), 1) // width
    merged = stacked[:rows]
    for head in range(1, heads):
        merged = jnp.where(lane == head, stacked[head * rows : (head + 1) * rows], merged)
    return merged


def attend(query, key, value, heads, length):
    scores = nt(stack_heads(query, heads), key)
    column = lax.broadcasted_iota(jnp.int32, scores.shape, 1)
    scores = jnp.where(column < length, scores, NEGATIVE)
    raised = jnp.exp(scores - jnp.max(scores, -1, keepdims=True))
    attention = (raised / jnp.sum(raised, -1, keepdims=True)).astype(low_type)
    return merge_heads(nn(attention, value), heads)


def attend_back(query, key, value, grad, heads, length):
    queries = stack_heads(query, heads)
    grads = stack_heads(grad, heads)
    scores = nt(key, queries)
    place = lax.broadcasted_iota(jnp.int32, scores.shape, 0)
    scores = jnp.where(place < length, scores, NEGATIVE)
    raised = jnp.exp(scores - jnp.max(scores, 0, keepdims=True))
    attention = raised * (1.0 / jnp.sum(raised, 0, keepdims=True))
    inner = nt(value, grads)
    grad_scores = (attention * (inner - jnp.sum(inner * attention, 0, keepdims=True))).astype(low_type)
    grad_value = nn(attention.astype(low_type), grads)
    grad_key = nn(grad_scores, queries)
    grad_query = merge_heads(tn(grad_scores, key), heads)
    return grad_query, grad_key, grad_value


def attend_back_many(batch, query, key, value, grad, heads, length):
    rows = query.shape[0] // batch
    spans = [slice(image * rows, (image + 1) * rows) for image in range(batch)]
    queries = [stack_heads(query[span], heads) for span in spans]
    grads = [stack_heads(grad[span], heads) for span in spans]
    scores = jnp.concatenate([nt(key[span], item) for span, item in zip(spans, queries)], 0)
    inner = jnp.concatenate([nt(value[span], item) for span, item in zip(spans, grads)], 0)
    scores = scores.reshape(batch, rows, scores.shape[1])
    inner = inner.reshape(batch, rows, inner.shape[1])
    place = lax.broadcasted_iota(jnp.int32, scores.shape, 1)
    scores = jnp.where(place < length, scores, NEGATIVE)
    raised = jnp.exp(scores - jnp.max(scores, 1, keepdims=True))
    attention = raised * (1.0 / jnp.sum(raised, 1, keepdims=True))
    grad_scores = (attention * (inner - jnp.sum(inner * attention, 1, keepdims=True))).astype(low_type)
    attention = attention.astype(low_type)
    grad_value = [nn(attention[image], grads[image]) for image in range(batch)]
    grad_key = [nn(grad_scores[image], queries[image]) for image in range(batch)]
    grad_query = [merge_heads(tn(grad_scores[image], key[spans[image]]), heads) for image in range(batch)]
    return tuple(jnp.concatenate(item, 0) for item in (grad_query, grad_key, grad_value))


def wide_kernel(blocks, wide):
    count, _, width = blocks.shape
    for index in range(count):
        wide[:, index * width : (index + 1) * width] = blocks[index]


def enc_embed(batch, pick, patches, wide, vec, pos, kept, start):
    rows = ENC_ROWS
    for image in range(batch):
        span = pl.ds(image * rows, rows)
        kept[span] = nn(pick[image], patches[image]).astype(low_type)
    start[...] = nn(kept[...], wide[:, :D]) + vec[0:1]
    parts = three_way(pos[...])
    for image in range(batch):
        span = pl.ds(image * rows, rows)
        picks = pick[image]
        placed = nn(picks, parts[0]) + nn(picks, parts[1]) + nn(picks, parts[2])
        inner = lax.broadcasted_iota(jnp.int32, placed.shape, 0)
        start[span] = jnp.where(inner == CLASS_ENC, vec[1:2], start[span] + placed)


def enc_project(wide, vec, start, normed, qkv):
    unit, _ = standard(start[...])
    normed[...] = (unit * vec[2:3] + vec[3:4]).astype(low_type)
    scale = 1.0 / math.sqrt(D // HE)
    rows_in = normed[...]
    qkv[:, :D] = ((nn(rows_in, wide[:, D : 2 * D]) + vec[4:5]) * scale).astype(low_type)
    qkv[:, D : 2 * D] = nn(rows_in, wide[:, 2 * D : 3 * D]).astype(low_type)
    qkv[:, 2 * D :] = (nn(rows_in, wide[:, 3 * D : 4 * D]) + vec[5:6]).astype(low_type)


def enc_mix(batch, qkv, mixed):
    rows = ENC_ROWS
    heads = LANES * HE // D
    for image in range(batch):
        span = pl.ds(image * rows, rows)
        for group in range(D // LANES):
            lane = group * LANES
            mixed[span, lane : lane + LANES] = attend(
                qkv[span, lane : lane + LANES],
                qkv[span, D + lane : D + lane + LANES],
                qkv[span, 2 * D + lane : 2 * D + lane + LANES],
                heads,
                KEEP + 1,
            ).astype(low_type)


def enc_join(wide, vec, start, mixed, middle, normed_two):
    middle[...] = start[...] + (nn(mixed[...], wide[:, 4 * D :]) + vec[6:7])
    unit, _ = standard(middle[...])
    normed_two[...] = (unit * vec[7:8] + vec[8:9]).astype(low_type)


def enc_attend_kernel(batch, pick, patches, wide, vec, pos, kept, start, normed, qkv, mixed, middle, normed_two):
    enc_embed(batch, pick, patches, wide, vec, pos, kept, start)
    enc_project(wide, vec, start, normed, qkv)
    enc_mix(batch, qkv, mixed)
    enc_join(wide, vec, start, mixed, middle, normed_two)


def enc_ffn_kernel(last, middle, normed_two, ffn, vec, up_bias, slope, active, output, latent):
    step = pl.program_id(0)

    @pl.when(step == 0)
    def _():
        output[...] = middle[...] + vec[9:10]

    value, gain = gelu_pair(nn(normed_two[...], ffn[0]) + up_bias[...])
    slope[...] = gain
    value = value.astype(low_type)
    active[...] = value
    output[...] += nt(value, ffn[1])

    @pl.when(step == last)
    def _():
        unit, _ = standard(output[...])
        latent[...] = (unit * vec[10:11] + vec[11:12]).astype(low_type)


def dec_attend_kernel(latent, proj, picked, pos, wide, vec, start, normed, qkv, mixed, middle, normed_two):
    picks = picked[0]
    kept = jnp.sum(picks.astype(high_type), 1, keepdims=True)
    entry = nn(latent[...], proj[...]) + vec[0:1]
    rows = place_rows(picks, entry) + (1.0 - kept) * vec[1:2] + pos[...]
    start[...] = rows
    unit, _ = standard(rows)
    rows_in = (unit * vec[2:3] + vec[3:4]).astype(low_type)
    normed[...] = rows_in
    scale = 1.0 / math.sqrt(E // HD)
    qkv[:, :E] = ((nn(rows_in, wide[0, :, :E]) + vec[4:5]) * scale).astype(low_type)
    qkv[:, E : 2 * E] = nn(rows_in, wide[0, :, E : 2 * E]).astype(low_type)
    qkv[:, 2 * E :] = (nn(rows_in, wide[0, :, 2 * E : 3 * E]) + vec[5:6]).astype(low_type)
    heads = LANES * HD // E
    for group in range(E // LANES):
        lane = group * LANES
        mixed[:, lane : lane + LANES] = attend(
            qkv[:, lane : lane + LANES],
            qkv[:, E + lane : E + lane + LANES],
            qkv[:, 2 * E + lane : 2 * E + lane + LANES],
            heads,
            PATCHES + 1,
        ).astype(low_type)
    total = rows + (nn(mixed[...], wide[0, :, 3 * E :]) + vec[6:7])
    middle[...] = total
    unit, _ = standard(total)
    normed_two[...] = (unit * vec[7:8] + vec[8:9]).astype(low_type)


def send_tiles(acc, blob, sem, tiles, rows, per_block, base, stride):
    def go(index, carry):
        tile, part = index // 4, index % 4
        block, inner = tile // per_block, tile % per_block
        pltpu.make_async_copy(
            acc.at[tile, pl.ds(pl.multiple_of(part * rows, 16), rows)],
            blob.at[block, part, pl.ds(pl.multiple_of(base + inner * stride, 16), rows)],
            sem,
        ).start()
        return carry

    lax.fori_loop(0, tiles * 4, go, 0)


def wait_tiles(acc, sem):
    pltpu.make_async_copy(acc, acc, sem).wait()


def dec_ffn_kernel(images, last, count, middle, normed_two, mixed, pixels, picked, weights, head, vec, up_bias, head_bias,
                   grad_middle, grad_mixed, grad_head, vec_grad, up_grad, bias_grad, loss, blob,
                   active, slope, acc_up, acc_down, acc_out, sems):
    step = pl.program_id(0)
    source = normed_two[...]
    rows = source.shape[0]

    @pl.when(step == 0)
    def _():
        grad_head[...] = jnp.zeros_like(grad_head)
        vec_grad[...] = jnp.zeros_like(vec_grad)
        up_grad[...] = jnp.zeros_like(up_grad)
        bias_grad[...] = jnp.zeros_like(bias_grad)
        loss[...] = jnp.zeros_like(loss)
        acc_up[...] = jnp.zeros_like(acc_up)
        acc_down[...] = jnp.zeros_like(acc_down)
        acc_out[...] = jnp.zeros_like(acc_out)

    wide = 512
    total = middle[...] + vec[9:10]
    for place in range(0, H, wide):
        span = slice(place, place + wide)
        value, gain = gelu_pair(nn(source, weights[1, :, span]) + up_bias[:, span])
        slope[:, span] = gain
        value = value.astype(low_type)
        active[:, span] = value
        total = total + nt(value, weights[2, :, span])
    unit, rate = standard(total)
    final = (unit * vec[10:11] + vec[11:12]).astype(low_type)
    predict = nn(final, head[...]) + head_bias[...]
    target, _ = standard(pixels[...].astype(high_type))
    kept = jnp.concatenate([jnp.sum(picked[image].astype(high_type), 1, keepdims=True) for image in range(images)], 0)
    inner = lax.broadcasted_iota(jnp.int32, (rows, 1), 0) % DEC_ROWS
    masked = jnp.where(inner < PATCHES, 1.0 - kept, 0.0)
    error = predict - target
    loss[...] += jnp.sum(masked * error * error)
    grad_predict = (2.0 * masked * error / count).astype(low_type)
    grad_head[...] += tn(final, grad_predict)
    bias_grad[...] += col_sum(grad_predict)
    grad_final = nt(grad_predict, head[...])
    vec_grad[10:11] += col_sum(grad_final * unit)
    vec_grad[11:12] += col_sum(grad_final)
    grad_out = standard_back(unit, rate, grad_final * vec[10:11])
    grad_down = grad_out.astype(low_type)
    vec_grad[9:10] += col_sum(grad_down)
    grad_source = jnp.zeros_like(total)
    for place in range(0, H, wide):
        span = slice(place, place + wide)
        grad_up = (slope[:, span] * nn(grad_down, weights[2, :, span])).astype(low_type)
        up_grad[:, span] += col_sum(grad_up)
        grad_source = grad_source + nt(grad_up, weights[1, :, span])
        piece = tn(grad_down, active[:, span])
        other = tn(source, grad_up)
        for tile in range(wide // LANES):
            lane = slice(tile * LANES, (tile + 1) * LANES)
            acc_down[place // LANES + tile] += piece[:, lane]
            acc_up[place // LANES + tile] += other[:, lane]
    unit, rate = standard(middle[...])
    vec_grad[7:8] += col_sum(grad_source * unit)
    vec_grad[8:9] += col_sum(grad_source)
    grad_rows = standard_back(unit, rate, grad_source * vec[7:8]) + grad_out
    grad_middle[...] = grad_rows
    branch = grad_rows.astype(low_type)
    vec_grad[6:7] += col_sum(branch)
    piece = tn(mixed[...], branch)
    for tile in range(E // LANES):
        acc_out[tile] += piece[:, tile * LANES : (tile + 1) * LANES]
    grad_mixed[...] = nt(branch, weights[0, :, 3 * E :]).astype(low_type)

    @pl.when(step == last)
    def _():
        rows_block = E // 4
        send_tiles(acc_up, blob, sems.at[0], H // LANES, rows_block, 2, 2176, rows_block)
        send_tiles(acc_down, blob, sems.at[1], H // LANES, rows_block, 2, 2432, rows_block)
        send_tiles(acc_out, blob.at[pl.ds(6, 2)], sems.at[2], E // LANES, rows_block, 2, 1920, rows_block)
        wait_tiles(acc_up, sems.at[0])
        wait_tiles(acc_down, sems.at[1])
        wait_tiles(acc_out, sems.at[2])


def dec_back_kernel(last, blob_in, qkv, normed, start, grad_middle, grad_mixed, pick, picked, weights, vec,
                    grad_entry, vec_grad, blob, grads, acc, sem):
    step = pl.program_id(0)

    @pl.when(step == 0)
    def _():
        vec_grad[...] = jnp.zeros_like(vec_grad)
        acc[...] = jnp.zeros_like(acc)

    scale = 1.0 / math.sqrt(E // HD)
    heads = LANES * HD // E
    for group in range(E // LANES):
        lane = group * LANES
        span = slice(lane, lane + LANES)
        query, key, value = attend_back(
            qkv[:, lane : lane + LANES],
            qkv[:, E + lane : E + lane + LANES],
            qkv[:, 2 * E + lane : 2 * E + lane + LANES],
            grad_mixed[:, span],
            heads,
            PATCHES + 1,
        )
        grads[:, span] = (query * scale).astype(low_type)
        grads[:, E + lane : E + lane + LANES] = key.astype(low_type)
        grads[:, 2 * E + lane : 2 * E + lane + LANES] = value.astype(low_type)
    vec_grad[4:5] += col_sum(grads[:, :E])
    vec_grad[5:6] += col_sum(grads[:, 2 * E :])
    rows = normed[...]
    for part in range(3):
        piece = tn(rows, grads[:, part * E : (part + 1) * E])
        for tile in range(E // LANES):
            acc[part * (E // LANES) + tile] += piece[:, tile * LANES : (tile + 1) * LANES]
    grad_normed = nt(grads[...], weights[0, :, : 3 * E])
    unit, rate = standard(start[...])
    vec_grad[2:3] += col_sum(grad_normed * unit)
    vec_grad[3:4] += col_sum(grad_normed)
    grad_rows = standard_back(unit, rate, grad_normed * vec[2:3]) + grad_middle[...]
    kept = jnp.sum(picked[0].astype(high_type), 1, keepdims=True)
    vec_grad[1:2] += col_sum((1.0 - kept) * grad_rows)
    grad_entry[...] = nn(pick[0], grad_rows.astype(low_type)).astype(low_type)

    @pl.when(step == last)
    def _():
        rows_block = E // 4
        send_tiles(acc, blob, sem, 3 * E // LANES, rows_block, 2, 1920, rows_block)
        wait_tiles(acc, sem)


def enc_ffn_back_kernel(last, blob_in, grad_entry, latent, output, middle, normed_two, slope, active, ffn, proj, vec,
                        grad_middle, vec_grad, up_grad, entry_grad, blob,
                        grad_out, grad_down, grad_source, folded, acc_up, acc_down, fold_sem, sems):
    step = pl.program_id(0)
    fold_copy = pltpu.make_async_copy(folded, blob.at[:, :, pl.ds(2688, 96)], fold_sem)
    part_rows = D // 4

    @pl.when(step == 0)
    def _():
        vec_grad[...] = jnp.zeros_like(vec_grad)
        entries = grad_entry[...]
        entry_grad[...] = col_sum(entries)
        grad_proj = tn(latent[...], entries)
        lane = lax.broadcasted_iota(jnp.int32, (96, LANES), 1)
        for part in range(4):
            for pair in range(4):
                first = grad_proj[part * 192 : part * 192 + 96, pair * LANES : (pair + 1) * LANES]
                second = grad_proj[part * 192 + 96 : part * 192 + 192, pair * LANES : (pair + 1) * LANES]
                folded[2 * pair, part] = jnp.where(lane < 64, first, pltpu.roll(second, 64, 1))
                folded[2 * pair + 1, part] = jnp.where(lane < 64, pltpu.roll(first, 64, 1), second)
        fold_copy.start()
        grad_latent = nt(entries, proj[...])
        unit, rate = standard(output[...])
        vec_grad[10:11] = col_sum(grad_latent * unit)
        vec_grad[11:12] = col_sum(grad_latent)
        rows = standard_back(unit, rate, grad_latent * vec[10:11])
        grad_out[...] = rows
        grad_down[...] = rows.astype(low_type)
        vec_grad[9:10] = col_sum(rows.astype(low_type))
        grad_source[...] = jnp.zeros_like(grad_source)

    slot = step % 2

    @pl.when(step >= 2)
    def _():
        wait_tiles(acc_up.at[slot], sems.at[0, slot])
        wait_tiles(acc_down.at[slot], sems.at[1, slot])

    grads = grad_down[...]
    grad_up = (slope[...] * nn(grads, ffn[1])).astype(low_type)
    up_grad[...] = col_sum(grad_up)
    grad_source[...] += nt(grad_up, ffn[0])
    piece = tn(grads, active[...])
    other = tn(normed_two[...], grad_up)
    count = grad_up.shape[1] // LANES
    for tile in range(count):
        lane = slice(tile * LANES, (tile + 1) * LANES)
        acc_down[slot, tile] = piece[:, lane]
        acc_up[slot, tile] = other[:, lane]

    def go(index, carry):
        tile, part = index // 4, index % 4
        place = step * count + tile
        block, inner = place // 3, place % 3
        rows = pl.ds(pl.multiple_of(part * part_rows, 16), part_rows)
        for number, (acc, base) in enumerate(((acc_up, 768), (acc_down, 1344))):
            pltpu.make_async_copy(
                acc.at[slot, tile, rows],
                blob.at[block, part, pl.ds(pl.multiple_of(base + inner * part_rows, 16), part_rows)],
                sems.at[number, slot],
            ).start()
        return carry

    lax.fori_loop(0, count * 4, go, 0)

    @pl.when(step == last)
    def _():
        unit, rate = standard(middle[...])
        vec_grad[7:8] = col_sum(grad_source[...] * unit)
        vec_grad[8:9] = col_sum(grad_source[...])
        grad_rows = standard_back(unit, rate, grad_source[...] * vec[7:8]) + grad_out[...]
        grad_middle[...] = grad_rows
        vec_grad[6:7] = col_sum(grad_rows.astype(low_type))
        fold_copy.wait()
        for item in (0, 1):
            wait_tiles(acc_up.at[item], sems.at[0, item])
            wait_tiles(acc_down.at[item], sems.at[1, item])


def enc_back_kernel(batch, blob_in, qkv, kept, normed, start, mixed, grad_middle, wide, vec,
                    vec_grad, blob, grads, grad_wide, tiles, sem):
    rows = ENC_ROWS
    vec_grad[...] = jnp.zeros_like(vec_grad)
    branch = grad_middle[...].astype(low_type)
    grad_mixed = nt(branch, wide[:, 4 * D :]).astype(low_type)
    grad_wide[:, 4 * D :] = tn(mixed[...], branch)
    scale = 1.0 / math.sqrt(D // HE)
    heads = LANES * HE // D
    for group in range(D // LANES):
        lane = group * LANES
        query, key, value = attend_back_many(
            batch,
            qkv[:, lane : lane + LANES],
            qkv[:, D + lane : D + lane + LANES],
            qkv[:, 2 * D + lane : 2 * D + lane + LANES],
            grad_mixed[:, lane : lane + LANES],
            heads,
            KEEP + 1,
        )
        grads[:, lane : lane + LANES] = (query * scale).astype(low_type)
        grads[:, D + lane : D + lane + LANES] = key.astype(low_type)
        grads[:, 2 * D + lane : 2 * D + lane + LANES] = value.astype(low_type)
    vec_grad[4:5] = col_sum(grads[:, :D])
    vec_grad[5:6] = col_sum(grads[:, 2 * D :])
    rows_in = normed[...]
    for part in range(3):
        grad_wide[:, (part + 1) * D : (part + 2) * D] = tn(rows_in, grads[:, part * D : (part + 1) * D])
    width = 5 * D // 8
    tall = D // 4

    def assemble(block):
        for part in range(4):
            span = slice(part * tall, (part + 1) * tall)
            piece = grad_wide[span, block * width : (block + 1) * width]
            for tile in range(4):
                size = min(LANES, width - tile * LANES)
                value = piece[:, tile * LANES : tile * LANES + size]
                if size < LANES:
                    value = jnp.concatenate([value, jnp.zeros((tall, LANES - size), high_type)], 1)
                tiles[block, part, tile * tall : (tile + 1) * tall] = value
        pltpu.make_async_copy(tiles.at[block], blob.at[block, :, pl.ds(0, 4 * tall)], sem).start()

    for block in range(2, 8):
        assemble(block)
    grad_normed = nt(grads[...], wide[:, D : 4 * D])
    unit, rate = standard(start[...])
    vec_grad[2:3] = col_sum(grad_normed * unit)
    vec_grad[3:4] = col_sum(grad_normed)
    grad_rows = standard_back(unit, rate, grad_normed * vec[2:3]) + grad_middle[...]
    inner = lax.broadcasted_iota(jnp.int32, (grad_rows.shape[0], 1), 0) % rows
    vec_grad[1:2] = col_sum(jnp.where(inner == CLASS_ENC, grad_rows, 0.0))
    embed = jnp.where(inner < KEEP, grad_rows, 0.0).astype(low_type)
    vec_grad[0:1] = col_sum(embed)
    grad_wide[:, :D] = tn(kept[...], embed)
    assemble(0)
    assemble(1)
    wait_tiles(tiles, sem)


def adam_parts(weight, grad, first, second, decay):
    first_new = 0.5 * first + 0.5 * grad
    second_new = 0.5 * second + 0.5 * grad * grad
    bias = 1.0 - 0.5**STEP
    direction = first_new / bias / (jnp.sqrt(second_new / bias) + 1e-08)
    return weight - 0.02 * (direction + decay * weight), first_new, second_new


def adam_kernel(count, *refs):
    summed, head, small = refs[:3]
    ins, outs, loss = refs[3:24], refs[24:45], refs[45]

    def update(index, place, grad, decay=0.05):
        for target, value in zip(
            range(3), adam_parts(ins[index][place], grad, ins[7 + index][place], ins[14 + index][place], decay)
        ):
            outs[7 * target + index][place] = value

    base = 0
    for index, lead, tall, width in ((0, None, 192, 480), (1, 0, 192, 384), (1, 1, 192, 384),
                                     (3, None, 128, 256), (4, 0, 128, 256), (4, 1, 128, 256)):
        for lane in range(0, width, LANES):
            size = min(LANES, width - lane)
            place = (slice(None), slice(lane, lane + size))
            update(index, place if lead is None else (lead,) + place, summed[base : base + tall, :size])
            base += tall
    folded = summed[base : base + 96]
    turned = jnp.concatenate([folded, jnp.zeros((32, LANES), high_type)], 0).T
    update(2, (slice(None), slice(0, 96)), turned[:64, :96])
    update(2, (slice(None), slice(96, 192)), turned[64:, :96])
    update(5, (slice(None),), head[...])
    tall = ins[6].shape[0]
    update(6, (slice(None),), small[:tall], 0.0)
    loss[...] = small[tall : tall + 1, :1] / count


SMALL_ROWS = 256
SMALL_PARTS = ((12, D), (1, F), (12, E), (1, H), (1, P_SIZE))


def prepare_kernel(enc_w, enc_ffn, proj_turned, dec_w, dec_ffn, head, smalls, shuffle, patches,
                   own_enc, own_ffn, own_proj, own_dec, head_low, enc_vec, enc_up, dec_vec, dec_up, head_bias,
                   pick, picked, padded):
    own_enc[...] = enc_w[...].astype(low_type)
    own_ffn[...] = enc_ffn[...].astype(low_type)
    own_proj[...] = proj_turned[...].T.astype(low_type)
    own_dec[0] = dec_w[...].astype(low_type)
    own_dec[1] = dec_ffn[0].astype(low_type)
    own_dec[2] = dec_ffn[1].astype(low_type)
    head_low[...] = head[...].astype(low_type)
    place = 0
    for target in (enc_vec, enc_up, dec_vec, dec_up, head_bias):
        for index in range(target.shape[0]):
            for lane in range(0, target.shape[1], LANES):
                target[index : index + 1, lane : lane + LANES] = smalls[place : place + 1]
                place += 1
    slot = lax.broadcasted_iota(jnp.int32, (DEC_ROWS, ENC_ROWS), 0)
    order = lax.broadcasted_iota(jnp.int32, (DEC_ROWS, ENC_ROWS), 1)
    for image in range(patches.shape[0]):
        keep = jnp.where(order < KEEP, shuffle[image : image + 1, :ENC_ROWS], jnp.where(order == CLASS_ENC, CLASS_DEC, -1))
        chosen = jnp.where(keep == slot, 1.0, 0.0)
        picked[image] = chosen.astype(low_type)
        pick[image] = chosen.T.astype(low_type)
        padded[image, DEC_ROWS - 16 :] = jnp.zeros((16, P_SIZE), low_type)
        padded[image, :PATCHES] = patches[image]


def prepare(enc_w, enc_ffn, dec_proj, dec_w, dec_ffn, head, smalls, shuffle, patches):
    batch = patches.shape[0]
    shape = jax.ShapeDtypeStruct
    outs = [shape(item.shape, low_type) for item in (enc_w, enc_ffn, dec_proj)]
    outs += [shape((3,) + dec_w.shape, low_type), shape(head.shape, low_type)]
    outs += [shape(item, high_type) for item in SMALL_PARTS]
    outs += [
        shape((batch, ENC_ROWS, DEC_ROWS), low_type),
        shape((batch, DEC_ROWS, ENC_ROWS), low_type),
        shape((batch, DEC_ROWS, P_SIZE), low_type),
    ]
    return pl.pallas_call(
        prepare_kernel,
        out_shape=tuple(outs),
        in_specs=[whole()] * 9,
        out_specs=[whole()] * 13,
        compiler_params=params(),
        name="prepare",
    )(enc_w, enc_ffn, dec_proj.T, dec_w, dec_ffn, head, smalls.reshape(-1, LANES), shuffle, patches)


def pack_kernel(enc_one, enc_two, enc_up, dec_one, dec_two, entry, dec_up, head_bias, loss, small):
    place = 0

    def put(value):
        nonlocal place
        for index in range(value.shape[0]):
            for lane in range(0, value.shape[1], LANES):
                small[place : place + 1] = value[index : index + 1, lane : lane + LANES]
                place += 1

    put(enc_one[...] + enc_two[...])
    put(enc_up[...])
    put(entry[...])
    put(dec_one[1:] + dec_two[1:])
    put(dec_up[...])
    put(head_bias[...])
    small[place : place + 1] = loss[:1]
    place += 1
    small[place:] = jnp.zeros((SMALL_ROWS - place, LANES), high_type)


def table_of(width, rows):
    quarter = width // 4
    omega = (np.float32(1.0) / np.float32(10000.0) ** (np.arange(quarter, dtype=np.float32) / np.float32(quarter))).astype(np.float32)
    coord = np.arange(SIDE * SIDE)

    def half(place):
        angle = place.astype(np.float32)[:, None] * omega[None, :]
        return np.concatenate([np.sin(angle), np.cos(angle)], 1)

    table = np.concatenate([half(coord // SIDE), half(coord % SIDE)], 1).astype(np.float32)
    return np.concatenate([table, np.zeros((rows - table.shape[0], width), np.float32)], 0)


def whole():
    return pl.BlockSpec(memory_space=pltpu.VMEM)


def hbm():
    return pl.BlockSpec(memory_space=pltpu.HBM)


def params(**more):
    return pltpu.CompilerParams(vmem_limit_bytes=60 << 20, **more)


def by_image(*block):
    return pl.BlockSpec(block, lambda i: (i,) + (0,) * (len(block) - 1))


def fixed(*block):
    return pl.BlockSpec(block, lambda i: (0,) * len(block))


def encoder_shapes(batch):
    rows = batch * ENC_ROWS
    shape = jax.ShapeDtypeStruct
    first = (
        shape((rows, D), low_type),
        shape((rows, D), high_type),
        shape((rows, D), low_type),
        shape((rows, 3 * D), low_type),
        shape((rows, D), low_type),
        shape((rows, D), high_type),
        shape((rows, D), low_type),
    )
    second = (
        shape((rows, F), high_type),
        shape((rows, F), low_type),
        shape((rows, D), high_type),
        shape((rows, D), low_type),
    )
    return first, second


def encode_images(enc_blocks, enc_ffn, enc_vec, enc_up, pick, padded):
    batch = padded.shape[0]
    rows = batch * ENC_ROWS
    first, second = encoder_shapes(batch)
    wide = pl.pallas_call(
        wide_kernel,
        out_shape=jax.ShapeDtypeStruct((D, 5 * D), low_type),
        in_specs=[whole()],
        out_specs=whole(),
        compiler_params=params(),
        name="wide",
    )(enc_blocks)
    early = pl.pallas_call(
        functools.partial(enc_attend_kernel, batch),
        out_shape=first,
        in_specs=[whole()] * 5,
        out_specs=[whole()] * 7,
        compiler_params=params(),
        name="enc_attend",
    )(pick, padded, wide, enc_vec, jnp.asarray(table_of(D, DEC_ROWS)))
    chunk = 512
    late = pl.pallas_call(
        functools.partial(enc_ffn_kernel, F // chunk - 1),
        grid=(F // chunk,),
        out_shape=second,
        in_specs=[
            fixed(rows, D),
            fixed(rows, D),
            pl.BlockSpec((2, D, chunk), lambda i: (0, 0, i)),
            fixed(12, D),
            pl.BlockSpec((1, chunk), lambda i: (0, i)),
        ],
        out_specs=[
            pl.BlockSpec((rows, chunk), lambda i: (0, i)),
            pl.BlockSpec((rows, chunk), lambda i: (0, i)),
            fixed(rows, D),
            fixed(rows, D),
        ],
        compiler_params=params(),
        name="enc_ffn",
    )(early[5], early[6], enc_ffn, enc_vec, enc_up)
    return wide, early + tuple(late)


def local_grads(wide, enc_ffn, proj, dec3, encoded, head_low, vectors, pick, picked, padded, count):
    enc_vec, _, dec_vec, dec_up, head_bias = vectors
    kept, start, normed, qkv, mixed, middle, normed_two, slope, active, enc_out, latent = encoded
    batch = padded.shape[0]
    shape = jax.ShapeDtypeStruct
    dec_pos = jnp.asarray(table_of(E, DEC_ROWS))
    rows, dec_rows = batch * ENC_ROWS, batch * DEC_ROWS
    chunk = 512

    dec_start, dec_normed, dec_qkv, dec_mixed, dec_middle, dec_normed_two = pl.pallas_call(
        dec_attend_kernel,
        grid=(batch,),
        out_shape=(
            shape((dec_rows, E), high_type),
            shape((dec_rows, E), low_type),
            shape((dec_rows, 3 * E), low_type),
            shape((dec_rows, E), low_type),
            shape((dec_rows, E), high_type),
            shape((dec_rows, E), low_type),
        ),
        in_specs=[
            by_image(ENC_ROWS, D),
            fixed(D, E),
            by_image(1, DEC_ROWS, ENC_ROWS),
            fixed(DEC_ROWS, E),
            fixed(1, E, 4 * E),
            fixed(12, E),
        ],
        out_specs=[
            by_image(DEC_ROWS, E),
            by_image(DEC_ROWS, E),
            by_image(DEC_ROWS, 3 * E),
            by_image(DEC_ROWS, E),
            by_image(DEC_ROWS, E),
            by_image(DEC_ROWS, E),
        ],
        compiler_params=params(),
        name="dec_attend",
    )(latent, proj, picked, dec_pos, dec3, dec_vec)

    images = 2 if batch % 2 == 0 else 1
    block = images * DEC_ROWS
    blob_shape = shape((8, 4, 2784, LANES), high_type)
    vm = pltpu.VMEM
    dma = pltpu.SemaphoreType.DMA
    grad_middle, grad_mixed, grad_head, dec_grad_one, dec_up_grad, head_bias_grad, loss, blob = pl.pallas_call(
        functools.partial(dec_ffn_kernel, images, batch // images - 1, count),
        grid=(batch // images,),
        out_shape=(
            shape((dec_rows, E), high_type),
            shape((dec_rows, E), low_type),
            shape((E, P_SIZE), high_type),
            shape((12, E), high_type),
            shape((1, H), high_type),
            shape((1, P_SIZE), high_type),
            shape((8, LANES), high_type),
            blob_shape,
        ),
        in_specs=[
            by_image(block, E),
            by_image(block, E),
            by_image(block, E),
            by_image(block, P_SIZE),
            by_image(images, DEC_ROWS, ENC_ROWS),
            fixed(3, E, H),
            fixed(E, P_SIZE),
            fixed(12, E),
            fixed(1, H),
            fixed(1, P_SIZE),
        ],
        out_specs=[
            by_image(block, E),
            by_image(block, E),
            fixed(E, P_SIZE),
            fixed(12, E),
            fixed(1, H),
            fixed(1, P_SIZE),
            fixed(8, LANES),
            hbm(),
        ],
        scratch_shapes=[
            vm((block, H), low_type),
            vm((block, H), high_type),
            vm((H // LANES, E, LANES), high_type),
            vm((H // LANES, E, LANES), high_type),
            vm((E // LANES, E, LANES), high_type),
            dma((3,)),
        ],
        compiler_params=params(),
        name="dec_ffn",
    )(dec_middle, dec_normed_two, dec_mixed, padded.reshape(dec_rows, P_SIZE), picked, dec3, head_low, dec_vec, dec_up, head_bias)

    grad_entry, dec_grad_two, blob = pl.pallas_call(
        functools.partial(dec_back_kernel, batch - 1),
        grid=(batch,),
        out_shape=(shape((rows, E), low_type), shape((12, E), high_type), blob_shape),
        in_specs=[
            hbm(),
            by_image(DEC_ROWS, 3 * E),
            by_image(DEC_ROWS, E),
            by_image(DEC_ROWS, E),
            by_image(DEC_ROWS, E),
            by_image(DEC_ROWS, E),
            by_image(1, ENC_ROWS, DEC_ROWS),
            by_image(1, DEC_ROWS, ENC_ROWS),
            fixed(1, E, 4 * E),
            fixed(12, E),
        ],
        out_specs=[by_image(ENC_ROWS, E), fixed(12, E), hbm()],
        scratch_shapes=[vm((DEC_ROWS, 3 * E), low_type), vm((3 * E // LANES, E, LANES), high_type), dma],
        input_output_aliases={0: 2},
        compiler_params=params(),
        name="dec_back",
    )(blob, dec_qkv, dec_normed, dec_start, grad_middle, grad_mixed, pick, picked, dec3, dec_vec)

    enc_grad_middle, enc_grad_one, enc_up_grad, entry_grad, blob = pl.pallas_call(
        functools.partial(enc_ffn_back_kernel, F // chunk - 1),
        grid=(F // chunk,),
        out_shape=(
            shape((rows, D), high_type),
            shape((12, D), high_type),
            shape((1, F), high_type),
            shape((1, E), high_type),
            blob_shape,
        ),
        in_specs=[
            hbm(),
            fixed(rows, E),
            fixed(rows, D),
            fixed(rows, D),
            fixed(rows, D),
            fixed(rows, D),
            pl.BlockSpec((rows, chunk), lambda i: (0, i)),
            pl.BlockSpec((rows, chunk), lambda i: (0, i)),
            pl.BlockSpec((2, D, chunk), lambda i: (0, 0, i)),
            fixed(D, E),
            fixed(12, D),
        ],
        out_specs=[
            fixed(rows, D),
            fixed(12, D),
            pl.BlockSpec((1, chunk), lambda i: (0, i)),
            fixed(1, E),
            hbm(),
        ],
        scratch_shapes=[
            vm((rows, D), high_type),
            vm((rows, D), low_type),
            vm((rows, D), high_type),
            vm((8, 4, 96, LANES), high_type),
            vm((2, chunk // LANES, D, LANES), high_type),
            vm((2, chunk // LANES, D, LANES), high_type),
            dma,
            dma((2, 2)),
        ],
        input_output_aliases={0: 4},
        compiler_params=params(),
        name="enc_ffn_back",
    )(blob, grad_entry, latent, enc_out, middle, normed_two, slope, active, enc_ffn, proj, enc_vec)
    enc_grad_two, blob = pl.pallas_call(
        functools.partial(enc_back_kernel, batch),
        out_shape=(shape((12, D), high_type), blob_shape),
        in_specs=[hbm()] + [whole()] * 8,
        out_specs=[whole(), hbm()],
        scratch_shapes=[
            vm((rows, 3 * D), low_type),
            vm((D, 5 * D), high_type),
            vm((8, 4, D, LANES), high_type),
            dma,
        ],
        input_output_aliases={0: 1},
        compiler_params=params(),
        name="enc_back",
    )(blob, qkv, kept, normed, start, mixed, enc_grad_middle, wide, enc_vec)
    small = pl.pallas_call(
        pack_kernel,
        out_shape=shape((SMALL_ROWS, LANES), high_type),
        in_specs=[whole()] * 9,
        out_specs=whole(),
        compiler_params=params(),
        name="pack",
    )(enc_grad_one, enc_grad_two, enc_up_grad, dec_grad_one, dec_grad_two, entry_grad, dec_up_grad, head_bias_grad, loss)
    return blob, grad_head, small


def untile(block, rows, width):
    tiles = -(-width // LANES)
    return block.reshape(tiles, rows, LANES).transpose(1, 0, 2).reshape(rows, tiles * LANES)[:, :width]


def unfold_proj(block):
    width = block.shape[1] // 2
    return jnp.concatenate([block[:, :width], block[:, width:]], 0)


def unpack_shards(blob):
    cuts = [0, 768, 576, 576, 256, 256, 256, 96]
    places = [sum(cuts[: index + 1]) for index in range(len(cuts))]
    piece = [blob[places[index] : places[index + 1]] for index in range(7)]
    return (
        untile(piece[0], 192, 480),
        jnp.stack([untile(piece[1], 192, 384), untile(piece[2], 192, 384)]),
        unfold_proj(piece[6]),
        untile(piece[3], 128, 256),
        jnp.stack([untile(piece[4], 128, 256), untile(piece[5], 128, 256)]),
    )


def whole_arrays(blob):
    col_size, row_size = blob.shape[:2]
    parts = jax.vmap(jax.vmap(unpack_shards))(blob)

    def joined(array):
        if array.ndim == 4:
            return array.transpose(1, 2, 0, 3).reshape(row_size * array.shape[2], col_size * array.shape[3])
        return array.transpose(2, 1, 3, 0, 4).reshape(2, row_size * array.shape[3], col_size * array.shape[4])

    return tuple(joined(item) for item in parts)


def on_small_plane():
    return lax.axis_size("row") == 4 and lax.axis_size("col") == 8


def gather_and_encode(shards, enc_vec, enc_up, pick, padded):
    if on_small_plane():
        ffn, proj, dec, wide, encoded = gather_encode(
            *shards, lax.axis_size("col") // 2, pick, padded, enc_vec, enc_up
        )
        return wide, ffn, proj.transpose(1, 0, 2).reshape(D, E), dec, encoded
    full = []
    for item in shards:
        rowed = lax.all_gather(item, "row", axis=item.ndim - 2, tiled=True)
        full.append(lax.all_gather(rowed, "col", axis=item.ndim - 1, tiled=True))
    blocks = full[0].reshape(D, 8, 5 * D // 8).transpose(1, 0, 2)
    wide, encoded = encode_images(blocks, full[1], enc_vec, enc_up, pick, padded)
    return wide, full[1], full[2], full[3], encoded


def apply_updates(blob, grad_head, small, count, params_now, firsts, seconds):
    summed_head = lax.psum(grad_head, ("row", "col"))
    if on_small_plane():
        summed, small = reduce_blocks(blob, small.reshape(32, 8, LANES), lax.axis_size("col") // 2, 6)
        flat = lambda group: group[:2] + (group[2].T,) + group[3:6] + (group[6].reshape(-1, LANES),)
        ins = flat(params_now) + flat(firsts) + flat(seconds)
        shape = jax.ShapeDtypeStruct
        outs = pl.pallas_call(
            functools.partial(adam_kernel, count),
            out_shape=tuple(shape(item.shape, high_type) for item in ins) + (shape((1, 1), high_type),),
            in_specs=[whole()] * 24,
            out_specs=[whole()] * 22,
            compiler_params=params(),
            name="adam",
        )(summed, summed_head, small.reshape(SMALL_ROWS, LANES), *ins)
        back = {2: lambda item: item.T, 6: lambda item: item.reshape(-1)}
        return [back.get(index % 7, lambda item: item)(item) for index, item in enumerate(outs[:21])], outs[21].reshape(())
    shards = []
    for item in whole_arrays(blob):
        done = lax.psum_scatter(item, "col", scatter_dimension=item.ndim - 1, tiled=True)
        shards.append(lax.psum_scatter(done, "row", scatter_dimension=item.ndim - 2, tiled=True))
    small = lax.psum(small, ("row", "col")).reshape(-1)
    size = params_now[6].shape[0]
    grads = tuple(shards) + (summed_head, small[:size])
    decays = (0.05,) * 6 + (0.0,)
    results = [adam_parts(*item) for item in zip(params_now, grads, firsts, seconds, decays)]
    return [item[kind] for kind in range(3) for item in results], small[size] / count


def body(
    patches,
    shuffle,
    enc_w,
    enc_ffn,
    dec_proj,
    dec_w,
    dec_ffn,
    head_w,
    smalls,
    first_enc_w,
    first_enc_ffn,
    first_dec_proj,
    first_dec_w,
    first_dec_ffn,
    first_head_w,
    first_smalls,
    second_enc_w,
    second_enc_ffn,
    second_dec_proj,
    second_dec_w,
    second_dec_ffn,
    second_head_w,
    second_smalls,
):
    prepared = prepare(enc_w, enc_ffn, dec_proj, dec_w, dec_ffn, head_w, smalls, shuffle, patches)
    shards, head_low, vectors, (pick, picked, padded) = prepared[:4], prepared[4], prepared[5:10], prepared[10:]
    wide, ffn, proj, dec, encoded = gather_and_encode(shards, vectors[0], vectors[1], pick, padded)
    count = patches.shape[0] * lax.axis_size("row") * lax.axis_size("col") * (PATCHES - KEEP) * P_SIZE
    blob, grad_head, small = local_grads(
        wide, ffn, proj, dec, encoded, head_low, vectors, pick, picked, padded, count
    )
    params_now = (enc_w, enc_ffn, dec_proj, dec_w, dec_ffn, head_w, smalls)
    firsts = (
        first_enc_w,
        first_enc_ffn,
        first_dec_proj,
        first_dec_w,
        first_dec_ffn,
        first_head_w,
        first_smalls,
    )
    seconds = (
        second_enc_w,
        second_enc_ffn,
        second_dec_proj,
        second_dec_w,
        second_dec_ffn,
        second_head_w,
        second_smalls,
    )
    outs, loss = apply_updates(blob, grad_head, small, count, params_now, firsts, seconds)
    return tuple(outs) + (loss,)


def solution(mesh):
    in_specs = (
        P(("row", "col"), None, None),
        P(("row", "col"), None),
        P("row", "col"),
        P(None, "row", "col"),
        P("row", "col"),
        P("row", "col"),
        P(None, "row", "col"),
        P(),
        P(),
        P("row", "col"),
        P(None, "row", "col"),
        P("row", "col"),
        P("row", "col"),
        P(None, "row", "col"),
        P(),
        P(),
        P("row", "col"),
        P(None, "row", "col"),
        P("row", "col"),
        P("row", "col"),
        P(None, "row", "col"),
        P(),
        P(),
    )
    out_specs = (
        P("row", "col"),
        P(None, "row", "col"),
        P("row", "col"),
        P("row", "col"),
        P(None, "row", "col"),
        P(),
        P(),
        P("row", "col"),
        P(None, "row", "col"),
        P("row", "col"),
        P("row", "col"),
        P(None, "row", "col"),
        P(),
        P(),
        P("row", "col"),
        P(None, "row", "col"),
        P("row", "col"),
        P("row", "col"),
        P(None, "row", "col"),
        P(),
        P(),
        P(),
    )
    return jax.shard_map(body, mesh=mesh, in_specs=in_specs, out_specs=out_specs, check_vma=False)
```

```python
import functools
import math

import jax
import jax.numpy as jnp
import numpy as np
from jax import lax
from jax.experimental import pallas as pl
from jax.experimental.pallas import tpu as pltpu
from jax.sharding import PartitionSpec as P

D = 768
HE = 12
F = 3072
E = 512
HD = 16
H = 2048
P_SIZE = 768
SIDE = 14
KEEP = 49
STEP = 5
PATCHES = 196
LANES = 128

norm_eps = 1e-06
low_type = jnp.bfloat16
high_type = jnp.float32


MESH = pl.DeviceIdType.MESH
LAGS = (2, 4, 6)


class Group:
    def __init__(self, copies):
        self.copies = copies

    def start(self):
        for item in self.copies:
            item.start()

    def wait_recv(self):
        for item in self.copies:
            item.wait_recv()

    def wait_send(self):
        for item in self.copies:
            item.wait_send()

    def wait(self):
        for item in self.copies:
            item.wait()


def gather_steps(depth, place_ids, own, cut, sems):
    row, row_x, row_y, row_d, z, k, near_x, near_y, twin, lower, upper, has_lower, has_upper = place_ids
    zs, zr, xs, xr, ys, yr, dxs, dxr, dys, dyr, cs, cr = sems
    levels = [(0, 0)] + [(d, way) for d in range(1, depth) for way in (0, 1)]
    level_of = {item: number for number, item in enumerate(levels)}

    def place(level):
        d, way = level
        return z - d if way == 0 else z + d

    def valid(level):
        d, way = level
        return z - d >= 0 if way == 0 else z + d < depth

    def slot(level, row_now, half=None):
        return cut(place(level) * 2 + k, row_now, half)

    def source(level):
        return own if level == (0, 0) else slot(level, row)

    def copy(src, dst, send, recv, target):
        return Group(
            [
                pltpu.make_async_remote_copy(
                    src_ref=src[item],
                    dst_ref=dst[item],
                    send_sem=send.at[item],
                    recv_sem=recv.at[item],
                    device_id=target,
                    device_id_type=MESH,
                )
                for item in range(len(own))
            ]
        )

    def z_copy(level, way):
        d = level[0]
        n = level_of[level]
        return copy(source(level), slot(level, row), zs.at[n, way], zr.at[d, way], upper if way == 0 else lower)

    def x_copy(level):
        n = level_of[level]
        return copy(source(level), slot(level, row), xs.at[n], xr.at[n], near_x)

    def y_copy(level):
        n = level_of[level]
        return copy(source(level), slot(level, row), ys.at[n], yr.at[n], near_y)

    def dx_copy(level):
        n = level_of[level]
        refs = slot(level, row_y, 1)
        return copy(refs, refs, dxs.at[n], dxr.at[n], near_x)

    def dy_copy(level):
        n = level_of[level]
        refs = slot(level, row_x, 0)
        return copy(refs, refs, dys.at[n], dyr.at[n], near_y)

    def twin_copy(level, kind):
        n = level_of[level]
        row_now = (row, row_x, row_y, row_d)[kind]
        src = source(level) if kind == 0 else slot(level, row_now)
        return copy(src, slot(level, row_now), cs.at[n, kind], cr.at[n, kind], twin)

    def guarded(level, action):
        if level == (0, 0):
            action()
        else:
            pl.when(valid(level))(action)

    def spread(level):
        d, way = level

        def action():
            if level != (0, 0):
                z_copy((d - 1, way if d > 1 else 0), way).wait_recv()
            for direction in (0, 1):
                if level == (0, 0) or direction == way:
                    @pl.when(has_upper if direction == 0 else has_lower)
                    def _():
                        z_copy(level, direction).start()
            x_copy(level).start()
            y_copy(level).start()
            twin_copy(level, 0).start()

        guarded(level, action)

    def turn(level):
        def action():
            x_copy(level).wait_recv()
            dy_copy(level).start()
            twin_copy(level, 1).start()
            y_copy(level).wait_recv()
            dx_copy(level).start()
            twin_copy(level, 2).start()

        guarded(level, action)

    def close(level):
        def action():
            dx_copy(level).wait_recv()
            dy_copy(level).wait_recv()
            twin_copy(level, 3).start()

        guarded(level, action)

    def drain(level):
        d, way = level

        def action():
            for direction in (0, 1):
                if level == (0, 0) or direction == way:
                    @pl.when(has_upper if direction == 0 else has_lower)
                    def _():
                        z_copy(level, direction).wait_send()
            x_copy(level).wait_send()
            y_copy(level).wait_send()
            dx_copy(level).wait_send()
            dy_copy(level).wait_send()
            for kind in range(4):
                twin_copy(level, kind).wait()

        guarded(level, action)

    def step_action(step):
        for level in levels:
            if level[0] == step:
                spread(level)
        for level in levels:
            if level[0] == step - 1:
                turn(level)
        for level in levels:
            if level[0] == step - 2:
                close(level)

    def finish():
        for level in levels:
            drain(level)

    return step_action, finish


def gather_steps_late(depth, place_ids, own, cut, sems):
    row, row_x, row_y, row_d, z, k, near_x, near_y, twin, lower, upper, has_lower, has_upper = place_ids
    zs, zr, xs, xr, ys, yr, dxs, dxr, dys, dyr, cs, cr = sems
    kinds = (row, row_x, row_y, row_d)
    levels = [(0, 0)] + [(d, way) for d in range(1, depth) for way in (0, 1)]
    level_of = {item: number for number, item in enumerate(levels)}

    def refs(level, kind, half=None):
        d, way = level
        return cut((z - d if way == 0 else z + d) * 2 + k, kinds[kind], half)

    def valid(level):
        d, way = level
        return z - d >= 0 if way == 0 else z + d < depth

    def copy(src, dst, send, recv, target):
        return Group(
            [
                pltpu.make_async_remote_copy(
                    src_ref=src[item],
                    dst_ref=dst[item],
                    send_sem=send.at[item],
                    recv_sem=recv.at[item],
                    device_id=target,
                    device_id_type=MESH,
                )
                for item in range(len(own))
            ]
        )

    home = (0, 0)

    def source(level, kind):
        return own if level == home and kind == 0 else refs(level, kind)

    def x_copy():
        return copy(own, refs(home, 0), xs, xr, near_x)

    def y_copy():
        return copy(own, refs(home, 0), ys, yr, near_y)

    def dx_copy():
        return copy(refs(home, 2, 1), refs(home, 2, 1), dxs, dxr, near_x)

    def dy_copy():
        return copy(refs(home, 1, 0), refs(home, 1, 0), dys, dyr, near_y)

    def z_copy(level, way, kind):
        d = level[0]
        target = upper if way == 0 else lower
        return copy(source(level, kind), refs(level, kind), zs.at[d, way, kind], zr.at[d, way, kind], target)

    def twin_copy(level, kind):
        n = level_of[level]
        return copy(source(level, kind), refs(level, kind), cs.at[n, kind], cr.at[n, kind], twin)

    def outward(level, kind, action):
        for way in (0, 1):
            if (level == home or way == level[1]) and level[0] < depth - 1:
                @pl.when(has_upper if way == 0 else has_lower)
                def _():
                    action(z_copy(level, way, kind))

    def pass_on(level, kind):
        outward(level, kind, lambda item: item.start())
        twin_copy(level, kind).start()

    def arrive(level, kind):
        d, way = level

        @pl.when(valid(level))
        def _():
            z_copy((d - 1, way if d > 1 else 0), way, kind).wait_recv()
            pass_on(level, kind)

    delay = (0, 1, 1, 2)

    def step_action(step):
        if step == 0:
            x_copy().start()
            y_copy().start()
            pass_on(home, 0)
        if step == 1:
            x_copy().wait_recv()
            dy_copy().start()
            pass_on(home, 1)
            y_copy().wait_recv()
            dx_copy().start()
            pass_on(home, 2)
        if step == 2:
            dx_copy().wait_recv()
            dy_copy().wait_recv()
            pass_on(home, 3)
        for level in levels[1:]:
            for kind in range(4):
                if step == level[0] + delay[kind]:
                    arrive(level, kind)

    def finish():
        for item in (x_copy(), y_copy(), dx_copy(), dy_copy()):
            item.wait_send()
        for level in levels:
            def action():
                for kind in range(4):
                    outward(level, kind, lambda item: item.wait_send())
                    twin_copy(level, kind).wait()

            if level == home:
                action()
            else:
                pl.when(valid(level))(action)

    return step_action, finish


def gather_encode_kernel(depth, batch, own_enc, own_ffn, own_proj, own_dec, pick, patches, vec, up_bias, pos,
                         ffn, proj, dec, wide_out, *rest):
    outs, rest = rest[:11], rest[11:]
    blocks, wide, ffn_here = rest[:3]
    held = rest[3:14]
    kept, start, normed, qkv, mixed, middle, normed_two, slope, active, output, latent = held
    first_sems, second_sems, late_sems = rest[14:26], rest[26:38], rest[38:50]
    local, load_sem, wide_sem, out_sems = rest[50:]
    row = lax.axis_index("row")
    col = lax.axis_index("col")
    y, x, z, k = row // 2, row % 2, col // 2, col % 2
    row_x = y * 2 + (1 - x)
    row_y = (1 - y) * 2 + x
    row_d = (1 - y) * 2 + (1 - x)
    near_x, near_y = (row_x, col), (row_y, col)
    twin = (row, z * 2 + (1 - k))
    lower, upper = (row, col - 2), (row, col + 2)
    has_lower, has_upper = z > 0, z < depth - 1

    barrier = pltpu.get_barrier_semaphore()
    for other in (near_x, near_y, twin):
        pl.semaphore_signal(barrier, inc=1, device_id=other, device_id_type=MESH)

    @pl.when(has_lower)
    def _():
        pl.semaphore_signal(barrier, inc=1, device_id=lower, device_id_type=MESH)

    @pl.when(has_upper)
    def _():
        pl.semaphore_signal(barrier, inc=1, device_id=upper, device_id_type=MESH)

    pl.semaphore_wait(barrier, 3 + jnp.where(has_lower, 1, 0) + jnp.where(has_upper, 1, 0))
    ids = (row, row_x, row_y, row_d, z, k, near_x, near_y, twin, lower, upper, has_lower, has_upper)
    tall, short = own_enc.shape[0], own_dec.shape[1]
    broad, thin = own_ffn.shape[2], own_dec.shape[2]

    early = tall - 32

    def rows_of(row_now, size, half, start=0, count=None):
        count = size if count is None else count
        part = count if half is None else count // 2
        first = start if half is None else start + half * part
        return pl.ds(pl.multiple_of(row_now * size + first, 16), part)

    def enc_refs(index, rows):
        return blocks.at[index, rows], ffn.at[:, rows, pl.ds(pl.multiple_of(index * broad, LANES), broad)]

    def cut_first(index, row_now, half=None):
        return enc_refs(index, rows_of(row_now, tall, half, 0, early))

    def cut_late(index, row_now, half=None):
        return enc_refs(index, rows_of(row_now, tall, half, early, tall - early))

    def cut_second(index, row_now, half=None):
        return (
            proj.at[index, rows_of(row_now, tall, half)],
            dec.at[:, rows_of(row_now, short, half), pl.ds(pl.multiple_of(index * thin, LANES), thin)],
        )

    own_second = (own_proj, own_dec)
    own_first = (own_enc.at[pl.ds(0, early)], own_ffn.at[:, pl.ds(0, early)])
    own_late = (own_enc.at[pl.ds(early, tall - early)], own_ffn.at[:, pl.ds(early, tall - early)])
    step_first, finish_first = gather_steps(depth, ids, own_first, cut_first, first_sems)
    step_late, finish_late = gather_steps_late(depth, ids, own_late, cut_late, late_sems)
    step_second, finish_second = gather_steps(depth, ids, own_second, cut_second, second_sems)
    keep = [
        pltpu.make_async_copy(src, dst, local.at[item])
        for item, (src, dst) in enumerate(
            zip(own_first + own_late + own_second, cut_first(col, row) + cut_late(col, row) + cut_second(col, row))
        )
    ]
    for item in keep:
        item.start()
    for step in range(depth + 1):
        step_first(step)
        step_late(step)
    step_second(0)
    step_first(depth + 1)
    step_late(depth + 1)
    finish_first()
    finish_late()
    for item in keep:
        item.wait()
    load = pltpu.make_async_copy(ffn, ffn_here, load_sem)
    load.start()
    count, _, width = blocks.shape

    def assemble(first, last):
        for index in range(first, last):
            wide[:, index * width : (index + 1) * width] = blocks[index]

    def flush(index):
        return pltpu.make_async_copy(held[index], outs[index], out_sems.at[index])

    assemble(0, count // 2)
    step_second(1)
    assemble(count // 2, count)
    wide_copy = pltpu.make_async_copy(wide, wide_out, wide_sem)
    wide_copy.start()
    enc_embed(batch, pick, patches, wide, vec, pos, kept, start)
    flush(0).start()
    flush(1).start()
    step_second(2)
    enc_project(wide, vec, start, normed, qkv)
    flush(2).start()
    flush(3).start()
    enc_mix(batch, qkv, mixed)
    flush(4).start()
    step_second(3)
    enc_join(wide, vec, start, mixed, middle, normed_two)
    flush(5).start()
    flush(6).start()
    load.wait()
    total = middle[...] + vec[9:10]
    source = normed_two[...]
    step = 512
    for place in range(0, F, step):
        span = slice(place, place + step)
        value, gain = gelu_pair(nn(source, ffn_here[0, :, span]) + up_bias[:, span])
        slope[:, span] = gain
        value = value.astype(low_type)
        active[:, span] = value
        total = total + nt(value, ffn_here[1, :, span])
        if place == 2 * step:
            step_second(4)
    flush(7).start()
    flush(8).start()
    step_second(5)
    output[...] = total
    unit, _ = standard(total)
    latent[...] = (unit * vec[10:11] + vec[11:12]).astype(low_type)
    flush(9).start()
    flush(10).start()
    for step in range(6, depth + 2):
        step_second(step)
    finish_second()
    wide_copy.wait()
    for index in range(11):
        flush(index).wait()


def gather_encode(own_enc, own_ffn, own_proj, own_dec, depth, pick, padded, vec, up_bias):
    count = 2 * depth - 1
    cols = 2 * depth
    dma = pltpu.SemaphoreType.DMA
    tall, width = own_enc.shape
    shape = jax.ShapeDtypeStruct
    kind = own_enc.dtype
    batch = padded.shape[0]
    first, second = encoder_shapes(batch)
    made = first + second
    sems = [dma((count, 2, 2)), dma((depth, 2, 2))] + [dma((count, 2)) for _ in range(8)]
    sems = sems + [dma((count, 4, 2)), dma((count, 4, 2))]
    outs = pl.pallas_call(
        functools.partial(gather_encode_kernel, depth, batch),
        out_shape=(
            shape((2, 4 * tall, cols * own_ffn.shape[2]), kind),
            shape((cols, 4 * tall, own_proj.shape[1]), kind),
            shape((3, 4 * own_dec.shape[1], cols * own_dec.shape[2]), kind),
            shape((D, 5 * D), kind),
        )
        + made,
        in_specs=[hbm()] * 4 + [whole()] * 5,
        out_specs=[hbm()] * 15,
        scratch_shapes=[
            pltpu.VMEM((cols, 4 * tall, width), kind),
            pltpu.VMEM((D, 5 * D), kind),
            pltpu.VMEM((2, D, F), kind),
        ]
        + [pltpu.VMEM(item.shape, item.dtype) for item in made]
        + sems
        + sems
        + [dma((depth, 2, 4, 2)), dma((depth, 2, 4, 2))]
        + [dma((2,)) for _ in range(8)]
        + [dma((count, 4, 2)), dma((count, 4, 2))]
        + [dma((6,)), dma, dma, dma((11,))],
        compiler_params=pltpu.CompilerParams(
            collective_id=0, has_side_effects=True, vmem_limit_bytes=60 << 20
        ),
        name="gather_encode",
    )(own_enc, own_ffn, own_proj, own_dec, pick, padded, vec, up_bias, jnp.asarray(table_of(D, DEC_ROWS)))
    ffn, proj, dec, wide = outs[:4]
    return ffn, proj, dec, wide, tuple(outs[4:])


def far_first(depth):
    orders = []
    for z in range(depth):
        orders.append(sorted(range(depth), key=lambda t: (-abs(t - z), -abs(2 * t - depth + 1))))
    return orders


code_type = jnp.int16
code_top = 32767.0


def encode(values):
    peak = jnp.max(jnp.abs(values), axis=0, keepdims=True)
    unit = jnp.maximum(peak, 1e-30) * (1.0 / code_top)
    codes = jnp.round(values * (1.0 / unit))
    codes = jnp.clip(codes, -code_top, code_top)
    return codes.astype(jnp.int32).astype(code_type), unit


def decode(codes, unit):
    return codes.astype(jnp.int32).astype(high_type) * unit


def reduce_kernel(depth, devices, cols, parts, chunk, half, blob, small, out, small_out,
                  arrived, mine, stage_x, stage_y, recv_x, recv_y, turn_x, turn_y, back_x, back_y, line_out, line,
                  units_out, units_in, line_units, box,
                  s_load, s_cs, s_cr, s_xs, s_xr, s_ys, s_yr, s_txs, s_txr, s_tys, s_tyr, s_zs, s_zr,
                  u_xs, u_xr, u_ys, u_yr, u_txs, u_txr, u_tys, u_tyr, u_zs, u_zr,
                  s_ps, s_pr, s_qs, s_qr):
    row = lax.axis_index("row")
    col = lax.axis_index("col")
    y, x, z, k = row // 2, row % 2, col // 2, col % 2
    me = row * cols + col
    near_x, near_y = (y * 2 + (1 - x), col), ((1 - y) * 2 + x, col)
    twin = (row, z * 2 + (1 - k))
    lower, upper = (row, col - 2), (row, col + 2)
    has_lower, has_upper = z > 0, z < depth - 1
    steps = depth * parts
    slots = mine.shape[0]
    ahead = slots - 1
    a_rows, b_rows = pl.ds(0, half), pl.ds(half, chunk - half)

    def device(offset):
        index = (me + offset) % devices
        return (index // cols, index % cols)

    barrier = pltpu.get_barrier_semaphore()
    for offset in range(1, devices):
        pl.semaphore_signal(barrier, inc=1, device_id=device(offset), device_id_type=MESH)
    pl.semaphore_wait(barrier, devices - 1)

    def copy(src, dst, send, recv, target):
        return pltpu.make_async_remote_copy(
            src_ref=src, dst_ref=dst, send_sem=send, recv_sem=recv, device_id=target, device_id_type=MESH
        )

    orders = far_first(depth)

    def goal(t):
        turn = t // parts
        value = 0
        for a in range(depth):
            for b in range(depth):
                value = jnp.where((z == a) & (turn == b), orders[a][b], value)
        return value

    def span(t):
        return pl.ds(pl.multiple_of((t % parts) * chunk, 16), chunk)

    def load(t):
        return pltpu.make_async_copy(
            blob.at[goal(t) * 2 + k, :, span(t)], mine.at[t % slots], s_load.at[t % slots]
        )

    def core(t):
        return copy(blob.at[goal(t) * 2 + (1 - k), :, span(t)], arrived.at[t], s_cs.at[t], s_cr.at[t], twin)

    def paired(kind, src, dst, send, recv, unit_send, unit_recv, target):
        def make(t):
            return Group([
                copy(src.at[t], dst.at[t], send.at[t], recv.at[t], target),
                copy(units_out.at[t, kind], units_in.at[t, kind], unit_send.at[t], unit_recv.at[t], target),
            ])

        return make

    first_x = paired(0, stage_x, recv_x, s_xs, s_xr, u_xs, u_xr, near_x)
    first_y = paired(1, stage_y, recv_y, s_ys, s_yr, u_ys, u_yr, near_y)
    second_x = paired(2, turn_x, back_x, s_txs, s_txr, u_txs, u_txr, near_x)
    second_y = paired(3, turn_y, back_y, s_tys, s_tyr, u_tys, u_tyr, near_y)

    def along(t, index, target):
        return Group([
            copy(line_out.at[t], line.at[index], s_zs.at[t], s_zr.at[index], target),
            copy(units_out.at[t, 4], line_units.at[index], u_zs.at[t], u_zr.at[index], target),
        ])

    def upper_index(t):
        return (goal(t) + 1) * parts + t % parts

    def lower_index(t):
        return goal(t) * parts + t % parts

    def to_upper(t):
        return along(t, upper_index(t), upper)

    def to_lower(t):
        return along(t, lower_index(t), lower)

    def small_send(offset):
        target = device(offset)
        return copy(small.at[target[0] * cols + target[1]], box.at[offset], s_ps.at[offset], s_pr.at[offset], target)

    def small_back(offset):
        return copy(small_out.at[me], small_out.at[me], s_qs.at[offset], s_qr.at[offset], device(offset))

    def small_back_recv(offset):
        origin = (me + devices - offset) % devices
        return copy(small_out.at[origin], small_out.at[origin], s_qs.at[offset], s_qr.at[offset], device(offset))

    for t in range(ahead):
        load(t).start()
        core(t).start()
    for offset in range(1, devices):
        small_send(offset).start()

    def stage_one(t):
        load(t).wait()
        core(t).wait_recv()
        slot = t % slots
        for other in (0, 1):
            away = other * 2 + (1 - x)
            stay = other * 2 + x
            codes, unit = encode(mine[slot, away, a_rows] + arrived[t, away, a_rows])
            stage_x[t, other] = codes
            units_out[t, 0, pl.ds(other, 1)] = unit
            arrived[t, stay, a_rows] += mine[slot, stay, a_rows]
        first_x(t).start()
        for other in (0, 1):
            away = (1 - y) * 2 + other
            stay = y * 2 + other
            codes, unit = encode(mine[slot, away, b_rows] + arrived[t, away, b_rows])
            stage_y[t, other] = codes
            units_out[t, 1, pl.ds(other, 1)] = unit
            arrived[t, stay, b_rows] += mine[slot, stay, b_rows]
        first_y(t).start()

    def stage_two(t):
        first_x(t).wait_recv()
        away = (1 - y) * 2 + x
        codes, unit = encode(arrived[t, away, a_rows] + decode(recv_x[t, 1 - y], units_in[t, 0, pl.ds(1 - y, 1)]))
        turn_y[t] = codes
        units_out[t, 3, pl.ds(0, 1)] = unit
        second_y(t).start()
        arrived[t, row, a_rows] += decode(recv_x[t, y], units_in[t, 0, pl.ds(y, 1)])
        first_y(t).wait_recv()
        away = y * 2 + (1 - x)
        codes, unit = encode(arrived[t, away, b_rows] + decode(recv_y[t, 1 - x], units_in[t, 1, pl.ds(1 - x, 1)]))
        turn_x[t] = codes
        units_out[t, 2, pl.ds(0, 1)] = unit
        second_x(t).start()
        arrived[t, row, b_rows] += decode(recv_y[t, x], units_in[t, 1, pl.ds(x, 1)])

    def stage_three(t):
        second_y(t).wait_recv()
        arrived[t, row, a_rows] += decode(back_y[t], units_in[t, 3, pl.ds(0, 1)])
        second_x(t).wait_recv()
        arrived[t, row, b_rows] += decode(back_x[t], units_in[t, 2, pl.ds(0, 1)])

    def take(index):
        return decode(line[index], line_units[index, pl.ds(0, 1)])

    def pack(t):
        codes, unit = encode(arrived[t, row])
        line_out[t] = codes
        units_out[t, 4, pl.ds(0, 1)] = unit

    def stage_four(t):
        target = goal(t)

        @pl.when((target >= z) & has_lower)
        def _():
            to_upper(t).wait_recv()
            arrived[t, row] += take(upper_index(t))

        @pl.when((target <= z) & has_upper)
        def _():
            to_lower(t).wait_recv()
            arrived[t, row] += take(lower_index(t))

        @pl.when(target != z)
        def _():
            pack(t)

        @pl.when(target > z)
        def _():
            to_upper(t).start()

        @pl.when(target < z)
        def _():
            to_lower(t).start()

        @pl.when(target == z)
        def _():
            out[span(t)] = arrived[t, row]

    lags = LAGS

    def body(i, carry):
        @pl.when(i + ahead < steps)
        def _():
            load(i + ahead).start()
            core(i + ahead).start()

        @pl.when(i < steps)
        def _():
            stage_one(i)

        for lag, stage in zip(lags, (stage_two, stage_three, stage_four)):
            @pl.when((i >= lag) & (i - lag < steps))
            def _():
                stage(i - lag)

        @pl.when(i == steps // 2)
        def _():
            total = small[me]
            for offset in range(1, devices):
                small_send(offset).wait_recv()
                total = total + box[offset]
            small_out[me] = total
            for offset in range(1, devices):
                small_back(offset).start()

        return carry

    lax.fori_loop(0, steps + lags[-1], body, 0)

    def finish(t, carry):
        core(t).wait_send()
        first_x(t).wait_send()
        first_y(t).wait_send()
        second_x(t).wait_send()
        second_y(t).wait_send()

        @pl.when(goal(t) > z)
        def _():
            to_upper(t).wait_send()

        @pl.when(goal(t) < z)
        def _():
            to_lower(t).wait_send()

        return carry

    lax.fori_loop(0, steps, finish, 0)
    for offset in range(1, devices):
        small_send(offset).wait_send()
        small_back(offset).wait_send()
        small_back_recv(offset).wait_recv()


def reduce_blocks(blob, small, depth, parts):
    cols, _, rows, lanes = blob.shape
    devices = 4 * cols
    chunk = rows // parts
    half = -(-chunk // 32) * 16
    rest = chunk - half
    steps = depth * parts
    lines = (depth + 1) * parts
    dma = pltpu.SemaphoreType.DMA
    vm = pltpu.VMEM
    return pl.pallas_call(
        functools.partial(reduce_kernel, depth, devices, cols, parts, chunk, half),
        out_shape=(
            jax.ShapeDtypeStruct((rows, lanes), high_type),
            jax.ShapeDtypeStruct(small.shape, high_type),
        ),
        in_specs=[pl.BlockSpec(memory_space=pltpu.HBM), pl.BlockSpec(memory_space=pltpu.VMEM)],
        out_specs=[pl.BlockSpec(memory_space=pltpu.VMEM)] * 2,
        scratch_shapes=[
            vm((steps, 4, chunk, lanes), high_type),
            vm((4, 4, chunk, lanes), high_type),
            vm((steps, 2, half, lanes), code_type),
            vm((steps, 2, rest, lanes), code_type),
            vm((steps, 2, half, lanes), code_type),
            vm((steps, 2, rest, lanes), code_type),
            vm((steps, rest, lanes), code_type),
            vm((steps, half, lanes), code_type),
            vm((steps, rest, lanes), code_type),
            vm((steps, half, lanes), code_type),
            vm((steps, chunk, lanes), code_type),
            vm((lines, chunk, lanes), code_type),
            vm((steps, 5, 8, lanes), high_type),
            vm((steps, 4, 8, lanes), high_type),
            vm((lines, 8, lanes), high_type),
            vm((devices,) + small.shape[1:], high_type),
            dma((4,)),
        ]
        + ([dma((steps,)) for _ in range(11)] + [dma((lines,))])
        + ([dma((steps,)) for _ in range(9)] + [dma((lines,))])
        + [dma((devices,)) for _ in range(4)],
        compiler_params=pltpu.CompilerParams(
            collective_id=1, has_side_effects=True, vmem_limit_bytes=62 << 20
        ),
        name="reduce_blocks",
    )(blob, small)


ENC_ROWS = 64
DEC_ROWS = 208
CLASS_ENC = KEEP
CLASS_DEC = PATCHES
NEGATIVE = -1e30


def nn(left, right):
    return jnp.dot(left, right, preferred_element_type=high_type)


def nt(left, right):
    return lax.dot_general(left, right, (((1,), (1,)), ((), ())), preferred_element_type=high_type)


def tn(left, right):
    return lax.dot_general(left, right, (((0,), (0,)), ((), ())), preferred_element_type=high_type)


def standard(rows):
    mean = jnp.mean(rows, -1, keepdims=True)
    centred = rows - mean
    spread = jnp.mean(centred * centred, -1, keepdims=True)
    rate = lax.rsqrt(spread + norm_eps)
    return centred * rate, rate


def standard_back(unit, rate, grad):
    return rate * (grad - jnp.mean(grad, -1, keepdims=True) - unit * jnp.mean(grad * unit, -1, keepdims=True))


def col_sum(rows):
    return jnp.sum(rows.astype(high_type), 0, keepdims=True)


def gelu_pair(value):
    size = jnp.abs(value)
    below = 1.0 + (0.3275911 * math.sqrt(0.5)) * size
    t = pl.reciprocal(below, approx=True)
    t = t * (2.0 - below * t)
    t = t * (2.0 - below * t)
    fall = jnp.exp(-0.5 * value * value)
    series = 1.061405429
    for item in (-1.453152027, 1.421413741, -0.284496736, 0.254829592):
        series = series * t + item
    tail = 0.5 * series * t * fall
    part = jnp.where(value < 0.0, tail, 1.0 - tail)
    return value * part, part + value * fall * (1.0 / math.sqrt(2.0 * math.pi))


def three_way(value):
    high = value.astype(low_type)
    rest = value - high.astype(high_type)
    middle = rest.astype(low_type)
    return high, middle, (rest - middle.astype(high_type)).astype(low_type)


def place_rows(picks, value):
    parts = three_way(value)
    return nn(picks, parts[0]) + nn(picks, parts[1]) + nn(picks, parts[2])


def stack_heads(value, heads):
    width = LANES // heads
    lane = lax.broadcasted_iota(jnp.int32, value.shape, 1) // width
    return jnp.concatenate([jnp.where(lane == head, value, jnp.zeros_like(value)) for head in range(heads)], 0)


def merge_heads(stacked, heads):
    rows = stacked.shape[0] // heads
    width = LANES // heads
    lane = lax.broadcasted_iota(jnp.int32, (rows, LANES), 1) // width
    merged = stacked[:rows]
    for head in range(1, heads):
        merged = jnp.where(lane == head, stacked[head * rows : (head + 1) * rows], merged)
    return merged


def attend(query, key, value, heads, length):
    scores = nt(stack_heads(query, heads), key)
    column = lax.broadcasted_iota(jnp.int32, scores.shape, 1)
    scores = jnp.where(column < length, scores, NEGATIVE)
    raised = jnp.exp(scores - jnp.max(scores, -1, keepdims=True))
    attention = (raised / jnp.sum(raised, -1, keepdims=True)).astype(low_type)
    return merge_heads(nn(attention, value), heads)


def attend_back(query, key, value, grad, heads, length):
    queries = stack_heads(query, heads)
    grads = stack_heads(grad, heads)
    scores = nt(key, queries)
    place = lax.broadcasted_iota(jnp.int32, scores.shape, 0)
    scores = jnp.where(place < length, scores, NEGATIVE)
    raised = jnp.exp(scores - jnp.max(scores, 0, keepdims=True))
    attention = raised * (1.0 / jnp.sum(raised, 0, keepdims=True))
    inner = nt(value, grads)
    grad_scores = (attention * (inner - jnp.sum(inner * attention, 0, keepdims=True))).astype(low_type)
    grad_value = nn(attention.astype(low_type), grads)
    grad_key = nn(grad_scores, queries)
    grad_query = merge_heads(tn(grad_scores, key), heads)
    return grad_query, grad_key, grad_value


def attend_back_many(batch, query, key, value, grad, heads, length):
    rows = query.shape[0] // batch
    spans = [slice(image * rows, (image + 1) * rows) for image in range(batch)]
    queries = [stack_heads(query[span], heads) for span in spans]
    grads = [stack_heads(grad[span], heads) for span in spans]
    scores = jnp.concatenate([nt(key[span], item) for span, item in zip(spans, queries)], 0)
    inner = jnp.concatenate([nt(value[span], item) for span, item in zip(spans, grads)], 0)
    scores = scores.reshape(batch, rows, scores.shape[1])
    inner = inner.reshape(batch, rows, inner.shape[1])
    place = lax.broadcasted_iota(jnp.int32, scores.shape, 1)
    scores = jnp.where(place < length, scores, NEGATIVE)
    raised = jnp.exp(scores - jnp.max(scores, 1, keepdims=True))
    attention = raised * (1.0 / jnp.sum(raised, 1, keepdims=True))
    grad_scores = (attention * (inner - jnp.sum(inner * attention, 1, keepdims=True))).astype(low_type)
    attention = attention.astype(low_type)
    grad_value = [nn(attention[image], grads[image]) for image in range(batch)]
    grad_key = [nn(grad_scores[image], queries[image]) for image in range(batch)]
    grad_query = [merge_heads(tn(grad_scores[image], key[spans[image]]), heads) for image in range(batch)]
    return tuple(jnp.concatenate(item, 0) for item in (grad_query, grad_key, grad_value))


def wide_kernel(blocks, wide):
    count, _, width = blocks.shape
    for index in range(count):
        wide[:, index * width : (index + 1) * width] = blocks[index]


def enc_embed(batch, pick, patches, wide, vec, pos, kept, start):
    rows = ENC_ROWS
    for image in range(batch):
        span = pl.ds(image * rows, rows)
        kept[span] = nn(pick[image], patches[image]).astype(low_type)
    start[...] = nn(kept[...], wide[:, :D]) + vec[0:1]
    parts = three_way(pos[...])
    for image in range(batch):
        span = pl.ds(image * rows, rows)
        picks = pick[image]
        placed = nn(picks, parts[0]) + nn(picks, parts[1]) + nn(picks, parts[2])
        inner = lax.broadcasted_iota(jnp.int32, placed.shape, 0)
        start[span] = jnp.where(inner == CLASS_ENC, vec[1:2], start[span] + placed)


def enc_project(wide, vec, start, normed, qkv):
    unit, _ = standard(start[...])
    normed[...] = (unit * vec[2:3] + vec[3:4]).astype(low_type)
    scale = 1.0 / math.sqrt(D // HE)
    rows_in = normed[...]
    qkv[:, :D] = ((nn(rows_in, wide[:, D : 2 * D]) + vec[4:5]) * scale).astype(low_type)
    qkv[:, D : 2 * D] = nn(rows_in, wide[:, 2 * D : 3 * D]).astype(low_type)
    qkv[:, 2 * D :] = (nn(rows_in, wide[:, 3 * D : 4 * D]) + vec[5:6]).astype(low_type)


def enc_mix(batch, qkv, mixed):
    rows = ENC_ROWS
    heads = LANES * HE // D
    for image in range(batch):
        span = pl.ds(image * rows, rows)
        for group in range(D // LANES):
            lane = group * LANES
            mixed[span, lane : lane + LANES] = attend(
                qkv[span, lane : lane + LANES],
                qkv[span, D + lane : D + lane + LANES],
                qkv[span, 2 * D + lane : 2 * D + lane + LANES],
                heads,
                KEEP + 1,
            ).astype(low_type)


def enc_join(wide, vec, start, mixed, middle, normed_two):
    middle[...] = start[...] + (nn(mixed[...], wide[:, 4 * D :]) + vec[6:7])
    unit, _ = standard(middle[...])
    normed_two[...] = (unit * vec[7:8] + vec[8:9]).astype(low_type)


def enc_attend_kernel(batch, pick, patches, wide, vec, pos, kept, start, normed, qkv, mixed, middle, normed_two):
    enc_embed(batch, pick, patches, wide, vec, pos, kept, start)
    enc_project(wide, vec, start, normed, qkv)
    enc_mix(batch, qkv, mixed)
    enc_join(wide, vec, start, mixed, middle, normed_two)


def enc_ffn_kernel(last, middle, normed_two, ffn, vec, up_bias, slope, active, output, latent):
    step = pl.program_id(0)

    @pl.when(step == 0)
    def _():
        output[...] = middle[...] + vec[9:10]

    value, gain = gelu_pair(nn(normed_two[...], ffn[0]) + up_bias[...])
    slope[...] = gain
    value = value.astype(low_type)
    active[...] = value
    output[...] += nt(value, ffn[1])

    @pl.when(step == last)
    def _():
        unit, _ = standard(output[...])
        latent[...] = (unit * vec[10:11] + vec[11:12]).astype(low_type)


def dec_attend_kernel(latent, proj, picked, pos, wide, vec, start, normed, qkv, mixed, middle, normed_two):
    picks = picked[0]
    kept = jnp.sum(picks.astype(high_type), 1, keepdims=True)
    entry = nn(latent[...], proj[...]) + vec[0:1]
    rows = place_rows(picks, entry) + (1.0 - kept) * vec[1:2] + pos[...]
    start[...] = rows
    unit, _ = standard(rows)
    rows_in = (unit * vec[2:3] + vec[3:4]).astype(low_type)
    normed[...] = rows_in
    scale = 1.0 / math.sqrt(E // HD)
    qkv[:, :E] = ((nn(rows_in, wide[0, :, :E]) + vec[4:5]) * scale).astype(low_type)
    qkv[:, E : 2 * E] = nn(rows_in, wide[0, :, E : 2 * E]).astype(low_type)
    qkv[:, 2 * E :] = (nn(rows_in, wide[0, :, 2 * E : 3 * E]) + vec[5:6]).astype(low_type)
    heads = LANES * HD // E
    for group in range(E // LANES):
        lane = group * LANES
        mixed[:, lane : lane + LANES] = attend(
            qkv[:, lane : lane + LANES],
            qkv[:, E + lane : E + lane + LANES],
            qkv[:, 2 * E + lane : 2 * E + lane + LANES],
            heads,
            PATCHES + 1,
        ).astype(low_type)
    total = rows + (nn(mixed[...], wide[0, :, 3 * E :]) + vec[6:7])
    middle[...] = total
    unit, _ = standard(total)
    normed_two[...] = (unit * vec[7:8] + vec[8:9]).astype(low_type)


def send_tiles(acc, blob, sem, tiles, rows, per_block, base, stride):
    def go(index, carry):
        tile, part = index // 4, index % 4
        block, inner = tile // per_block, tile % per_block
        pltpu.make_async_copy(
            acc.at[tile, pl.ds(pl.multiple_of(part * rows, 16), rows)],
            blob.at[block, part, pl.ds(pl.multiple_of(base + inner * stride, 16), rows)],
            sem,
        ).start()
        return carry

    lax.fori_loop(0, tiles * 4, go, 0)


def wait_tiles(acc, sem):
    pltpu.make_async_copy(acc, acc, sem).wait()


def dec_ffn_kernel(images, last, count, middle, normed_two, mixed, pixels, picked, weights, head, vec, up_bias, head_bias,
                   grad_middle, grad_mixed, grad_head, vec_grad, up_grad, bias_grad, loss, blob,
                   active, slope, acc_up, acc_down, acc_out, sems):
    step = pl.program_id(0)
    source = normed_two[...]
    rows = source.shape[0]

    @pl.when(step == 0)
    def _():
        grad_head[...] = jnp.zeros_like(grad_head)
        vec_grad[...] = jnp.zeros_like(vec_grad)
        up_grad[...] = jnp.zeros_like(up_grad)
        bias_grad[...] = jnp.zeros_like(bias_grad)
        loss[...] = jnp.zeros_like(loss)
        acc_up[...] = jnp.zeros_like(acc_up)
        acc_down[...] = jnp.zeros_like(acc_down)
        acc_out[...] = jnp.zeros_like(acc_out)

    wide = 512
    total = middle[...] + vec[9:10]
    for place in range(0, H, wide):
        span = slice(place, place + wide)
        value, gain = gelu_pair(nn(source, weights[1, :, span]) + up_bias[:, span])
        slope[:, span] = gain
        value = value.astype(low_type)
        active[:, span] = value
        total = total + nt(value, weights[2, :, span])
    unit, rate = standard(total)
    final = (unit * vec[10:11] + vec[11:12]).astype(low_type)
    predict = nn(final, head[...]) + head_bias[...]
    target, _ = standard(pixels[...].astype(high_type))
    kept = jnp.concatenate([jnp.sum(picked[image].astype(high_type), 1, keepdims=True) for image in range(images)], 0)
    inner = lax.broadcasted_iota(jnp.int32, (rows, 1), 0) % DEC_ROWS
    masked = jnp.where(inner < PATCHES, 1.0 - kept, 0.0)
    error = predict - target
    loss[...] += jnp.sum(masked * error * error)
    grad_predict = (2.0 * masked * error / count).astype(low_type)
    grad_head[...] += tn(final, grad_predict)
    bias_grad[...] += col_sum(grad_predict)
    grad_final = nt(grad_predict, head[...])
    vec_grad[10:11] += col_sum(grad_final * unit)
    vec_grad[11:12] += col_sum(grad_final)
    grad_out = standard_back(unit, rate, grad_final * vec[10:11])
    grad_down = grad_out.astype(low_type)
    vec_grad[9:10] += col_sum(grad_down)
    grad_source = jnp.zeros_like(total)
    grad_turned, source_turned = grad_down.T, source.T
    for place in range(0, H, wide):
        span = slice(place, place + wide)
        grad_up = (slope[:, span] * nn(grad_down, weights[2, :, span])).astype(low_type)
        up_grad[:, span] += col_sum(grad_up)
        grad_source = grad_source + nt(grad_up, weights[1, :, span])
        piece = nn(grad_turned, active[:, span])
        other = nn(source_turned, grad_up)
        for tile in range(wide // LANES):
            lane = slice(tile * LANES, (tile + 1) * LANES)
            acc_down[place // LANES + tile] += piece[:, lane]
            acc_up[place // LANES + tile] += other[:, lane]

        @pl.when(step == last)
        def _():
            tiles = wide // LANES
            tile, block = place // LANES, place // LANES // 2
            rows_block = E // 4
            for number, (acc, base) in enumerate(((acc_up, 2176), (acc_down, 2432))):
                send_tiles(
                    acc.at[pl.ds(tile, tiles)], blob.at[pl.ds(block, tiles // 2)], sems.at[number], tiles,
                    rows_block, 2, base, rows_block,
                )

    unit, rate = standard(middle[...])
    vec_grad[7:8] += col_sum(grad_source * unit)
    vec_grad[8:9] += col_sum(grad_source)
    grad_rows = standard_back(unit, rate, grad_source * vec[7:8]) + grad_out
    grad_middle[...] = grad_rows
    branch = grad_rows.astype(low_type)
    vec_grad[6:7] += col_sum(branch)
    piece = tn(mixed[...], branch)
    for tile in range(E // LANES):
        acc_out[tile] += piece[:, tile * LANES : (tile + 1) * LANES]
    grad_mixed[...] = nt(branch, weights[0, :, 3 * E :]).astype(low_type)

    @pl.when(step == last)
    def _():
        rows_block = E // 4
        send_tiles(acc_out, blob.at[pl.ds(6, 2)], sems.at[2], E // LANES, rows_block, 2, 1920, rows_block)
        wait_tiles(acc_up, sems.at[0])
        wait_tiles(acc_down, sems.at[1])
        wait_tiles(acc_out, sems.at[2])


def dec_back_kernel(last, blob_in, qkv, normed, start, grad_middle, grad_mixed, pick, picked, weights, vec,
                    grad_entry, vec_grad, blob, grads, acc, sem):
    step = pl.program_id(0)

    @pl.when(step == 0)
    def _():
        vec_grad[...] = jnp.zeros_like(vec_grad)
        acc[...] = jnp.zeros_like(acc)

    scale = 1.0 / math.sqrt(E // HD)
    heads = LANES * HD // E
    for group in range(E // LANES):
        lane = group * LANES
        span = slice(lane, lane + LANES)
        query, key, value = attend_back(
            qkv[:, lane : lane + LANES],
            qkv[:, E + lane : E + lane + LANES],
            qkv[:, 2 * E + lane : 2 * E + lane + LANES],
            grad_mixed[:, span],
            heads,
            PATCHES + 1,
        )
        grads[:, span] = (query * scale).astype(low_type)
        grads[:, E + lane : E + lane + LANES] = key.astype(low_type)
        grads[:, 2 * E + lane : 2 * E + lane + LANES] = value.astype(low_type)
    vec_grad[4:5] += col_sum(grads[:, :E])
    vec_grad[5:6] += col_sum(grads[:, 2 * E :])
    rows = normed[...].T
    for part in range(3):
        piece = nn(rows, grads[:, part * E : (part + 1) * E])
        for tile in range(E // LANES):
            acc[part * (E // LANES) + tile] += piece[:, tile * LANES : (tile + 1) * LANES]
    grad_normed = nt(grads[...], weights[0, :, : 3 * E])
    unit, rate = standard(start[...])
    vec_grad[2:3] += col_sum(grad_normed * unit)
    vec_grad[3:4] += col_sum(grad_normed)
    grad_rows = standard_back(unit, rate, grad_normed * vec[2:3]) + grad_middle[...]
    kept = jnp.sum(picked[0].astype(high_type), 1, keepdims=True)
    vec_grad[1:2] += col_sum((1.0 - kept) * grad_rows)
    grad_entry[...] = nn(pick[0], grad_rows.astype(low_type)).astype(low_type)

    @pl.when(step == last)
    def _():
        rows_block = E // 4
        send_tiles(acc, blob, sem, 3 * E // LANES, rows_block, 2, 1920, rows_block)
        wait_tiles(acc, sem)


def enc_ffn_back_kernel(last, blob_in, grad_entry, latent, output, middle, normed_two, slope, active, ffn, proj, vec,
                        grad_middle, vec_grad, up_grad, entry_grad, blob,
                        grad_out, grad_down, grad_turned, source_turned, grad_source, folded, acc_up, acc_down, fold_sem, sems):
    step = pl.program_id(0)
    fold_copy = pltpu.make_async_copy(folded, blob.at[:, :, pl.ds(2688, 96)], fold_sem)
    part_rows = D // 4

    @pl.when(step == 0)
    def _():
        vec_grad[...] = jnp.zeros_like(vec_grad)
        entries = grad_entry[...]
        entry_grad[...] = col_sum(entries)
        grad_proj = tn(latent[...], entries)
        lane = lax.broadcasted_iota(jnp.int32, (96, LANES), 1)
        for part in range(4):
            for pair in range(4):
                first = grad_proj[part * 192 : part * 192 + 96, pair * LANES : (pair + 1) * LANES]
                second = grad_proj[part * 192 + 96 : part * 192 + 192, pair * LANES : (pair + 1) * LANES]
                folded[2 * pair, part] = jnp.where(lane < 64, first, pltpu.roll(second, 64, 1))
                folded[2 * pair + 1, part] = jnp.where(lane < 64, pltpu.roll(first, 64, 1), second)
        fold_copy.start()
        grad_latent = nt(entries, proj[...])
        unit, rate = standard(output[...])
        vec_grad[10:11] = col_sum(grad_latent * unit)
        vec_grad[11:12] = col_sum(grad_latent)
        rows = standard_back(unit, rate, grad_latent * vec[10:11])
        grad_out[...] = rows
        grad_down[...] = rows.astype(low_type)
        grad_turned[...] = rows.T.astype(low_type)
        source_turned[...] = normed_two[...].T
        vec_grad[9:10] = col_sum(rows.astype(low_type))
        grad_source[...] = jnp.zeros_like(grad_source)

    slot = step % 2

    @pl.when(step >= 2)
    def _():
        wait_tiles(acc_up.at[slot], sems.at[0, slot])
        wait_tiles(acc_down.at[slot], sems.at[1, slot])

    grads = grad_down[...]
    grad_up = (slope[...] * nn(grads, ffn[1])).astype(low_type)
    up_grad[...] = col_sum(grad_up)
    grad_source[...] += nt(grad_up, ffn[0])
    piece = nn(grad_turned[...], active[...])
    other = nn(source_turned[...], grad_up)
    count = grad_up.shape[1] // LANES
    for tile in range(count):
        lane = slice(tile * LANES, (tile + 1) * LANES)
        acc_down[slot, tile] = piece[:, lane]
        acc_up[slot, tile] = other[:, lane]

    def go(index, carry):
        tile, part = index // 4, index % 4
        place = step * count + tile
        block, inner = place // 3, place % 3
        rows = pl.ds(pl.multiple_of(part * part_rows, 16), part_rows)
        for number, (acc, base) in enumerate(((acc_up, 768), (acc_down, 1344))):
            pltpu.make_async_copy(
                acc.at[slot, tile, rows],
                blob.at[block, part, pl.ds(pl.multiple_of(base + inner * part_rows, 16), part_rows)],
                sems.at[number, slot],
            ).start()
        return carry

    lax.fori_loop(0, count * 4, go, 0)

    @pl.when(step == last)
    def _():
        unit, rate = standard(middle[...])
        vec_grad[7:8] = col_sum(grad_source[...] * unit)
        vec_grad[8:9] = col_sum(grad_source[...])
        grad_rows = standard_back(unit, rate, grad_source[...] * vec[7:8]) + grad_out[...]
        grad_middle[...] = grad_rows
        vec_grad[6:7] = col_sum(grad_rows.astype(low_type))
        fold_copy.wait()
        for item in (0, 1):
            wait_tiles(acc_up.at[item], sems.at[0, item])
            wait_tiles(acc_down.at[item], sems.at[1, item])


def enc_back_kernel(batch, blob_in, qkv, kept, normed, start, mixed, grad_middle, wide, vec,
                    vec_grad, blob, grads, grad_wide, tiles, sem):
    rows = ENC_ROWS
    vec_grad[...] = jnp.zeros_like(vec_grad)
    branch = grad_middle[...].astype(low_type)
    grad_mixed = nt(branch, wide[:, 4 * D :]).astype(low_type)
    grad_wide[:, 4 * D :] = tn(mixed[...], branch)
    scale = 1.0 / math.sqrt(D // HE)
    heads = LANES * HE // D
    for group in range(D // LANES):
        lane = group * LANES
        query, key, value = attend_back_many(
            batch,
            qkv[:, lane : lane + LANES],
            qkv[:, D + lane : D + lane + LANES],
            qkv[:, 2 * D + lane : 2 * D + lane + LANES],
            grad_mixed[:, lane : lane + LANES],
            heads,
            KEEP + 1,
        )
        grads[:, lane : lane + LANES] = (query * scale).astype(low_type)
        grads[:, D + lane : D + lane + LANES] = key.astype(low_type)
        grads[:, 2 * D + lane : 2 * D + lane + LANES] = value.astype(low_type)
    vec_grad[4:5] = col_sum(grads[:, :D])
    vec_grad[5:6] = col_sum(grads[:, 2 * D :])
    rows_in = normed[...].T
    for part in range(3):
        grad_wide[:, (part + 1) * D : (part + 2) * D] = nn(rows_in, grads[:, part * D : (part + 1) * D])
    width = 5 * D // 8
    tall = D // 4

    def assemble(block):
        for part in range(4):
            span = slice(part * tall, (part + 1) * tall)
            piece = grad_wide[span, block * width : (block + 1) * width]
            for tile in range(4):
                size = min(LANES, width - tile * LANES)
                value = piece[:, tile * LANES : tile * LANES + size]
                if size < LANES:
                    value = jnp.concatenate([value, jnp.zeros((tall, LANES - size), high_type)], 1)
                tiles[block, part, tile * tall : (tile + 1) * tall] = value
        pltpu.make_async_copy(tiles.at[block], blob.at[block, :, pl.ds(0, 4 * tall)], sem).start()

    for block in range(2, 8):
        assemble(block)
    grad_normed = nt(grads[...], wide[:, D : 4 * D])
    unit, rate = standard(start[...])
    vec_grad[2:3] = col_sum(grad_normed * unit)
    vec_grad[3:4] = col_sum(grad_normed)
    grad_rows = standard_back(unit, rate, grad_normed * vec[2:3]) + grad_middle[...]
    inner = lax.broadcasted_iota(jnp.int32, (grad_rows.shape[0], 1), 0) % rows
    vec_grad[1:2] = col_sum(jnp.where(inner == CLASS_ENC, grad_rows, 0.0))
    embed = jnp.where(inner < KEEP, grad_rows, 0.0).astype(low_type)
    vec_grad[0:1] = col_sum(embed)
    grad_wide[:, :D] = tn(kept[...], embed)
    assemble(0)
    assemble(1)
    wait_tiles(tiles, sem)


def adam_parts(weight, grad, first, second, decay):
    first_new = 0.5 * first + 0.5 * grad
    second_new = 0.5 * second + 0.5 * grad * grad
    bias = 1.0 - 0.5**STEP
    direction = first_new / bias / (jnp.sqrt(second_new / bias) + 1e-08)
    return weight - 0.02 * (direction + decay * weight), first_new, second_new


def adam_kernel(count, *refs):
    summed, head, small = refs[:3]
    ins, outs, loss = refs[3:24], refs[24:45], refs[45]

    def update(index, place, grad, decay=0.05):
        for target, value in zip(
            range(3), adam_parts(ins[index][place], grad, ins[7 + index][place], ins[14 + index][place], decay)
        ):
            outs[7 * target + index][place] = value

    base = 0
    for index, lead, tall, width in ((0, None, 192, 480), (1, 0, 192, 384), (1, 1, 192, 384),
                                     (3, None, 128, 256), (4, 0, 128, 256), (4, 1, 128, 256)):
        for lane in range(0, width, LANES):
            size = min(LANES, width - lane)
            place = (slice(None), slice(lane, lane + size))
            update(index, place if lead is None else (lead,) + place, summed[base : base + tall, :size])
            base += tall
    folded = summed[base : base + 96]
    turned = jnp.concatenate([folded, jnp.zeros((32, LANES), high_type)], 0).T
    update(2, (slice(None), slice(0, 96)), turned[:64, :96])
    update(2, (slice(None), slice(96, 192)), turned[64:, :96])
    update(5, (slice(None),), head[...])
    tall = ins[6].shape[0]
    update(6, (slice(None),), small[:tall], 0.0)
    loss[...] = small[tall : tall + 1, :1] / count


SMALL_ROWS = 256
SMALL_PARTS = ((12, D), (1, F), (12, E), (1, H), (1, P_SIZE))


def prepare_kernel(enc_w, enc_ffn, proj_turned, dec_w, dec_ffn, head, smalls, shuffle, patches,
                   own_enc, own_ffn, own_proj, own_dec, head_low, enc_vec, enc_up, dec_vec, dec_up, head_bias,
                   pick, picked, padded):
    own_enc[...] = enc_w[...].astype(low_type)
    own_ffn[...] = enc_ffn[...].astype(low_type)
    own_proj[...] = proj_turned[...].T.astype(low_type)
    own_dec[0] = dec_w[...].astype(low_type)
    own_dec[1] = dec_ffn[0].astype(low_type)
    own_dec[2] = dec_ffn[1].astype(low_type)
    head_low[...] = head[...].astype(low_type)
    place = 0
    for target in (enc_vec, enc_up, dec_vec, dec_up, head_bias):
        for index in range(target.shape[0]):
            for lane in range(0, target.shape[1], LANES):
                target[index : index + 1, lane : lane + LANES] = smalls[place : place + 1]
                place += 1
    slot = lax.broadcasted_iota(jnp.int32, (DEC_ROWS, ENC_ROWS), 0)
    order = lax.broadcasted_iota(jnp.int32, (DEC_ROWS, ENC_ROWS), 1)
    for image in range(patches.shape[0]):
        keep = jnp.where(order < KEEP, shuffle[image : image + 1, :ENC_ROWS], jnp.where(order == CLASS_ENC, CLASS_DEC, -1))
        chosen = jnp.where(keep == slot, 1.0, 0.0)
        picked[image] = chosen.astype(low_type)
        pick[image] = chosen.T.astype(low_type)
        padded[image, DEC_ROWS - 16 :] = jnp.zeros((16, P_SIZE), low_type)
        padded[image, :PATCHES] = patches[image]


def prepare(enc_w, enc_ffn, dec_proj, dec_w, dec_ffn, head, smalls, shuffle, patches):
    batch = patches.shape[0]
    shape = jax.ShapeDtypeStruct
    outs = [shape(item.shape, low_type) for item in (enc_w, enc_ffn, dec_proj)]
    outs += [shape((3,) + dec_w.shape, low_type), shape(head.shape, low_type)]
    outs += [shape(item, high_type) for item in SMALL_PARTS]
    outs += [
        shape((batch, ENC_ROWS, DEC_ROWS), low_type),
        shape((batch, DEC_ROWS, ENC_ROWS), low_type),
        shape((batch, DEC_ROWS, P_SIZE), low_type),
    ]
    return pl.pallas_call(
        prepare_kernel,
        out_shape=tuple(outs),
        in_specs=[whole()] * 9,
        out_specs=[whole()] * 13,
        compiler_params=params(),
        name="prepare",
    )(enc_w, enc_ffn, dec_proj.T, dec_w, dec_ffn, head, smalls.reshape(-1, LANES), shuffle, patches)


def pack_kernel(enc_one, enc_two, enc_up, dec_one, dec_two, entry, dec_up, head_bias, loss, small):
    place = 0

    def put(value):
        nonlocal place
        for index in range(value.shape[0]):
            for lane in range(0, value.shape[1], LANES):
                small[place : place + 1] = value[index : index + 1, lane : lane + LANES]
                place += 1

    put(enc_one[...] + enc_two[...])
    put(enc_up[...])
    put(entry[...])
    put(dec_one[1:] + dec_two[1:])
    put(dec_up[...])
    put(head_bias[...])
    small[place : place + 1] = loss[:1]
    place += 1
    small[place:] = jnp.zeros((SMALL_ROWS - place, LANES), high_type)


def table_of(width, rows):
    quarter = width // 4
    omega = (np.float32(1.0) / np.float32(10000.0) ** (np.arange(quarter, dtype=np.float32) / np.float32(quarter))).astype(np.float32)
    coord = np.arange(SIDE * SIDE)

    def half(place):
        angle = place.astype(np.float32)[:, None] * omega[None, :]
        return np.concatenate([np.sin(angle), np.cos(angle)], 1)

    table = np.concatenate([half(coord // SIDE), half(coord % SIDE)], 1).astype(np.float32)
    return np.concatenate([table, np.zeros((rows - table.shape[0], width), np.float32)], 0)


def whole():
    return pl.BlockSpec(memory_space=pltpu.VMEM)


def hbm():
    return pl.BlockSpec(memory_space=pltpu.HBM)


def params(**more):
    return pltpu.CompilerParams(vmem_limit_bytes=60 << 20, **more)


def by_image(*block):
    return pl.BlockSpec(block, lambda i: (i,) + (0,) * (len(block) - 1))


def fixed(*block):
    return pl.BlockSpec(block, lambda i: (0,) * len(block))


def encoder_shapes(batch):
    rows = batch * ENC_ROWS
    shape = jax.ShapeDtypeStruct
    first = (
        shape((rows, D), low_type),
        shape((rows, D), high_type),
        shape((rows, D), low_type),
        shape((rows, 3 * D), low_type),
        shape((rows, D), low_type),
        shape((rows, D), high_type),
        shape((rows, D), low_type),
    )
    second = (
        shape((rows, F), high_type),
        shape((rows, F), low_type),
        shape((rows, D), high_type),
        shape((rows, D), low_type),
    )
    return first, second


def encode_images(enc_blocks, enc_ffn, enc_vec, enc_up, pick, padded):
    batch = padded.shape[0]
    rows = batch * ENC_ROWS
    first, second = encoder_shapes(batch)
    wide = pl.pallas_call(
        wide_kernel,
        out_shape=jax.ShapeDtypeStruct((D, 5 * D), low_type),
        in_specs=[whole()],
        out_specs=whole(),
        compiler_params=params(),
        name="wide",
    )(enc_blocks)
    early = pl.pallas_call(
        functools.partial(enc_attend_kernel, batch),
        out_shape=first,
        in_specs=[whole()] * 5,
        out_specs=[whole()] * 7,
        compiler_params=params(),
        name="enc_attend",
    )(pick, padded, wide, enc_vec, jnp.asarray(table_of(D, DEC_ROWS)))
    chunk = 512
    late = pl.pallas_call(
        functools.partial(enc_ffn_kernel, F // chunk - 1),
        grid=(F // chunk,),
        out_shape=second,
        in_specs=[
            fixed(rows, D),
            fixed(rows, D),
            pl.BlockSpec((2, D, chunk), lambda i: (0, 0, i)),
            fixed(12, D),
            pl.BlockSpec((1, chunk), lambda i: (0, i)),
        ],
        out_specs=[
            pl.BlockSpec((rows, chunk), lambda i: (0, i)),
            pl.BlockSpec((rows, chunk), lambda i: (0, i)),
            fixed(rows, D),
            fixed(rows, D),
        ],
        compiler_params=params(),
        name="enc_ffn",
    )(early[5], early[6], enc_ffn, enc_vec, enc_up)
    return wide, early + tuple(late)


def local_grads(wide, enc_ffn, proj, dec3, encoded, head_low, vectors, pick, picked, padded, count):
    enc_vec, _, dec_vec, dec_up, head_bias = vectors
    kept, start, normed, qkv, mixed, middle, normed_two, slope, active, enc_out, latent = encoded
    batch = padded.shape[0]
    shape = jax.ShapeDtypeStruct
    dec_pos = jnp.asarray(table_of(E, DEC_ROWS))
    rows, dec_rows = batch * ENC_ROWS, batch * DEC_ROWS
    chunk = 512

    dec_start, dec_normed, dec_qkv, dec_mixed, dec_middle, dec_normed_two = pl.pallas_call(
        dec_attend_kernel,
        grid=(batch,),
        out_shape=(
            shape((dec_rows, E), high_type),
            shape((dec_rows, E), low_type),
            shape((dec_rows, 3 * E), low_type),
            shape((dec_rows, E), low_type),
            shape((dec_rows, E), high_type),
            shape((dec_rows, E), low_type),
        ),
        in_specs=[
            by_image(ENC_ROWS, D),
            fixed(D, E),
            by_image(1, DEC_ROWS, ENC_ROWS),
            fixed(DEC_ROWS, E),
            fixed(1, E, 4 * E),
            fixed(12, E),
        ],
        out_specs=[
            by_image(DEC_ROWS, E),
            by_image(DEC_ROWS, E),
            by_image(DEC_ROWS, 3 * E),
            by_image(DEC_ROWS, E),
            by_image(DEC_ROWS, E),
            by_image(DEC_ROWS, E),
        ],
        compiler_params=params(),
        name="dec_attend",
    )(latent, proj, picked, dec_pos, dec3, dec_vec)

    images = 2 if batch % 2 == 0 else 1
    block = images * DEC_ROWS
    blob_shape = shape((8, 4, 2784, LANES), high_type)
    vm = pltpu.VMEM
    dma = pltpu.SemaphoreType.DMA
    grad_middle, grad_mixed, grad_head, dec_grad_one, dec_up_grad, head_bias_grad, loss, blob = pl.pallas_call(
        functools.partial(dec_ffn_kernel, images, batch // images - 1, count),
        grid=(batch // images,),
        out_shape=(
            shape((dec_rows, E), high_type),
            shape((dec_rows, E), low_type),
            shape((E, P_SIZE), high_type),
            shape((12, E), high_type),
            shape((1, H), high_type),
            shape((1, P_SIZE), high_type),
            shape((8, LANES), high_type),
            blob_shape,
        ),
        in_specs=[
            by_image(block, E),
            by_image(block, E),
            by_image(block, E),
            by_image(block, P_SIZE),
            by_image(images, DEC_ROWS, ENC_ROWS),
            fixed(3, E, H),
            fixed(E, P_SIZE),
            fixed(12, E),
            fixed(1, H),
            fixed(1, P_SIZE),
        ],
        out_specs=[
            by_image(block, E),
            by_image(block, E),
            fixed(E, P_SIZE),
            fixed(12, E),
            fixed(1, H),
            fixed(1, P_SIZE),
            fixed(8, LANES),
            hbm(),
        ],
        scratch_shapes=[
            vm((block, H), low_type),
            vm((block, H), high_type),
            vm((H // LANES, E, LANES), high_type),
            vm((H // LANES, E, LANES), high_type),
            vm((E // LANES, E, LANES), high_type),
            dma((3,)),
        ],
        compiler_params=params(),
        name="dec_ffn",
    )(dec_middle, dec_normed_two, dec_mixed, padded.reshape(dec_rows, P_SIZE), picked, dec3, head_low, dec_vec, dec_up, head_bias)

    grad_entry, dec_grad_two, blob = pl.pallas_call(
        functools.partial(dec_back_kernel, batch - 1),
        grid=(batch,),
        out_shape=(shape((rows, E), low_type), shape((12, E), high_type), blob_shape),
        in_specs=[
            hbm(),
            by_image(DEC_ROWS, 3 * E),
            by_image(DEC_ROWS, E),
            by_image(DEC_ROWS, E),
            by_image(DEC_ROWS, E),
            by_image(DEC_ROWS, E),
            by_image(1, ENC_ROWS, DEC_ROWS),
            by_image(1, DEC_ROWS, ENC_ROWS),
            fixed(1, E, 4 * E),
            fixed(12, E),
        ],
        out_specs=[by_image(ENC_ROWS, E), fixed(12, E), hbm()],
        scratch_shapes=[vm((DEC_ROWS, 3 * E), low_type), vm((3 * E // LANES, E, LANES), high_type), dma],
        input_output_aliases={0: 2},
        compiler_params=params(),
        name="dec_back",
    )(blob, dec_qkv, dec_normed, dec_start, grad_middle, grad_mixed, pick, picked, dec3, dec_vec)

    enc_grad_middle, enc_grad_one, enc_up_grad, entry_grad, blob = pl.pallas_call(
        functools.partial(enc_ffn_back_kernel, F // chunk - 1),
        grid=(F // chunk,),
        out_shape=(
            shape((rows, D), high_type),
            shape((12, D), high_type),
            shape((1, F), high_type),
            shape((1, E), high_type),
            blob_shape,
        ),
        in_specs=[
            hbm(),
            fixed(rows, E),
            fixed(rows, D),
            fixed(rows, D),
            fixed(rows, D),
            fixed(rows, D),
            pl.BlockSpec((rows, chunk), lambda i: (0, i)),
            pl.BlockSpec((rows, chunk), lambda i: (0, i)),
            pl.BlockSpec((2, D, chunk), lambda i: (0, 0, i)),
            fixed(D, E),
            fixed(12, D),
        ],
        out_specs=[
            fixed(rows, D),
            fixed(12, D),
            pl.BlockSpec((1, chunk), lambda i: (0, i)),
            fixed(1, E),
            hbm(),
        ],
        scratch_shapes=[
            vm((rows, D), high_type),
            vm((rows, D), low_type),
            vm((D, rows), low_type),
            vm((D, rows), low_type),
            vm((rows, D), high_type),
            vm((8, 4, 96, LANES), high_type),
            vm((2, chunk // LANES, D, LANES), high_type),
            vm((2, chunk // LANES, D, LANES), high_type),
            dma,
            dma((2, 2)),
        ],
        input_output_aliases={0: 4},
        compiler_params=params(),
        name="enc_ffn_back",
    )(blob, grad_entry, latent, enc_out, middle, normed_two, slope, active, enc_ffn, proj, enc_vec)
    enc_grad_two, blob = pl.pallas_call(
        functools.partial(enc_back_kernel, batch),
        out_shape=(shape((12, D), high_type), blob_shape),
        in_specs=[hbm()] + [whole()] * 8,
        out_specs=[whole(), hbm()],
        scratch_shapes=[
            vm((rows, 3 * D), low_type),
            vm((D, 5 * D), high_type),
            vm((8, 4, D, LANES), high_type),
            dma,
        ],
        input_output_aliases={0: 1},
        compiler_params=params(),
        name="enc_back",
    )(blob, qkv, kept, normed, start, mixed, enc_grad_middle, wide, enc_vec)
    small = pl.pallas_call(
        pack_kernel,
        out_shape=shape((SMALL_ROWS, LANES), high_type),
        in_specs=[whole()] * 9,
        out_specs=whole(),
        compiler_params=params(),
        name="pack",
    )(enc_grad_one, enc_grad_two, enc_up_grad, dec_grad_one, dec_grad_two, entry_grad, dec_up_grad, head_bias_grad, loss)
    return blob, grad_head, small


def untile(block, rows, width):
    tiles = -(-width // LANES)
    return block.reshape(tiles, rows, LANES).transpose(1, 0, 2).reshape(rows, tiles * LANES)[:, :width]


def unfold_proj(block):
    width = block.shape[1] // 2
    return jnp.concatenate([block[:, :width], block[:, width:]], 0)


def unpack_shards(blob):
    cuts = [0, 768, 576, 576, 256, 256, 256, 96]
    places = [sum(cuts[: index + 1]) for index in range(len(cuts))]
    piece = [blob[places[index] : places[index + 1]] for index in range(7)]
    return (
        untile(piece[0], 192, 480),
        jnp.stack([untile(piece[1], 192, 384), untile(piece[2], 192, 384)]),
        unfold_proj(piece[6]),
        untile(piece[3], 128, 256),
        jnp.stack([untile(piece[4], 128, 256), untile(piece[5], 128, 256)]),
    )


def whole_arrays(blob):
    col_size, row_size = blob.shape[:2]
    parts = jax.vmap(jax.vmap(unpack_shards))(blob)

    def joined(array):
        if array.ndim == 4:
            return array.transpose(1, 2, 0, 3).reshape(row_size * array.shape[2], col_size * array.shape[3])
        return array.transpose(2, 1, 3, 0, 4).reshape(2, row_size * array.shape[3], col_size * array.shape[4])

    return tuple(joined(item) for item in parts)


def on_small_plane():
    return lax.axis_size("row") == 4 and lax.axis_size("col") == 8


def gather_and_encode(shards, enc_vec, enc_up, pick, padded):
    if on_small_plane():
        ffn, proj, dec, wide, encoded = gather_encode(
            *shards, lax.axis_size("col") // 2, pick, padded, enc_vec, enc_up
        )
        return wide, ffn, proj.transpose(1, 0, 2).reshape(D, E), dec, encoded
    full = []
    for item in shards:
        rowed = lax.all_gather(item, "row", axis=item.ndim - 2, tiled=True)
        full.append(lax.all_gather(rowed, "col", axis=item.ndim - 1, tiled=True))
    blocks = full[0].reshape(D, 8, 5 * D // 8).transpose(1, 0, 2)
    wide, encoded = encode_images(blocks, full[1], enc_vec, enc_up, pick, padded)
    return wide, full[1], full[2], full[3], encoded


def apply_updates(blob, grad_head, small, count, params_now, firsts, seconds):
    summed_head = lax.psum(grad_head, ("row", "col"))
    if on_small_plane():
        summed, small = reduce_blocks(blob, small.reshape(32, 8, LANES), lax.axis_size("col") // 2, 6)
        flat = lambda group: group[:2] + (group[2].T,) + group[3:6] + (group[6].reshape(-1, LANES),)
        ins = flat(params_now) + flat(firsts) + flat(seconds)
        shape = jax.ShapeDtypeStruct
        outs = pl.pallas_call(
            functools.partial(adam_kernel, count),
            out_shape=tuple(shape(item.shape, high_type) for item in ins) + (shape((1, 1), high_type),),
            in_specs=[whole()] * 24,
            out_specs=[whole()] * 22,
            compiler_params=params(),
            name="adam",
        )(summed, summed_head, small.reshape(SMALL_ROWS, LANES), *ins)
        back = {2: lambda item: item.T, 6: lambda item: item.reshape(-1)}
        return [back.get(index % 7, lambda item: item)(item) for index, item in enumerate(outs[:21])], outs[21].reshape(())
    shards = []
    for item in whole_arrays(blob):
        done = lax.psum_scatter(item, "col", scatter_dimension=item.ndim - 1, tiled=True)
        shards.append(lax.psum_scatter(done, "row", scatter_dimension=item.ndim - 2, tiled=True))
    small = lax.psum(small, ("row", "col")).reshape(-1)
    size = params_now[6].shape[0]
    grads = tuple(shards) + (summed_head, small[:size])
    decays = (0.05,) * 6 + (0.0,)
    results = [adam_parts(*item) for item in zip(params_now, grads, firsts, seconds, decays)]
    return [item[kind] for kind in range(3) for item in results], small[size] / count


def body(
    patches,
    shuffle,
    enc_w,
    enc_ffn,
    dec_proj,
    dec_w,
    dec_ffn,
    head_w,
    smalls,
    first_enc_w,
    first_enc_ffn,
    first_dec_proj,
    first_dec_w,
    first_dec_ffn,
    first_head_w,
    first_smalls,
    second_enc_w,
    second_enc_ffn,
    second_dec_proj,
    second_dec_w,
    second_dec_ffn,
    second_head_w,
    second_smalls,
):
    prepared = prepare(enc_w, enc_ffn, dec_proj, dec_w, dec_ffn, head_w, smalls, shuffle, patches)
    shards, head_low, vectors, (pick, picked, padded) = prepared[:4], prepared[4], prepared[5:10], prepared[10:]
    wide, ffn, proj, dec, encoded = gather_and_encode(shards, vectors[0], vectors[1], pick, padded)
    count = patches.shape[0] * lax.axis_size("row") * lax.axis_size("col") * (PATCHES - KEEP) * P_SIZE
    blob, grad_head, small = local_grads(
        wide, ffn, proj, dec, encoded, head_low, vectors, pick, picked, padded, count
    )
    params_now = (enc_w, enc_ffn, dec_proj, dec_w, dec_ffn, head_w, smalls)
    firsts = (
        first_enc_w,
        first_enc_ffn,
        first_dec_proj,
        first_dec_w,
        first_dec_ffn,
        first_head_w,
        first_smalls,
    )
    seconds = (
        second_enc_w,
        second_enc_ffn,
        second_dec_proj,
        second_dec_w,
        second_dec_ffn,
        second_head_w,
        second_smalls,
    )
    outs, loss = apply_updates(blob, grad_head, small, count, params_now, firsts, seconds)
    return tuple(outs) + (loss,)


def solution(mesh):
    in_specs = (
        P(("row", "col"), None, None),
        P(("row", "col"), None),
        P("row", "col"),
        P(None, "row", "col"),
        P("row", "col"),
        P("row", "col"),
        P(None, "row", "col"),
        P(),
        P(),
        P("row", "col"),
        P(None, "row", "col"),
        P("row", "col"),
        P("row", "col"),
        P(None, "row", "col"),
        P(),
        P(),
        P("row", "col"),
        P(None, "row", "col"),
        P("row", "col"),
        P("row", "col"),
        P(None, "row", "col"),
        P(),
        P(),
    )
    out_specs = (
        P("row", "col"),
        P(None, "row", "col"),
        P("row", "col"),
        P("row", "col"),
        P(None, "row", "col"),
        P(),
        P(),
        P("row", "col"),
        P(None, "row", "col"),
        P("row", "col"),
        P("row", "col"),
        P(None, "row", "col"),
        P(),
        P(),
        P("row", "col"),
        P(None, "row", "col"),
        P("row", "col"),
        P("row", "col"),
        P(None, "row", "col"),
        P(),
        P(),
        P(),
    )
    return jax.shard_map(body, mesh=mesh, in_specs=in_specs, out_specs=out_specs, check_vma=False)
```

```python
import functools
import math

import jax
import jax.numpy as jnp
import numpy as np
from jax import lax
from jax.experimental import pallas as pl
from jax.experimental.pallas import tpu as pltpu
from jax.sharding import PartitionSpec as P

D = 768
HE = 12
F = 3072
E = 512
HD = 16
H = 2048
P_SIZE = 768
SIDE = 14
KEEP = 49
STEP = 5
PATCHES = 196
LANES = 128

norm_eps = 1e-06
low_type = jnp.bfloat16
high_type = jnp.float32


MESH = pl.DeviceIdType.MESH
LAGS = (2, 4, 6)


class Group:
    def __init__(self, copies):
        self.copies = copies

    def start(self):
        for item in self.copies:
            item.start()

    def wait_recv(self):
        for item in self.copies:
            item.wait_recv()

    def wait_send(self):
        for item in self.copies:
            item.wait_send()

    def wait(self):
        for item in self.copies:
            item.wait()


def gather_steps(depth, place_ids, own, cut, sems):
    row, row_x, row_y, row_d, z, k, near_x, near_y, twin, lower, upper, has_lower, has_upper = place_ids
    zs, zr, xs, xr, ys, yr, dxs, dxr, dys, dyr, cs, cr = sems
    levels = [(0, 0)] + [(d, way) for d in range(1, depth) for way in (0, 1)]
    level_of = {item: number for number, item in enumerate(levels)}

    def place(level):
        d, way = level
        return z - d if way == 0 else z + d

    def valid(level):
        d, way = level
        return z - d >= 0 if way == 0 else z + d < depth

    def slot(level, row_now, half=None):
        return cut(place(level) * 2 + k, row_now, half)

    def source(level):
        return own if level == (0, 0) else slot(level, row)

    def copy(src, dst, send, recv, target):
        return Group(
            [
                pltpu.make_async_remote_copy(
                    src_ref=src[item],
                    dst_ref=dst[item],
                    send_sem=send.at[item],
                    recv_sem=recv.at[item],
                    device_id=target,
                    device_id_type=MESH,
                )
                for item in range(len(own))
            ]
        )

    def z_copy(level, way):
        d = level[0]
        n = level_of[level]
        return copy(source(level), slot(level, row), zs.at[n, way], zr.at[d, way], upper if way == 0 else lower)

    def x_copy(level):
        n = level_of[level]
        return copy(source(level), slot(level, row), xs.at[n], xr.at[n], near_x)

    def y_copy(level):
        n = level_of[level]
        return copy(source(level), slot(level, row), ys.at[n], yr.at[n], near_y)

    def dx_copy(level):
        n = level_of[level]
        refs = slot(level, row_y, 1)
        return copy(refs, refs, dxs.at[n], dxr.at[n], near_x)

    def dy_copy(level):
        n = level_of[level]
        refs = slot(level, row_x, 0)
        return copy(refs, refs, dys.at[n], dyr.at[n], near_y)

    def twin_copy(level, kind):
        n = level_of[level]
        row_now = (row, row_x, row_y, row_d)[kind]
        src = source(level) if kind == 0 else slot(level, row_now)
        return copy(src, slot(level, row_now), cs.at[n, kind], cr.at[n, kind], twin)

    def guarded(level, action):
        if level == (0, 0):
            action()
        else:
            pl.when(valid(level))(action)

    def spread(level):
        d, way = level

        def action():
            if level != (0, 0):
                z_copy((d - 1, way if d > 1 else 0), way).wait_recv()
            for direction in (0, 1):
                if level == (0, 0) or direction == way:
                    @pl.when(has_upper if direction == 0 else has_lower)
                    def _():
                        z_copy(level, direction).start()
            x_copy(level).start()
            y_copy(level).start()
            twin_copy(level, 0).start()

        guarded(level, action)

    def turn(level):
        def action():
            x_copy(level).wait_recv()
            dy_copy(level).start()
            twin_copy(level, 1).start()
            y_copy(level).wait_recv()
            dx_copy(level).start()
            twin_copy(level, 2).start()

        guarded(level, action)

    def close(level):
        def action():
            dx_copy(level).wait_recv()
            dy_copy(level).wait_recv()
            twin_copy(level, 3).start()

        guarded(level, action)

    def drain(level):
        d, way = level

        def action():
            for direction in (0, 1):
                if level == (0, 0) or direction == way:
                    @pl.when(has_upper if direction == 0 else has_lower)
                    def _():
                        z_copy(level, direction).wait_send()
            x_copy(level).wait_send()
            y_copy(level).wait_send()
            dx_copy(level).wait_send()
            dy_copy(level).wait_send()
            for kind in range(4):
                twin_copy(level, kind).wait()

        guarded(level, action)

    def step_action(step):
        for level in levels:
            if level[0] == step:
                spread(level)
        for level in levels:
            if level[0] == step - 1:
                turn(level)
        for level in levels:
            if level[0] == step - 2:
                close(level)

    def finish():
        for level in levels:
            drain(level)

    return step_action, finish


def gather_steps_late(depth, place_ids, own, cut, sems):
    row, row_x, row_y, row_d, z, k, near_x, near_y, twin, lower, upper, has_lower, has_upper = place_ids
    zs, zr, xs, xr, ys, yr, dxs, dxr, dys, dyr, cs, cr = sems
    kinds = (row, row_x, row_y, row_d)
    levels = [(0, 0)] + [(d, way) for d in range(1, depth) for way in (0, 1)]
    level_of = {item: number for number, item in enumerate(levels)}

    def refs(level, kind, half=None):
        d, way = level
        return cut((z - d if way == 0 else z + d) * 2 + k, kinds[kind], half)

    def valid(level):
        d, way = level
        return z - d >= 0 if way == 0 else z + d < depth

    def copy(src, dst, send, recv, target):
        return Group(
            [
                pltpu.make_async_remote_copy(
                    src_ref=src[item],
                    dst_ref=dst[item],
                    send_sem=send.at[item],
                    recv_sem=recv.at[item],
                    device_id=target,
                    device_id_type=MESH,
                )
                for item in range(len(own))
            ]
        )

    home = (0, 0)

    def source(level, kind):
        return own if level == home and kind == 0 else refs(level, kind)

    def x_copy():
        return copy(own, refs(home, 0), xs, xr, near_x)

    def y_copy():
        return copy(own, refs(home, 0), ys, yr, near_y)

    def dx_copy():
        return copy(refs(home, 2, 1), refs(home, 2, 1), dxs, dxr, near_x)

    def dy_copy():
        return copy(refs(home, 1, 0), refs(home, 1, 0), dys, dyr, near_y)

    def z_copy(level, way, kind):
        d = level[0]
        target = upper if way == 0 else lower
        return copy(source(level, kind), refs(level, kind), zs.at[d, way, kind], zr.at[d, way, kind], target)

    def twin_copy(level, kind):
        n = level_of[level]
        return copy(source(level, kind), refs(level, kind), cs.at[n, kind], cr.at[n, kind], twin)

    def outward(level, kind, action):
        for way in (0, 1):
            if (level == home or way == level[1]) and level[0] < depth - 1:
                @pl.when(has_upper if way == 0 else has_lower)
                def _():
                    action(z_copy(level, way, kind))

    def pass_on(level, kind):
        outward(level, kind, lambda item: item.start())
        twin_copy(level, kind).start()

    def arrive(level, kind):
        d, way = level

        @pl.when(valid(level))
        def _():
            z_copy((d - 1, way if d > 1 else 0), way, kind).wait_recv()
            pass_on(level, kind)

    delay = (0, 1, 1, 2)

    def step_action(step):
        if step == 0:
            x_copy().start()
            y_copy().start()
            pass_on(home, 0)
        if step == 1:
            x_copy().wait_recv()
            dy_copy().start()
            pass_on(home, 1)
            y_copy().wait_recv()
            dx_copy().start()
            pass_on(home, 2)
        if step == 2:
            dx_copy().wait_recv()
            dy_copy().wait_recv()
            pass_on(home, 3)
        for level in levels[1:]:
            for kind in range(4):
                if step == level[0] + delay[kind]:
                    arrive(level, kind)

    def finish():
        for item in (x_copy(), y_copy(), dx_copy(), dy_copy()):
            item.wait_send()
        for level in levels:
            def action():
                for kind in range(4):
                    outward(level, kind, lambda item: item.wait_send())
                    twin_copy(level, kind).wait()

            if level == home:
                action()
            else:
                pl.when(valid(level))(action)

    return step_action, finish


def gather_encode_kernel(depth, batch, own_enc, own_ffn, own_proj, own_dec, pick, patches, vec, up_bias, pos,
                         ffn, proj, dec, wide_out, *rest):
    outs, rest = rest[:11], rest[11:]
    blocks, wide, ffn_here = rest[:3]
    held = rest[3:14]
    kept, start, normed, qkv, mixed, middle, normed_two, slope, active, output, latent = held
    first_sems, second_sems, late_sems = rest[14:26], rest[26:38], rest[38:50]
    local, load_sem, wide_sem, out_sems = rest[50:]
    row = lax.axis_index("row")
    col = lax.axis_index("col")
    y, x, z, k = row // 2, row % 2, col // 2, col % 2
    row_x = y * 2 + (1 - x)
    row_y = (1 - y) * 2 + x
    row_d = (1 - y) * 2 + (1 - x)
    near_x, near_y = (row_x, col), (row_y, col)
    twin = (row, z * 2 + (1 - k))
    lower, upper = (row, col - 2), (row, col + 2)
    has_lower, has_upper = z > 0, z < depth - 1

    barrier = pltpu.get_barrier_semaphore()
    for other in (near_x, near_y, twin):
        pl.semaphore_signal(barrier, inc=1, device_id=other, device_id_type=MESH)

    @pl.when(has_lower)
    def _():
        pl.semaphore_signal(barrier, inc=1, device_id=lower, device_id_type=MESH)

    @pl.when(has_upper)
    def _():
        pl.semaphore_signal(barrier, inc=1, device_id=upper, device_id_type=MESH)

    pl.semaphore_wait(barrier, 3 + jnp.where(has_lower, 1, 0) + jnp.where(has_upper, 1, 0))
    ids = (row, row_x, row_y, row_d, z, k, near_x, near_y, twin, lower, upper, has_lower, has_upper)
    tall, short = own_enc.shape[0], own_dec.shape[1]
    broad, thin = own_ffn.shape[2], own_dec.shape[2]

    early = tall - 32

    def rows_of(row_now, size, half, start=0, count=None):
        count = size if count is None else count
        part = count if half is None else count // 2
        first = start if half is None else start + half * part
        return pl.ds(pl.multiple_of(row_now * size + first, 16), part)

    def enc_refs(index, rows):
        return blocks.at[index, rows], ffn.at[:, rows, pl.ds(pl.multiple_of(index * broad, LANES), broad)]

    def cut_first(index, row_now, half=None):
        return enc_refs(index, rows_of(row_now, tall, half, 0, early))

    def cut_late(index, row_now, half=None):
        return enc_refs(index, rows_of(row_now, tall, half, early, tall - early))

    def cut_second(index, row_now, half=None):
        return (
            proj.at[index, rows_of(row_now, tall, half)],
            dec.at[:, rows_of(row_now, short, half), pl.ds(pl.multiple_of(index * thin, LANES), thin)],
        )

    own_second = (own_proj, own_dec)
    own_first = (own_enc.at[pl.ds(0, early)], own_ffn.at[:, pl.ds(0, early)])
    own_late = (own_enc.at[pl.ds(early, tall - early)], own_ffn.at[:, pl.ds(early, tall - early)])
    step_first, finish_first = gather_steps(depth, ids, own_first, cut_first, first_sems)
    step_late, finish_late = gather_steps_late(depth, ids, own_late, cut_late, late_sems)
    step_second, finish_second = gather_steps(depth, ids, own_second, cut_second, second_sems)
    keep = [
        pltpu.make_async_copy(src, dst, local.at[item])
        for item, (src, dst) in enumerate(
            zip(own_first + own_late + own_second, cut_first(col, row) + cut_late(col, row) + cut_second(col, row))
        )
    ]
    for item in keep:
        item.start()
    for step in range(depth + 1):
        step_first(step)
        step_late(step)
    step_second(0)
    step_first(depth + 1)
    step_late(depth + 1)
    finish_first()
    finish_late()
    for item in keep:
        item.wait()
    load = pltpu.make_async_copy(ffn, ffn_here, load_sem)
    load.start()
    count, _, width = blocks.shape

    def assemble(first, last):
        for index in range(first, last):
            wide[:, index * width : (index + 1) * width] = blocks[index]

    def flush(index):
        return pltpu.make_async_copy(held[index], outs[index], out_sems.at[index])

    assemble(0, count // 2)
    step_second(1)
    assemble(count // 2, count)
    wide_copy = pltpu.make_async_copy(wide, wide_out, wide_sem)
    wide_copy.start()
    enc_embed(batch, pick, patches, wide, vec, pos, kept, start)
    flush(0).start()
    flush(1).start()
    step_second(2)
    enc_project(wide, vec, start, normed, qkv)
    flush(2).start()
    flush(3).start()
    enc_mix(batch, qkv, mixed)
    flush(4).start()
    step_second(3)
    enc_join(wide, vec, start, mixed, middle, normed_two)
    flush(5).start()
    flush(6).start()
    load.wait()
    total = middle[...] + vec[9:10]
    source = normed_two[...]
    step = 512
    for place in range(0, F, step):
        span = slice(place, place + step)
        value, gain = gelu_pair(nn(source, ffn_here[0, :, span]) + up_bias[:, span])
        slope[:, span] = gain
        value = value.astype(low_type)
        active[:, span] = value
        total = total + nt(value, ffn_here[1, :, span])
        if place == 2 * step:
            step_second(4)
    flush(7).start()
    flush(8).start()
    step_second(5)
    output[...] = total
    unit, _ = standard(total)
    latent[...] = (unit * vec[10:11] + vec[11:12]).astype(low_type)
    flush(9).start()
    flush(10).start()
    for step in range(6, depth + 2):
        step_second(step)
    finish_second()
    wide_copy.wait()
    for index in range(11):
        flush(index).wait()


def gather_encode(own_enc, own_ffn, own_proj, own_dec, depth, pick, padded, vec, up_bias):
    count = 2 * depth - 1
    cols = 2 * depth
    dma = pltpu.SemaphoreType.DMA
    tall, width = own_enc.shape
    shape = jax.ShapeDtypeStruct
    kind = own_enc.dtype
    batch = padded.shape[0]
    first, second = encoder_shapes(batch)
    made = first + second
    sems = [dma((count, 2, 2)), dma((depth, 2, 2))] + [dma((count, 2)) for _ in range(8)]
    sems = sems + [dma((count, 4, 2)), dma((count, 4, 2))]
    outs = pl.pallas_call(
        functools.partial(gather_encode_kernel, depth, batch),
        out_shape=(
            shape((2, 4 * tall, cols * own_ffn.shape[2]), kind),
            shape((cols, 4 * tall, own_proj.shape[1]), kind),
            shape((3, 4 * own_dec.shape[1], cols * own_dec.shape[2]), kind),
            shape((D, 5 * D), kind),
        )
        + made,
        in_specs=[hbm()] * 4 + [whole()] * 5,
        out_specs=[hbm()] * 15,
        scratch_shapes=[
            pltpu.VMEM((cols, 4 * tall, width), kind),
            pltpu.VMEM((D, 5 * D), kind),
            pltpu.VMEM((2, D, F), kind),
        ]
        + [pltpu.VMEM(item.shape, item.dtype) for item in made]
        + sems
        + sems
        + [dma((depth, 2, 4, 2)), dma((depth, 2, 4, 2))]
        + [dma((2,)) for _ in range(8)]
        + [dma((count, 4, 2)), dma((count, 4, 2))]
        + [dma((6,)), dma, dma, dma((11,))],
        compiler_params=pltpu.CompilerParams(
            collective_id=0, has_side_effects=True, vmem_limit_bytes=60 << 20
        ),
        name="gather_encode",
    )(own_enc, own_ffn, own_proj, own_dec, pick, padded, vec, up_bias, jnp.asarray(table_of(D, DEC_ROWS)))
    ffn, proj, dec, wide = outs[:4]
    return ffn, proj, dec, wide, tuple(outs[4:])


def far_first(depth):
    orders = []
    for z in range(depth):
        orders.append(sorted(range(depth), key=lambda t: (-abs(t - z), -abs(2 * t - depth + 1))))
    return orders


code_type = jnp.int16
code_top = 32767.0


def encode(values):
    peak = jnp.max(jnp.abs(values), axis=0, keepdims=True)
    unit = jnp.maximum(peak, 1e-30) * (1.0 / code_top)
    codes = jnp.round(values * (1.0 / unit))
    codes = jnp.clip(codes, -code_top, code_top)
    return codes.astype(jnp.int32).astype(code_type), unit


def decode(codes, unit):
    return codes.astype(jnp.int32).astype(high_type) * unit


def reduce_kernel(depth, devices, cols, parts, chunk, half, blob, small, out, small_out,
                  arrived, mine, stage_x, stage_y, recv_x, recv_y, turn_x, turn_y, back_x, back_y, line_out, line,
                  units_out, units_in, line_units, box,
                  s_load, s_cs, s_cr, s_xs, s_xr, s_ys, s_yr, s_txs, s_txr, s_tys, s_tyr, s_zs, s_zr,
                  u_xs, u_xr, u_ys, u_yr, u_txs, u_txr, u_tys, u_tyr, u_zs, u_zr,
                  s_ps, s_pr, s_qs, s_qr):
    row = lax.axis_index("row")
    col = lax.axis_index("col")
    y, x, z, k = row // 2, row % 2, col // 2, col % 2
    me = row * cols + col
    near_x, near_y = (y * 2 + (1 - x), col), ((1 - y) * 2 + x, col)
    twin = (row, z * 2 + (1 - k))
    lower, upper = (row, col - 2), (row, col + 2)
    has_lower, has_upper = z > 0, z < depth - 1
    steps = depth * parts
    slots = mine.shape[0]
    ahead = slots - 1
    a_rows, b_rows = pl.ds(0, half), pl.ds(half, chunk - half)

    def device(offset):
        index = (me + offset) % devices
        return (index // cols, index % cols)

    barrier = pltpu.get_barrier_semaphore()
    for offset in range(1, devices):
        pl.semaphore_signal(barrier, inc=1, device_id=device(offset), device_id_type=MESH)
    pl.semaphore_wait(barrier, devices - 1)

    def copy(src, dst, send, recv, target):
        return pltpu.make_async_remote_copy(
            src_ref=src, dst_ref=dst, send_sem=send, recv_sem=recv, device_id=target, device_id_type=MESH
        )

    orders = far_first(depth)

    def goal(t):
        turn = t // parts
        value = 0
        for a in range(depth):
            for b in range(depth):
                value = jnp.where((z == a) & (turn == b), orders[a][b], value)
        return value

    def span(t):
        return pl.ds(pl.multiple_of((t % parts) * chunk, 16), chunk)

    def load(t):
        return pltpu.make_async_copy(
            blob.at[goal(t) * 2 + k, :, span(t)], mine.at[t % slots], s_load.at[t % slots]
        )

    def core(t):
        return copy(blob.at[goal(t) * 2 + (1 - k), :, span(t)], arrived.at[t], s_cs.at[t], s_cr.at[t], twin)

    def paired(kind, src, dst, send, recv, unit_send, unit_recv, target):
        def make(t):
            return Group([
                copy(src.at[t], dst.at[t], send.at[t], recv.at[t], target),
                copy(units_out.at[t, kind], units_in.at[t, kind], unit_send.at[t], unit_recv.at[t], target),
            ])

        return make

    first_x = paired(0, stage_x, recv_x, s_xs, s_xr, u_xs, u_xr, near_x)
    first_y = paired(1, stage_y, recv_y, s_ys, s_yr, u_ys, u_yr, near_y)
    second_x = paired(2, turn_x, back_x, s_txs, s_txr, u_txs, u_txr, near_x)
    second_y = paired(3, turn_y, back_y, s_tys, s_tyr, u_tys, u_tyr, near_y)

    def along(t, index, target):
        return Group([
            copy(line_out.at[t], line.at[index], s_zs.at[t], s_zr.at[index], target),
            copy(units_out.at[t, 4], line_units.at[index], u_zs.at[t], u_zr.at[index], target),
        ])

    def upper_index(t):
        return (goal(t) + 1) * parts + t % parts

    def lower_index(t):
        return goal(t) * parts + t % parts

    def to_upper(t):
        return along(t, upper_index(t), upper)

    def to_lower(t):
        return along(t, lower_index(t), lower)

    def small_send(offset):
        target = device(offset)
        return copy(small.at[target[0] * cols + target[1]], box.at[offset], s_ps.at[offset], s_pr.at[offset], target)

    def small_back(offset):
        return copy(small_out.at[me], small_out.at[me], s_qs.at[offset], s_qr.at[offset], device(offset))

    def small_back_recv(offset):
        origin = (me + devices - offset) % devices
        return copy(small_out.at[origin], small_out.at[origin], s_qs.at[offset], s_qr.at[offset], device(offset))

    for t in range(ahead):
        load(t).start()
        core(t).start()
    for offset in range(1, devices):
        small_send(offset).start()

    def stage_one(t):
        load(t).wait()
        core(t).wait_recv()
        slot = t % slots
        for other in (0, 1):
            away = other * 2 + (1 - x)
            stay = other * 2 + x
            codes, unit = encode(mine[slot, away, a_rows] + arrived[t, away, a_rows])
            stage_x[t, other] = codes
            units_out[t, 0, pl.ds(other, 1)] = unit
            arrived[t, stay, a_rows] += mine[slot, stay, a_rows]
        first_x(t).start()
        for other in (0, 1):
            away = (1 - y) * 2 + other
            stay = y * 2 + other
            codes, unit = encode(mine[slot, away, b_rows] + arrived[t, away, b_rows])
            stage_y[t, other] = codes
            units_out[t, 1, pl.ds(other, 1)] = unit
            arrived[t, stay, b_rows] += mine[slot, stay, b_rows]
        first_y(t).start()

    def stage_two(t):
        first_x(t).wait_recv()
        away = (1 - y) * 2 + x
        codes, unit = encode(arrived[t, away, a_rows] + decode(recv_x[t, 1 - y], units_in[t, 0, pl.ds(1 - y, 1)]))
        turn_y[t] = codes
        units_out[t, 3, pl.ds(0, 1)] = unit
        second_y(t).start()
        arrived[t, row, a_rows] += decode(recv_x[t, y], units_in[t, 0, pl.ds(y, 1)])
        first_y(t).wait_recv()
        away = y * 2 + (1 - x)
        codes, unit = encode(arrived[t, away, b_rows] + decode(recv_y[t, 1 - x], units_in[t, 1, pl.ds(1 - x, 1)]))
        turn_x[t] = codes
        units_out[t, 2, pl.ds(0, 1)] = unit
        second_x(t).start()
        arrived[t, row, b_rows] += decode(recv_y[t, x], units_in[t, 1, pl.ds(x, 1)])

    def stage_three(t):
        second_y(t).wait_recv()
        arrived[t, row, a_rows] += decode(back_y[t], units_in[t, 3, pl.ds(0, 1)])
        second_x(t).wait_recv()
        arrived[t, row, b_rows] += decode(back_x[t], units_in[t, 2, pl.ds(0, 1)])

    def take(index):
        return decode(line[index], line_units[index, pl.ds(0, 1)])

    def pack(t):
        codes, unit = encode(arrived[t, row])
        line_out[t] = codes
        units_out[t, 4, pl.ds(0, 1)] = unit

    def stage_four(t):
        target = goal(t)

        @pl.when((target >= z) & has_lower)
        def _():
            to_upper(t).wait_recv()
            arrived[t, row] += take(upper_index(t))

        @pl.when((target <= z) & has_upper)
        def _():
            to_lower(t).wait_recv()
            arrived[t, row] += take(lower_index(t))

        @pl.when(target != z)
        def _():
            pack(t)

        @pl.when(target > z)
        def _():
            to_upper(t).start()

        @pl.when(target < z)
        def _():
            to_lower(t).start()

        @pl.when(target == z)
        def _():
            out[span(t)] = arrived[t, row]

    lags = LAGS

    def body(i, carry):
        @pl.when(i + ahead < steps)
        def _():
            load(i + ahead).start()
            core(i + ahead).start()

        @pl.when(i < steps)
        def _():
            stage_one(i)

        for lag, stage in zip(lags, (stage_two, stage_three, stage_four)):
            @pl.when((i >= lag) & (i - lag < steps))
            def _():
                stage(i - lag)

        @pl.when(i == steps // 2)
        def _():
            total = small[me]
            for offset in range(1, devices):
                small_send(offset).wait_recv()
                total = total + box[offset]
            small_out[me] = total
            for offset in range(1, devices):
                small_back(offset).start()

        return carry

    lax.fori_loop(0, steps + lags[-1], body, 0)

    def finish(t, carry):
        core(t).wait_send()
        first_x(t).wait_send()
        first_y(t).wait_send()
        second_x(t).wait_send()
        second_y(t).wait_send()

        @pl.when(goal(t) > z)
        def _():
            to_upper(t).wait_send()

        @pl.when(goal(t) < z)
        def _():
            to_lower(t).wait_send()

        return carry

    lax.fori_loop(0, steps, finish, 0)
    for offset in range(1, devices):
        small_send(offset).wait_send()
        small_back(offset).wait_send()
        small_back_recv(offset).wait_recv()


def reduce_blocks(blob, small, depth, parts):
    cols, _, rows, lanes = blob.shape
    devices = 4 * cols
    chunk = rows // parts
    half = -(-chunk // 32) * 16
    rest = chunk - half
    steps = depth * parts
    lines = (depth + 1) * parts
    dma = pltpu.SemaphoreType.DMA
    vm = pltpu.VMEM
    return pl.pallas_call(
        functools.partial(reduce_kernel, depth, devices, cols, parts, chunk, half),
        out_shape=(
            jax.ShapeDtypeStruct((rows, lanes), high_type),
            jax.ShapeDtypeStruct(small.shape, high_type),
        ),
        in_specs=[pl.BlockSpec(memory_space=pltpu.HBM), pl.BlockSpec(memory_space=pltpu.VMEM)],
        out_specs=[pl.BlockSpec(memory_space=pltpu.VMEM)] * 2,
        scratch_shapes=[
            vm((steps, 4, chunk, lanes), high_type),
            vm((4, 4, chunk, lanes), high_type),
            vm((steps, 2, half, lanes), code_type),
            vm((steps, 2, rest, lanes), code_type),
            vm((steps, 2, half, lanes), code_type),
            vm((steps, 2, rest, lanes), code_type),
            vm((steps, rest, lanes), code_type),
            vm((steps, half, lanes), code_type),
            vm((steps, rest, lanes), code_type),
            vm((steps, half, lanes), code_type),
            vm((steps, chunk, lanes), code_type),
            vm((lines, chunk, lanes), code_type),
            vm((steps, 5, 8, lanes), high_type),
            vm((steps, 4, 8, lanes), high_type),
            vm((lines, 8, lanes), high_type),
            vm((devices,) + small.shape[1:], high_type),
            dma((4,)),
        ]
        + ([dma((steps,)) for _ in range(11)] + [dma((lines,))])
        + ([dma((steps,)) for _ in range(9)] + [dma((lines,))])
        + [dma((devices,)) for _ in range(4)],
        compiler_params=pltpu.CompilerParams(
            collective_id=1, has_side_effects=True, vmem_limit_bytes=62 << 20
        ),
        name="reduce_blocks",
    )(blob, small)


ENC_ROWS = 64
DEC_ROWS = 208
CLASS_ENC = KEEP
CLASS_DEC = PATCHES
NEGATIVE = -1e30


def nn(left, right):
    return jnp.dot(left, right, preferred_element_type=high_type)


def nt(left, right):
    return lax.dot_general(left, right, (((1,), (1,)), ((), ())), preferred_element_type=high_type)


def tn(left, right):
    return lax.dot_general(left, right, (((0,), (0,)), ((), ())), preferred_element_type=high_type)


def standard(rows):
    mean = jnp.mean(rows, -1, keepdims=True)
    centred = rows - mean
    spread = jnp.mean(centred * centred, -1, keepdims=True)
    rate = lax.rsqrt(spread + norm_eps)
    return centred * rate, rate


def standard_back(unit, rate, grad):
    return rate * (grad - jnp.mean(grad, -1, keepdims=True) - unit * jnp.mean(grad * unit, -1, keepdims=True))


def col_sum(rows):
    return jnp.sum(rows.astype(high_type), 0, keepdims=True)


def gelu_pair(value):
    size = jnp.abs(value)
    below = 1.0 + (0.3275911 * math.sqrt(0.5)) * size
    t = pl.reciprocal(below, approx=True)
    t = t * (2.0 - below * t)
    t = t * (2.0 - below * t)
    fall = jnp.exp(-0.5 * value * value)
    series = 1.061405429
    for item in (-1.453152027, 1.421413741, -0.284496736, 0.254829592):
        series = series * t + item
    tail = 0.5 * series * t * fall
    part = jnp.where(value < 0.0, tail, 1.0 - tail)
    return value * part, part + value * fall * (1.0 / math.sqrt(2.0 * math.pi))


def three_way(value):
    high = value.astype(low_type)
    rest = value - high.astype(high_type)
    middle = rest.astype(low_type)
    return high, middle, (rest - middle.astype(high_type)).astype(low_type)


def place_rows(picks, value):
    parts = three_way(value)
    return nn(picks, parts[0]) + nn(picks, parts[1]) + nn(picks, parts[2])


def stack_heads(value, heads):
    width = LANES // heads
    lane = lax.broadcasted_iota(jnp.int32, value.shape, 1) // width
    return jnp.concatenate([jnp.where(lane == head, value, jnp.zeros_like(value)) for head in range(heads)], 0)


def merge_heads(stacked, heads):
    rows = stacked.shape[0] // heads
    width = LANES // heads
    lane = lax.broadcasted_iota(jnp.int32, (rows, LANES), 1) // width
    merged = stacked[:rows]
    for head in range(1, heads):
        merged = jnp.where(lane == head, stacked[head * rows : (head + 1) * rows], merged)
    return merged


def attend(query, key, value, heads, length):
    scores = nt(stack_heads(query, heads), key)
    column = lax.broadcasted_iota(jnp.int32, scores.shape, 1)
    scores = jnp.where(column < length, scores, NEGATIVE)
    raised = jnp.exp(scores - jnp.max(scores, -1, keepdims=True))
    attention = (raised / jnp.sum(raised, -1, keepdims=True)).astype(low_type)
    return merge_heads(nn(attention, value), heads)


def attend_back(query, key, value, grad, heads, length):
    queries = stack_heads(query, heads)
    grads = stack_heads(grad, heads)
    scores = nt(key, queries)
    place = lax.broadcasted_iota(jnp.int32, scores.shape, 0)
    scores = jnp.where(place < length, scores, NEGATIVE)
    raised = jnp.exp(scores - jnp.max(scores, 0, keepdims=True))
    attention = raised * (1.0 / jnp.sum(raised, 0, keepdims=True))
    inner = nt(value, grads)
    grad_scores = (attention * (inner - jnp.sum(inner * attention, 0, keepdims=True))).astype(low_type)
    grad_value = nn(attention.astype(low_type), grads)
    grad_key = nn(grad_scores, queries)
    grad_query = merge_heads(tn(grad_scores, key), heads)
    return grad_query, grad_key, grad_value


def attend_back_many(batch, query, key, value, grad, heads, length):
    rows = query.shape[0] // batch
    spans = [slice(image * rows, (image + 1) * rows) for image in range(batch)]
    queries = [stack_heads(query[span], heads) for span in spans]
    grads = [stack_heads(grad[span], heads) for span in spans]
    scores = jnp.concatenate([nt(key[span], item) for span, item in zip(spans, queries)], 0)
    inner = jnp.concatenate([nt(value[span], item) for span, item in zip(spans, grads)], 0)
    scores = scores.reshape(batch, rows, scores.shape[1])
    inner = inner.reshape(batch, rows, inner.shape[1])
    place = lax.broadcasted_iota(jnp.int32, scores.shape, 1)
    scores = jnp.where(place < length, scores, NEGATIVE)
    raised = jnp.exp(scores - jnp.max(scores, 1, keepdims=True))
    attention = raised * (1.0 / jnp.sum(raised, 1, keepdims=True))
    grad_scores = (attention * (inner - jnp.sum(inner * attention, 1, keepdims=True))).astype(low_type)
    attention = attention.astype(low_type)
    grad_value = [nn(attention[image], grads[image]) for image in range(batch)]
    grad_key = [nn(grad_scores[image], queries[image]) for image in range(batch)]
    grad_query = [merge_heads(tn(grad_scores[image], key[spans[image]]), heads) for image in range(batch)]
    return tuple(jnp.concatenate(item, 0) for item in (grad_query, grad_key, grad_value))


def wide_kernel(blocks, wide):
    count, _, width = blocks.shape
    for index in range(count):
        wide[:, index * width : (index + 1) * width] = blocks[index]


def enc_embed(batch, pick, patches, wide, vec, pos, kept, start):
    rows = ENC_ROWS
    for image in range(batch):
        span = pl.ds(image * rows, rows)
        kept[span] = nn(pick[image], patches[image]).astype(low_type)
    start[...] = nn(kept[...], wide[:, :D]) + vec[0:1]
    parts = three_way(pos[...])
    for image in range(batch):
        span = pl.ds(image * rows, rows)
        picks = pick[image]
        placed = nn(picks, parts[0]) + nn(picks, parts[1]) + nn(picks, parts[2])
        inner = lax.broadcasted_iota(jnp.int32, placed.shape, 0)
        start[span] = jnp.where(inner == CLASS_ENC, vec[1:2], start[span] + placed)


def enc_project(wide, vec, start, normed, qkv):
    unit, _ = standard(start[...])
    normed[...] = (unit * vec[2:3] + vec[3:4]).astype(low_type)
    scale = 1.0 / math.sqrt(D // HE)
    rows_in = normed[...]
    qkv[:, :D] = ((nn(rows_in, wide[:, D : 2 * D]) + vec[4:5]) * scale).astype(low_type)
    qkv[:, D : 2 * D] = nn(rows_in, wide[:, 2 * D : 3 * D]).astype(low_type)
    qkv[:, 2 * D :] = (nn(rows_in, wide[:, 3 * D : 4 * D]) + vec[5:6]).astype(low_type)


def enc_mix(batch, qkv, mixed):
    rows = ENC_ROWS
    heads = LANES * HE // D
    for image in range(batch):
        span = pl.ds(image * rows, rows)
        for group in range(D // LANES):
            lane = group * LANES
            mixed[span, lane : lane + LANES] = attend(
                qkv[span, lane : lane + LANES],
                qkv[span, D + lane : D + lane + LANES],
                qkv[span, 2 * D + lane : 2 * D + lane + LANES],
                heads,
                KEEP + 1,
            ).astype(low_type)


def enc_join(wide, vec, start, mixed, middle, normed_two):
    middle[...] = start[...] + (nn(mixed[...], wide[:, 4 * D :]) + vec[6:7])
    unit, _ = standard(middle[...])
    normed_two[...] = (unit * vec[7:8] + vec[8:9]).astype(low_type)


def enc_attend_kernel(batch, pick, patches, wide, vec, pos, kept, start, normed, qkv, mixed, middle, normed_two):
    enc_embed(batch, pick, patches, wide, vec, pos, kept, start)
    enc_project(wide, vec, start, normed, qkv)
    enc_mix(batch, qkv, mixed)
    enc_join(wide, vec, start, mixed, middle, normed_two)


def enc_ffn_kernel(last, middle, normed_two, ffn, vec, up_bias, slope, active, output, latent):
    step = pl.program_id(0)

    @pl.when(step == 0)
    def _():
        output[...] = middle[...] + vec[9:10]

    value, gain = gelu_pair(nn(normed_two[...], ffn[0]) + up_bias[...])
    slope[...] = gain
    value = value.astype(low_type)
    active[...] = value
    output[...] += nt(value, ffn[1])

    @pl.when(step == last)
    def _():
        unit, _ = standard(output[...])
        latent[...] = (unit * vec[10:11] + vec[11:12]).astype(low_type)


def dec_attend_kernel(latent, proj, picked, pos, wide, vec, start, normed, qkv, mixed, middle, normed_two):
    picks = picked[0]
    kept = jnp.sum(picks.astype(high_type), 1, keepdims=True)
    entry = nn(latent[...], proj[...]) + vec[0:1]
    rows = place_rows(picks, entry) + (1.0 - kept) * vec[1:2] + pos[...]
    start[...] = rows
    unit, _ = standard(rows)
    rows_in = (unit * vec[2:3] + vec[3:4]).astype(low_type)
    normed[...] = rows_in
    scale = 1.0 / math.sqrt(E // HD)
    qkv[:, :E] = ((nn(rows_in, wide[0, :, :E]) + vec[4:5]) * scale).astype(low_type)
    qkv[:, E : 2 * E] = nn(rows_in, wide[0, :, E : 2 * E]).astype(low_type)
    qkv[:, 2 * E :] = (nn(rows_in, wide[0, :, 2 * E : 3 * E]) + vec[5:6]).astype(low_type)
    heads = LANES * HD // E
    for group in range(E // LANES):
        lane = group * LANES
        mixed[:, lane : lane + LANES] = attend(
            qkv[:, lane : lane + LANES],
            qkv[:, E + lane : E + lane + LANES],
            qkv[:, 2 * E + lane : 2 * E + lane + LANES],
            heads,
            PATCHES + 1,
        ).astype(low_type)
    total = rows + (nn(mixed[...], wide[0, :, 3 * E :]) + vec[6:7])
    middle[...] = total
    unit, _ = standard(total)
    normed_two[...] = (unit * vec[7:8] + vec[8:9]).astype(low_type)


def send_tiles(acc, blob, sem, tiles, rows, per_block, base, stride):
    def go(index, carry):
        tile, part = index // 4, index % 4
        block, inner = tile // per_block, tile % per_block
        pltpu.make_async_copy(
            acc.at[tile, pl.ds(pl.multiple_of(part * rows, 16), rows)],
            blob.at[block, part, pl.ds(pl.multiple_of(base + inner * stride, 16), rows)],
            sem,
        ).start()
        return carry

    lax.fori_loop(0, tiles * 4, go, 0)


def wait_tiles(acc, sem):
    pltpu.make_async_copy(acc, acc, sem).wait()


def dec_ffn_kernel(images, last, count, middle, normed_two, mixed, pixels, picked, weights, head, vec, up_bias, head_bias,
                   grad_middle, grad_mixed, grad_head, vec_grad, up_grad, bias_grad, loss, blob,
                   active, slope, acc_up, acc_down, acc_out, sems):
    step = pl.program_id(0)
    source = normed_two[...]
    rows = source.shape[0]

    @pl.when(step == 0)
    def _():
        grad_head[...] = jnp.zeros_like(grad_head)
        vec_grad[...] = jnp.zeros_like(vec_grad)
        up_grad[...] = jnp.zeros_like(up_grad)
        bias_grad[...] = jnp.zeros_like(bias_grad)
        loss[...] = jnp.zeros_like(loss)
        acc_up[...] = jnp.zeros_like(acc_up)
        acc_down[...] = jnp.zeros_like(acc_down)
        acc_out[...] = jnp.zeros_like(acc_out)

    wide = 512
    total = middle[...] + vec[9:10]
    for place in range(0, H, wide):
        span = slice(place, place + wide)
        value, gain = gelu_pair(nn(source, weights[1, :, span]) + up_bias[:, span])
        slope[:, span] = gain
        value = value.astype(low_type)
        active[:, span] = value
        total = total + nt(value, weights[2, :, span])
    unit, rate = standard(total)
    final = (unit * vec[10:11] + vec[11:12]).astype(low_type)
    predict = nn(final, head[...]) + head_bias[...]
    target, _ = standard(pixels[...].astype(high_type))
    kept = jnp.concatenate([jnp.sum(picked[image].astype(high_type), 1, keepdims=True) for image in range(images)], 0)
    inner = lax.broadcasted_iota(jnp.int32, (rows, 1), 0) % DEC_ROWS
    masked = jnp.where(inner < PATCHES, 1.0 - kept, 0.0)
    error = predict - target
    loss[...] += jnp.sum(masked * error * error)
    grad_predict = (2.0 * masked * error / count).astype(low_type)
    grad_head[...] += tn(final, grad_predict)
    bias_grad[...] += col_sum(grad_predict)
    grad_final = nt(grad_predict, head[...])
    vec_grad[10:11] += col_sum(grad_final * unit)
    vec_grad[11:12] += col_sum(grad_final)
    grad_out = standard_back(unit, rate, grad_final * vec[10:11])
    grad_down = grad_out.astype(low_type)
    vec_grad[9:10] += col_sum(grad_down)
    grad_source = jnp.zeros_like(total)
    for place in range(0, H, wide):
        span = slice(place, place + wide)
        grad_up = (slope[:, span] * nn(grad_down, weights[2, :, span])).astype(low_type)
        up_grad[:, span] += col_sum(grad_up)
        grad_source = grad_source + nt(grad_up, weights[1, :, span])
        piece = tn(grad_down, active[:, span])
        other = tn(source, grad_up)
        for tile in range(wide // LANES):
            lane = slice(tile * LANES, (tile + 1) * LANES)
            acc_down[place // LANES + tile] += piece[:, lane]
            acc_up[place // LANES + tile] += other[:, lane]
    unit, rate = standard(middle[...])
    vec_grad[7:8] += col_sum(grad_source * unit)
    vec_grad[8:9] += col_sum(grad_source)
    grad_rows = standard_back(unit, rate, grad_source * vec[7:8]) + grad_out
    grad_middle[...] = grad_rows
    branch = grad_rows.astype(low_type)
    vec_grad[6:7] += col_sum(branch)
    piece = tn(mixed[...], branch)
    for tile in range(E // LANES):
        acc_out[tile] += piece[:, tile * LANES : (tile + 1) * LANES]
    grad_mixed[...] = nt(branch, weights[0, :, 3 * E :]).astype(low_type)

    @pl.when(step == last)
    def _():
        rows_block = E // 4
        send_tiles(acc_up, blob, sems.at[0], H // LANES, rows_block, 2, 2176, rows_block)
        send_tiles(acc_down, blob, sems.at[1], H // LANES, rows_block, 2, 2432, rows_block)
        send_tiles(acc_out, blob.at[pl.ds(6, 2)], sems.at[2], E // LANES, rows_block, 2, 1920, rows_block)
        wait_tiles(acc_up, sems.at[0])
        wait_tiles(acc_down, sems.at[1])
        wait_tiles(acc_out, sems.at[2])


def dec_back_kernel(last, blob_in, qkv, normed, start, grad_middle, grad_mixed, pick, picked, weights, vec,
                    grad_entry, vec_grad, blob, grads, acc, sem):
    step = pl.program_id(0)

    @pl.when(step == 0)
    def _():
        vec_grad[...] = jnp.zeros_like(vec_grad)
        acc[...] = jnp.zeros_like(acc)

    scale = 1.0 / math.sqrt(E // HD)
    heads = LANES * HD // E
    for group in range(E // LANES):
        lane = group * LANES
        span = slice(lane, lane + LANES)
        query, key, value = attend_back(
            qkv[:, lane : lane + LANES],
            qkv[:, E + lane : E + lane + LANES],
            qkv[:, 2 * E + lane : 2 * E + lane + LANES],
            grad_mixed[:, span],
            heads,
            PATCHES + 1,
        )
        grads[:, span] = (query * scale).astype(low_type)
        grads[:, E + lane : E + lane + LANES] = key.astype(low_type)
        grads[:, 2 * E + lane : 2 * E + lane + LANES] = value.astype(low_type)
    vec_grad[4:5] += col_sum(grads[:, :E])
    vec_grad[5:6] += col_sum(grads[:, 2 * E :])
    rows = normed[...]
    for part in range(3):
        piece = tn(rows, grads[:, part * E : (part + 1) * E])
        for tile in range(E // LANES):
            acc[part * (E // LANES) + tile] += piece[:, tile * LANES : (tile + 1) * LANES]
    grad_normed = nt(grads[...], weights[0, :, : 3 * E])
    unit, rate = standard(start[...])
    vec_grad[2:3] += col_sum(grad_normed * unit)
    vec_grad[3:4] += col_sum(grad_normed)
    grad_rows = standard_back(unit, rate, grad_normed * vec[2:3]) + grad_middle[...]
    kept = jnp.sum(picked[0].astype(high_type), 1, keepdims=True)
    vec_grad[1:2] += col_sum((1.0 - kept) * grad_rows)
    grad_entry[...] = nn(pick[0], grad_rows.astype(low_type)).astype(low_type)

    @pl.when(step == last)
    def _():
        rows_block = E // 4
        send_tiles(acc, blob, sem, 3 * E // LANES, rows_block, 2, 1920, rows_block)
        wait_tiles(acc, sem)


def enc_ffn_back_kernel(last, blob_in, grad_entry, latent, output, middle, normed_two, slope, active, ffn, proj, vec,
                        grad_middle, vec_grad, up_grad, entry_grad, blob,
                        grad_out, grad_down, grad_source, folded, acc_up, acc_down, fold_sem, sems):
    step = pl.program_id(0)
    fold_copy = pltpu.make_async_copy(folded, blob.at[:, :, pl.ds(2688, 96)], fold_sem)
    part_rows = D // 4

    @pl.when(step == 0)
    def _():
        vec_grad[...] = jnp.zeros_like(vec_grad)
        entries = grad_entry[...]
        entry_grad[...] = col_sum(entries)
        grad_proj = tn(latent[...], entries)
        lane = lax.broadcasted_iota(jnp.int32, (96, LANES), 1)
        for part in range(4):
            for pair in range(4):
                first = grad_proj[part * 192 : part * 192 + 96, pair * LANES : (pair + 1) * LANES]
                second = grad_proj[part * 192 + 96 : part * 192 + 192, pair * LANES : (pair + 1) * LANES]
                folded[2 * pair, part] = jnp.where(lane < 64, first, pltpu.roll(second, 64, 1))
                folded[2 * pair + 1, part] = jnp.where(lane < 64, pltpu.roll(first, 64, 1), second)
        fold_copy.start()
        grad_latent = nt(entries, proj[...])
        unit, rate = standard(output[...])
        vec_grad[10:11] = col_sum(grad_latent * unit)
        vec_grad[11:12] = col_sum(grad_latent)
        rows = standard_back(unit, rate, grad_latent * vec[10:11])
        grad_out[...] = rows
        grad_down[...] = rows.astype(low_type)
        vec_grad[9:10] = col_sum(rows.astype(low_type))
        grad_source[...] = jnp.zeros_like(grad_source)

    slot = step % 2

    @pl.when(step >= 2)
    def _():
        wait_tiles(acc_up.at[slot], sems.at[0, slot])
        wait_tiles(acc_down.at[slot], sems.at[1, slot])

    grads = grad_down[...]
    grad_up = (slope[...] * nn(grads, ffn[1])).astype(low_type)
    up_grad[...] = col_sum(grad_up)
    grad_source[...] += nt(grad_up, ffn[0])
    piece = tn(grads, active[...])
    other = tn(normed_two[...], grad_up)
    count = grad_up.shape[1] // LANES
    for tile in range(count):
        lane = slice(tile * LANES, (tile + 1) * LANES)
        acc_down[slot, tile] = piece[:, lane]
        acc_up[slot, tile] = other[:, lane]

    def go(index, carry):
        tile, part = index // 4, index % 4
        place = step * count + tile
        block, inner = place // 3, place % 3
        rows = pl.ds(pl.multiple_of(part * part_rows, 16), part_rows)
        for number, (acc, base) in enumerate(((acc_up, 768), (acc_down, 1344))):
            pltpu.make_async_copy(
                acc.at[slot, tile, rows],
                blob.at[block, part, pl.ds(pl.multiple_of(base + inner * part_rows, 16), part_rows)],
                sems.at[number, slot],
            ).start()
        return carry

    lax.fori_loop(0, count * 4, go, 0)

    @pl.when(step == last)
    def _():
        unit, rate = standard(middle[...])
        vec_grad[7:8] = col_sum(grad_source[...] * unit)
        vec_grad[8:9] = col_sum(grad_source[...])
        grad_rows = standard_back(unit, rate, grad_source[...] * vec[7:8]) + grad_out[...]
        grad_middle[...] = grad_rows
        vec_grad[6:7] = col_sum(grad_rows.astype(low_type))
        fold_copy.wait()
        for item in (0, 1):
            wait_tiles(acc_up.at[item], sems.at[0, item])
            wait_tiles(acc_down.at[item], sems.at[1, item])


def enc_back_kernel(batch, blob_in, qkv, kept, normed, start, mixed, grad_middle, wide, vec,
                    vec_grad, blob, grads, grad_wide, tiles, sem):
    rows = ENC_ROWS
    vec_grad[...] = jnp.zeros_like(vec_grad)
    branch = grad_middle[...].astype(low_type)
    grad_mixed = nt(branch, wide[:, 4 * D :]).astype(low_type)
    grad_wide[:, 4 * D :] = tn(mixed[...], branch)
    scale = 1.0 / math.sqrt(D // HE)
    heads = LANES * HE // D
    for group in range(D // LANES):
        lane = group * LANES
        query, key, value = attend_back_many(
            batch,
            qkv[:, lane : lane + LANES],
            qkv[:, D + lane : D + lane + LANES],
            qkv[:, 2 * D + lane : 2 * D + lane + LANES],
            grad_mixed[:, lane : lane + LANES],
            heads,
            KEEP + 1,
        )
        grads[:, lane : lane + LANES] = (query * scale).astype(low_type)
        grads[:, D + lane : D + lane + LANES] = key.astype(low_type)
        grads[:, 2 * D + lane : 2 * D + lane + LANES] = value.astype(low_type)
    vec_grad[4:5] = col_sum(grads[:, :D])
    vec_grad[5:6] = col_sum(grads[:, 2 * D :])
    rows_in = normed[...]
    for part in range(3):
        grad_wide[:, (part + 1) * D : (part + 2) * D] = tn(rows_in, grads[:, part * D : (part + 1) * D])
    width = 5 * D // 8
    tall = D // 4

    def assemble(block):
        for part in range(4):
            span = slice(part * tall, (part + 1) * tall)
            piece = grad_wide[span, block * width : (block + 1) * width]
            for tile in range(4):
                size = min(LANES, width - tile * LANES)
                value = piece[:, tile * LANES : tile * LANES + size]
                if size < LANES:
                    value = jnp.concatenate([value, jnp.zeros((tall, LANES - size), high_type)], 1)
                tiles[block, part, tile * tall : (tile + 1) * tall] = value
        pltpu.make_async_copy(tiles.at[block], blob.at[block, :, pl.ds(0, 4 * tall)], sem).start()

    for block in range(2, 8):
        assemble(block)
    grad_normed = nt(grads[...], wide[:, D : 4 * D])
    unit, rate = standard(start[...])
    vec_grad[2:3] = col_sum(grad_normed * unit)
    vec_grad[3:4] = col_sum(grad_normed)
    grad_rows = standard_back(unit, rate, grad_normed * vec[2:3]) + grad_middle[...]
    inner = lax.broadcasted_iota(jnp.int32, (grad_rows.shape[0], 1), 0) % rows
    vec_grad[1:2] = col_sum(jnp.where(inner == CLASS_ENC, grad_rows, 0.0))
    embed = jnp.where(inner < KEEP, grad_rows, 0.0).astype(low_type)
    vec_grad[0:1] = col_sum(embed)
    grad_wide[:, :D] = tn(kept[...], embed)
    assemble(0)
    assemble(1)
    wait_tiles(tiles, sem)


def adam_parts(weight, grad, first, second, decay):
    first_new = 0.5 * first + 0.5 * grad
    second_new = 0.5 * second + 0.5 * grad * grad
    bias = 1.0 - 0.5**STEP
    direction = first_new / bias / (jnp.sqrt(second_new / bias) + 1e-08)
    return weight - 0.02 * (direction + decay * weight), first_new, second_new


def adam_kernel(count, *refs):
    summed, head, small = refs[:3]
    ins, outs, loss = refs[3:24], refs[24:45], refs[45]

    def update(index, place, grad, decay=0.05):
        for target, value in zip(
            range(3), adam_parts(ins[index][place], grad, ins[7 + index][place], ins[14 + index][place], decay)
        ):
            outs[7 * target + index][place] = value

    base = 0
    for index, lead, tall, width in ((0, None, 192, 480), (1, 0, 192, 384), (1, 1, 192, 384),
                                     (3, None, 128, 256), (4, 0, 128, 256), (4, 1, 128, 256)):
        for lane in range(0, width, LANES):
            size = min(LANES, width - lane)
            place = (slice(None), slice(lane, lane + size))
            update(index, place if lead is None else (lead,) + place, summed[base : base + tall, :size])
            base += tall
    folded = summed[base : base + 96]
    turned = jnp.concatenate([folded, jnp.zeros((32, LANES), high_type)], 0).T
    update(2, (slice(None), slice(0, 96)), turned[:64, :96])
    update(2, (slice(None), slice(96, 192)), turned[64:, :96])
    update(5, (slice(None),), head[...])
    tall = ins[6].shape[0]
    update(6, (slice(None),), small[:tall], 0.0)
    loss[...] = small[tall : tall + 1, :1] / count


SMALL_ROWS = 256
SMALL_PARTS = ((12, D), (1, F), (12, E), (1, H), (1, P_SIZE))


def prepare_kernel(enc_w, enc_ffn, proj_turned, dec_w, dec_ffn, head, smalls, shuffle, patches,
                   own_enc, own_ffn, own_proj, own_dec, head_low, enc_vec, enc_up, dec_vec, dec_up, head_bias,
                   pick, picked, padded):
    own_enc[...] = enc_w[...].astype(low_type)
    own_ffn[...] = enc_ffn[...].astype(low_type)
    own_proj[...] = proj_turned[...].T.astype(low_type)
    own_dec[0] = dec_w[...].astype(low_type)
    own_dec[1] = dec_ffn[0].astype(low_type)
    own_dec[2] = dec_ffn[1].astype(low_type)
    head_low[...] = head[...].astype(low_type)
    place = 0
    for target in (enc_vec, enc_up, dec_vec, dec_up, head_bias):
        for index in range(target.shape[0]):
            for lane in range(0, target.shape[1], LANES):
                target[index : index + 1, lane : lane + LANES] = smalls[place : place + 1]
                place += 1
    slot = lax.broadcasted_iota(jnp.int32, (DEC_ROWS, ENC_ROWS), 0)
    order = lax.broadcasted_iota(jnp.int32, (DEC_ROWS, ENC_ROWS), 1)
    for image in range(patches.shape[0]):
        keep = jnp.where(order < KEEP, shuffle[image : image + 1, :ENC_ROWS], jnp.where(order == CLASS_ENC, CLASS_DEC, -1))
        chosen = jnp.where(keep == slot, 1.0, 0.0)
        picked[image] = chosen.astype(low_type)
        pick[image] = chosen.T.astype(low_type)
        padded[image, DEC_ROWS - 16 :] = jnp.zeros((16, P_SIZE), low_type)
        padded[image, :PATCHES] = patches[image]


def prepare(enc_w, enc_ffn, dec_proj, dec_w, dec_ffn, head, smalls, shuffle, patches):
    batch = patches.shape[0]
    shape = jax.ShapeDtypeStruct
    outs = [shape(item.shape, low_type) for item in (enc_w, enc_ffn, dec_proj)]
    outs += [shape((3,) + dec_w.shape, low_type), shape(head.shape, low_type)]
    outs += [shape(item, high_type) for item in SMALL_PARTS]
    outs += [
        shape((batch, ENC_ROWS, DEC_ROWS), low_type),
        shape((batch, DEC_ROWS, ENC_ROWS), low_type),
        shape((batch, DEC_ROWS, P_SIZE), low_type),
    ]
    return pl.pallas_call(
        prepare_kernel,
        out_shape=tuple(outs),
        in_specs=[whole()] * 9,
        out_specs=[whole()] * 13,
        compiler_params=params(),
        name="prepare",
    )(enc_w, enc_ffn, dec_proj.T, dec_w, dec_ffn, head, smalls.reshape(-1, LANES), shuffle, patches)


def pack_kernel(enc_one, enc_two, enc_up, dec_one, dec_two, entry, dec_up, head_bias, loss, small):
    place = 0

    def put(value):
        nonlocal place
        for index in range(value.shape[0]):
            for lane in range(0, value.shape[1], LANES):
                small[place : place + 1] = value[index : index + 1, lane : lane + LANES]
                place += 1

    put(enc_one[...] + enc_two[...])
    put(enc_up[...])
    put(entry[...])
    put(dec_one[1:] + dec_two[1:])
    put(dec_up[...])
    put(head_bias[...])
    small[place : place + 1] = loss[:1]
    place += 1
    small[place:] = jnp.zeros((SMALL_ROWS - place, LANES), high_type)


def table_of(width, rows):
    quarter = width // 4
    omega = (np.float32(1.0) / np.float32(10000.0) ** (np.arange(quarter, dtype=np.float32) / np.float32(quarter))).astype(np.float32)
    coord = np.arange(SIDE * SIDE)

    def half(place):
        angle = place.astype(np.float32)[:, None] * omega[None, :]
        return np.concatenate([np.sin(angle), np.cos(angle)], 1)

    table = np.concatenate([half(coord // SIDE), half(coord % SIDE)], 1).astype(np.float32)
    return np.concatenate([table, np.zeros((rows - table.shape[0], width), np.float32)], 0)


def whole():
    return pl.BlockSpec(memory_space=pltpu.VMEM)


def hbm():
    return pl.BlockSpec(memory_space=pltpu.HBM)


def params(**more):
    return pltpu.CompilerParams(vmem_limit_bytes=60 << 20, **more)


def by_image(*block):
    return pl.BlockSpec(block, lambda i: (i,) + (0,) * (len(block) - 1))


def fixed(*block):
    return pl.BlockSpec(block, lambda i: (0,) * len(block))


def encoder_shapes(batch):
    rows = batch * ENC_ROWS
    shape = jax.ShapeDtypeStruct
    first = (
        shape((rows, D), low_type),
        shape((rows, D), high_type),
        shape((rows, D), low_type),
        shape((rows, 3 * D), low_type),
        shape((rows, D), low_type),
        shape((rows, D), high_type),
        shape((rows, D), low_type),
    )
    second = (
        shape((rows, F), high_type),
        shape((rows, F), low_type),
        shape((rows, D), high_type),
        shape((rows, D), low_type),
    )
    return first, second


def encode_images(enc_blocks, enc_ffn, enc_vec, enc_up, pick, padded):
    batch = padded.shape[0]
    rows = batch * ENC_ROWS
    first, second = encoder_shapes(batch)
    wide = pl.pallas_call(
        wide_kernel,
        out_shape=jax.ShapeDtypeStruct((D, 5 * D), low_type),
        in_specs=[whole()],
        out_specs=whole(),
        compiler_params=params(),
        name="wide",
    )(enc_blocks)
    early = pl.pallas_call(
        functools.partial(enc_attend_kernel, batch),
        out_shape=first,
        in_specs=[whole()] * 5,
        out_specs=[whole()] * 7,
        compiler_params=params(),
        name="enc_attend",
    )(pick, padded, wide, enc_vec, jnp.asarray(table_of(D, DEC_ROWS)))
    chunk = 512
    late = pl.pallas_call(
        functools.partial(enc_ffn_kernel, F // chunk - 1),
        grid=(F // chunk,),
        out_shape=second,
        in_specs=[
            fixed(rows, D),
            fixed(rows, D),
            pl.BlockSpec((2, D, chunk), lambda i: (0, 0, i)),
            fixed(12, D),
            pl.BlockSpec((1, chunk), lambda i: (0, i)),
        ],
        out_specs=[
            pl.BlockSpec((rows, chunk), lambda i: (0, i)),
            pl.BlockSpec((rows, chunk), lambda i: (0, i)),
            fixed(rows, D),
            fixed(rows, D),
        ],
        compiler_params=params(),
        name="enc_ffn",
    )(early[5], early[6], enc_ffn, enc_vec, enc_up)
    return wide, early + tuple(late)


def local_grads(wide, enc_ffn, proj, dec3, encoded, head_low, vectors, pick, picked, padded, count):
    enc_vec, _, dec_vec, dec_up, head_bias = vectors
    kept, start, normed, qkv, mixed, middle, normed_two, slope, active, enc_out, latent = encoded
    batch = padded.shape[0]
    shape = jax.ShapeDtypeStruct
    dec_pos = jnp.asarray(table_of(E, DEC_ROWS))
    rows, dec_rows = batch * ENC_ROWS, batch * DEC_ROWS
    chunk = 512

    dec_start, dec_normed, dec_qkv, dec_mixed, dec_middle, dec_normed_two = pl.pallas_call(
        dec_attend_kernel,
        grid=(batch,),
        out_shape=(
            shape((dec_rows, E), high_type),
            shape((dec_rows, E), low_type),
            shape((dec_rows, 3 * E), low_type),
            shape((dec_rows, E), low_type),
            shape((dec_rows, E), high_type),
            shape((dec_rows, E), low_type),
        ),
        in_specs=[
            by_image(ENC_ROWS, D),
            fixed(D, E),
            by_image(1, DEC_ROWS, ENC_ROWS),
            fixed(DEC_ROWS, E),
            fixed(1, E, 4 * E),
            fixed(12, E),
        ],
        out_specs=[
            by_image(DEC_ROWS, E),
            by_image(DEC_ROWS, E),
            by_image(DEC_ROWS, 3 * E),
            by_image(DEC_ROWS, E),
            by_image(DEC_ROWS, E),
            by_image(DEC_ROWS, E),
        ],
        compiler_params=params(),
        name="dec_attend",
    )(latent, proj, picked, dec_pos, dec3, dec_vec)

    images = 2 if batch % 2 == 0 else 1
    block = images * DEC_ROWS
    blob_shape = shape((8, 4, 2784, LANES), high_type)
    vm = pltpu.VMEM
    dma = pltpu.SemaphoreType.DMA
    grad_middle, grad_mixed, grad_head, dec_grad_one, dec_up_grad, head_bias_grad, loss, blob = pl.pallas_call(
        functools.partial(dec_ffn_kernel, images, batch // images - 1, count),
        grid=(batch // images,),
        out_shape=(
            shape((dec_rows, E), high_type),
            shape((dec_rows, E), low_type),
            shape((E, P_SIZE), high_type),
            shape((12, E), high_type),
            shape((1, H), high_type),
            shape((1, P_SIZE), high_type),
            shape((8, LANES), high_type),
            blob_shape,
        ),
        in_specs=[
            by_image(block, E),
            by_image(block, E),
            by_image(block, E),
            by_image(block, P_SIZE),
            by_image(images, DEC_ROWS, ENC_ROWS),
            fixed(3, E, H),
            fixed(E, P_SIZE),
            fixed(12, E),
            fixed(1, H),
            fixed(1, P_SIZE),
        ],
        out_specs=[
            by_image(block, E),
            by_image(block, E),
            fixed(E, P_SIZE),
            fixed(12, E),
            fixed(1, H),
            fixed(1, P_SIZE),
            fixed(8, LANES),
            hbm(),
        ],
        scratch_shapes=[
            vm((block, H), low_type),
            vm((block, H), high_type),
            vm((H // LANES, E, LANES), high_type),
            vm((H // LANES, E, LANES), high_type),
            vm((E // LANES, E, LANES), high_type),
            dma((3,)),
        ],
        compiler_params=params(),
        name="dec_ffn",
    )(dec_middle, dec_normed_two, dec_mixed, padded.reshape(dec_rows, P_SIZE), picked, dec3, head_low, dec_vec, dec_up, head_bias)

    grad_entry, dec_grad_two, blob = pl.pallas_call(
        functools.partial(dec_back_kernel, batch - 1),
        grid=(batch,),
        out_shape=(shape((rows, E), low_type), shape((12, E), high_type), blob_shape),
        in_specs=[
            hbm(),
            by_image(DEC_ROWS, 3 * E),
            by_image(DEC_ROWS, E),
            by_image(DEC_ROWS, E),
            by_image(DEC_ROWS, E),
            by_image(DEC_ROWS, E),
            by_image(1, ENC_ROWS, DEC_ROWS),
            by_image(1, DEC_ROWS, ENC_ROWS),
            fixed(1, E, 4 * E),
            fixed(12, E),
        ],
        out_specs=[by_image(ENC_ROWS, E), fixed(12, E), hbm()],
        scratch_shapes=[vm((DEC_ROWS, 3 * E), low_type), vm((3 * E // LANES, E, LANES), high_type), dma],
        input_output_aliases={0: 2},
        compiler_params=params(),
        name="dec_back",
    )(blob, dec_qkv, dec_normed, dec_start, grad_middle, grad_mixed, pick, picked, dec3, dec_vec)

    enc_grad_middle, enc_grad_one, enc_up_grad, entry_grad, blob = pl.pallas_call(
        functools.partial(enc_ffn_back_kernel, F // chunk - 1),
        grid=(F // chunk,),
        out_shape=(
            shape((rows, D), high_type),
            shape((12, D), high_type),
            shape((1, F), high_type),
            shape((1, E), high_type),
            blob_shape,
        ),
        in_specs=[
            hbm(),
            fixed(rows, E),
            fixed(rows, D),
            fixed(rows, D),
            fixed(rows, D),
            fixed(rows, D),
            pl.BlockSpec((rows, chunk), lambda i: (0, i)),
            pl.BlockSpec((rows, chunk), lambda i: (0, i)),
            pl.BlockSpec((2, D, chunk), lambda i: (0, 0, i)),
            fixed(D, E),
            fixed(12, D),
        ],
        out_specs=[
            fixed(rows, D),
            fixed(12, D),
            pl.BlockSpec((1, chunk), lambda i: (0, i)),
            fixed(1, E),
            hbm(),
        ],
        scratch_shapes=[
            vm((rows, D), high_type),
            vm((rows, D), low_type),
            vm((rows, D), high_type),
            vm((8, 4, 96, LANES), high_type),
            vm((2, chunk // LANES, D, LANES), high_type),
            vm((2, chunk // LANES, D, LANES), high_type),
            dma,
            dma((2, 2)),
        ],
        input_output_aliases={0: 4},
        compiler_params=params(),
        name="enc_ffn_back",
    )(blob, grad_entry, latent, enc_out, middle, normed_two, slope, active, enc_ffn, proj, enc_vec)
    enc_grad_two, blob = pl.pallas_call(
        functools.partial(enc_back_kernel, batch),
        out_shape=(shape((12, D), high_type), blob_shape),
        in_specs=[hbm()] + [whole()] * 8,
        out_specs=[whole(), hbm()],
        scratch_shapes=[
            vm((rows, 3 * D), low_type),
            vm((D, 5 * D), high_type),
            vm((8, 4, D, LANES), high_type),
            dma,
        ],
        input_output_aliases={0: 1},
        compiler_params=params(),
        name="enc_back",
    )(blob, qkv, kept, normed, start, mixed, enc_grad_middle, wide, enc_vec)
    small = pl.pallas_call(
        pack_kernel,
        out_shape=shape((SMALL_ROWS, LANES), high_type),
        in_specs=[whole()] * 9,
        out_specs=whole(),
        compiler_params=params(),
        name="pack",
    )(enc_grad_one, enc_grad_two, enc_up_grad, dec_grad_one, dec_grad_two, entry_grad, dec_up_grad, head_bias_grad, loss)
    return blob, grad_head, small


def untile(block, rows, width):
    tiles = -(-width // LANES)
    return block.reshape(tiles, rows, LANES).transpose(1, 0, 2).reshape(rows, tiles * LANES)[:, :width]


def unfold_proj(block):
    width = block.shape[1] // 2
    return jnp.concatenate([block[:, :width], block[:, width:]], 0)


def unpack_shards(blob):
    cuts = [0, 768, 576, 576, 256, 256, 256, 96]
    places = [sum(cuts[: index + 1]) for index in range(len(cuts))]
    piece = [blob[places[index] : places[index + 1]] for index in range(7)]
    return (
        untile(piece[0], 192, 480),
        jnp.stack([untile(piece[1], 192, 384), untile(piece[2], 192, 384)]),
        unfold_proj(piece[6]),
        untile(piece[3], 128, 256),
        jnp.stack([untile(piece[4], 128, 256), untile(piece[5], 128, 256)]),
    )


def whole_arrays(blob):
    col_size, row_size = blob.shape[:2]
    parts = jax.vmap(jax.vmap(unpack_shards))(blob)

    def joined(array):
        if array.ndim == 4:
            return array.transpose(1, 2, 0, 3).reshape(row_size * array.shape[2], col_size * array.shape[3])
        return array.transpose(2, 1, 3, 0, 4).reshape(2, row_size * array.shape[3], col_size * array.shape[4])

    return tuple(joined(item) for item in parts)


def on_small_plane():
    return lax.axis_size("row") == 4 and lax.axis_size("col") == 8


def gather_and_encode(shards, enc_vec, enc_up, pick, padded):
    if on_small_plane():
        ffn, proj, dec, wide, encoded = gather_encode(
            *shards, lax.axis_size("col") // 2, pick, padded, enc_vec, enc_up
        )
        return wide, ffn, proj.transpose(1, 0, 2).reshape(D, E), dec, encoded
    full = []
    for item in shards:
        rowed = lax.all_gather(item, "row", axis=item.ndim - 2, tiled=True)
        full.append(lax.all_gather(rowed, "col", axis=item.ndim - 1, tiled=True))
    blocks = full[0].reshape(D, 8, 5 * D // 8).transpose(1, 0, 2)
    wide, encoded = encode_images(blocks, full[1], enc_vec, enc_up, pick, padded)
    return wide, full[1], full[2], full[3], encoded


def apply_updates(blob, grad_head, small, count, params_now, firsts, seconds):
    summed_head = lax.psum(grad_head, ("row", "col"))
    if on_small_plane():
        summed, small = reduce_blocks(blob, small.reshape(32, 8, LANES), lax.axis_size("col") // 2, 6)
        flat = lambda group: group[:2] + (group[2].T,) + group[3:6] + (group[6].reshape(-1, LANES),)
        ins = flat(params_now) + flat(firsts) + flat(seconds)
        shape = jax.ShapeDtypeStruct
        outs = pl.pallas_call(
            functools.partial(adam_kernel, count),
            out_shape=tuple(shape(item.shape, high_type) for item in ins) + (shape((1, 1), high_type),),
            in_specs=[whole()] * 24,
            out_specs=[whole()] * 22,
            compiler_params=params(),
            name="adam",
        )(summed, summed_head, small.reshape(SMALL_ROWS, LANES), *ins)
        back = {2: lambda item: item.T, 6: lambda item: item.reshape(-1)}
        return [back.get(index % 7, lambda item: item)(item) for index, item in enumerate(outs[:21])], outs[21].reshape(())
    shards = []
    for item in whole_arrays(blob):
        done = lax.psum_scatter(item, "col", scatter_dimension=item.ndim - 1, tiled=True)
        shards.append(lax.psum_scatter(done, "row", scatter_dimension=item.ndim - 2, tiled=True))
    small = lax.psum(small, ("row", "col")).reshape(-1)
    size = params_now[6].shape[0]
    grads = tuple(shards) + (summed_head, small[:size])
    decays = (0.05,) * 6 + (0.0,)
    results = [adam_parts(*item) for item in zip(params_now, grads, firsts, seconds, decays)]
    return [item[kind] for kind in range(3) for item in results], small[size] / count


def body(
    patches,
    shuffle,
    enc_w,
    enc_ffn,
    dec_proj,
    dec_w,
    dec_ffn,
    head_w,
    smalls,
    first_enc_w,
    first_enc_ffn,
    first_dec_proj,
    first_dec_w,
    first_dec_ffn,
    first_head_w,
    first_smalls,
    second_enc_w,
    second_enc_ffn,
    second_dec_proj,
    second_dec_w,
    second_dec_ffn,
    second_head_w,
    second_smalls,
):
    prepared = prepare(enc_w, enc_ffn, dec_proj, dec_w, dec_ffn, head_w, smalls, shuffle, patches)
    shards, head_low, vectors, (pick, picked, padded) = prepared[:4], prepared[4], prepared[5:10], prepared[10:]
    wide, ffn, proj, dec, encoded = gather_and_encode(shards, vectors[0], vectors[1], pick, padded)
    count = patches.shape[0] * lax.axis_size("row") * lax.axis_size("col") * (PATCHES - KEEP) * P_SIZE
    blob, grad_head, small = local_grads(
        wide, ffn, proj, dec, encoded, head_low, vectors, pick, picked, padded, count
    )
    params_now = (enc_w, enc_ffn, dec_proj, dec_w, dec_ffn, head_w, smalls)
    firsts = (
        first_enc_w,
        first_enc_ffn,
        first_dec_proj,
        first_dec_w,
        first_dec_ffn,
        first_head_w,
        first_smalls,
    )
    seconds = (
        second_enc_w,
        second_enc_ffn,
        second_dec_proj,
        second_dec_w,
        second_dec_ffn,
        second_head_w,
        second_smalls,
    )
    outs, loss = apply_updates(blob, grad_head, small, count, params_now, firsts, seconds)
    return tuple(outs) + (loss,)


def solution(mesh):
    in_specs = (
        P(("row", "col"), None, None),
        P(("row", "col"), None),
        P("row", "col"),
        P(None, "row", "col"),
        P("row", "col"),
        P("row", "col"),
        P(None, "row", "col"),
        P(),
        P(),
        P("row", "col"),
        P(None, "row", "col"),
        P("row", "col"),
        P("row", "col"),
        P(None, "row", "col"),
        P(),
        P(),
        P("row", "col"),
        P(None, "row", "col"),
        P("row", "col"),
        P("row", "col"),
        P(None, "row", "col"),
        P(),
        P(),
    )
    out_specs = (
        P("row", "col"),
        P(None, "row", "col"),
        P("row", "col"),
        P("row", "col"),
        P(None, "row", "col"),
        P(),
        P(),
        P("row", "col"),
        P(None, "row", "col"),
        P("row", "col"),
        P("row", "col"),
        P(None, "row", "col"),
        P(),
        P(),
        P("row", "col"),
        P(None, "row", "col"),
        P("row", "col"),
        P("row", "col"),
        P(None, "row", "col"),
        P(),
        P(),
        P(),
    )
    return jax.shard_map(body, mesh=mesh, in_specs=in_specs, out_specs=out_specs, check_vma=False)
```
